32 devices in a mesh: head: 4 (over y, core), blk: 8 (over z, x).
Axes of the slice: x: 2, y: 2, z: 4, core: 2. Of those that a mesh axis runs over, the one named last changes fastest.
Arguments:
- tokens: bfloat16 [4, 2048, 1024], P(None, ('head', 'blk')), may hold values from -6 to 6
- chosen: int32 [4, 256], replicated, may hold values from 0 to 2047, as said below
- w_qkv: bfloat16 [1024, 3072], P(('head', 'blk')), may hold values from -0.1875 to 0.1875
- w_out: bfloat16 [1024, 1024], P(('head', 'blk')), may hold values from -1.5 to 1.5
- w_up: bfloat16 [1024, 4096], P(('head', 'blk')), may hold values from -0.1875 to 0.1875
- w_down: bfloat16 [4096, 1024], P(('head', 'blk')), may hold values from -0.09375 to 0.09375
- gain_attn: bfloat16 [1024], P(('head', 'blk')), may hold values from 0.099609375 to 1.8984375
- gain_mlp: bfloat16 [1024], P(('head', 'blk')), may hold values from 0.099609375 to 1.8984375
- router: bfloat16 [1024], P(('head', 'blk')), may hold values from -0.1875 to 0.1875
- cotangent: bfloat16 [4, 2048, 1024], P(None, ('head', 'blk')), may hold values from -6 to 6
Outputs:
- output: bfloat16 [4, 2048, 1024], P(None, ('head', 'blk'))
- grad_tokens: bfloat16 [4, 2048, 1024], P(None, ('head', 'blk'))
- grad_qkv: float32 [1024, 3072], P(('head', 'blk'))
- grad_out: float32 [1024, 1024], P(('head', 'blk'))
- grad_up: float32 [1024, 4096], P(('head', 'blk'))
- grad_down: float32 [4096, 1024], P(('head', 'blk'))
- grad_gain_attn: float32 [1024], P(('head', 'blk'))
- grad_gain_mlp: float32 [1024], P(('head', 'blk'))
- grad_router: float32 [1024], P(('head', 'blk'))
The draws below stay inside these ranges and needn't reach their ends.
Inputs may be any that keep to these rules, and one draw needn't show every extreme that they name: `chosen`: each row lists 256 distinct positions of one sequence in ascending order. Of the 64 positions that one device holds, at most 16 are listed; in every sequence some device holds exactly 16 and some device none.
All inputs are finite; a program needn't handle non-finite values.
Results may differ from the reference program's by a relative error of at most 0.024.
Values may be sent and summed in bfloat16 or wider, within the bound.
No kernel may reach another device: no remote copies, remote signals or barrier semaphores. Data moves between devices by JAX's collectives and lax.ppermute only.
A program may use at most 192 MiB of HBM per device.

```python
from functools import partial
import jax
import jax.numpy as jnp
from jax import lax

D = 1024
HEADS = 16
HDIM = 64
FF = 4096
SEG = 64
SEQS = 4
SHARDS = 32
LEN = 2048
ROUTED = 256
CAP = 16


def draw_chosen(key, part):

    def one_sequence(seq_key):
        key_pair, key_perm, key_rank = jax.random.split(seq_key, 3)
        half_count = SHARDS // 2
        amounts = jax.random.randint(key_pair, (half_count,), 0, CAP + 1)
        amounts = amounts.at[0].set(CAP)
        paired = jnp.concatenate([amounts, CAP - amounts]).astype(jnp.int32)
        order = jax.random.permutation(key_perm, SHARDS)
        shard_load = jnp.zeros((SHARDS,), jnp.int32).at[order].set(paired)
        noise = jax.random.randint(key_rank, (SHARDS, SEG), 0, 1 << 20) * SEG + jnp.arange(SEG, dtype=jnp.int32)[None, :]
        ranks = jnp.argsort(jnp.argsort(noise, axis=1), axis=1)
        marked = (ranks < shard_load[:, None]).reshape(LEN)
        return jnp.nonzero(marked, size=ROUTED)[0].astype(jnp.int32)
    seq_keys = jax.random.split(jax.random.fold_in(key, 7), SEQS)
    return jax.vmap(one_sequence)(seq_keys)


def spiked(entries, rng, source, target, blocks, factor):
    owner, partner = [(jnp.arange(entries.shape[position]) // (entries.shape[position] // blocks)).reshape([-1 if axis == position else 1 for axis in range(entries.ndim)]) for position in (source, target)]
    chosen = jax.random.permutation(rng, blocks)[partner]
    strong = (owner == chosen) | (owner == (partner + blocks // 2) % blocks)
    return jnp.where(strong, factor * entries, entries)


def block_scale(key, dims, cuts, smallest, largest):
    gain, own = 1.0, jax.random.fold_in(key, 6)
    for axis_at, parts in cuts:
        draws = jnp.exp(jax.random.uniform(jax.random.fold_in(own, axis_at), (parts,), jnp.float32, smallest / len(cuts), largest / len(cuts)))
        gain = gain * jnp.repeat(draws, dims[axis_at] // parts).reshape([-1 if axis == axis_at else 1 for axis in range(len(dims))])
    return gain


def centred(key, dims, deviation, most, cuts=(), kind=jnp.bfloat16):
    gain = block_scale(key, dims, cuts, -0.22, 0.18) if cuts else 1.0
    values = jax.random.normal(key, dims, jnp.float32) * deviation * gain
    return jnp.minimum(jnp.maximum(values, -most), most).astype(kind)


def heavy_noise(own_key, extent, width, limit, cuts, heavy, kind=jnp.bfloat16):
    array = width * jax.random.normal(own_key, extent, jnp.float32)
    if cuts:
        array = array * block_scale(own_key, extent, cuts, -0.22, 0.18)
    return jnp.clip(spiked(array, jax.random.fold_in(own_key, 3), *heavy), -limit, limit).astype(kind)


def setup_inputs(seed: int = 0) -> dict:
    key_list = jax.random.split(jax.random.key(seed), 11)
    tokens = heavy_noise(key_list[0], (SEQS, LEN, D), 1.0, 6.0, ((1, 32),), (1, 2, 32, 2.75))
    chosen = draw_chosen(jax.random.fold_in(key_list[10], 71), 0)
    w_qkv = centred(key_list[2], (D, 3 * D), D ** -0.5, 0.1875, ((0, 32),))
    w_out = centred(key_list[3], (D, D), (D // 64) ** -0.5, 1.5, ((0, 32),))
    w_up = centred(key_list[4], (D, FF), D ** -0.5, 0.1875, ((0, 32),))
    w_down = centred(key_list[5], (FF, D), FF ** -0.5, 0.09375, ((0, 32),))
    gain_attn = jnp.clip(1.0 + 0.18 * jax.random.normal(key_list[6], (D,), jnp.float32), 0.099609375, 1.8984375).astype(jnp.bfloat16)
    gain_mlp = jnp.clip(1.0 + 0.18 * jax.random.normal(key_list[7], (D,), jnp.float32), 0.099609375, 1.8984375).astype(jnp.bfloat16)
    router = centred(key_list[8], (D,), D ** -0.5, 0.1875, ((0, 32),))
    cotangent = centred(key_list[9], (SEQS, LEN, D), 1.0, 6.0, ((1, 32),))
    return {"tokens": tokens, "chosen": chosen, "w_qkv": w_qkv, "w_out": w_out, "w_up": w_up, "w_down": w_down, "gain_attn": gain_attn, "gain_mlp": gain_mlp, "router": router, "cotangent": cotangent}


@jax.custom_vjp
def low(v):
    return lax.optimization_barrier(v.astype(jnp.bfloat16)).astype(jnp.float32)

@jax.custom_vjp
def low_back(v):
    return v

def low_keep(v):
    return (low(v), None)

def low_pass(kept, grad):
    return (grad,)

def back_keep(v):
    return (v, None)

def back_low(kept, grad):
    return (low(grad),)
low.defvjp(low_keep, low_pass)
low_back.defvjp(back_keep, back_low)
epsilon = 1e-06
neg_large = -1e+30
highest = lax.Precision.HIGHEST

def rms_norm(values, gain_vec):
    inverse_rms = lax.rsqrt(lax.optimization_barrier(jnp.mean(values * values, axis=-1, keepdims=True)) + epsilon)
    return values * inverse_rms * gain_vec

def matmul_high(left_side, right_side):
    return jnp.dot(left_side, right_side, precision=highest, preferred_element_type=jnp.float32)

def head_attention(positions, pieces):
    query_head, key_head, value_head = pieces
    scores = low_back(matmul_high(query_head, key_head.T) * HDIM ** (-0.5))
    allowed = positions[None, :] <= positions[:, None]
    masked = jnp.where(allowed, scores, neg_large)
    row_max = lax.optimization_barrier(jnp.max(masked, axis=1, keepdims=True))
    weights = jnp.where(allowed, jnp.exp(masked - row_max), 0.0)
    row_total = lax.optimization_barrier(jnp.sum(weights, axis=1, keepdims=True))
    return matmul_high(low(weights), value_head) / row_total

def sequence_forward(chosen_row, params, seq_tokens):
    w_qkv, w_out, w_up, w_down, gain_attn, gain_mlp, router = params
    picked = seq_tokens[chosen_row]
    router_gate = jax.nn.sigmoid(matmul_high(picked, router))
    normed = low(rms_norm(picked, gain_attn))
    joined = low_back(low(matmul_high(normed, w_qkv)))
    per_head = joined.reshape(ROUTED, 3, HEADS, HDIM).transpose(1, 2, 0, 3)
    attend = jax.checkpoint(partial(head_attention, chosen_row))
    heads_out = lax.map(attend, (per_head[0], per_head[1], per_head[2]))
    attended = low_back(low(heads_out.transpose(1, 0, 2).reshape(ROUTED, HEADS * HDIM)))
    branch = low_back(matmul_high(attended, w_out))
    hidden_state = picked + branch
    normed_mlp = low(rms_norm(hidden_state, gain_mlp))
    upper = low_back(matmul_high(normed_mlp, w_up))
    active = low(jax.nn.gelu(upper, approximate=False))
    result = low_back(matmul_high(active, w_down))
    update = router_gate[:, None] * (branch + result)
    return seq_tokens.at[chosen_row].add(update)

def reference(tokens, chosen, w_qkv, w_out, w_up, w_down, gain_attn, gain_mlp, router, cotangent):
    params = (w_qkv.astype(jnp.float32), w_out.astype(jnp.float32), w_up.astype(jnp.float32), w_down.astype(jnp.float32), gain_attn.astype(jnp.float32), gain_mlp.astype(jnp.float32), router.astype(jnp.float32))

    def one_sequence(running, inputs):
        seq_tokens, chosen_row, seq_cot = inputs
        seq_output, pullback = jax.vjp(partial(sequence_forward, chosen_row), params, seq_tokens.astype(jnp.float32))
        grad_params, seq_grad = pullback(seq_cot.astype(jnp.float32))
        running = jax.tree.map(jnp.add, running, grad_params)
        return (running, (seq_output.astype(jnp.bfloat16), seq_grad.astype(jnp.bfloat16)))
    zero_grads = jax.tree.map(jnp.zeros_like, params)
    totals, (outputs, grad_tokens) = lax.scan(one_sequence, zero_grads, (tokens, chosen, cotangent))
    return (outputs, grad_tokens, totals[0], totals[1], totals[2], totals[3], totals[4], totals[5], totals[6])
```

```python
from functools import partial

import jax
import jax.numpy as jnp
from jax import lax
from jax.sharding import PartitionSpec as P

HEADS = 16
HDIM = 64


epsilon = 1e-06
neg_large = -1e30


def rms_norm(values, gain_vec):
    inverse_rms = lax.rsqrt(jnp.mean(values * values, axis=-1, keepdims=True) + epsilon)
    return values * inverse_rms * gain_vec


def exact_gelu(values):
    return jax.nn.gelu(values, approximate=False)


def take_rows(seq_rows, row_index):
    return seq_rows[row_index]


def add_rows(seq_rows, row_index, additions):
    return seq_rows.at[row_index].add(additions)


def shards(tokens, chosen, w_qkv, w_out, w_up, w_down, gain_attn, gain_mlp, router, cotangent):
    head_count = lax.axis_size("head")
    block_count = lax.axis_size("blk")
    shard_count = head_count * block_count
    seq_count, seg_len, model_width = tokens.shape
    cap_len = seg_len // 4
    routed_count = chosen.shape[1]
    seq_len = seg_len * shard_count
    local_heads = HEADS // head_count
    slot_rows = head_count * cap_len
    scale_factor = HDIM ** (-0.5)
    head_index = lax.axis_index("head")
    block_index = lax.axis_index("blk")
    my_shard = head_index * block_count + block_index
    bounds = jnp.arange(shard_count + 1, dtype=jnp.int32) * seg_len
    before = jax.vmap(lambda chosen_row: jnp.searchsorted(chosen_row, bounds, side="left"))(chosen)
    first_index = before[:, :-1]
    shard_load = before[:, 1:] - first_index
    slot_iota = jnp.arange(cap_len, dtype=jnp.int32)
    live_table = slot_iota[None, None, :] < shard_load[:, :, None]
    lookup = jnp.minimum(first_index[:, :, None] + slot_iota[None, None, :], routed_count - 1)
    place_table = jnp.take_along_axis(
        chosen, lookup.reshape(seq_count, shard_count * cap_len), axis=1
    )
    place_table = jnp.where(
        live_table, place_table.reshape(seq_count, shard_count, cap_len), seq_len
    )
    my_positions = lax.dynamic_index_in_dim(place_table, my_shard, 1, False)
    my_live = lax.dynamic_index_in_dim(live_table, my_shard, 1, False)
    local_rows = jnp.clip(my_positions - my_shard * seg_len, 0, seg_len - 1)
    cycle_positions = place_table.reshape(seq_count, head_count, block_count, cap_len).transpose(
        0, 2, 1, 3
    )
    cycle_positions = cycle_positions.reshape(seq_count, block_count * slot_rows)
    query_positions = lax.dynamic_slice_in_dim(
        cycle_positions, block_index * slot_rows, slot_rows, 1
    )
    live_weight = my_live.astype(jnp.float32)[:, :, None]
    gathered = (
        lax.all_gather(w_qkv, ("head", "blk"), axis=0, tiled=True),
        lax.all_gather(w_out, ("head", "blk"), axis=0, tiled=True),
        lax.all_gather(w_up, ("head", "blk"), axis=0, tiled=True),
        lax.all_gather(w_down, ("head", "blk"), axis=0, tiled=True),
        lax.all_gather(gain_attn, ("head", "blk"), axis=0, tiled=True),
        lax.all_gather(gain_mlp, ("head", "blk"), axis=0, tiled=True),
        lax.all_gather(router, ("head", "blk"), axis=0, tiled=True),
    )
    full_qkv, full_out, full_up, full_down, full_gain_attn, full_gain_mlp, full_router = gathered
    picked = jax.vmap(take_rows)(tokens, local_rows)
    picked = jnp.where(my_live[:, :, None], picked, jnp.zeros_like(picked))
    picked_exact = picked.astype(jnp.float32)
    router_gate = jax.nn.sigmoid(
        jnp.einsum("scd,d->sc", picked, full_router, preferred_element_type=jnp.float32)
    )
    normed_exact, norm_attn_back = jax.vjp(
        rms_norm, picked_exact, full_gain_attn.astype(jnp.float32)
    )
    normed = normed_exact.astype(jnp.bfloat16)
    joined = jnp.einsum("scd,de->sce", normed, full_qkv, preferred_element_type=jnp.float32).astype(
        jnp.bfloat16
    )
    to_heads = lax.all_to_all(
        joined.reshape(seq_count, cap_len, 3, model_width),
        "head",
        split_axis=3,
        concat_axis=1,
        tiled=True,
    )
    queries_tok = to_heads[:, :, 0]
    queries_heads = queries_tok.reshape(seq_count, slot_rows, local_heads, HDIM)
    key_values = to_heads[:, :, 1:3]
    my_keys = key_values[:, :, 0].reshape(seq_count, slot_rows, local_heads, HDIM)
    my_values = key_values[:, :, 1].reshape(seq_count, slot_rows, local_heads, HDIM)
    stat_shape = (seq_count, local_heads, slot_rows)
    piece = lax.all_gather(key_values, "blk", axis=1, tiled=True)
    run_max = jnp.full(stat_shape, neg_large, jnp.float32)
    piece_rows = piece.shape[1]
    key_pos = cycle_positions
    keys_piece = piece[:, :, 0].reshape(seq_count, piece_rows, local_heads, HDIM)
    values_piece = piece[:, :, 1].reshape(seq_count, piece_rows, local_heads, HDIM)
    scores = (
        jnp.einsum("sqhd,skhd->shqk", queries_heads, keys_piece, preferred_element_type=jnp.float32)
        * scale_factor
    )
    allowed = key_pos[:, None, None, :] <= query_positions[:, None, :, None]
    scores = jnp.where(allowed, scores, neg_large)
    new_max = jnp.maximum(run_max, jnp.max(scores, axis=3))
    prob_block = jnp.where(allowed, jnp.exp(scores - new_max[..., None]), 0.0)
    new_total = jnp.sum(prob_block, axis=3)
    added = jnp.einsum(
        "shqk,skhd->sqhd",
        prob_block.astype(jnp.bfloat16),
        values_piece,
        preferred_element_type=jnp.float32,
    )
    attended_exact = added / new_total.transpose(0, 2, 1)[..., None]
    log_sum = new_max + jnp.log(new_total)
    attended_tok = attended_exact.astype(jnp.bfloat16).reshape(
        seq_count, slot_rows, local_heads * HDIM
    )
    attended = lax.all_to_all(attended_tok, "head", split_axis=1, concat_axis=2, tiled=True)
    branch = jnp.einsum("sce,ed->scd", attended, full_out, preferred_element_type=jnp.float32)
    hidden_state = picked_exact + branch
    normed_mlp_exact, norm_mlp_back = jax.vjp(
        rms_norm, hidden_state, full_gain_mlp.astype(jnp.float32)
    )
    normed_mlp = normed_mlp_exact.astype(jnp.bfloat16)
    upper = jnp.einsum("scd,di->sci", normed_mlp, full_up, preferred_element_type=jnp.float32)
    active_exact, gelu_back = jax.vjp(exact_gelu, upper)
    active = active_exact.astype(jnp.bfloat16)
    result = jnp.einsum("sci,id->scd", active, full_down, preferred_element_type=jnp.float32)
    combined = branch + result
    update = router_gate[:, :, None] * combined * live_weight
    output = jax.vmap(add_rows)(tokens.astype(jnp.float32), local_rows, update).astype(jnp.bfloat16)
    regathered = (
        lax.all_gather(w_qkv, ("head", "blk"), axis=0, tiled=True),
        lax.all_gather(w_out, ("head", "blk"), axis=0, tiled=True),
        lax.all_gather(w_up, ("head", "blk"), axis=0, tiled=True),
        lax.all_gather(w_down, ("head", "blk"), axis=0, tiled=True),
        lax.all_gather(gain_attn, ("head", "blk"), axis=0, tiled=True),
        lax.all_gather(gain_mlp, ("head", "blk"), axis=0, tiled=True),
        lax.all_gather(router, ("head", "blk"), axis=0, tiled=True),
    )
    back_qkv, back_out, back_up, back_down, back_gain_attn, back_gain_mlp, back_router = regathered
    picked_cot = jax.vmap(take_rows)(cotangent, local_rows).astype(jnp.float32) * live_weight
    d_update = router_gate[:, :, None] * picked_cot
    d_logit = jnp.sum(picked_cot * combined, axis=2) * router_gate * (1.0 - router_gate)
    grad_router = jnp.einsum("sc,scd->d", d_logit, picked_exact, precision=lax.Precision.HIGHEST)
    d_result = d_update.astype(jnp.bfloat16)
    d_active = jnp.einsum("scd,id->sci", d_result, back_down, preferred_element_type=jnp.float32)
    d_upper = gelu_back(d_active)[0].astype(jnp.bfloat16)
    d_normed_mlp = jnp.einsum("sci,di->scd", d_upper, back_up, preferred_element_type=jnp.float32)
    d_hidden, grad_gain_mlp = norm_mlp_back(d_normed_mlp)
    d_branch = (d_update + d_hidden).astype(jnp.bfloat16)
    d_attended = jnp.einsum(
        "scd,ed->sce", d_branch, back_out, preferred_element_type=jnp.float32
    ).astype(jnp.bfloat16)
    d_att_tok = lax.all_to_all(d_attended, "head", split_axis=2, concat_axis=1, tiled=True)
    d_att_heads = d_att_tok.reshape(seq_count, slot_rows, local_heads, HDIM)
    delta_tok = jnp.sum(d_att_heads.astype(jnp.float32) * attended_exact, axis=3)
    delta_sq = delta_tok.transpose(0, 2, 1)
    piece = lax.all_gather(key_values, "blk", axis=1, tiled=True)
    piece_rows = piece.shape[1]
    key_pos = cycle_positions
    keys_piece = piece[:, :, 0].reshape(seq_count, piece_rows, local_heads, HDIM)
    values_piece = piece[:, :, 1].reshape(seq_count, piece_rows, local_heads, HDIM)
    scores = (
        jnp.einsum("sqhd,skhd->shqk", queries_heads, keys_piece, preferred_element_type=jnp.float32)
        * scale_factor
    )
    allowed = key_pos[:, None, None, :] <= query_positions[:, None, :, None]
    prob_block = jnp.where(allowed, jnp.exp(scores - log_sum[..., None]), 0.0)
    d_prob = jnp.einsum(
        "sqhd,skhd->shqk", d_att_heads, values_piece, preferred_element_type=jnp.float32
    )
    d_scores = (prob_block * (d_prob - delta_sq[..., None])).astype(jnp.bfloat16)
    d_queries = (
        jnp.einsum("shqk,skhd->sqhd", d_scores, keys_piece, preferred_element_type=jnp.float32)
        * scale_factor
    )
    lse_tok = log_sum.transpose(0, 2, 1)
    lse_high = lse_tok.astype(jnp.bfloat16)
    lse_low = (lse_tok - lse_high.astype(jnp.float32)).astype(jnp.bfloat16)
    delta_high = delta_tok.astype(jnp.bfloat16)
    delta_low = (delta_tok - delta_high.astype(jnp.float32)).astype(jnp.bfloat16)
    query_piece = lax.all_gather(queries_tok, "blk", axis=1, tiled=True)
    dout_piece = lax.all_gather(d_att_tok, "blk", axis=1, tiled=True)
    piece_lse_high = lax.all_gather(lse_high, "blk", axis=1, tiled=True)
    piece_lse_low = lax.all_gather(lse_low, "blk", axis=1, tiled=True)
    piece_delta_high = lax.all_gather(delta_high, "blk", axis=1, tiled=True)
    piece_delta_low = lax.all_gather(delta_low, "blk", axis=1, tiled=True)
    piece_rows = query_piece.shape[1]
    query_heads = query_piece.reshape(seq_count, piece_rows, local_heads, HDIM)
    dout_heads = dout_piece.reshape(seq_count, piece_rows, local_heads, HDIM)
    piece_lse = (piece_lse_high.astype(jnp.float32) + piece_lse_low.astype(jnp.float32)).transpose(
        0, 2, 1
    )
    piece_delta = (
        piece_delta_high.astype(jnp.float32) + piece_delta_low.astype(jnp.float32)
    ).transpose(0, 2, 1)
    scores = (
        jnp.einsum("sqhd,skhd->shqk", query_heads, my_keys, preferred_element_type=jnp.float32)
        * scale_factor
    )
    allowed = query_positions[:, None, None, :] <= cycle_positions[:, None, :, None]
    prob_block = jnp.where(allowed, jnp.exp(scores - piece_lse[..., None]), 0.0)
    grad_values = jnp.einsum(
        "shqk,sqhd->skhd",
        prob_block.astype(jnp.bfloat16),
        dout_heads,
        preferred_element_type=jnp.float32,
    )
    d_prob = jnp.einsum(
        "sqhd,skhd->shqk", dout_heads, my_values, preferred_element_type=jnp.float32
    )
    d_scores = (prob_block * (d_prob - piece_delta[..., None])).astype(jnp.bfloat16)
    grad_keys = (
        jnp.einsum("shqk,sqhd->skhd", d_scores, query_heads, preferred_element_type=jnp.float32)
        * scale_factor
    )
    d_heads = jnp.stack(
        [
            d_queries.astype(jnp.bfloat16),
            grad_keys.astype(jnp.bfloat16),
            grad_values.astype(jnp.bfloat16),
        ],
        axis=2,
    )
    d_heads = d_heads.reshape(seq_count, slot_rows, 3, local_heads * HDIM)
    d_joined = lax.all_to_all(d_heads, "head", split_axis=1, concat_axis=3, tiled=True).reshape(
        seq_count, cap_len, 3 * model_width
    )
    d_normed = jnp.einsum("sce,de->scd", d_joined, back_qkv, preferred_element_type=jnp.float32)
    d_picked_norm, grad_gain_attn = norm_attn_back(d_normed)
    d_picked = (
        d_hidden
        + d_picked_norm
        + d_logit[:, :, None] * back_router.astype(jnp.float32)[None, None, :]
    )
    grad_tokens = jax.vmap(add_rows)(
        cotangent.astype(jnp.float32), local_rows, d_picked * live_weight
    ).astype(jnp.bfloat16)
    grad_qkv = jnp.einsum("scd,sce->de", normed, d_joined, preferred_element_type=jnp.float32)
    grad_out = jnp.einsum("sce,scd->ed", attended, d_branch, preferred_element_type=jnp.float32)
    grad_up = jnp.einsum("scd,sci->di", normed_mlp, d_upper, preferred_element_type=jnp.float32)
    grad_down = jnp.einsum("sci,scd->id", active, d_result, preferred_element_type=jnp.float32)
    owned = (
        lax.psum_scatter(grad_qkv, ("head", "blk"), scatter_dimension=0, tiled=True),
        lax.psum_scatter(grad_out, ("head", "blk"), scatter_dimension=0, tiled=True),
        lax.psum_scatter(grad_up, ("head", "blk"), scatter_dimension=0, tiled=True),
        lax.psum_scatter(grad_down, ("head", "blk"), scatter_dimension=0, tiled=True),
        lax.psum_scatter(grad_gain_attn, ("head", "blk"), scatter_dimension=0, tiled=True),
        lax.psum_scatter(grad_gain_mlp, ("head", "blk"), scatter_dimension=0, tiled=True),
        lax.psum_scatter(grad_router, ("head", "blk"), scatter_dimension=0, tiled=True),
    )
    return (
        output,
        grad_tokens,
        owned[0],
        owned[1],
        owned[2],
        owned[3],
        owned[4],
        owned[5],
        owned[6],
    )


def flips(count):
    return [[(i, i ^ k) for i in range(count)] for k in range(count)]


def gather_group(own):
    blocks = [own] + [lax.ppermute(own, "z", f) for f in flips(lax.axis_size("z"))[1:]]
    blocks = jnp.stack(blocks)
    rest = [lax.ppermute(blocks, "c", f) for f in flips(lax.axis_size("c"))[1:]]
    return jnp.concatenate([blocks] + rest)


def scatter_group(parts):
    depth = lax.axis_size("z")
    total = parts[:depth].astype(jnp.float32)
    for k, f in enumerate(flips(lax.axis_size("c"))[1:], 1):
        piece = parts[k * depth : (k + 1) * depth].astype(jnp.bfloat16)
        total = total + lax.ppermute(piece, "c", f).astype(jnp.float32)
    mine = total[0]
    low = total.astype(jnp.bfloat16)
    for k, f in enumerate(flips(depth)[1:], 1):
        mine = mine + lax.ppermute(low[k], "z", f).astype(jnp.float32)
    return mine


def xor_blocks(rows, bits):
    shape = rows.shape
    rows = rows.reshape((2,) * len(bits) + (-1,))
    for axis, bit in enumerate(bits):
        rows = jnp.where(bit == 1, jnp.flip(rows, axis), rows)
    return rows.reshape(shape)


def index_bits(index, count):
    return [(index >> k) & 1 for k in reversed(range(count.bit_length() - 1))]


def split_two(values):
    high = values.astype(jnp.bfloat16)
    return high, (values - high.astype(jnp.float32)).astype(jnp.bfloat16)


def grouped(
    tokens, chosen, w_qkv, w_out, w_up, w_down, gain_attn, gain_mlp, router, cotangent
):
    f32, bf16 = jnp.float32, jnp.bfloat16
    dot = partial(jnp.einsum, preferred_element_type=f32)
    ny, nc, nz, nx = (lax.axis_size(a) for a in ("y", "c", "z", "x"))
    y, c, z, x = (lax.axis_index(a) for a in ("y", "c", "z", "x"))
    seq_count, seg_len, width = tokens.shape
    cap = seg_len // 4
    routed = chosen.shape[1]
    members, lines = nc * nz, ny * nx
    member = c * nz + z
    line = y * nx + x
    shard = ((y * nc + c) * nz + z) * nx + x
    rows, ff_rows = w_qkv.shape[0], w_down.shape[0]
    heads = HEADS // members
    own = routed // members
    scale_factor = HDIM ** (-0.5)
    line_axes, group_axes = ("y", "x"), ("c", "z")
    bits = index_bits(c, nc) + index_bits(z, nz)

    send_qkv = w_qkv.reshape(rows, 3, heads, members, HDIM).transpose(3, 0, 1, 2, 4)
    send_qkv = send_qkv.reshape(members, rows, 3 * heads * HDIM)
    vectors = jnp.stack([gain_attn, gain_mlp, router])
    vec_rows = jnp.pad(vectors, ((0, 5), (0, 3 * heads * HDIM - rows)))
    send_qkv = jnp.concatenate(
        [send_qkv, jnp.broadcast_to(vec_rows, (members,) + vec_rows.shape)], 1
    )
    send_up = w_up.reshape(rows, ny, members, nx, ff_rows).transpose(2, 0, 1, 3, 4)
    send_up = send_up.reshape(members, rows, lines * ff_rows)

    def along_lines(block):
        return lax.all_to_all(
            jnp.broadcast_to(block, (lines,) + block.shape), line_axes, 0, 0, tiled=True
        )

    got_qkv = along_lines(lax.all_to_all(send_qkv, group_axes, 0, 0, tiled=True))
    got_up = along_lines(lax.all_to_all(send_up, group_axes, 0, 0, tiled=True))
    full_down = along_lines(w_down).reshape(lines * ff_rows, width)
    full_out = along_lines(w_out).reshape(lines * rows, width)

    def natural(got):
        got = got.reshape((ny, nx, members) + got.shape[2:])
        got = got.transpose((0, 2, 1) + tuple(range(3, got.ndim)))
        return got.reshape((width,) + got.shape[4:])

    full_qkv = natural(got_qkv[:, :, :rows])
    full_up = natural(got_up)
    vecs = got_qkv[:, :, rows : rows + 3, :rows].reshape(ny, nx, members, 3, rows)
    vecs = vecs.transpose(3, 0, 2, 1, 4).reshape(3, width).astype(f32)
    full_gain_attn, full_gain_mlp, full_router = vecs[0], vecs[1], vecs[2]

    base = shard * seg_len
    places = base + jnp.arange(seg_len, dtype=jnp.int32)
    at = chosen[:, :, None]
    present = jnp.any(at == places, 1)
    rank = jnp.sum((at >= base) & (at < places), 1, dtype=jnp.int32)
    slots = jnp.arange(cap, dtype=jnp.int32)
    pick = (present[:, None, :] & (rank[:, None, :] == slots[:, None])).astype(bf16)
    mine = lax.dynamic_index_in_dim(chosen, line, 0, False)
    owner = mine // seg_len
    order = jnp.arange(routed, dtype=jnp.int32)
    slot = jnp.sum(
        (owner[:, None] == owner[None, :]) & (order[None, :] < order[:, None]), 1, dtype=jnp.int32
    )
    ox, oz = owner % nx, (owner // nx) % nz
    oc, oy = (owner // (nx * nz)) % nc, owner // (nx * nz * nc)
    cell = ((((oc ^ c) * nz + (oz ^ z)) * ny + oy) * nx + ox) * cap + slot
    cell = xor_blocks(cell, bits)
    stand = xor_blocks(mine, bits)
    spots = members * lines * cap
    spread = (cell[:, None] == jnp.arange(spots, dtype=jnp.int32)).astype(bf16)

    picked_slots = dot("scp,spd->scd", pick, tokens).astype(bf16)
    cot_slots = dot("scp,spd->scd", pick, cotangent).astype(bf16)
    both = jnp.stack([picked_slots, cot_slots], 1)
    both = lax.all_to_all(both, line_axes, 0, 0, tiled=True)
    picked_pad = gather_group(both[:, 0].reshape(lines * cap, width)).reshape(spots, width)
    cot_pad = gather_group(both[:, 1].reshape(lines * cap, width)).reshape(spots, width)
    picked_low = dot("rj,jd->rd", spread, picked_pad).astype(bf16)
    picked = picked_low.astype(f32)
    cot_low = dot("rj,jd->rd", spread, cot_pad).astype(bf16)
    cot = cot_low.astype(f32)
    gate = jax.nn.sigmoid(jnp.sum(picked * full_router, 1, keepdims=True))

    inv = lax.rsqrt(jnp.mean(picked * picked, 1, keepdims=True) + epsilon)
    normed = (picked * inv * full_gain_attn).astype(bf16)
    joined = dot("rd,de->re", normed, full_qkv).astype(bf16).reshape(routed, 3, heads, HDIM)
    queries, keys, values = joined[:, 0], joined[:, 1], joined[:, 2]
    allowed = stand[None, :] <= stand[:, None]
    scores = dot("qhd,khd->hqk", queries, keys) * scale_factor
    scores = jnp.where(allowed, scores, neg_large)
    top = jnp.max(scores, 2, keepdims=True)
    probs = jnp.where(allowed, jnp.exp(scores - top), 0.0)
    total = jnp.sum(probs, 2, keepdims=True)
    probs_low = probs.astype(bf16)
    attended_exact = dot("hqk,khd->hqd", probs_low, values) / total
    attended = attended_exact.astype(bf16).transpose(1, 0, 2).reshape(routed, heads * HDIM)
    branch_part = dot("re,ed->rd", attended, full_out)
    branch = scatter_group(branch_part.reshape(members, own, width))
    picked_own = picked[:own]
    hidden = picked_own + branch
    inv_mlp = lax.rsqrt(jnp.mean(hidden * hidden, 1, keepdims=True) + epsilon)
    normed_mlp = gather_group((hidden * inv_mlp * full_gain_mlp).astype(bf16))
    normed_mlp = normed_mlp.reshape(routed, width)

    upper = dot("rd,di->ri", normed_mlp, full_up)
    active_exact, gelu_back = jax.vjp(exact_gelu, upper)
    active = active_exact.astype(bf16)
    combined_part = branch_part + dot("ri,id->rd", active, full_down)
    d_update = gate * cot
    d_result = d_update.astype(bf16)
    d_active = dot("rd,id->ri", d_result, full_down)
    d_upper = gelu_back(d_active)[0].astype(bf16)
    d_normed_mlp_part = dot("ri,di->rd", d_upper, full_up)
    logit_part = jnp.sum(cot * combined_part, 1, keepdims=True)
    logit_high, logit_low = split_two(logit_part)
    logit_cols = jnp.concatenate([logit_high, logit_low], 1).astype(f32)
    d_parts = jnp.concatenate(
        [d_normed_mlp_part, jnp.pad(logit_cols, ((0, 0), (0, 126)))], 1
    )
    d_own = scatter_group(d_parts.reshape(members, own, width + 128))
    d_normed_mlp = d_own[:, :width]
    gate_own = gate[:own]
    d_logit = jnp.sum(d_own[:, width:], 1, keepdims=True) * gate_own * (1.0 - gate_own)
    u = d_normed_mlp * full_gain_mlp
    d_hidden = inv_mlp * u - hidden * inv_mlp**3 * jnp.mean(u * hidden, 1, keepdims=True)
    d_branch = gather_group((d_update[:own] + d_hidden).astype(bf16)).reshape(routed, width)
    vec_mlp = jnp.sum(d_normed_mlp * hidden * inv_mlp, 0)
    vec_router = jnp.sum(d_logit * picked_own, 0)

    d_attended = dot("rd,ed->re", d_branch, full_out).astype(bf16)
    d_att = d_attended.reshape(routed, heads, HDIM).transpose(1, 0, 2)
    delta = jnp.sum(d_att.astype(f32) * attended_exact, 2, keepdims=True)
    d_prob = dot("hqd,khd->hqk", d_att, values)
    d_scores = (probs / total * (d_prob - delta)).astype(bf16)
    d_queries = dot("hqk,khd->qhd", d_scores, keys) * scale_factor
    d_keys = dot("hqk,qhd->khd", d_scores, queries) * scale_factor
    d_values = dot("hqk,hqd->khd", probs_low, (d_att.astype(f32) / total).astype(bf16))
    d_joined = jnp.stack([d_queries, d_keys, d_values], 1).astype(bf16)
    d_joined = d_joined.reshape(routed, 3 * heads * HDIM)
    d_normed_part = dot("re,de->rd", d_joined, full_qkv)
    v = d_normed_part * full_gain_attn
    d_picked_part = inv * v - picked * inv**3 * jnp.mean(v * picked, 1, keepdims=True)
    d_picked_part = d_picked_part.at[:own].add(d_hidden + d_logit * full_router)
    vec_attn = jnp.sum(d_normed_part * picked * inv, 0)

    def to_slots(part):
        pad = dot("rj,rd->jd", spread, part.astype(bf16)).astype(bf16)
        mine = scatter_group(pad.reshape(members, lines * cap, width)).astype(bf16)
        return lax.all_to_all(mine.reshape(lines, cap, width), line_axes, 0, 0, tiled=True)

    update = to_slots(gate * combined_part)
    d_picked = to_slots(d_picked_part)
    output = (tokens.astype(f32) + dot("scp,scd->spd", pick, update)).astype(bf16)
    grad_tokens = (cotangent.astype(f32) + dot("scp,scd->spd", pick, d_picked)).astype(bf16)

    def sum_lines(part):
        got = lax.all_to_all(part.astype(bf16), line_axes, 0, 0, tiled=True)
        return jnp.sum(got.astype(f32), 0)

    def by_line(part):
        part = part.reshape((ny, members, nx, rows) + part.shape[1:])
        part = part.transpose((0, 2, 1, 3) + tuple(range(4, part.ndim)))
        return part.reshape((lines, members) + part.shape[3:])

    grad_down = sum_lines(
        dot("ri,rd->id", active, d_result).reshape(lines, ff_rows, width)
    )
    grad_out = sum_lines(dot("re,rd->ed", attended, d_branch).reshape(lines, rows, width))
    grad_up = sum_lines(by_line(dot("rd,ri->di", normed_mlp, d_upper))).astype(bf16)
    grad_up = lax.all_to_all(grad_up, group_axes, 0, 0, tiled=True).astype(f32)
    grad_up = grad_up.reshape(members, rows, ny, nx, ff_rows).transpose(1, 2, 0, 3, 4)
    grad_up = grad_up.reshape(rows, ny * members * nx * ff_rows)
    cols = 3 * heads * HDIM
    grad_qkv = by_line(dot("rd,re->de", normed, d_joined)).astype(bf16)
    vec_parts = by_line(jnp.stack([vec_attn, vec_mlp, vec_router], 1))
    vec_parts = vec_parts.transpose(0, 1, 3, 2).reshape(lines, members, 3 * rows)

    def pack(vec):
        vec = jnp.concatenate(split_two(vec), -1)[..., None, :]
        pads = [(0, 0)] * (vec.ndim - 2) + [(0, 7), (0, cols - 6 * rows)]
        return jnp.pad(vec, pads)

    qkv_sum = sum_lines(jnp.concatenate([grad_qkv, pack(vec_parts)], 2))
    vec_sum = qkv_sum[:, rows, : 3 * rows] + qkv_sum[:, rows, 3 * rows : 6 * rows]
    send = jnp.concatenate([qkv_sum[:, :rows].astype(bf16), pack(vec_sum)], 1)
    got = lax.all_to_all(send, group_axes, 0, 0, tiled=True).astype(f32)
    grad_qkv = got[:, :rows].reshape(members, rows, 3, heads, HDIM).transpose(1, 2, 3, 0, 4)
    grad_qkv = grad_qkv.reshape(rows, 3 * HEADS * HDIM)
    vec_own = jnp.sum(got[:, rows, : 6 * rows], 0)
    vec_own = (vec_own[: 3 * rows] + vec_own[3 * rows :]).reshape(3, rows)
    return (
        output,
        grad_tokens,
        grad_qkv,
        grad_out,
        grad_up,
        grad_down,
        vec_own[0],
        vec_own[1],
        vec_own[2],
    )


def fits(mesh):
    head_count, block_count = mesh.devices.shape
    members = (head_count // 2) * (block_count // 2)
    power = members & (members - 1) == 0
    return power and HEADS == 2 * members


def solution(mesh):
    if fits(mesh):
        head_count, block_count = mesh.devices.shape
        devices = mesh.devices.reshape(2, head_count // 2, block_count // 2, 2)
        mesh = jax.sharding.Mesh(devices, ("y", "c", "z", "x"))
        body, all_axes = grouped, ("y", "c", "z", "x")
    else:
        body, all_axes = shards, ("head", "blk")
    seqs, mats, vecs = P(None, all_axes, None), P(all_axes, None), P(all_axes)
    in_specs = (seqs, P(), mats, mats, mats, mats, vecs, vecs, vecs, seqs)
    out_specs = (seqs, seqs, mats, mats, mats, mats, vecs, vecs, vecs)
    return jax.shard_map(body, mesh=mesh, in_specs=in_specs, out_specs=out_specs, check_vma=False)
```

```python
import math
from functools import partial

import jax
import jax.numpy as jnp
from jax import lax
from jax.experimental import pallas as pl
from jax.experimental.pallas import tpu as pltpu
from jax.sharding import PartitionSpec as P

HEADS = 16
HDIM = 64


epsilon = 1e-06
neg_large = -1e30


def rms_norm(values, gain_vec):
    inverse_rms = lax.rsqrt(jnp.mean(values * values, axis=-1, keepdims=True) + epsilon)
    return values * inverse_rms * gain_vec


def exact_gelu(values):
    return jax.nn.gelu(values, approximate=False)


def take_rows(seq_rows, row_index):
    return seq_rows[row_index]


def add_rows(seq_rows, row_index, additions):
    return seq_rows.at[row_index].add(additions)


def shards(tokens, chosen, w_qkv, w_out, w_up, w_down, gain_attn, gain_mlp, router, cotangent):
    head_count = lax.axis_size("head")
    block_count = lax.axis_size("blk")
    shard_count = head_count * block_count
    seq_count, seg_len, model_width = tokens.shape
    cap_len = seg_len // 4
    routed_count = chosen.shape[1]
    seq_len = seg_len * shard_count
    local_heads = HEADS // head_count
    slot_rows = head_count * cap_len
    scale_factor = HDIM ** (-0.5)
    head_index = lax.axis_index("head")
    block_index = lax.axis_index("blk")
    my_shard = head_index * block_count + block_index
    bounds = jnp.arange(shard_count + 1, dtype=jnp.int32) * seg_len
    before = jax.vmap(lambda chosen_row: jnp.searchsorted(chosen_row, bounds, side="left"))(chosen)
    first_index = before[:, :-1]
    shard_load = before[:, 1:] - first_index
    slot_iota = jnp.arange(cap_len, dtype=jnp.int32)
    live_table = slot_iota[None, None, :] < shard_load[:, :, None]
    lookup = jnp.minimum(first_index[:, :, None] + slot_iota[None, None, :], routed_count - 1)
    place_table = jnp.take_along_axis(
        chosen, lookup.reshape(seq_count, shard_count * cap_len), axis=1
    )
    place_table = jnp.where(
        live_table, place_table.reshape(seq_count, shard_count, cap_len), seq_len
    )
    my_positions = lax.dynamic_index_in_dim(place_table, my_shard, 1, False)
    my_live = lax.dynamic_index_in_dim(live_table, my_shard, 1, False)
    local_rows = jnp.clip(my_positions - my_shard * seg_len, 0, seg_len - 1)
    cycle_positions = place_table.reshape(seq_count, head_count, block_count, cap_len).transpose(
        0, 2, 1, 3
    )
    cycle_positions = cycle_positions.reshape(seq_count, block_count * slot_rows)
    query_positions = lax.dynamic_slice_in_dim(
        cycle_positions, block_index * slot_rows, slot_rows, 1
    )
    live_weight = my_live.astype(jnp.float32)[:, :, None]
    gathered = (
        lax.all_gather(w_qkv, ("head", "blk"), axis=0, tiled=True),
        lax.all_gather(w_out, ("head", "blk"), axis=0, tiled=True),
        lax.all_gather(w_up, ("head", "blk"), axis=0, tiled=True),
        lax.all_gather(w_down, ("head", "blk"), axis=0, tiled=True),
        lax.all_gather(gain_attn, ("head", "blk"), axis=0, tiled=True),
        lax.all_gather(gain_mlp, ("head", "blk"), axis=0, tiled=True),
        lax.all_gather(router, ("head", "blk"), axis=0, tiled=True),
    )
    full_qkv, full_out, full_up, full_down, full_gain_attn, full_gain_mlp, full_router = gathered
    picked = jax.vmap(take_rows)(tokens, local_rows)
    picked = jnp.where(my_live[:, :, None], picked, jnp.zeros_like(picked))
    picked_exact = picked.astype(jnp.float32)
    router_gate = jax.nn.sigmoid(
        jnp.einsum("scd,d->sc", picked, full_router, preferred_element_type=jnp.float32)
    )
    normed_exact, norm_attn_back = jax.vjp(
        rms_norm, picked_exact, full_gain_attn.astype(jnp.float32)
    )
    normed = normed_exact.astype(jnp.bfloat16)
    joined = jnp.einsum("scd,de->sce", normed, full_qkv, preferred_element_type=jnp.float32).astype(
        jnp.bfloat16
    )
    to_heads = lax.all_to_all(
        joined.reshape(seq_count, cap_len, 3, model_width),
        "head",
        split_axis=3,
        concat_axis=1,
        tiled=True,
    )
    queries_tok = to_heads[:, :, 0]
    queries_heads = queries_tok.reshape(seq_count, slot_rows, local_heads, HDIM)
    key_values = to_heads[:, :, 1:3]
    my_keys = key_values[:, :, 0].reshape(seq_count, slot_rows, local_heads, HDIM)
    my_values = key_values[:, :, 1].reshape(seq_count, slot_rows, local_heads, HDIM)
    stat_shape = (seq_count, local_heads, slot_rows)
    piece = lax.all_gather(key_values, "blk", axis=1, tiled=True)
    run_max = jnp.full(stat_shape, neg_large, jnp.float32)
    piece_rows = piece.shape[1]
    key_pos = cycle_positions
    keys_piece = piece[:, :, 0].reshape(seq_count, piece_rows, local_heads, HDIM)
    values_piece = piece[:, :, 1].reshape(seq_count, piece_rows, local_heads, HDIM)
    scores = (
        jnp.einsum("sqhd,skhd->shqk", queries_heads, keys_piece, preferred_element_type=jnp.float32)
        * scale_factor
    )
    allowed = key_pos[:, None, None, :] <= query_positions[:, None, :, None]
    scores = jnp.where(allowed, scores, neg_large)
    new_max = jnp.maximum(run_max, jnp.max(scores, axis=3))
    prob_block = jnp.where(allowed, jnp.exp(scores - new_max[..., None]), 0.0)
    new_total = jnp.sum(prob_block, axis=3)
    added = jnp.einsum(
        "shqk,skhd->sqhd",
        prob_block.astype(jnp.bfloat16),
        values_piece,
        preferred_element_type=jnp.float32,
    )
    attended_exact = added / new_total.transpose(0, 2, 1)[..., None]
    log_sum = new_max + jnp.log(new_total)
    attended_tok = attended_exact.astype(jnp.bfloat16).reshape(
        seq_count, slot_rows, local_heads * HDIM
    )
    attended = lax.all_to_all(attended_tok, "head", split_axis=1, concat_axis=2, tiled=True)
    branch = jnp.einsum("sce,ed->scd", attended, full_out, preferred_element_type=jnp.float32)
    hidden_state = picked_exact + branch
    normed_mlp_exact, norm_mlp_back = jax.vjp(
        rms_norm, hidden_state, full_gain_mlp.astype(jnp.float32)
    )
    normed_mlp = normed_mlp_exact.astype(jnp.bfloat16)
    upper = jnp.einsum("scd,di->sci", normed_mlp, full_up, preferred_element_type=jnp.float32)
    active_exact, gelu_back = jax.vjp(exact_gelu, upper)
    active = active_exact.astype(jnp.bfloat16)
    result = jnp.einsum("sci,id->scd", active, full_down, preferred_element_type=jnp.float32)
    combined = branch + result
    update = router_gate[:, :, None] * combined * live_weight
    output = jax.vmap(add_rows)(tokens.astype(jnp.float32), local_rows, update).astype(jnp.bfloat16)
    regathered = (
        lax.all_gather(w_qkv, ("head", "blk"), axis=0, tiled=True),
        lax.all_gather(w_out, ("head", "blk"), axis=0, tiled=True),
        lax.all_gather(w_up, ("head", "blk"), axis=0, tiled=True),
        lax.all_gather(w_down, ("head", "blk"), axis=0, tiled=True),
        lax.all_gather(gain_attn, ("head", "blk"), axis=0, tiled=True),
        lax.all_gather(gain_mlp, ("head", "blk"), axis=0, tiled=True),
        lax.all_gather(router, ("head", "blk"), axis=0, tiled=True),
    )
    back_qkv, back_out, back_up, back_down, back_gain_attn, back_gain_mlp, back_router = regathered
    picked_cot = jax.vmap(take_rows)(cotangent, local_rows).astype(jnp.float32) * live_weight
    d_update = router_gate[:, :, None] * picked_cot
    d_logit = jnp.sum(picked_cot * combined, axis=2) * router_gate * (1.0 - router_gate)
    grad_router = jnp.einsum("sc,scd->d", d_logit, picked_exact, precision=lax.Precision.HIGHEST)
    d_result = d_update.astype(jnp.bfloat16)
    d_active = jnp.einsum("scd,id->sci", d_result, back_down, preferred_element_type=jnp.float32)
    d_upper = gelu_back(d_active)[0].astype(jnp.bfloat16)
    d_normed_mlp = jnp.einsum("sci,di->scd", d_upper, back_up, preferred_element_type=jnp.float32)
    d_hidden, grad_gain_mlp = norm_mlp_back(d_normed_mlp)
    d_branch = (d_update + d_hidden).astype(jnp.bfloat16)
    d_attended = jnp.einsum(
        "scd,ed->sce", d_branch, back_out, preferred_element_type=jnp.float32
    ).astype(jnp.bfloat16)
    d_att_tok = lax.all_to_all(d_attended, "head", split_axis=2, concat_axis=1, tiled=True)
    d_att_heads = d_att_tok.reshape(seq_count, slot_rows, local_heads, HDIM)
    delta_tok = jnp.sum(d_att_heads.astype(jnp.float32) * attended_exact, axis=3)
    delta_sq = delta_tok.transpose(0, 2, 1)
    piece = lax.all_gather(key_values, "blk", axis=1, tiled=True)
    piece_rows = piece.shape[1]
    key_pos = cycle_positions
    keys_piece = piece[:, :, 0].reshape(seq_count, piece_rows, local_heads, HDIM)
    values_piece = piece[:, :, 1].reshape(seq_count, piece_rows, local_heads, HDIM)
    scores = (
        jnp.einsum("sqhd,skhd->shqk", queries_heads, keys_piece, preferred_element_type=jnp.float32)
        * scale_factor
    )
    allowed = key_pos[:, None, None, :] <= query_positions[:, None, :, None]
    prob_block = jnp.where(allowed, jnp.exp(scores - log_sum[..., None]), 0.0)
    d_prob = jnp.einsum(
        "sqhd,skhd->shqk", d_att_heads, values_piece, preferred_element_type=jnp.float32
    )
    d_scores = (prob_block * (d_prob - delta_sq[..., None])).astype(jnp.bfloat16)
    d_queries = (
        jnp.einsum("shqk,skhd->sqhd", d_scores, keys_piece, preferred_element_type=jnp.float32)
        * scale_factor
    )
    lse_tok = log_sum.transpose(0, 2, 1)
    lse_high = lse_tok.astype(jnp.bfloat16)
    lse_low = (lse_tok - lse_high.astype(jnp.float32)).astype(jnp.bfloat16)
    delta_high = delta_tok.astype(jnp.bfloat16)
    delta_low = (delta_tok - delta_high.astype(jnp.float32)).astype(jnp.bfloat16)
    query_piece = lax.all_gather(queries_tok, "blk", axis=1, tiled=True)
    dout_piece = lax.all_gather(d_att_tok, "blk", axis=1, tiled=True)
    piece_lse_high = lax.all_gather(lse_high, "blk", axis=1, tiled=True)
    piece_lse_low = lax.all_gather(lse_low, "blk", axis=1, tiled=True)
    piece_delta_high = lax.all_gather(delta_high, "blk", axis=1, tiled=True)
    piece_delta_low = lax.all_gather(delta_low, "blk", axis=1, tiled=True)
    piece_rows = query_piece.shape[1]
    query_heads = query_piece.reshape(seq_count, piece_rows, local_heads, HDIM)
    dout_heads = dout_piece.reshape(seq_count, piece_rows, local_heads, HDIM)
    piece_lse = (piece_lse_high.astype(jnp.float32) + piece_lse_low.astype(jnp.float32)).transpose(
        0, 2, 1
    )
    piece_delta = (
        piece_delta_high.astype(jnp.float32) + piece_delta_low.astype(jnp.float32)
    ).transpose(0, 2, 1)
    scores = (
        jnp.einsum("sqhd,skhd->shqk", query_heads, my_keys, preferred_element_type=jnp.float32)
        * scale_factor
    )
    allowed = query_positions[:, None, None, :] <= cycle_positions[:, None, :, None]
    prob_block = jnp.where(allowed, jnp.exp(scores - piece_lse[..., None]), 0.0)
    grad_values = jnp.einsum(
        "shqk,sqhd->skhd",
        prob_block.astype(jnp.bfloat16),
        dout_heads,
        preferred_element_type=jnp.float32,
    )
    d_prob = jnp.einsum(
        "sqhd,skhd->shqk", dout_heads, my_values, preferred_element_type=jnp.float32
    )
    d_scores = (prob_block * (d_prob - piece_delta[..., None])).astype(jnp.bfloat16)
    grad_keys = (
        jnp.einsum("shqk,sqhd->skhd", d_scores, query_heads, preferred_element_type=jnp.float32)
        * scale_factor
    )
    d_heads = jnp.stack(
        [
            d_queries.astype(jnp.bfloat16),
            grad_keys.astype(jnp.bfloat16),
            grad_values.astype(jnp.bfloat16),
        ],
        axis=2,
    )
    d_heads = d_heads.reshape(seq_count, slot_rows, 3, local_heads * HDIM)
    d_joined = lax.all_to_all(d_heads, "head", split_axis=1, concat_axis=3, tiled=True).reshape(
        seq_count, cap_len, 3 * model_width
    )
    d_normed = jnp.einsum("sce,de->scd", d_joined, back_qkv, preferred_element_type=jnp.float32)
    d_picked_norm, grad_gain_attn = norm_attn_back(d_normed)
    d_picked = (
        d_hidden
        + d_picked_norm
        + d_logit[:, :, None] * back_router.astype(jnp.float32)[None, None, :]
    )
    grad_tokens = jax.vmap(add_rows)(
        cotangent.astype(jnp.float32), local_rows, d_picked * live_weight
    ).astype(jnp.bfloat16)
    grad_qkv = jnp.einsum("scd,sce->de", normed, d_joined, preferred_element_type=jnp.float32)
    grad_out = jnp.einsum("sce,scd->ed", attended, d_branch, preferred_element_type=jnp.float32)
    grad_up = jnp.einsum("scd,sci->di", normed_mlp, d_upper, preferred_element_type=jnp.float32)
    grad_down = jnp.einsum("sci,scd->id", active, d_result, preferred_element_type=jnp.float32)
    owned = (
        lax.psum_scatter(grad_qkv, ("head", "blk"), scatter_dimension=0, tiled=True),
        lax.psum_scatter(grad_out, ("head", "blk"), scatter_dimension=0, tiled=True),
        lax.psum_scatter(grad_up, ("head", "blk"), scatter_dimension=0, tiled=True),
        lax.psum_scatter(grad_down, ("head", "blk"), scatter_dimension=0, tiled=True),
        lax.psum_scatter(grad_gain_attn, ("head", "blk"), scatter_dimension=0, tiled=True),
        lax.psum_scatter(grad_gain_mlp, ("head", "blk"), scatter_dimension=0, tiled=True),
        lax.psum_scatter(grad_router, ("head", "blk"), scatter_dimension=0, tiled=True),
    )
    return (
        output,
        grad_tokens,
        owned[0],
        owned[1],
        owned[2],
        owned[3],
        owned[4],
        owned[5],
        owned[6],
    )


F32, BF16 = jnp.float32, jnp.bfloat16
NN = (((1,), (0,)), ((), ()))
NT = (((1,), (1,)), ((), ()))
TN = (((0,), (0,)), ((), ()))


def mm(left, right, dims=NN):
    return lax.dot_general(left, right, dims, preferred_element_type=F32)


def local_call(body, outs, args, flops=0, scratch=(), scalars=0):
    shapes = [jax.ShapeDtypeStruct(s, d) for s, d in outs]
    spaces = [pltpu.SMEM] * scalars + [pltpu.VMEM] * (len(args) - scalars)
    size = sum(math.prod(a.shape) * a.dtype.itemsize for a in list(args) + shapes)
    return pl.pallas_call(
        body,
        out_shape=shapes,
        in_specs=[pl.BlockSpec(memory_space=s) for s in spaces],
        out_specs=[pl.BlockSpec(memory_space=pltpu.VMEM)] * len(shapes),
        scratch_shapes=list(scratch),
        compiler_params=pltpu.CompilerParams(vmem_limit_bytes=32 * 2**20),
        cost_estimate=pl.CostEstimate(flops=int(flops), bytes_accessed=size, transcendentals=0),
    )(*args)


def flips(count):
    return [[(i, i ^ k) for i in range(count)] for k in range(count)]


def send_z(blocks):
    return [lax.ppermute(b, "z", f) for b, f in zip(blocks, flips(lax.axis_size("z"))[1:])]


def send_c(block):
    return lax.ppermute(block, "c", flips(2)[1])


def gather_group(own):
    blocks = [own] + send_z([own] * (lax.axis_size("z") - 1))
    return blocks + [send_c(b) for b in blocks]


def half_sum_kernel(near, far, mine, *low):
    for k in range(near.shape[0]):
        total = near[k].astype(F32) + far[k].astype(F32)
        if k == 0:
            mine[...] = total
        else:
            low[k - 1][...] = total.astype(BF16)


def scatter_group(near, far):
    depth, rows, lanes = near.shape
    outs = [((rows, lanes), F32)] + [((rows, lanes), BF16)] * (depth - 1)
    mine, *low = local_call(half_sum_kernel, outs, (near, send_c(far)))
    return [mine] + send_z(low)


def add_up(refs):
    total = refs[0][...]
    for ref in refs[1:]:
        total = total + ref[...].astype(F32)
    return total


def xor_order(blocks, index):
    step = 1
    while step < len(blocks):
        swap = (index & step) != 0
        blocks = [jnp.where(swap, blocks[b ^ step], blocks[b]) for b in range(len(blocks))]
        step *= 2
    return blocks


def columns_kernel(dims, w_qkv, w_up, vecs, out):
    ny, members, nx, ff_rows = dims
    cols = 3 * ny * HDIM
    for g in range(members):
        parts = []
        for t in range(3):
            for y in range(ny):
                at = (t * HEADS + y * members + g) * HDIM
                parts.append(w_qkv[:, at : at + HDIM])
        out[g, :, :cols] = jnp.concatenate(parts, 1)
        out[g, :, cols : cols + 128] = vecs[...]
        for y in range(ny):
            for x in range(nx):
                at = ((y * members + g) * nx + x) * ff_rows
                to = cols + 128 + (y * nx + x) * ff_rows
                out[g, :, to : to + ff_rows] = w_up[:, at : at + ff_rows]


def pick_kernel(cap, where, chosen_t, tokens, cot, rows, pick):
    seq_count, seg_len = tokens.shape[:2]
    base = where[4] * seg_len
    places = base + lax.broadcasted_iota(jnp.int32, (chosen_t.shape[0], seg_len), 1)
    slots = lax.broadcasted_iota(jnp.int32, (cap, seg_len), 0)
    for s in range(seq_count):
        at = chosen_t[:, s : s + 1]
        present = jnp.sum((at == places).astype(F32), 0, keepdims=True)
        rank = jnp.sum(((at >= base) & (at < places)).astype(F32), 0, keepdims=True)
        hot = jnp.where(rank.astype(jnp.int32) == slots, present, 0.0).astype(BF16)
        pick[s] = hot
        rows[s, :cap] = mm(hot, tokens[s]).astype(BF16)
        rows[s, cap:] = mm(hot, cot[s]).astype(BF16)


def spread_kernel(dims, where, chosen, chosen_t, spread):
    ny, nc, nz, nx, seg_len, cap = dims
    c, z, line = where[0], where[1], where[2]
    routed = chosen_t.shape[0]
    members = nc * nz

    def owner_of(mine):
        return lax.div(mine, jnp.int32(seg_len))

    mine_col = chosen_t[:, 0:1]
    mine_row = chosen[0:1, :]
    for s in range(1, chosen.shape[0]):
        mine_col = jnp.where(line == s, chosen_t[:, s : s + 1], mine_col)
        mine_row = jnp.where(line == s, chosen[s : s + 1, :], mine_row)
    owner, owner_row = owner_of(mine_col), owner_of(mine_row)
    order = lax.broadcasted_iota(jnp.int32, (routed, routed), 0)
    other = lax.broadcasted_iota(jnp.int32, (routed, routed), 1)
    same = (owner == owner_row) & (other < order)
    slot = jnp.sum(same.astype(F32), 1, keepdims=True).astype(jnp.int32)
    ox, rest = lax.rem(owner, jnp.int32(nx)), lax.div(owner, jnp.int32(nx))
    oz, rest = lax.rem(rest, jnp.int32(nz)), lax.div(rest, jnp.int32(nz))
    oc, oy = lax.rem(rest, jnp.int32(nc)), lax.div(rest, jnp.int32(nc))
    cell = ((((oc ^ c) * nz + (oz ^ z)) * ny + oy) * nx + ox) * cap + slot
    own = routed // members
    cells = [cell[b * own : (b + 1) * own] for b in range(members)]
    for b, block in enumerate(xor_order(cells, where[3])):
        lanes = lax.broadcasted_iota(jnp.int32, (own, spread.shape[1]), 1)
        spread[b * own : (b + 1) * own] = (block == lanes).astype(F32).astype(BF16)


def kept_pairs(member, routed, own):
    down = lax.broadcasted_iota(jnp.int32, (routed, routed), 0)
    across = lax.broadcasted_iota(jnp.int32, (routed, routed), 1)
    shift = own.bit_length() - 1
    first = ((down >> shift) ^ member) * own + (down & (own - 1))
    second = ((across >> shift) ^ member) * own + (across & (own - 1))
    return second <= first


def probabilities(queries, keys, kept):
    scores = jnp.where(kept, mm(queries, keys, NT) * HDIM ** (-0.5), neg_large)
    top = jnp.max(scores, 1, keepdims=True)
    probs = jnp.where(kept, jnp.exp(scores - top), 0.0)
    return probs, jnp.sum(probs, 1, keepdims=True)


def inverse_rms(values):
    return lax.rsqrt(jnp.mean(values * values, 1, keepdims=True) + epsilon)


def line_rows(got, first, count):
    return jnp.concatenate([got[q, first : first + count] for q in range(got.shape[0])], 0)


def natural_rows(got, dims, first, count, out):
    ny, members, nx, rows = dims
    for y in range(ny):
        for g in range(members):
            for x in range(nx):
                to = ((y * members + g) * nx + x) * rows
                out[to : to + rows] = got[y * nx + x, g, :, first : first + count]


def attention_kernel(dims, members, where, spread, got_rows, got_qkv, *refs):
    ny, nx, rows, cap, ff_rows = dims
    blocks, outs = refs[:members], refs[members:]
    picked_o, normed_o, w_o, vecs_o, joined_o, att_o, exact_o, near_o, far_o, vec_s = outs
    heads = ny
    cols = 3 * heads * HDIM
    routed, width = picked_o.shape
    own = routed // members
    spots = jnp.concatenate(
        [b[q, :cap] for b in blocks for q in range(b.shape[0])], 0
    )
    picked_low = mm(spread[...], spots).astype(BF16)
    picked_o[...] = picked_low
    picked = picked_low.astype(F32)
    natural_rows(got_qkv, (ny, members, nx, rows), 0, cols, w_o)
    natural_rows(got_qkv, (ny, members, nx, rows), cols, 128, vec_s)
    eye = lax.broadcasted_iota(jnp.int32, (8, 128), 0)
    eye = (eye == lax.broadcasted_iota(jnp.int32, (8, 128), 1)).astype(F32).astype(BF16)
    vecs = mm(eye, vec_s[...], NT)
    vecs_o[...] = vecs
    normed = (picked * inverse_rms(picked) * vecs[0:1]).astype(BF16)
    normed_o[...] = normed
    joined = mm(normed, w_o[...]).astype(BF16)
    joined_o[...] = joined
    kept = kept_pairs(where[3], routed, own)
    parts = []
    for h in range(heads):
        queries, keys, values = (
            joined[:, (t * heads + h) * HDIM : (t * heads + h + 1) * HDIM] for t in range(3)
        )
        probs, total = probabilities(queries, keys, kept)
        parts.append(mm(probs.astype(BF16), values) / total)
    exact = jnp.concatenate(parts, 1)
    exact_o[...] = exact
    attended = exact.astype(BF16)
    att_o[...] = attended
    branch = mm(attended, line_rows(got_rows, ff_rows, rows)).astype(BF16)
    put_halves(branch, near_o, far_o)


def put_halves(values, near, far):
    depth, own = near.shape[:2]
    for k in range(depth):
        near[k] = values[k * own : (k + 1) * own]
        far[k] = values[(depth + k) * own : (depth + k + 1) * own]


def update_kernel(dims, members, spread, got_rows, picked, vecs, *refs):
    cap, ff_rows = dims
    blocks, (cot_o, gate_o, d_result_o, d_active_o) = refs[:members], refs[members:]
    spots = jnp.concatenate(
        [b[q, cap:] for b in blocks for q in range(b.shape[0])], 0
    )
    cot_low = mm(spread[...], spots).astype(BF16)
    cot_o[...] = cot_low
    logit = jnp.sum(picked[...].astype(F32) * vecs[2:3, :], 1, keepdims=True)
    gate = 1.0 / (1.0 + jnp.exp(-logit))
    gate_o[...] = gate
    d_result = (gate * cot_low.astype(F32)).astype(BF16)
    d_result_o[...] = d_result
    d_active_o[...] = mm(d_result, line_rows(got_rows, 0, ff_rows), NT)


def hidden_kernel(own, picked, vecs, *refs):
    *terms, hidden_o, normed_o = refs
    hidden = picked[:own, :].astype(F32) + add_up(terms)
    hidden_o[...] = hidden
    normed_o[...] = (hidden * inverse_rms(hidden) * vecs[1:2, :]).astype(BF16)


def forward_kernel(dims, members, got_up, d_active, *refs):
    blocks, (active_o, d_upper_o, near_o, far_o, w_s) = refs[:members], refs[members:]
    natural_rows(got_up, dims, 0, got_up.shape[3], w_s)
    normed = jnp.concatenate([b[...] for b in blocks], 0)
    upper = mm(normed, w_s[...])
    below = 0.5 * (1.0 + lax.erf(upper * (0.5**0.5)))
    active_o[...] = (upper * below).astype(BF16)
    slope = below + upper * jnp.exp(-0.5 * upper * upper) * ((2.0 * math.pi) ** -0.5)
    d_upper = (d_active[...] * slope).astype(BF16)
    d_upper_o[...] = d_upper
    put_halves(mm(d_upper, w_s[...], NT).astype(BF16), near_o, far_o)


def ff_grads_kernel(dims, members, active, d_upper, d_result, *refs):
    ny, nx, rows, ff_rows = dims
    blocks, (sums_o,) = refs[:members], refs[members:]
    lines = ny * nx
    normed = jnp.concatenate([b[...] for b in blocks], 0)
    down = mm(active[...], d_result[...], TN).astype(BF16)
    up = mm(normed, d_upper[...], TN).astype(BF16)
    wide = up.shape[1]
    each = ff_rows + members * rows // 2
    for y in range(ny):
        for x in range(nx):
            q = y * nx + x
            sums_o[q * each : q * each + ff_rows] = down[q * ff_rows : (q + 1) * ff_rows]
            for g in range(members):
                at = ((y * members + g) * nx + x) * rows
                half, row = divmod(g * rows, members * rows // 2)
                to = q * each + ff_rows + row
                sums_o[to : to + rows, half * wide : (half + 1) * wide] = up[at : at + rows]


def result_kernel(dims, active, attended, got_rows, cot, gate, spread, logit_o, near_o, far_o):
    rows, ff_rows = dims
    result = mm(active[...], line_rows(got_rows, 0, ff_rows))
    combined = result + mm(attended[...], line_rows(got_rows, ff_rows, rows))
    logit = jnp.sum(cot[...].astype(F32) * combined, 1, keepdims=True)
    logit_o[...] = logit * gate[...] * (1.0 - gate[...])
    update = (gate[...] * combined).astype(BF16)
    put_halves(mm(spread[...], update, TN).astype(BF16), near_o, far_o)


def hidden_back_kernel(own, hidden_r, vecs, gate, cot, *refs):
    *terms, d_branch_o, d_hidden_o, gain_o = refs
    d_normed = add_up(terms)
    hidden = hidden_r[...]
    inv = inverse_rms(hidden)
    u = d_normed * vecs[1:2, :]
    d_hidden = inv * u - hidden * (inv * inv * inv * jnp.mean(u * hidden, 1, keepdims=True))
    d_hidden_o[...] = d_hidden
    gain_o[...] = (d_normed * hidden * inv).astype(BF16)
    d_update = gate[:own, :] * cot[:own, :].astype(F32)
    d_branch_o[...] = (d_update + d_hidden).astype(BF16)


def attention_back_kernel(dims, members, where, *refs):
    rows, ff_rows = dims
    got_rows, joined_r, exact_r, w, vecs, picked_r, logit, d_hidden, spread = refs[:9]
    blocks = refs[9 : 9 + members]
    near_o, far_o, d_joined_o, gain_o = refs[9 + members :]
    routed, width = picked_r.shape
    own = routed // members
    heads = joined_r.shape[1] // (3 * HDIM)
    d_branch = jnp.concatenate([b[...] for b in blocks], 0)
    d_attended = mm(d_branch, line_rows(got_rows, ff_rows, rows), NT).astype(BF16)
    joined = joined_r[...]
    exact = exact_r[...]
    kept = kept_pairs(where[3], routed, own)
    grads = [[], [], []]
    for h in range(heads):
        queries, keys, values = (
            joined[:, (t * heads + h) * HDIM : (t * heads + h + 1) * HDIM] for t in range(3)
        )
        probs, total = probabilities(queries, keys, kept)
        d_att = d_attended[:, h * HDIM : (h + 1) * HDIM]
        d_wide = d_att.astype(F32)
        delta = jnp.sum(d_wide * exact[:, h * HDIM : (h + 1) * HDIM], 1, keepdims=True)
        d_scores = (probs / total * (mm(d_att, values, NT) - delta)).astype(BF16)
        grads[0].append(mm(d_scores, keys) * HDIM ** (-0.5))
        grads[1].append(mm(d_scores, queries, TN) * HDIM ** (-0.5))
        grads[2].append(mm(probs.astype(BF16), (d_wide / total).astype(BF16), TN))
    d_joined = jnp.concatenate(grads[0] + grads[1] + grads[2], 1).astype(BF16)
    d_joined_o[...] = d_joined
    d_normed = mm(d_joined, w[...], NT)
    picked = picked_r[...].astype(F32)
    inv = inverse_rms(picked)
    gain_o[...] = (d_normed * picked * inv).astype(BF16)
    v = d_normed * vecs[0:1, :]
    d_picked = inv * v - picked * (inv * inv * inv * jnp.mean(v * picked, 1, keepdims=True))
    d_picked = d_picked + logit[...] * vecs[2:3, :]
    first = d_picked[:own] + d_hidden[...]
    d_picked = jnp.concatenate([first, d_picked[own:]], 0).astype(BF16)
    put_halves(mm(spread[...], d_picked, TN).astype(BF16), near_o, far_o)


def grads_kernel(dims, members, normed, d_joined, attended, gain_a, gain_m, picked, logit, *refs):
    ny, nx, rows = dims
    blocks, (sums_o,) = refs[:members], refs[members:]
    cols = d_joined.shape[1]
    routed, width = normed.shape
    own = gain_m.shape[0]
    main = mm(normed[...], d_joined[...], TN).astype(BF16)
    lanes = lax.broadcasted_iota(jnp.int32, (routed, 128), 1)

    def lane(k, count):
        return (lanes[:count] == k).astype(F32)

    vec = mm(gain_a[...], lane(0, routed).astype(BF16), TN)
    vec = vec + mm(gain_m[...], lane(1, own).astype(BF16), TN)
    high = logit[...].astype(BF16)
    low = (logit[...] - high.astype(F32)).astype(BF16)
    vec = vec + mm(picked[...], (lane(2, routed) * high.astype(F32)).astype(BF16), TN)
    vec = vec + mm(picked[...], (lane(2, routed) * low.astype(F32)).astype(BF16), TN)
    vec = vec.astype(BF16)
    out = mm(attended[...], jnp.concatenate([b[...] for b in blocks], 0), TN).astype(BF16)
    for y in range(ny):
        for x in range(nx):
            q = y * nx + x
            for g in range(members):
                at = ((y * members + g) * nx + x) * rows
                sums_o[q, g * rows : (g + 1) * rows, :cols] = main[at : at + rows]
                sums_o[q, g * rows : (g + 1) * rows, cols:] = vec[at : at + rows]
            half = width // 2
            end = members * rows
            for k in range(2):
                piece = out[q * rows : (q + 1) * rows, k * half : (k + 1) * half]
                sums_o[q, end + k * rows : end + (k + 1) * rows, :] = piece


def join_slots_kernel(cap, *refs):
    *terms, rows_o = refs
    half = len(terms) // 2
    for k in range(2):
        total = add_up(terms[k * half : (k + 1) * half]).astype(BF16)
        for q in range(rows_o.shape[0]):
            rows_o[q, k * cap : (k + 1) * cap] = total[q * cap : (q + 1) * cap]


def place_kernel(cap, got, pick, tokens, cot, out_o, grad_o):
    for s in range(tokens.shape[0]):
        hot = pick[s]
        out_o[s] = (tokens[s].astype(F32) + mm(hot, got[s, :cap], TN)).astype(BF16)
        grad_o[s] = (cot[s].astype(F32) + mm(hot, got[s, cap:], TN)).astype(BF16)


def line_sums_kernel(dims, got, ff, send_o, out_o, down_o):
    members, rows, ff_rows = dims
    cols = got.shape[2]
    wide = ff.shape[1] // 2
    total = got[0].astype(F32)
    for q in range(1, got.shape[0]):
        total = total + got[q].astype(F32)
    for g in range(members):
        send_o[g, :, :cols] = total[g * rows : (g + 1) * rows].astype(BF16)
        half, row = divmod(g * rows, members * rows // 2)
        at = ff_rows + row
        send_o[g, :, cols:] = ff[at : at + rows, half * wide : (half + 1) * wide]
    end = members * rows
    out_o[...] = jnp.concatenate([total[end : end + rows], total[end + rows :]], 1)
    down_o[...] = ff[:ff_rows, :].astype(F32)


def unpack_kernel(dims, got, qkv_o, up_o, vec_o):
    ny, members, nx, ff_rows = dims
    cols = 3 * ny * HDIM
    for t in range(3):
        for y in range(ny):
            from_ = (t * ny + y) * HDIM
            row = [got[g, :, from_ : from_ + HDIM] for g in range(members)]
            at = (t * HEADS + y * members) * HDIM
            qkv_o[:, at : at + members * HDIM] = jnp.concatenate(row, 1).astype(F32)
    for y in range(ny):
        for g in range(members):
            for x in range(nx):
                at = ((y * members + g) * nx + x) * ff_rows
                from_ = cols + 128 + (y * nx + x) * ff_rows
                up_o[:, at : at + ff_rows] = got[g, :, from_ : from_ + ff_rows].astype(F32)
    vec = got[0, :, cols : cols + 128].astype(F32)
    for g in range(1, members):
        vec = vec + got[g, :, cols : cols + 128].astype(F32)
    vec_o[...] = vec


def grouped(
    tokens, chosen, w_qkv, w_out, w_up, w_down, gain_attn, gain_mlp, router, cotangent
):
    ny, nc, nz, nx = (lax.axis_size(a) for a in ("y", "c", "z", "x"))
    y, c, z, x = (lax.axis_index(a) for a in ("y", "c", "z", "x"))
    seq_count, seg_len, width = tokens.shape
    cap = seg_len // 4
    routed = chosen.shape[1]
    members, lines = nc * nz, ny * nx
    member, line = c * nz + z, y * nx + x
    shard = ((y * nc + c) * nz + z) * nx + x
    rows, ff_rows = w_qkv.shape[0], w_down.shape[0]
    heads = HEADS // members
    own = routed // members
    cols, wide = 3 * heads * HDIM, lines * ff_rows
    line_axes, group_axes = ("y", "x"), ("c", "z")
    where = jnp.stack([c, z, line, member, shard]).astype(jnp.int32)
    chosen_t = chosen.T
    block = (own, width)
    halves = [((nz, own, width), BF16)] * 2
    slot_halves = [((nz, lines * cap, width), BF16)] * 2

    vecs = jnp.pad(jnp.stack([gain_attn, gain_mlp, router], 1), ((0, 0), (0, 125)))
    (columns,) = local_call(
        partial(columns_kernel, (ny, members, nx, ff_rows)),
        [((members, rows, cols + 128 + wide), BF16)],
        (w_qkv, w_up, vecs),
    )
    got_rows = lax.all_gather(jnp.concatenate([w_down, w_out]), line_axes)
    got_cols = lax.all_to_all(columns, group_axes, 0, 0, tiled=True)
    got_qkv = got_cols[:, :, : cols + 128]
    got_qkv = lax.all_to_all(
        jnp.broadcast_to(got_qkv, (lines,) + got_qkv.shape), line_axes, 0, 0, tiled=True
    )
    got_up = lax.all_gather(got_cols[:, :, cols + 128 :], line_axes)

    picked_rows, pick = local_call(
        partial(pick_kernel, cap),
        [((seq_count, 2 * cap, width), BF16), ((seq_count, cap, seg_len), BF16)],
        (where, chosen_t, tokens, cotangent),
        scalars=1,
    )
    (spread,) = local_call(
        partial(spread_kernel, (ny, nc, nz, nx, seg_len, cap)),
        [((routed, members * lines * cap), BF16)],
        (where, chosen, chosen_t),
        scalars=1,
    )
    slots = gather_group(lax.all_to_all(picked_rows, line_axes, 0, 0, tiled=True))

    picked, normed, full_qkv, full_vecs, joined, attended, exact, near, far = local_call(
        partial(attention_kernel, (ny, nx, rows, cap, ff_rows), members),
        [
            ((routed, width), BF16),
            ((routed, width), BF16),
            ((width, cols), BF16),
            ((8, width), F32),
            ((routed, cols), BF16),
            ((routed, heads * HDIM), BF16),
            ((routed, heads * HDIM), F32),
        ]
        + halves,
        (where, spread, got_rows, got_qkv, *slots),
        flops=1.2e9,
        scratch=[pltpu.VMEM((width, 128), BF16)],
        scalars=1,
    )
    terms = scatter_group(near, far)
    cot, gate, d_result, d_active = local_call(
        partial(update_kernel, (cap, ff_rows), members),
        [
            ((routed, width), BF16),
            ((routed, 1), F32),
            ((routed, width), BF16),
            ((routed, wide), F32),
        ],
        (spread, got_rows, picked, full_vecs, *slots),
        flops=8e8,
    )
    hidden, normed_own = local_call(
        partial(hidden_kernel, own), [(block, F32), (block, BF16)], (picked, full_vecs, *terms)
    )
    normed_mlp = gather_group(normed_own)

    active, d_upper, near, far = local_call(
        partial(forward_kernel, (ny, members, nx, rows), members),
        [((routed, wide), BF16)] * 2 + halves,
        (got_up, d_active, *normed_mlp),
        flops=6e8,
        scratch=[pltpu.VMEM((width, wide), BF16)],
    )
    terms = scatter_group(near, far)
    (ff_part,) = local_call(
        partial(ff_grads_kernel, (ny, nx, rows, ff_rows), members),
        [((lines * (ff_rows + members * rows // 2), width), BF16)],
        (active, d_upper, d_result, *normed_mlp),
        flops=6e8,
    )
    ff_sum = lax.psum_scatter(ff_part, line_axes, tiled=True)
    logit, up_near, up_far = local_call(
        partial(result_kernel, (rows, ff_rows)),
        [((routed, 1), F32)] + slot_halves,
        (active, attended, got_rows, cot, gate, spread),
        flops=8e8,
    )
    d_branch_own, d_hidden, gain_m = local_call(
        partial(hidden_back_kernel, own),
        [(block, BF16), (block, F32), (block, BF16)],
        (hidden, full_vecs, gate, cot, *terms),
    )
    d_branch = gather_group(d_branch_own)
    update_terms = scatter_group(up_near, up_far)

    near, far, d_joined, gain_a = local_call(
        partial(attention_back_kernel, (rows, ff_rows), members),
        slot_halves + [((routed, cols), BF16), ((routed, width), BF16)],
        (where, got_rows, joined, exact, full_qkv, full_vecs, picked, logit, d_hidden, spread)
        + tuple(d_branch),
        flops=1.2e9,
        scalars=1,
    )
    picked_terms = scatter_group(near, far)
    (part,) = local_call(
        partial(grads_kernel, (ny, nx, rows), members),
        [((lines, members * rows + 2 * rows, cols + 128), BF16)],
        (normed, d_joined, attended, gain_a, gain_m, picked, logit, *d_branch),
        flops=5e8,
    )
    got_part = lax.all_to_all(part, line_axes, 0, 0, tiled=True)
    (slot_rows,) = local_call(
        partial(join_slots_kernel, cap),
        [((lines, 2 * cap, width), BF16)],
        (*update_terms, *picked_terms),
    )
    slot_rows = lax.all_to_all(slot_rows, line_axes, 0, 0, tiled=True)
    send, grad_out, grad_down = local_call(
        partial(line_sums_kernel, (members, rows, ff_rows)),
        [
            ((members, rows, cols + 128 + wide), BF16),
            ((rows, width), F32),
            ((ff_rows, width), F32),
        ],
        (got_part, ff_sum),
    )
    got = lax.all_to_all(send, group_axes, 0, 0, tiled=True)
    output, grad_tokens = local_call(
        partial(place_kernel, cap),
        [(tokens.shape, BF16), (tokens.shape, BF16)],
        (slot_rows, pick, tokens, cotangent),
    )
    grad_qkv, grad_up, grad_vecs = local_call(
        partial(unpack_kernel, (ny, members, nx, ff_rows)),
        [(w_qkv.shape, F32), (w_up.shape, F32), ((rows, 128), F32)],
        (got,),
    )
    return (
        output,
        grad_tokens,
        grad_qkv,
        grad_out,
        grad_up,
        grad_down,
        grad_vecs[:, 0],
        grad_vecs[:, 1],
        grad_vecs[:, 2],
    )


def fits(mesh):
    head_count, block_count = mesh.devices.shape
    members = (head_count // 2) * (block_count // 2)
    power = members & (members - 1) == 0
    return power and head_count == 4 and HEADS == 2 * members


def solution(mesh):
    if fits(mesh):
        head_count, block_count = mesh.devices.shape
        devices = mesh.devices.reshape(2, head_count // 2, block_count // 2, 2)
        mesh = jax.sharding.Mesh(devices, ("y", "c", "z", "x"))
        body, all_axes = grouped, ("y", "c", "z", "x")
    else:
        body, all_axes = shards, ("head", "blk")
    seqs, mats, vecs = P(None, all_axes, None), P(all_axes, None), P(all_axes)
    in_specs = (seqs, P(), mats, mats, mats, mats, vecs, vecs, vecs, seqs)
    out_specs = (seqs, seqs, mats, mats, mats, mats, vecs, vecs, vecs)
    return jax.shard_map(body, mesh=mesh, in_specs=in_specs, out_specs=out_specs, check_vma=False)
```

```python
import math
from functools import partial

import jax
import jax.numpy as jnp
from jax import lax
from jax.experimental import pallas as pl
from jax.experimental.pallas import tpu as pltpu
from jax.sharding import PartitionSpec as P

HEADS = 16
HDIM = 64


epsilon = 1e-06
neg_large = -1e30


def rms_norm(values, gain_vec):
    inverse_rms = lax.rsqrt(jnp.mean(values * values, axis=-1, keepdims=True) + epsilon)
    return values * inverse_rms * gain_vec


def exact_gelu(values):
    return jax.nn.gelu(values, approximate=False)


def take_rows(seq_rows, row_index):
    return seq_rows[row_index]


def add_rows(seq_rows, row_index, additions):
    return seq_rows.at[row_index].add(additions)


def shards(tokens, chosen, w_qkv, w_out, w_up, w_down, gain_attn, gain_mlp, router, cotangent):
    head_count = lax.axis_size("head")
    block_count = lax.axis_size("blk")
    shard_count = head_count * block_count
    seq_count, seg_len, model_width = tokens.shape
    cap_len = seg_len // 4
    routed_count = chosen.shape[1]
    seq_len = seg_len * shard_count
    local_heads = HEADS // head_count
    slot_rows = head_count * cap_len
    scale_factor = HDIM ** (-0.5)
    head_index = lax.axis_index("head")
    block_index = lax.axis_index("blk")
    my_shard = head_index * block_count + block_index
    bounds = jnp.arange(shard_count + 1, dtype=jnp.int32) * seg_len
    before = jax.vmap(lambda chosen_row: jnp.searchsorted(chosen_row, bounds, side="left"))(chosen)
    first_index = before[:, :-1]
    shard_load = before[:, 1:] - first_index
    slot_iota = jnp.arange(cap_len, dtype=jnp.int32)
    live_table = slot_iota[None, None, :] < shard_load[:, :, None]
    lookup = jnp.minimum(first_index[:, :, None] + slot_iota[None, None, :], routed_count - 1)
    place_table = jnp.take_along_axis(
        chosen, lookup.reshape(seq_count, shard_count * cap_len), axis=1
    )
    place_table = jnp.where(
        live_table, place_table.reshape(seq_count, shard_count, cap_len), seq_len
    )
    my_positions = lax.dynamic_index_in_dim(place_table, my_shard, 1, False)
    my_live = lax.dynamic_index_in_dim(live_table, my_shard, 1, False)
    local_rows = jnp.clip(my_positions - my_shard * seg_len, 0, seg_len - 1)
    cycle_positions = place_table.reshape(seq_count, head_count, block_count, cap_len).transpose(
        0, 2, 1, 3
    )
    cycle_positions = cycle_positions.reshape(seq_count, block_count * slot_rows)
    query_positions = lax.dynamic_slice_in_dim(
        cycle_positions, block_index * slot_rows, slot_rows, 1
    )
    live_weight = my_live.astype(jnp.float32)[:, :, None]
    gathered = (
        lax.all_gather(w_qkv, ("head", "blk"), axis=0, tiled=True),
        lax.all_gather(w_out, ("head", "blk"), axis=0, tiled=True),
        lax.all_gather(w_up, ("head", "blk"), axis=0, tiled=True),
        lax.all_gather(w_down, ("head", "blk"), axis=0, tiled=True),
        lax.all_gather(gain_attn, ("head", "blk"), axis=0, tiled=True),
        lax.all_gather(gain_mlp, ("head", "blk"), axis=0, tiled=True),
        lax.all_gather(router, ("head", "blk"), axis=0, tiled=True),
    )
    full_qkv, full_out, full_up, full_down, full_gain_attn, full_gain_mlp, full_router = gathered
    picked = jax.vmap(take_rows)(tokens, local_rows)
    picked = jnp.where(my_live[:, :, None], picked, jnp.zeros_like(picked))
    picked_exact = picked.astype(jnp.float32)
    router_gate = jax.nn.sigmoid(
        jnp.einsum("scd,d->sc", picked, full_router, preferred_element_type=jnp.float32)
    )
    normed_exact, norm_attn_back = jax.vjp(
        rms_norm, picked_exact, full_gain_attn.astype(jnp.float32)
    )
    normed = normed_exact.astype(jnp.bfloat16)
    joined = jnp.einsum("scd,de->sce", normed, full_qkv, preferred_element_type=jnp.float32).astype(
        jnp.bfloat16
    )
    to_heads = lax.all_to_all(
        joined.reshape(seq_count, cap_len, 3, model_width),
        "head",
        split_axis=3,
        concat_axis=1,
        tiled=True,
    )
    queries_tok = to_heads[:, :, 0]
    queries_heads = queries_tok.reshape(seq_count, slot_rows, local_heads, HDIM)
    key_values = to_heads[:, :, 1:3]
    my_keys = key_values[:, :, 0].reshape(seq_count, slot_rows, local_heads, HDIM)
    my_values = key_values[:, :, 1].reshape(seq_count, slot_rows, local_heads, HDIM)
    stat_shape = (seq_count, local_heads, slot_rows)
    piece = lax.all_gather(key_values, "blk", axis=1, tiled=True)
    run_max = jnp.full(stat_shape, neg_large, jnp.float32)
    piece_rows = piece.shape[1]
    key_pos = cycle_positions
    keys_piece = piece[:, :, 0].reshape(seq_count, piece_rows, local_heads, HDIM)
    values_piece = piece[:, :, 1].reshape(seq_count, piece_rows, local_heads, HDIM)
    scores = (
        jnp.einsum("sqhd,skhd->shqk", queries_heads, keys_piece, preferred_element_type=jnp.float32)
        * scale_factor
    )
    allowed = key_pos[:, None, None, :] <= query_positions[:, None, :, None]
    scores = jnp.where(allowed, scores, neg_large)
    new_max = jnp.maximum(run_max, jnp.max(scores, axis=3))
    prob_block = jnp.where(allowed, jnp.exp(scores - new_max[..., None]), 0.0)
    new_total = jnp.sum(prob_block, axis=3)
    added = jnp.einsum(
        "shqk,skhd->sqhd",
        prob_block.astype(jnp.bfloat16),
        values_piece,
        preferred_element_type=jnp.float32,
    )
    attended_exact = added / new_total.transpose(0, 2, 1)[..., None]
    log_sum = new_max + jnp.log(new_total)
    attended_tok = attended_exact.astype(jnp.bfloat16).reshape(
        seq_count, slot_rows, local_heads * HDIM
    )
    attended = lax.all_to_all(attended_tok, "head", split_axis=1, concat_axis=2, tiled=True)
    branch = jnp.einsum("sce,ed->scd", attended, full_out, preferred_element_type=jnp.float32)
    hidden_state = picked_exact + branch
    normed_mlp_exact, norm_mlp_back = jax.vjp(
        rms_norm, hidden_state, full_gain_mlp.astype(jnp.float32)
    )
    normed_mlp = normed_mlp_exact.astype(jnp.bfloat16)
    upper = jnp.einsum("scd,di->sci", normed_mlp, full_up, preferred_element_type=jnp.float32)
    active_exact, gelu_back = jax.vjp(exact_gelu, upper)
    active = active_exact.astype(jnp.bfloat16)
    result = jnp.einsum("sci,id->scd", active, full_down, preferred_element_type=jnp.float32)
    combined = branch + result
    update = router_gate[:, :, None] * combined * live_weight
    output = jax.vmap(add_rows)(tokens.astype(jnp.float32), local_rows, update).astype(jnp.bfloat16)
    regathered = (
        lax.all_gather(w_qkv, ("head", "blk"), axis=0, tiled=True),
        lax.all_gather(w_out, ("head", "blk"), axis=0, tiled=True),
        lax.all_gather(w_up, ("head", "blk"), axis=0, tiled=True),
        lax.all_gather(w_down, ("head", "blk"), axis=0, tiled=True),
        lax.all_gather(gain_attn, ("head", "blk"), axis=0, tiled=True),
        lax.all_gather(gain_mlp, ("head", "blk"), axis=0, tiled=True),
        lax.all_gather(router, ("head", "blk"), axis=0, tiled=True),
    )
    back_qkv, back_out, back_up, back_down, back_gain_attn, back_gain_mlp, back_router = regathered
    picked_cot = jax.vmap(take_rows)(cotangent, local_rows).astype(jnp.float32) * live_weight
    d_update = router_gate[:, :, None] * picked_cot
    d_logit = jnp.sum(picked_cot * combined, axis=2) * router_gate * (1.0 - router_gate)
    grad_router = jnp.einsum("sc,scd->d", d_logit, picked_exact, precision=lax.Precision.HIGHEST)
    d_result = d_update.astype(jnp.bfloat16)
    d_active = jnp.einsum("scd,id->sci", d_result, back_down, preferred_element_type=jnp.float32)
    d_upper = gelu_back(d_active)[0].astype(jnp.bfloat16)
    d_normed_mlp = jnp.einsum("sci,di->scd", d_upper, back_up, preferred_element_type=jnp.float32)
    d_hidden, grad_gain_mlp = norm_mlp_back(d_normed_mlp)
    d_branch = (d_update + d_hidden).astype(jnp.bfloat16)
    d_attended = jnp.einsum(
        "scd,ed->sce", d_branch, back_out, preferred_element_type=jnp.float32
    ).astype(jnp.bfloat16)
    d_att_tok = lax.all_to_all(d_attended, "head", split_axis=2, concat_axis=1, tiled=True)
    d_att_heads = d_att_tok.reshape(seq_count, slot_rows, local_heads, HDIM)
    delta_tok = jnp.sum(d_att_heads.astype(jnp.float32) * attended_exact, axis=3)
    delta_sq = delta_tok.transpose(0, 2, 1)
    piece = lax.all_gather(key_values, "blk", axis=1, tiled=True)
    piece_rows = piece.shape[1]
    key_pos = cycle_positions
    keys_piece = piece[:, :, 0].reshape(seq_count, piece_rows, local_heads, HDIM)
    values_piece = piece[:, :, 1].reshape(seq_count, piece_rows, local_heads, HDIM)
    scores = (
        jnp.einsum("sqhd,skhd->shqk", queries_heads, keys_piece, preferred_element_type=jnp.float32)
        * scale_factor
    )
    allowed = key_pos[:, None, None, :] <= query_positions[:, None, :, None]
    prob_block = jnp.where(allowed, jnp.exp(scores - log_sum[..., None]), 0.0)
    d_prob = jnp.einsum(
        "sqhd,skhd->shqk", d_att_heads, values_piece, preferred_element_type=jnp.float32
    )
    d_scores = (prob_block * (d_prob - delta_sq[..., None])).astype(jnp.bfloat16)
    d_queries = (
        jnp.einsum("shqk,skhd->sqhd", d_scores, keys_piece, preferred_element_type=jnp.float32)
        * scale_factor
    )
    lse_tok = log_sum.transpose(0, 2, 1)
    lse_high = lse_tok.astype(jnp.bfloat16)
    lse_low = (lse_tok - lse_high.astype(jnp.float32)).astype(jnp.bfloat16)
    delta_high = delta_tok.astype(jnp.bfloat16)
    delta_low = (delta_tok - delta_high.astype(jnp.float32)).astype(jnp.bfloat16)
    query_piece = lax.all_gather(queries_tok, "blk", axis=1, tiled=True)
    dout_piece = lax.all_gather(d_att_tok, "blk", axis=1, tiled=True)
    piece_lse_high = lax.all_gather(lse_high, "blk", axis=1, tiled=True)
    piece_lse_low = lax.all_gather(lse_low, "blk", axis=1, tiled=True)
    piece_delta_high = lax.all_gather(delta_high, "blk", axis=1, tiled=True)
    piece_delta_low = lax.all_gather(delta_low, "blk", axis=1, tiled=True)
    piece_rows = query_piece.shape[1]
    query_heads = query_piece.reshape(seq_count, piece_rows, local_heads, HDIM)
    dout_heads = dout_piece.reshape(seq_count, piece_rows, local_heads, HDIM)
    piece_lse = (piece_lse_high.astype(jnp.float32) + piece_lse_low.astype(jnp.float32)).transpose(
        0, 2, 1
    )
    piece_delta = (
        piece_delta_high.astype(jnp.float32) + piece_delta_low.astype(jnp.float32)
    ).transpose(0, 2, 1)
    scores = (
        jnp.einsum("sqhd,skhd->shqk", query_heads, my_keys, preferred_element_type=jnp.float32)
        * scale_factor
    )
    allowed = query_positions[:, None, None, :] <= cycle_positions[:, None, :, None]
    prob_block = jnp.where(allowed, jnp.exp(scores - piece_lse[..., None]), 0.0)
    grad_values = jnp.einsum(
        "shqk,sqhd->skhd",
        prob_block.astype(jnp.bfloat16),
        dout_heads,
        preferred_element_type=jnp.float32,
    )
    d_prob = jnp.einsum(
        "sqhd,skhd->shqk", dout_heads, my_values, preferred_element_type=jnp.float32
    )
    d_scores = (prob_block * (d_prob - piece_delta[..., None])).astype(jnp.bfloat16)
    grad_keys = (
        jnp.einsum("shqk,sqhd->skhd", d_scores, query_heads, preferred_element_type=jnp.float32)
        * scale_factor
    )
    d_heads = jnp.stack(
        [
            d_queries.astype(jnp.bfloat16),
            grad_keys.astype(jnp.bfloat16),
            grad_values.astype(jnp.bfloat16),
        ],
        axis=2,
    )
    d_heads = d_heads.reshape(seq_count, slot_rows, 3, local_heads * HDIM)
    d_joined = lax.all_to_all(d_heads, "head", split_axis=1, concat_axis=3, tiled=True).reshape(
        seq_count, cap_len, 3 * model_width
    )
    d_normed = jnp.einsum("sce,de->scd", d_joined, back_qkv, preferred_element_type=jnp.float32)
    d_picked_norm, grad_gain_attn = norm_attn_back(d_normed)
    d_picked = (
        d_hidden
        + d_picked_norm
        + d_logit[:, :, None] * back_router.astype(jnp.float32)[None, None, :]
    )
    grad_tokens = jax.vmap(add_rows)(
        cotangent.astype(jnp.float32), local_rows, d_picked * live_weight
    ).astype(jnp.bfloat16)
    grad_qkv = jnp.einsum("scd,sce->de", normed, d_joined, preferred_element_type=jnp.float32)
    grad_out = jnp.einsum("sce,scd->ed", attended, d_branch, preferred_element_type=jnp.float32)
    grad_up = jnp.einsum("scd,sci->di", normed_mlp, d_upper, preferred_element_type=jnp.float32)
    grad_down = jnp.einsum("sci,scd->id", active, d_result, preferred_element_type=jnp.float32)
    owned = (
        lax.psum_scatter(grad_qkv, ("head", "blk"), scatter_dimension=0, tiled=True),
        lax.psum_scatter(grad_out, ("head", "blk"), scatter_dimension=0, tiled=True),
        lax.psum_scatter(grad_up, ("head", "blk"), scatter_dimension=0, tiled=True),
        lax.psum_scatter(grad_down, ("head", "blk"), scatter_dimension=0, tiled=True),
        lax.psum_scatter(grad_gain_attn, ("head", "blk"), scatter_dimension=0, tiled=True),
        lax.psum_scatter(grad_gain_mlp, ("head", "blk"), scatter_dimension=0, tiled=True),
        lax.psum_scatter(grad_router, ("head", "blk"), scatter_dimension=0, tiled=True),
    )
    return (
        output,
        grad_tokens,
        owned[0],
        owned[1],
        owned[2],
        owned[3],
        owned[4],
        owned[5],
        owned[6],
    )


F32, BF16 = jnp.float32, jnp.bfloat16
NN = (((1,), (0,)), ((), ()))
NT = (((1,), (1,)), ((), ()))
TN = (((0,), (0,)), ((), ()))


def mm(left, right, dims=NN):
    return lax.dot_general(left, right, dims, preferred_element_type=F32)


def local_call(body, outs, args, flops=0, scratch=(), scalars=0, after=()):
    shapes = [jax.ShapeDtypeStruct(s, d) for s, d in outs]
    spaces = [pltpu.SMEM] * scalars + [pltpu.VMEM] * (len(args) - scalars) + [pl.ANY] * len(after)
    count = len(args)
    args = tuple(args) + tuple(after)

    def run(*refs):
        body(*refs[:count], *refs[len(args) :])

    size = sum(math.prod(a.shape) * a.dtype.itemsize for a in list(args) + shapes)
    return list(pl.pallas_call(
        run,
        out_shape=shapes,
        in_specs=[pl.BlockSpec(memory_space=s) for s in spaces],
        out_specs=[pl.BlockSpec(memory_space=pltpu.VMEM)] * len(shapes),
        scratch_shapes=list(scratch),
        compiler_params=pltpu.CompilerParams(vmem_limit_bytes=32 * 2**20),
        cost_estimate=pl.CostEstimate(flops=int(flops), bytes_accessed=size, transcendentals=0),
    )(*args))


def flips(count):
    return [[(i, i ^ k) for i in range(count)] for k in range(count)]


def send_z(blocks):
    return [lax.ppermute(b, "z", f) for b, f in zip(blocks, flips(lax.axis_size("z"))[1:])]


def send_lines(blocks):
    count = lax.axis_size("y") * lax.axis_size("x")
    return [lax.ppermute(b, ("y", "x"), f) for b, f in zip(blocks, flips(count)[1:])]


def gather_lines(own):
    return [own] + send_lines([own] * (lax.axis_size("y") * lax.axis_size("x") - 1))


def send_c(block):
    return lax.ppermute(block, "c", flips(2)[1])


def gather_group(own):
    lists = [own] + [list(t) for t in zip(*[send_z([o] * (lax.axis_size("z") - 1)) for o in own])]
    blocks = [b for one in lists for b in one]
    return blocks + [send_c(b) for b in blocks]


def half_sum_kernel(near, far, mine, *low):
    for k in range(near.shape[0]):
        total = near[k].astype(F32) + far[k].astype(F32)
        if k == 0:
            mine[...] = total
        else:
            low[k - 1][...] = total.astype(BF16)


def scatter_group(near, far, after=()):
    depth, rows, lanes = near.shape
    outs = [((rows, lanes), F32)] + [((rows, lanes), BF16)] * (depth - 1)
    mine, *low = local_call(half_sum_kernel, outs, (near, send_c(far)), after=after)
    return [mine] + send_z(low)


def add_up(refs):
    total = refs[0][...]
    for ref in refs[1:]:
        total = total + ref[...].astype(F32)
    return total


def xor_order(blocks, index):
    step = 1
    while step < len(blocks):
        swap = (index & step) != 0
        blocks = [jnp.where(swap, blocks[b ^ step], blocks[b]) for b in range(len(blocks))]
        step *= 2
    return blocks


def columns_kernel(dims, w_qkv, w_up, gain_attn, gain_mlp, router, out, vec_s):
    ny, members, nx, ff_rows = dims
    cols = 3 * ny * HDIM
    vec_s[...] = jnp.zeros_like(vec_s)
    for k, vec in enumerate((gain_attn, gain_mlp, router)):
        vec_s[k : k + 1] = vec[...].astype(F32)
    vecs = mm(vec_s[...].astype(BF16), eye_rows(), TN).astype(BF16)
    for g in range(members):
        parts = []
        for t in range(3):
            for y in range(ny):
                at = (t * HEADS + y * members + g) * HDIM
                parts.append(w_qkv[:, at : at + HDIM])
        out[g, :, :cols] = jnp.concatenate(parts, 1)
        out[g, :, cols : cols + 128] = vecs
        for y in range(ny):
            for x in range(nx):
                at = ((y * members + g) * nx + x) * ff_rows
                to = cols + 128 + (y * nx + x) * ff_rows
                out[g, :, to : to + ff_rows] = w_up[:, at : at + ff_rows]


def eye_rows():
    down = lax.broadcasted_iota(jnp.int32, (8, 128), 0)
    return (down == lax.broadcasted_iota(jnp.int32, (8, 128), 1)).astype(F32).astype(BF16)


def pick_kernel(cap, where, chosen_t, tokens, cot, pick, *refs):
    *outs, rows = refs
    seq_count, seg_len = tokens.shape[:2]
    base = where[4] * seg_len
    places = base + lax.broadcasted_iota(jnp.int32, (chosen_t.shape[0], seg_len), 1)
    slots = lax.broadcasted_iota(jnp.int32, (cap, seg_len), 0)
    for s in range(seq_count):
        at = chosen_t[:, s : s + 1]
        present = jnp.sum((at == places).astype(F32), 0, keepdims=True)
        rank = jnp.sum(((at >= base) & (at < places)).astype(F32), 0, keepdims=True)
        hot = jnp.where(rank.astype(jnp.int32) == slots, present, 0.0).astype(BF16)
        pick[s] = hot
        rows[s, :cap] = mm(hot, tokens[s]).astype(BF16)
        rows[s, cap:] = mm(hot, cot[s]).astype(BF16)
    for k, out in enumerate(outs):
        out[...] = rows[where[2] ^ k]


def stack_kernel(cap, *refs):
    *blocks, out = refs
    for k, block in enumerate(blocks):
        for j in range(2):
            to = (j * len(blocks) + k) * cap
            out[to : to + cap] = block[j * cap : (j + 1) * cap]


def relay_kernel(got, w_out, w_down, first, second):
    members, rows, lanes = got.shape
    half, width = lanes // 2, w_down.shape[1]
    for g in range(members):
        first[g * rows : (g + 1) * rows] = got[g, :, :half]
        second[g * rows : (g + 1) * rows] = got[g, :, half:]
    for out, block in ((first, w_out), (second, w_down)):
        size = block.shape[0]
        for j in range(2):
            to = members * rows + j * size
            out[to : to + size] = block[:, j * (width // 2) : (j + 1) * (width // 2)]


def spread_kernel(dims, where, chosen, chosen_t, spread):
    ny, nc, nz, nx, seg_len, cap = dims
    c, z, line = where[0], where[1], where[2]
    routed = chosen_t.shape[0]
    members = nc * nz

    def owner_of(mine):
        return lax.div(mine, jnp.int32(seg_len))

    mine_col = chosen_t[:, 0:1]
    mine_row = chosen[0:1, :]
    for s in range(1, chosen.shape[0]):
        mine_col = jnp.where(line == s, chosen_t[:, s : s + 1], mine_col)
        mine_row = jnp.where(line == s, chosen[s : s + 1, :], mine_row)
    owner, owner_row = owner_of(mine_col), owner_of(mine_row)
    order = lax.broadcasted_iota(jnp.int32, (routed, routed), 0)
    other = lax.broadcasted_iota(jnp.int32, (routed, routed), 1)
    same = (owner == owner_row) & (other < order)
    slot = jnp.sum(same.astype(F32), 1, keepdims=True).astype(jnp.int32)
    ox, rest = lax.rem(owner, jnp.int32(nx)), lax.div(owner, jnp.int32(nx))
    oz, rest = lax.rem(rest, jnp.int32(nz)), lax.div(rest, jnp.int32(nz))
    oc, oy = lax.rem(rest, jnp.int32(nc)), lax.div(rest, jnp.int32(nc))
    cell = (((oc ^ c) * nz + (oz ^ z)) * (ny * nx) + ((oy * nx + ox) ^ line)) * cap + slot
    own = routed // members
    cells = [cell[b * own : (b + 1) * own] for b in range(members)]
    for b, block in enumerate(xor_order(cells, where[3])):
        lanes = lax.broadcasted_iota(jnp.int32, (own, spread.shape[1]), 1)
        spread[b * own : (b + 1) * own] = (block == lanes).astype(F32).astype(BF16)


def kept_pairs(member, routed, own):
    down = lax.broadcasted_iota(jnp.int32, (routed, routed), 0)
    across = lax.broadcasted_iota(jnp.int32, (routed, routed), 1)
    shift = own.bit_length() - 1
    first = ((down >> shift) ^ member) * own + (down & (own - 1))
    second = ((across >> shift) ^ member) * own + (across & (own - 1))
    return second <= first


def probabilities(queries, keys, kept):
    scores = jnp.where(kept, mm(queries, keys, NT) * HDIM ** (-0.5), neg_large)
    top = jnp.max(scores, 1, keepdims=True)
    probs = jnp.where(kept, jnp.exp(scores - top), 0.0)
    return probs, jnp.sum(probs, 1, keepdims=True)


def inverse_rms(values):
    return lax.rsqrt(jnp.mean(values * values, 1, keepdims=True) + epsilon)


def line_rows(where, blocks, start, out):
    lines, half = len(blocks), out.shape[1] // 2
    size = out.shape[0] // lines
    for k, block in enumerate(blocks):
        to = pl.ds(pl.multiple_of((where[2] ^ k) * size, size), size)
        for j in range(2):
            piece = block[start + j * size : start + (j + 1) * size]
            out[to, j * half : (j + 1) * half] = piece


def natural_rows(where, blocks, dims, first, count, out):
    ny, members, nx, rows = dims
    for k, block in enumerate(blocks):
        line = where[2] ^ k
        y, x = lax.div(line, jnp.int32(nx)), lax.rem(line, jnp.int32(nx))
        for g in range(members):
            to = pl.multiple_of(((y * members + g) * nx + x) * rows, rows)
            out[pl.ds(to, rows)] = block[g * rows : (g + 1) * rows, first : first + count]


def slot_rows(blocks, first, count):
    return jnp.concatenate([b[first : first + count] for b in blocks], 0)


def attention_kernel(dims, members, where, spread, *refs):
    ny, nx, rows, cap = dims
    lines = ny * nx
    qkv_blocks, refs = refs[:lines], refs[lines:]
    blocks, outs = refs[:members], refs[members:]
    picked_o, normed_o, w_o, wo_o, vecs_o, joined_o, att_o, exact_o, near_o, far_o, vec_s = outs
    heads = ny
    cols = 3 * heads * HDIM
    routed, width = picked_o.shape
    own = routed // members
    spots = slot_rows(blocks, 0, lines * cap)
    picked_low = mm(spread[...], spots).astype(BF16)
    picked_o[...] = picked_low
    picked = picked_low.astype(F32)
    natural_rows(where, qkv_blocks, (ny, members, nx, rows), 0, cols, w_o)
    natural_rows(where, qkv_blocks, (ny, members, nx, rows), cols, 128, vec_s)
    line_rows(where, qkv_blocks, members * rows, wo_o)
    vecs = mm(eye_rows(), vec_s[...], NT)
    vecs_o[...] = vecs
    normed = (picked * inverse_rms(picked) * vecs[0:1]).astype(BF16)
    normed_o[...] = normed
    joined = mm(normed, w_o[...]).astype(BF16)
    joined_o[...] = joined
    kept = kept_pairs(where[3], routed, own)
    parts = []
    for h in range(heads):
        queries, keys, values = (
            joined[:, (t * heads + h) * HDIM : (t * heads + h + 1) * HDIM] for t in range(3)
        )
        probs, total = probabilities(queries, keys, kept)
        parts.append(mm(probs.astype(BF16), values) / total)
    exact = jnp.concatenate(parts, 1)
    exact_o[...] = exact
    attended = exact.astype(BF16)
    att_o[...] = attended
    branch = mm(attended, wo_o[...]).astype(BF16)
    put_halves(branch, near_o, far_o)


def put_halves(values, near, far):
    depth, own = near.shape[:2]
    for k in range(depth):
        near[k] = values[k * own : (k + 1) * own]
        far[k] = values[(depth + k) * own : (depth + k + 1) * own]


def update_kernel(dims, members, where, spread, picked, vecs, *refs):
    lines, cap, start = dims
    downs, refs = refs[:lines], refs[lines:]
    blocks, (cot_o, gate_o, d_result_o, d_active_o, w_o) = refs[:members], refs[members:]
    spots = slot_rows(blocks, lines * cap, lines * cap)
    cot_low = mm(spread[...], spots).astype(BF16)
    cot_o[...] = cot_low
    logit = jnp.sum(picked[...].astype(F32) * vecs[2:3, :], 1, keepdims=True)
    gate = 1.0 / (1.0 + jnp.exp(-logit))
    gate_o[...] = gate
    d_result = (gate * cot_low.astype(F32)).astype(BF16)
    d_result_o[...] = d_result
    line_rows(where, downs, start, w_o)
    d_active_o[...] = mm(d_result, w_o[...], NT)


def hidden_kernel(own, picked, vecs, *refs):
    *terms, hidden_o, normed_o = refs
    hidden = picked[:own, :].astype(F32) + add_up(terms)
    hidden_o[...] = hidden
    normed_o[...] = (hidden * inverse_rms(hidden) * vecs[1:2, :]).astype(BF16)


def forward_kernel(dims, members, where, d_active, *refs):
    lines = dims[0] * dims[2]
    ups, refs = refs[:lines], refs[lines:]
    blocks, (active_o, d_upper_o, near_o, far_o, w_s) = refs[:members], refs[members:]
    natural_rows(where, ups, dims, 0, ups[0].shape[1], w_s)
    normed = jnp.concatenate([b[...] for b in blocks], 0)
    upper = mm(normed, w_s[...])
    below = 0.5 * (1.0 + lax.erf(upper * (0.5**0.5)))
    active_o[...] = (upper * below).astype(BF16)
    slope = below + upper * jnp.exp(-0.5 * upper * upper) * ((2.0 * math.pi) ** -0.5)
    d_upper = (d_active[...] * slope).astype(BF16)
    d_upper_o[...] = d_upper
    put_halves(mm(d_upper, w_s[...], NT).astype(BF16), near_o, far_o)


def ff_grads_kernel(dims, members, where, active, d_upper, d_result, *refs):
    ny, nx, rows, ff_rows = dims
    lines = ny * nx
    blocks, sums, (down, up) = refs[:members], refs[members : members + lines], refs[-2:]
    normed = jnp.concatenate([b[...] for b in blocks], 0)
    down[...] = mm(active[...], d_result[...], TN).astype(BF16)
    up[...] = mm(normed, d_upper[...], TN).astype(BF16)
    wide = up.shape[1]
    for k in range(lines):
        line = where[2] ^ k
        y, x = lax.div(line, jnp.int32(nx)), lax.rem(line, jnp.int32(nx))
        sums[k][:ff_rows] = down[pl.ds(pl.multiple_of(line * ff_rows, ff_rows), ff_rows)]
        for g in range(members):
            at = pl.multiple_of(((y * members + g) * nx + x) * rows, rows)
            half, row = divmod(g * rows, members * rows // 2)
            to = ff_rows + row
            sums[k][to : to + rows, half * wide : (half + 1) * wide] = up[pl.ds(at, rows)]


def result_kernel(active, attended, w_down, w_out, cot, gate, spread, logit_o, near_o, far_o):
    combined = mm(active[...], w_down[...]) + mm(attended[...], w_out[...])
    logit = jnp.sum(cot[...].astype(F32) * combined, 1, keepdims=True)
    logit_o[...] = logit * gate[...] * (1.0 - gate[...])
    update = (gate[...] * combined).astype(BF16)
    put_halves(mm(spread[...], update, TN).astype(BF16), near_o, far_o)


def hidden_back_kernel(own, hidden_r, vecs, gate, cot, *refs):
    *terms, d_branch_o, d_hidden_o, gain_o = refs
    d_normed = add_up(terms)
    hidden = hidden_r[...]
    inv = inverse_rms(hidden)
    u = d_normed * vecs[1:2, :]
    d_hidden = inv * u - hidden * (inv * inv * inv * jnp.mean(u * hidden, 1, keepdims=True))
    d_hidden_o[...] = d_hidden
    gain_o[...] = (d_normed * hidden * inv).astype(BF16)
    d_update = gate[:own, :] * cot[:own, :].astype(F32)
    d_branch_o[...] = (d_update + d_hidden).astype(BF16)


def attention_back_kernel(members, where, *refs):
    w_out, joined_r, exact_r, w, vecs, picked_r, logit, d_hidden, spread = refs[:9]
    blocks = refs[9 : 9 + members]
    near_o, far_o, d_joined_o, gain_o = refs[9 + members :]
    routed, width = picked_r.shape
    own = routed // members
    heads = joined_r.shape[1] // (3 * HDIM)
    d_branch = jnp.concatenate([b[...] for b in blocks], 0)
    d_attended = mm(d_branch, w_out[...], NT).astype(BF16)
    joined = joined_r[...]
    exact = exact_r[...]
    kept = kept_pairs(where[3], routed, own)
    grads = [[], [], []]
    for h in range(heads):
        queries, keys, values = (
            joined[:, (t * heads + h) * HDIM : (t * heads + h + 1) * HDIM] for t in range(3)
        )
        probs, total = probabilities(queries, keys, kept)
        d_att = d_attended[:, h * HDIM : (h + 1) * HDIM]
        d_wide = d_att.astype(F32)
        delta = jnp.sum(d_wide * exact[:, h * HDIM : (h + 1) * HDIM], 1, keepdims=True)
        d_scores = (probs / total * (mm(d_att, values, NT) - delta)).astype(BF16)
        grads[0].append(mm(d_scores, keys) * HDIM ** (-0.5))
        grads[1].append(mm(d_scores, queries, TN) * HDIM ** (-0.5))
        grads[2].append(mm(probs.astype(BF16), (d_wide / total).astype(BF16), TN))
    d_joined = jnp.concatenate(grads[0] + grads[1] + grads[2], 1).astype(BF16)
    d_joined_o[...] = d_joined
    d_normed = mm(d_joined, w[...], NT)
    picked = picked_r[...].astype(F32)
    inv = inverse_rms(picked)
    gain_o[...] = (d_normed * picked * inv).astype(BF16)
    v = d_normed * vecs[0:1, :]
    d_picked = inv * v - picked * (inv * inv * inv * jnp.mean(v * picked, 1, keepdims=True))
    d_picked = d_picked + logit[...] * vecs[2:3, :]
    first = d_picked[:own] + d_hidden[...]
    d_picked = jnp.concatenate([first, d_picked[own:]], 0).astype(BF16)
    put_halves(mm(spread[...], d_picked, TN).astype(BF16), near_o, far_o)


def grads_kernel(dims, members, where, normed, d_joined, attended, gain_a, gain_m, *refs):
    ny, nx, rows = dims
    lines = ny * nx
    picked, logit, refs = refs[0], refs[1], refs[2:]
    blocks, sums, (main, vec_s, out) = refs[:members], refs[members : members + lines], refs[-3:]
    cols = d_joined.shape[1]
    routed, width = normed.shape
    own = gain_m.shape[0]
    main[...] = mm(normed[...], d_joined[...], TN).astype(BF16)
    lanes = lax.broadcasted_iota(jnp.int32, (routed, 128), 1)

    def lane(k, count):
        return (lanes[:count] == k).astype(F32)

    vec = mm(gain_a[...], lane(0, routed).astype(BF16), TN)
    vec = vec + mm(gain_m[...], lane(1, own).astype(BF16), TN)
    high = logit[...].astype(BF16)
    low = (logit[...] - high.astype(F32)).astype(BF16)
    vec = vec + mm(picked[...], (lane(2, routed) * high.astype(F32)).astype(BF16), TN)
    vec = vec + mm(picked[...], (lane(2, routed) * low.astype(F32)).astype(BF16), TN)
    vec_s[...] = vec.astype(BF16)
    out[...] = mm(attended[...], jnp.concatenate([b[...] for b in blocks], 0), TN).astype(BF16)
    for k in range(lines):
        line = where[2] ^ k
        y, x = lax.div(line, jnp.int32(nx)), lax.rem(line, jnp.int32(nx))
        for g in range(members):
            at = pl.multiple_of(((y * members + g) * nx + x) * rows, rows)
            sums[k][g * rows : (g + 1) * rows, :cols] = main[pl.ds(at, rows)]
            sums[k][g * rows : (g + 1) * rows, cols:] = vec_s[pl.ds(at, rows)]
        half, end = width // 2, members * rows
        at = pl.multiple_of(line * rows, rows)
        for j in range(2):
            piece = out[pl.ds(at, rows), j * half : (j + 1) * half]
            sums[k][end + j * rows : end + (j + 1) * rows, :] = piece


def join_slots_kernel(cap, lines, *refs):
    terms, outs = refs[:-lines], refs[-lines:]
    half = len(terms) // 2
    for j in range(2):
        total = add_up(terms[j * half : (j + 1) * half]).astype(BF16)
        for k in range(lines):
            outs[k][j * cap : (j + 1) * cap] = total[k * cap : (k + 1) * cap]


def place_kernel(cap, lines, where, pick, tokens, cot, *refs):
    blocks, (out_o, grad_o, got) = refs[:lines], refs[lines:]
    for k, block in enumerate(blocks):
        got[where[2] ^ k] = block[...]
    for s in range(tokens.shape[0]):
        hot = pick[s]
        out_o[s] = (tokens[s].astype(F32) + mm(hot, got[s, :cap], TN)).astype(BF16)
        grad_o[s] = (cot[s].astype(F32) + mm(hot, got[s, cap:], TN)).astype(BF16)


def line_sums_kernel(dims, lines, *refs):
    members, rows, ff_rows = dims
    parts, ffs, (send_o, out_o, down_o) = refs[:lines], refs[lines : 2 * lines], refs[2 * lines :]
    cols = parts[0].shape[1]
    wide = ffs[0].shape[1] // 2

    def total(blocks):
        sums = blocks[0][...].astype(F32)
        for block in blocks[1:]:
            sums = sums + block[...].astype(F32)
        return sums

    main, ff = total(parts), total(ffs)
    for g in range(members):
        send_o[g, :, :cols] = main[g * rows : (g + 1) * rows].astype(BF16)
        half, row = divmod(g * rows, members * rows // 2)
        at = ff_rows + row
        piece = ff[at : at + rows, half * wide : (half + 1) * wide]
        send_o[g, :, cols:] = piece.astype(BF16)
    end = members * rows
    out_o[...] = jnp.concatenate([main[end : end + rows], main[end + rows :]], 1)
    down_o[...] = ff[:ff_rows]


def unpack_kernel(dims, got, qkv_o, up_o, *vec_o):
    ny, members, nx, ff_rows = dims
    cols = 3 * ny * HDIM
    for t in range(3):
        for y in range(ny):
            from_ = (t * ny + y) * HDIM
            row = [got[g, :, from_ : from_ + HDIM] for g in range(members)]
            at = (t * HEADS + y * members) * HDIM
            qkv_o[:, at : at + members * HDIM] = jnp.concatenate(row, 1).astype(F32)
    for y in range(ny):
        for g in range(members):
            for x in range(nx):
                at = ((y * members + g) * nx + x) * ff_rows
                from_ = cols + 128 + (y * nx + x) * ff_rows
                up_o[:, at : at + ff_rows] = got[g, :, from_ : from_ + ff_rows].astype(F32)
    vec = got[0, :, cols : cols + 128].astype(F32)
    for g in range(1, members):
        vec = vec + got[g, :, cols : cols + 128].astype(F32)
    high = vec.astype(BF16)
    low = (vec - high.astype(F32)).astype(BF16)
    vec = mm(eye_rows(), high, NT) + mm(eye_rows(), low, NT)
    for k, out in enumerate(vec_o):
        out[...] = vec[k : k + 1]


def grouped(
    tokens, chosen, w_qkv, w_out, w_up, w_down, gain_attn, gain_mlp, router, cotangent
):
    ny, nc, nz, nx = (lax.axis_size(a) for a in ("y", "c", "z", "x"))
    y, c, z, x = (lax.axis_index(a) for a in ("y", "c", "z", "x"))
    seq_count, seg_len, width = tokens.shape
    cap = seg_len // 4
    routed = chosen.shape[1]
    members, lines = nc * nz, ny * nx
    member, line = c * nz + z, y * nx + x
    shard = ((y * nc + c) * nz + z) * nx + x
    rows, ff_rows = w_qkv.shape[0], w_down.shape[0]
    heads = HEADS // members
    own = routed // members
    cols, wide = 3 * heads * HDIM, lines * ff_rows
    where = jnp.stack([c, z, line, member, shard]).astype(jnp.int32)
    chosen_t = chosen.T
    block = (own, width)
    slot_block = (2 * cap, width)
    halves = [((nz, own, width), BF16)] * 2
    slot_halves = [((nz, lines * cap, width), BF16)] * 2

    pick, *picked_rows = local_call(
        partial(pick_kernel, cap),
        [((seq_count, cap, seg_len), BF16)] + [(slot_block, BF16)] * lines,
        (where, chosen_t, tokens, cotangent),
        scratch=[pltpu.VMEM((seq_count, 2 * cap, width), BF16)],
        scalars=1,
    )
    line_slots = picked_rows[:1] + send_lines(picked_rows[1:])
    (spread,) = local_call(
        partial(spread_kernel, (ny, nc, nz, nx, seg_len, cap)),
        [((routed, members * lines * cap), BF16)],
        (where, chosen, chosen_t),
        scalars=1,
    )
    (line_slots,) = local_call(
        partial(stack_kernel, cap), [((lines * 2 * cap, width), BF16)], line_slots
    )
    slots = gather_group([line_slots])

    (columns,) = local_call(
        partial(columns_kernel, (ny, members, nx, ff_rows)),
        [((members, rows, cols + 128 + wide), BF16)],
        (w_qkv, w_up) + tuple(v.reshape(1, rows) for v in (gain_attn, gain_mlp, router)),
        scratch=[pltpu.VMEM((8, rows), F32)],
    )
    got_cols = lax.all_to_all(columns, ("c", "z"), 0, 0, tiled=True)
    first, second = local_call(
        relay_kernel,
        [
            ((members * rows + 2 * rows, width // 2), BF16),
            ((members * rows + 2 * ff_rows, width // 2), BF16),
        ],
        (got_cols, w_out, w_down),
    )
    first, second = gather_lines(first), gather_lines(second)

    picked, normed, full_qkv, full_out, full_vecs, joined, attended, exact, near, far = local_call(
        partial(attention_kernel, (ny, nx, rows, cap), members),
        [
            ((routed, width), BF16),
            ((routed, width), BF16),
            ((width, cols), BF16),
            ((heads * HDIM, width), BF16),
            ((8, width), F32),
            ((routed, cols), BF16),
            ((routed, heads * HDIM), BF16),
            ((routed, heads * HDIM), F32),
        ]
        + halves,
        (where, spread, *first, *slots),
        flops=1.2e9,
        scratch=[pltpu.VMEM((width, 128), BF16)],
        scalars=1,
    )
    terms = scatter_group(near, far)
    cot, gate, d_result, d_active, full_down = local_call(
        partial(update_kernel, (lines, cap, members * rows), members),
        [
            ((routed, width), BF16),
            ((routed, 1), F32),
            ((routed, width), BF16),
            ((routed, wide), F32),
            ((wide, width), BF16),
        ],
        (where, spread, picked, full_vecs, *second, *slots),
        flops=8e8,
        scalars=1,
    )
    hidden, normed_own = local_call(
        partial(hidden_kernel, own), [(block, F32), (block, BF16)], (picked, full_vecs, *terms)
    )
    normed_mlp = gather_group([normed_own])

    active, d_upper, near, far = local_call(
        partial(forward_kernel, (ny, members, nx, rows), members),
        [((routed, wide), BF16)] * 2 + halves,
        (where, d_active, *second, *normed_mlp),
        flops=6e8,
        scratch=[pltpu.VMEM((width, wide), BF16)],
        scalars=1,
    )
    terms = scatter_group(near, far)
    ff_parts = local_call(
        partial(ff_grads_kernel, (ny, nx, rows, ff_rows), members),
        [((ff_rows + members * rows // 2, width), BF16)] * lines,
        (where, active, d_upper, d_result, *normed_mlp),
        flops=6e8,
        scratch=[pltpu.VMEM((wide, width), BF16), pltpu.VMEM((width, wide), BF16)],
        scalars=1,
    )
    ff_parts = ff_parts[:1] + send_lines(ff_parts[1:])
    logit, up_near, up_far = local_call(
        result_kernel,
        [((routed, 1), F32)] + slot_halves,
        (active, attended, full_down, full_out, cot, gate, spread),
        flops=8e8,
    )
    d_branch_own, d_hidden, gain_m = local_call(
        partial(hidden_back_kernel, own),
        [(block, BF16), (block, F32), (block, BF16)],
        (hidden, full_vecs, gate, cot, *terms),
    )
    d_branch = gather_group([d_branch_own])
    update_terms = scatter_group(up_near, up_far)

    near, far, d_joined, gain_a = local_call(
        partial(attention_back_kernel, members),
        slot_halves + [((routed, cols), BF16), ((routed, width), BF16)],
        (where, full_out, joined, exact, full_qkv, full_vecs, picked, logit, d_hidden, spread)
        + tuple(d_branch),
        flops=1.2e9,
        scalars=1,
    )
    picked_terms = scatter_group(near, far, after=update_terms[1:])
    parts = local_call(
        partial(grads_kernel, (ny, nx, rows), members),
        [((members * rows + 2 * rows, cols + 128), BF16)] * lines,
        (where, normed, d_joined, attended, gain_a, gain_m, picked, logit, *d_branch),
        flops=5e8,
        scratch=[
            pltpu.VMEM((width, cols), BF16),
            pltpu.VMEM((width, 128), BF16),
            pltpu.VMEM((heads * HDIM, width), BF16),
        ],
        scalars=1,
    )
    parts = parts[:1] + send_lines(parts[1:])
    back_rows = local_call(
        partial(join_slots_kernel, cap, lines),
        [(slot_block, BF16)] * lines,
        (*update_terms, *picked_terms),
    )
    back_rows = back_rows[:1] + send_lines(back_rows[1:])
    send, grad_out, grad_down = local_call(
        partial(line_sums_kernel, (members, rows, ff_rows), lines),
        [
            ((members, rows, cols + 128 + wide), BF16),
            ((rows, width), F32),
            ((ff_rows, width), F32),
        ],
        (*parts, *ff_parts),
        after=back_rows[:1],
    )
    got = lax.all_to_all(send, ("c", "z"), 0, 0, tiled=True)
    output, grad_tokens = local_call(
        partial(place_kernel, cap, lines),
        [(tokens.shape, BF16), (tokens.shape, BF16)],
        (where, pick, tokens, cotangent, *back_rows),
        scratch=[pltpu.VMEM((seq_count, 2 * cap, width), BF16)],
        scalars=1,
    )
    grad_qkv, grad_up, *grad_vecs = local_call(
        partial(unpack_kernel, (ny, members, nx, ff_rows)),
        [(w_qkv.shape, F32), (w_up.shape, F32)] + [((1, rows), F32)] * 3,
        (got,),
    )
    return (
        output,
        grad_tokens,
        grad_qkv,
        grad_out,
        grad_up,
        grad_down,
        *(v.reshape(rows) for v in grad_vecs),
    )


def fits(mesh):
    head_count, block_count = mesh.devices.shape
    members = (head_count // 2) * (block_count // 2)
    power = members & (members - 1) == 0
    return power and head_count == 4 and HEADS == 2 * members


def solution(mesh):
    if fits(mesh):
        head_count, block_count = mesh.devices.shape
        devices = mesh.devices.reshape(2, head_count // 2, block_count // 2, 2)
        mesh = jax.sharding.Mesh(devices, ("y", "c", "z", "x"))
        body, all_axes = grouped, ("y", "c", "z", "x")
    else:
        body, all_axes = shards, ("head", "blk")
    seqs, mats, vecs = P(None, all_axes, None), P(all_axes, None), P(all_axes)
    in_specs = (seqs, P(), mats, mats, mats, mats, vecs, vecs, vecs, seqs)
    out_specs = (seqs, seqs, mats, mats, mats, mats, vecs, vecs, vecs)
    return jax.shard_map(body, mesh=mesh, in_specs=in_specs, out_specs=out_specs, check_vma=False)
```

```python
import math
from functools import partial

import jax
import jax.numpy as jnp
from jax import lax
from jax.experimental import pallas as pl
from jax.experimental.pallas import tpu as pltpu
from jax.sharding import PartitionSpec as P

HEADS = 16
HDIM = 64


epsilon = 1e-06
neg_large = -1e30


def rms_norm(values, gain_vec):
    inverse_rms = lax.rsqrt(jnp.mean(values * values, axis=-1, keepdims=True) + epsilon)
    return values * inverse_rms * gain_vec


def exact_gelu(values):
    return jax.nn.gelu(values, approximate=False)


def take_rows(seq_rows, row_index):
    return seq_rows[row_index]


def add_rows(seq_rows, row_index, additions):
    return seq_rows.at[row_index].add(additions)


def shards(tokens, chosen, w_qkv, w_out, w_up, w_down, gain_attn, gain_mlp, router, cotangent):
    head_count = lax.axis_size("head")
    block_count = lax.axis_size("blk")
    shard_count = head_count * block_count
    seq_count, seg_len, model_width = tokens.shape
    cap_len = seg_len // 4
    routed_count = chosen.shape[1]
    seq_len = seg_len * shard_count
    local_heads = HEADS // head_count
    slot_rows = head_count * cap_len
    scale_factor = HDIM ** (-0.5)
    head_index = lax.axis_index("head")
    block_index = lax.axis_index("blk")
    my_shard = head_index * block_count + block_index
    bounds = jnp.arange(shard_count + 1, dtype=jnp.int32) * seg_len
    before = jax.vmap(lambda chosen_row: jnp.searchsorted(chosen_row, bounds, side="left"))(chosen)
    first_index = before[:, :-1]
    shard_load = before[:, 1:] - first_index
    slot_iota = jnp.arange(cap_len, dtype=jnp.int32)
    live_table = slot_iota[None, None, :] < shard_load[:, :, None]
    lookup = jnp.minimum(first_index[:, :, None] + slot_iota[None, None, :], routed_count - 1)
    place_table = jnp.take_along_axis(
        chosen, lookup.reshape(seq_count, shard_count * cap_len), axis=1
    )
    place_table = jnp.where(
        live_table, place_table.reshape(seq_count, shard_count, cap_len), seq_len
    )
    my_positions = lax.dynamic_index_in_dim(place_table, my_shard, 1, False)
    my_live = lax.dynamic_index_in_dim(live_table, my_shard, 1, False)
    local_rows = jnp.clip(my_positions - my_shard * seg_len, 0, seg_len - 1)
    cycle_positions = place_table.reshape(seq_count, head_count, block_count, cap_len).transpose(
        0, 2, 1, 3
    )
    cycle_positions = cycle_positions.reshape(seq_count, block_count * slot_rows)
    query_positions = lax.dynamic_slice_in_dim(
        cycle_positions, block_index * slot_rows, slot_rows, 1
    )
    live_weight = my_live.astype(jnp.float32)[:, :, None]
    gathered = (
        lax.all_gather(w_qkv, ("head", "blk"), axis=0, tiled=True),
        lax.all_gather(w_out, ("head", "blk"), axis=0, tiled=True),
        lax.all_gather(w_up, ("head", "blk"), axis=0, tiled=True),
        lax.all_gather(w_down, ("head", "blk"), axis=0, tiled=True),
        lax.all_gather(gain_attn, ("head", "blk"), axis=0, tiled=True),
        lax.all_gather(gain_mlp, ("head", "blk"), axis=0, tiled=True),
        lax.all_gather(router, ("head", "blk"), axis=0, tiled=True),
    )
    full_qkv, full_out, full_up, full_down, full_gain_attn, full_gain_mlp, full_router = gathered
    picked = jax.vmap(take_rows)(tokens, local_rows)
    picked = jnp.where(my_live[:, :, None], picked, jnp.zeros_like(picked))
    picked_exact = picked.astype(jnp.float32)
    router_gate = jax.nn.sigmoid(
        jnp.einsum("scd,d->sc", picked, full_router, preferred_element_type=jnp.float32)
    )
    normed_exact, norm_attn_back = jax.vjp(
        rms_norm, picked_exact, full_gain_attn.astype(jnp.float32)
    )
    normed = normed_exact.astype(jnp.bfloat16)
    joined = jnp.einsum("scd,de->sce", normed, full_qkv, preferred_element_type=jnp.float32).astype(
        jnp.bfloat16
    )
    to_heads = lax.all_to_all(
        joined.reshape(seq_count, cap_len, 3, model_width),
        "head",
        split_axis=3,
        concat_axis=1,
        tiled=True,
    )
    queries_tok = to_heads[:, :, 0]
    queries_heads = queries_tok.reshape(seq_count, slot_rows, local_heads, HDIM)
    key_values = to_heads[:, :, 1:3]
    my_keys = key_values[:, :, 0].reshape(seq_count, slot_rows, local_heads, HDIM)
    my_values = key_values[:, :, 1].reshape(seq_count, slot_rows, local_heads, HDIM)
    stat_shape = (seq_count, local_heads, slot_rows)
    piece = lax.all_gather(key_values, "blk", axis=1, tiled=True)
    run_max = jnp.full(stat_shape, neg_large, jnp.float32)
    piece_rows = piece.shape[1]
    key_pos = cycle_positions
    keys_piece = piece[:, :, 0].reshape(seq_count, piece_rows, local_heads, HDIM)
    values_piece = piece[:, :, 1].reshape(seq_count, piece_rows, local_heads, HDIM)
    scores = (
        jnp.einsum("sqhd,skhd->shqk", queries_heads, keys_piece, preferred_element_type=jnp.float32)
        * scale_factor
    )
    allowed = key_pos[:, None, None, :] <= query_positions[:, None, :, None]
    scores = jnp.where(allowed, scores, neg_large)
    new_max = jnp.maximum(run_max, jnp.max(scores, axis=3))
    prob_block = jnp.where(allowed, jnp.exp(scores - new_max[..., None]), 0.0)
    new_total = jnp.sum(prob_block, axis=3)
    added = jnp.einsum(
        "shqk,skhd->sqhd",
        prob_block.astype(jnp.bfloat16),
        values_piece,
        preferred_element_type=jnp.float32,
    )
    attended_exact = added / new_total.transpose(0, 2, 1)[..., None]
    log_sum = new_max + jnp.log(new_total)
    attended_tok = attended_exact.astype(jnp.bfloat16).reshape(
        seq_count, slot_rows, local_heads * HDIM
    )
    attended = lax.all_to_all(attended_tok, "head", split_axis=1, concat_axis=2, tiled=True)
    branch = jnp.einsum("sce,ed->scd", attended, full_out, preferred_element_type=jnp.float32)
    hidden_state = picked_exact + branch
    normed_mlp_exact, norm_mlp_back = jax.vjp(
        rms_norm, hidden_state, full_gain_mlp.astype(jnp.float32)
    )
    normed_mlp = normed_mlp_exact.astype(jnp.bfloat16)
    upper = jnp.einsum("scd,di->sci", normed_mlp, full_up, preferred_element_type=jnp.float32)
    active_exact, gelu_back = jax.vjp(exact_gelu, upper)
    active = active_exact.astype(jnp.bfloat16)
    result = jnp.einsum("sci,id->scd", active, full_down, preferred_element_type=jnp.float32)
    combined = branch + result
    update = router_gate[:, :, None] * combined * live_weight
    output = jax.vmap(add_rows)(tokens.astype(jnp.float32), local_rows, update).astype(jnp.bfloat16)
    regathered = (
        lax.all_gather(w_qkv, ("head", "blk"), axis=0, tiled=True),
        lax.all_gather(w_out, ("head", "blk"), axis=0, tiled=True),
        lax.all_gather(w_up, ("head", "blk"), axis=0, tiled=True),
        lax.all_gather(w_down, ("head", "blk"), axis=0, tiled=True),
        lax.all_gather(gain_attn, ("head", "blk"), axis=0, tiled=True),
        lax.all_gather(gain_mlp, ("head", "blk"), axis=0, tiled=True),
        lax.all_gather(router, ("head", "blk"), axis=0, tiled=True),
    )
    back_qkv, back_out, back_up, back_down, back_gain_attn, back_gain_mlp, back_router = regathered
    picked_cot = jax.vmap(take_rows)(cotangent, local_rows).astype(jnp.float32) * live_weight
    d_update = router_gate[:, :, None] * picked_cot
    d_logit = jnp.sum(picked_cot * combined, axis=2) * router_gate * (1.0 - router_gate)
    grad_router = jnp.einsum("sc,scd->d", d_logit, picked_exact, precision=lax.Precision.HIGHEST)
    d_result = d_update.astype(jnp.bfloat16)
    d_active = jnp.einsum("scd,id->sci", d_result, back_down, preferred_element_type=jnp.float32)
    d_upper = gelu_back(d_active)[0].astype(jnp.bfloat16)
    d_normed_mlp = jnp.einsum("sci,di->scd", d_upper, back_up, preferred_element_type=jnp.float32)
    d_hidden, grad_gain_mlp = norm_mlp_back(d_normed_mlp)
    d_branch = (d_update + d_hidden).astype(jnp.bfloat16)
    d_attended = jnp.einsum(
        "scd,ed->sce", d_branch, back_out, preferred_element_type=jnp.float32
    ).astype(jnp.bfloat16)
    d_att_tok = lax.all_to_all(d_attended, "head", split_axis=2, concat_axis=1, tiled=True)
    d_att_heads = d_att_tok.reshape(seq_count, slot_rows, local_heads, HDIM)
    delta_tok = jnp.sum(d_att_heads.astype(jnp.float32) * attended_exact, axis=3)
    delta_sq = delta_tok.transpose(0, 2, 1)
    piece = lax.all_gather(key_values, "blk", axis=1, tiled=True)
    piece_rows = piece.shape[1]
    key_pos = cycle_positions
    keys_piece = piece[:, :, 0].reshape(seq_count, piece_rows, local_heads, HDIM)
    values_piece = piece[:, :, 1].reshape(seq_count, piece_rows, local_heads, HDIM)
    scores = (
        jnp.einsum("sqhd,skhd->shqk", queries_heads, keys_piece, preferred_element_type=jnp.float32)
        * scale_factor
    )
    allowed = key_pos[:, None, None, :] <= query_positions[:, None, :, None]
    prob_block = jnp.where(allowed, jnp.exp(scores - log_sum[..., None]), 0.0)
    d_prob = jnp.einsum(
        "sqhd,skhd->shqk", d_att_heads, values_piece, preferred_element_type=jnp.float32
    )
    d_scores = (prob_block * (d_prob - delta_sq[..., None])).astype(jnp.bfloat16)
    d_queries = (
        jnp.einsum("shqk,skhd->sqhd", d_scores, keys_piece, preferred_element_type=jnp.float32)
        * scale_factor
    )
    lse_tok = log_sum.transpose(0, 2, 1)
    lse_high = lse_tok.astype(jnp.bfloat16)
    lse_low = (lse_tok - lse_high.astype(jnp.float32)).astype(jnp.bfloat16)
    delta_high = delta_tok.astype(jnp.bfloat16)
    delta_low = (delta_tok - delta_high.astype(jnp.float32)).astype(jnp.bfloat16)
    query_piece = lax.all_gather(queries_tok, "blk", axis=1, tiled=True)
    dout_piece = lax.all_gather(d_att_tok, "blk", axis=1, tiled=True)
    piece_lse_high = lax.all_gather(lse_high, "blk", axis=1, tiled=True)
    piece_lse_low = lax.all_gather(lse_low, "blk", axis=1, tiled=True)
    piece_delta_high = lax.all_gather(delta_high, "blk", axis=1, tiled=True)
    piece_delta_low = lax.all_gather(delta_low, "blk", axis=1, tiled=True)
    piece_rows = query_piece.shape[1]
    query_heads = query_piece.reshape(seq_count, piece_rows, local_heads, HDIM)
    dout_heads = dout_piece.reshape(seq_count, piece_rows, local_heads, HDIM)
    piece_lse = (piece_lse_high.astype(jnp.float32) + piece_lse_low.astype(jnp.float32)).transpose(
        0, 2, 1
    )
    piece_delta = (
        piece_delta_high.astype(jnp.float32) + piece_delta_low.astype(jnp.float32)
    ).transpose(0, 2, 1)
    scores = (
        jnp.einsum("sqhd,skhd->shqk", query_heads, my_keys, preferred_element_type=jnp.float32)
        * scale_factor
    )
    allowed = query_positions[:, None, None, :] <= cycle_positions[:, None, :, None]
    prob_block = jnp.where(allowed, jnp.exp(scores - piece_lse[..., None]), 0.0)
    grad_values = jnp.einsum(
        "shqk,sqhd->skhd",
        prob_block.astype(jnp.bfloat16),
        dout_heads,
        preferred_element_type=jnp.float32,
    )
    d_prob = jnp.einsum(
        "sqhd,skhd->shqk", dout_heads, my_values, preferred_element_type=jnp.float32
    )
    d_scores = (prob_block * (d_prob - piece_delta[..., None])).astype(jnp.bfloat16)
    grad_keys = (
        jnp.einsum("shqk,sqhd->skhd", d_scores, query_heads, preferred_element_type=jnp.float32)
        * scale_factor
    )
    d_heads = jnp.stack(
        [
            d_queries.astype(jnp.bfloat16),
            grad_keys.astype(jnp.bfloat16),
            grad_values.astype(jnp.bfloat16),
        ],
        axis=2,
    )
    d_heads = d_heads.reshape(seq_count, slot_rows, 3, local_heads * HDIM)
    d_joined = lax.all_to_all(d_heads, "head", split_axis=1, concat_axis=3, tiled=True).reshape(
        seq_count, cap_len, 3 * model_width
    )
    d_normed = jnp.einsum("sce,de->scd", d_joined, back_qkv, preferred_element_type=jnp.float32)
    d_picked_norm, grad_gain_attn = norm_attn_back(d_normed)
    d_picked = (
        d_hidden
        + d_picked_norm
        + d_logit[:, :, None] * back_router.astype(jnp.float32)[None, None, :]
    )
    grad_tokens = jax.vmap(add_rows)(
        cotangent.astype(jnp.float32), local_rows, d_picked * live_weight
    ).astype(jnp.bfloat16)
    grad_qkv = jnp.einsum("scd,sce->de", normed, d_joined, preferred_element_type=jnp.float32)
    grad_out = jnp.einsum("sce,scd->ed", attended, d_branch, preferred_element_type=jnp.float32)
    grad_up = jnp.einsum("scd,sci->di", normed_mlp, d_upper, preferred_element_type=jnp.float32)
    grad_down = jnp.einsum("sci,scd->id", active, d_result, preferred_element_type=jnp.float32)
    owned = (
        lax.psum_scatter(grad_qkv, ("head", "blk"), scatter_dimension=0, tiled=True),
        lax.psum_scatter(grad_out, ("head", "blk"), scatter_dimension=0, tiled=True),
        lax.psum_scatter(grad_up, ("head", "blk"), scatter_dimension=0, tiled=True),
        lax.psum_scatter(grad_down, ("head", "blk"), scatter_dimension=0, tiled=True),
        lax.psum_scatter(grad_gain_attn, ("head", "blk"), scatter_dimension=0, tiled=True),
        lax.psum_scatter(grad_gain_mlp, ("head", "blk"), scatter_dimension=0, tiled=True),
        lax.psum_scatter(grad_router, ("head", "blk"), scatter_dimension=0, tiled=True),
    )
    return (
        output,
        grad_tokens,
        owned[0],
        owned[1],
        owned[2],
        owned[3],
        owned[4],
        owned[5],
        owned[6],
    )


F32, BF16 = jnp.float32, jnp.bfloat16
NN = (((1,), (0,)), ((), ()))
NT = (((1,), (1,)), ((), ()))
TN = (((0,), (0,)), ((), ()))


def mm(left, right, dims=NN):
    return lax.dot_general(left, right, dims, preferred_element_type=F32)


class Far:
    def __init__(self, item, rows=None, start=0):
        self.item, self.rows, self.start = item, rows, start


class Loaded:
    def __init__(self, copy, ref):
        self.copy, self.ref, self.shape, self.waited = copy, ref, ref.shape, False

    def __getitem__(self, index):
        self.wait()
        return self.ref[index]

    def wait(self):
        if not self.waited:
            self.copy.wait()
        self.waited = True


class Stored:
    def __init__(self, copy, ref):
        self.copy, self.ref, self.shape, self.started = copy, ref, ref.shape, False

    def __getitem__(self, index):
        return self.ref[index]

    def __setitem__(self, index, value):
        self.ref[index] = value
        if index is Ellipsis:
            self.start()

    def start(self):
        if not self.started:
            self.copy.start()
        self.started = True


def local_call(body, outs, args, flops=0, scratch=(), scalars=0, after=()):
    far_in = [a if isinstance(a, Far) else None for a in args]
    far_out = [isinstance(o, Far) for o in outs]
    outs = [o.item if f else o for o, f in zip(outs, far_out)]
    args = [pltpu.with_memory_space_constraint(f.item, pltpu.HBM) if f else a for a, f in zip(args, far_in)]
    shapes = [pltpu.HBM(s, d) if f else jax.ShapeDtypeStruct(s, d) for (s, d), f in zip(outs, far_out)]
    spaces = [pltpu.SMEM] * scalars
    spaces += [pltpu.HBM if f else pltpu.VMEM for f in far_in[scalars:]]
    spaces += [pl.ANY] * len(after)
    stages = []
    for f in far_in:
        if f:
            shape = f.item.shape if f.rows is None else (f.rows,) + f.item.shape[1:]
            stages.append(pltpu.VMEM(shape, f.item.dtype))
    stages += [pltpu.VMEM(s, d) for (s, d), f in zip(outs, far_out) if f]
    n_in, n_out, n_far = len(args), len(outs), len(stages)
    first_out = n_in + len(after)
    if n_far:
        stages.append(pltpu.SemaphoreType.DMA((n_far,)))

    def run(*refs):
        ins, results = list(refs[:n_in]), list(refs[first_out : first_out + n_out])
        rest = refs[first_out + n_out :]
        own, stage = rest[: len(scratch)], rest[len(scratch) :]
        at, loads, stores = 0, [], []
        for i, f in enumerate(far_in):
            if f:
                source = ins[i] if f.rows is None else ins[i].at[pl.ds(f.start, f.rows)]
                copy = pltpu.make_async_copy(source, stage[at], stage[-1].at[at])
                copy.start()
                ins[i] = Loaded(copy, stage[at])
                loads.append(ins[i])
                at += 1
        for i, f in enumerate(far_out):
            if f:
                copy = pltpu.make_async_copy(stage[at], results[i], stage[-1].at[at])
                results[i] = Stored(copy, stage[at])
                stores.append(results[i])
                at += 1
        body(*ins, *results, *own)
        for load in loads:
            load.wait()
        for store in stores:
            store.start()
        for store in stores:
            store.copy.wait()

    return list(
        pl.pallas_call(
            run,
            out_shape=shapes,
            in_specs=[pl.BlockSpec(memory_space=s) for s in spaces],
            out_specs=[
                pl.BlockSpec(memory_space=pltpu.HBM if f else pltpu.VMEM) for f in far_out
            ],
            scratch_shapes=list(scratch) + stages,
            compiler_params=pltpu.CompilerParams(vmem_limit_bytes=32 * 2**20),
            cost_estimate=pl.CostEstimate(flops=int(flops), bytes_accessed=0, transcendentals=0),
        )(*args, *after)
    )


def flips(count):
    return [[(i, i ^ k) for i in range(count)] for k in range(count)]


def send_z(blocks):
    return [lax.ppermute(b, "z", f) for b, f in zip(blocks, flips(lax.axis_size("z"))[1:])]


def send_lines(blocks):
    count = lax.axis_size("y") * lax.axis_size("x")
    return [lax.ppermute(b, ("y", "x"), f) for b, f in zip(blocks, flips(count)[1:])]


def gather_lines(own):
    return [own] + send_lines([own] * (lax.axis_size("y") * lax.axis_size("x") - 1))


def send_c(block):
    return lax.ppermute(block, "c", flips(2)[1])


def gather_group(own):
    lists = [own] + [list(t) for t in zip(*[send_z([o] * (lax.axis_size("z") - 1)) for o in own])]
    blocks = [b for one in lists for b in one]
    return blocks + [send_c(b) for b in blocks]


def half_sum_kernel(near, far, mine, *low):
    for k in range(near.shape[0]):
        total = near[k].astype(F32) + far[k].astype(F32)
        if k == 0:
            mine[...] = total
        else:
            low[k - 1][...] = total.astype(BF16)


def slot_sum_kernel(*refs):
    pairs, (mine, *low) = refs[:4], refs[4:]
    size = pairs[0].shape[1]
    for j in range(2):
        near, far = pairs[2 * j], pairs[2 * j + 1]
        rows = slice(j * size, (j + 1) * size)
        for k in range(near.shape[0]):
            total = near[k].astype(F32) + far[k].astype(F32)
            if k == 0:
                mine[rows] = total
            else:
                low[k - 1][rows] = total.astype(BF16)


def scatter_group(near, far, after=()):
    depth, rows, lanes = near.shape
    outs = [((rows, lanes), F32)] + [((rows, lanes), BF16)] * (depth - 1)
    mine, *low = local_call(half_sum_kernel, outs, (near, send_c(far)), after=after)
    return [mine] + send_z(low)


def add_up(refs):
    total = refs[0][...]
    for ref in refs[1:]:
        total = total + ref[...].astype(F32)
    return total


def xor_order(blocks, index):
    step = 1
    while step < len(blocks):
        swap = (index & step) != 0
        blocks = [jnp.where(swap, blocks[b ^ step], blocks[b]) for b in range(len(blocks))]
        step *= 2
    return blocks


def columns_kernel(dims, w_qkv, w_up, gain_attn, gain_mlp, router, out, vec_s):
    ny, members, nx, ff_rows = dims
    cols = 3 * ny * HDIM
    vec_s[...] = jnp.zeros_like(vec_s)
    for k, vec in enumerate((gain_attn, gain_mlp, router)):
        vec_s[k : k + 1] = vec[...].astype(F32)
    vecs = mm(vec_s[...].astype(BF16), eye_rows(), TN).astype(BF16)
    for g in range(members):
        parts = []
        for t in range(3):
            for y in range(ny):
                at = (t * HEADS + y * members + g) * HDIM
                parts.append(w_qkv[:, at : at + HDIM])
        out[g, :, :cols] = jnp.concatenate(parts, 1)
        out[g, :, cols : cols + 128] = vecs
        for y in range(ny):
            for x in range(nx):
                at = ((y * members + g) * nx + x) * ff_rows
                to = cols + 128 + (y * nx + x) * ff_rows
                out[g, :, to : to + ff_rows] = w_up[:, at : at + ff_rows]


def eye_rows():
    down = lax.broadcasted_iota(jnp.int32, (8, 128), 0)
    return (down == lax.broadcasted_iota(jnp.int32, (8, 128), 1)).astype(F32).astype(BF16)


def pick_kernel(cap, where, chosen_t, tokens, cot, pick, *refs):
    *outs, rows = refs
    seq_count, seg_len = tokens.shape[:2]
    base = where[4] * seg_len
    places = base + lax.broadcasted_iota(jnp.int32, (chosen_t.shape[0], seg_len), 1)
    slots = lax.broadcasted_iota(jnp.int32, (cap, seg_len), 0)
    for s in range(seq_count):
        at = chosen_t[:, s : s + 1]
        present = jnp.sum((at == places).astype(F32), 0, keepdims=True)
        rank = jnp.sum(((at >= base) & (at < places)).astype(F32), 0, keepdims=True)
        hot = jnp.where(rank.astype(jnp.int32) == slots, present, 0.0).astype(BF16)
        pick[s] = hot
        rows[s, :cap] = mm(hot, tokens[s]).astype(BF16)
        rows[s, cap:] = mm(hot, cot[s]).astype(BF16)
    for k, out in enumerate(outs):
        out[...] = rows[where[2] ^ k]


def stack_kernel(cap, *refs):
    *blocks, out = refs
    for k, block in enumerate(blocks):
        for j in range(2):
            to = (j * len(blocks) + k) * cap
            out[to : to + cap] = block[j * cap : (j + 1) * cap]


def relay_kernel(got, w_out, w_down, first, second):
    members, rows, lanes = got.shape
    half = lanes // 2
    for line in range(first.shape[0]):
        for g in range(members):
            first[line, g * rows : (g + 1) * rows] = got[g, :, :half]
        for j in range(2):
            to = (members + j) * rows
            first[line, to : to + rows] = w_out[:, j * half : (j + 1) * half]
    size = w_down.shape[0]
    for g in range(members):
        second[g * rows : (g + 1) * rows] = got[g, :, half:]
    for j in range(2):
        to = members * rows + j * size
        second[to : to + size] = w_down[:, j * half : (j + 1) * half]


def spread_kernel(dims, where, chosen, chosen_t, spread):
    ny, nc, nz, nx, seg_len, cap = dims
    c, z, line = where[0], where[1], where[2]
    routed = chosen_t.shape[0]
    members = nc * nz

    def owner_of(mine):
        return lax.div(mine, jnp.int32(seg_len))

    mine_col = chosen_t[:, 0:1]
    mine_row = chosen[0:1, :]
    for s in range(1, chosen.shape[0]):
        mine_col = jnp.where(line == s, chosen_t[:, s : s + 1], mine_col)
        mine_row = jnp.where(line == s, chosen[s : s + 1, :], mine_row)
    owner, owner_row = owner_of(mine_col), owner_of(mine_row)
    order = lax.broadcasted_iota(jnp.int32, (routed, routed), 0)
    other = lax.broadcasted_iota(jnp.int32, (routed, routed), 1)
    same = (owner == owner_row) & (other < order)
    slot = jnp.sum(same.astype(F32), 1, keepdims=True).astype(jnp.int32)
    ox, rest = lax.rem(owner, jnp.int32(nx)), lax.div(owner, jnp.int32(nx))
    oz, rest = lax.rem(rest, jnp.int32(nz)), lax.div(rest, jnp.int32(nz))
    oc, oy = lax.rem(rest, jnp.int32(nc)), lax.div(rest, jnp.int32(nc))
    cell = (((oc ^ c) * nz + (oz ^ z)) * (ny * nx) + ((oy * nx + ox) ^ line)) * cap + slot
    own = routed // members
    cells = [cell[b * own : (b + 1) * own] for b in range(members)]
    for b, block in enumerate(xor_order(cells, where[3])):
        lanes = lax.broadcasted_iota(jnp.int32, (own, spread.shape[1]), 1)
        spread[b * own : (b + 1) * own] = (block == lanes).astype(F32).astype(BF16)


def kept_pairs(member, routed, own):
    down = lax.broadcasted_iota(jnp.int32, (routed, routed), 0)
    across = lax.broadcasted_iota(jnp.int32, (routed, routed), 1)
    shift = own.bit_length() - 1
    first = ((down >> shift) ^ member) * own + (down & (own - 1))
    second = ((across >> shift) ^ member) * own + (across & (own - 1))
    return second <= first


def probabilities(queries, keys, kept):
    scores = jnp.where(kept, mm(queries, keys, NT) * HDIM ** (-0.5), neg_large)
    top = jnp.max(scores, 1, keepdims=True)
    probs = jnp.where(kept, jnp.exp(scores - top), 0.0)
    return probs, jnp.sum(probs, 1, keepdims=True)


def inverse_rms(values):
    return lax.rsqrt(jnp.mean(values * values, 1, keepdims=True) + epsilon)


def line_rows(blocks, start, out):
    half = out.shape[1] // 2
    size = out.shape[0] // blocks.shape[0]
    for q in range(blocks.shape[0]):
        for j in range(2):
            piece = blocks[q, start + j * size : start + (j + 1) * size]
            out[q * size : (q + 1) * size, j * half : (j + 1) * half] = piece


def own_line_rows(where, blocks, start, out):
    half = out.shape[1] // 2
    size = out.shape[0] // len(blocks)
    for k, block in enumerate(blocks):
        to = pl.ds(pl.multiple_of((where[2] ^ k) * size, size), size)
        for j in range(2):
            piece = block[start + j * size : start + (j + 1) * size]
            out[to, j * half : (j + 1) * half] = piece


def own_order_rows(where, blocks, dims, out):
    ny, members, nx, rows = dims
    for k, block in enumerate(blocks):
        line = where[2] ^ k
        y, x = lax.div(line, jnp.int32(nx)), lax.rem(line, jnp.int32(nx))
        for g in range(members):
            to = pl.multiple_of(((y * members + g) * nx + x) * rows, rows)
            out[pl.ds(to, rows)] = block[g * rows : (g + 1) * rows, :]


def natural_rows(blocks, dims, first, count, out):
    ny, members, nx, rows = dims
    for y in range(ny):
        for g in range(members):
            for x in range(nx):
                to = ((y * members + g) * nx + x) * rows
                piece = blocks[y * nx + x, g * rows : (g + 1) * rows, first : first + count]
                out[to : to + rows] = piece


def attention_kernel(dims, members, where, spread, qkv_blocks, *refs):
    ny, nx, rows, cap = dims
    blocks, outs = refs[:members], refs[members:]
    picked_o, normed_o, w_o, first_o, wo_o, vecs_o = outs[:6]
    joined_o, att_o, exact_o, near_o, far_o, vec_s = outs[6:]
    heads = ny
    cols = 3 * heads * HDIM
    routed, width = picked_o.shape
    own = routed // members
    picked_low = mm(spread[...], jnp.concatenate([b[...] for b in blocks], 0)).astype(BF16)
    picked_o[...] = picked_low
    picked = picked_low.astype(F32)
    first_o[...] = picked_low[:own]
    natural_rows(qkv_blocks, (ny, members, nx, rows), 0, cols, w_o)
    natural_rows(qkv_blocks, (ny, members, nx, rows), cols, 128, vec_s)
    line_rows(qkv_blocks, members * rows, wo_o)
    vecs = mm(eye_rows(), vec_s[...], NT)
    vecs_o[...] = vecs
    normed = (picked * inverse_rms(picked) * vecs[0:1]).astype(BF16)
    normed_o[...] = normed
    joined = mm(normed, w_o[...]).astype(BF16)
    joined_o[...] = joined
    kept = kept_pairs(where[3], routed, own)
    parts = []
    for h in range(heads):
        queries, keys, values = (
            joined[:, (t * heads + h) * HDIM : (t * heads + h + 1) * HDIM] for t in range(3)
        )
        probs, total = probabilities(queries, keys, kept)
        parts.append(mm(probs.astype(BF16), values) / total)
    exact = jnp.concatenate(parts, 1)
    exact_o[...] = exact
    attended = exact.astype(BF16)
    att_o[...] = attended
    branch = mm(attended, wo_o[...]).astype(BF16)
    put_halves(branch, near_o, far_o)


def put_halves(values, near, far):
    depth, own = near.shape[:2]
    for k in range(depth):
        near[k] = values[k * own : (k + 1) * own]
        far[k] = values[(depth + k) * own : (depth + k + 1) * own]


def update_kernel(dims, where, spread, picked, vecs, *refs):
    lines, members, start = dims
    downs, refs = refs[:lines], refs[lines:]
    blocks, outs = refs[:members], refs[members:]
    gate_o, cot_o, first_o, d_result_o, d_active_o, w_o = outs
    logit = jnp.sum(picked[...].astype(F32) * vecs[2:3, :], 1, keepdims=True)
    gate = 1.0 / (1.0 + jnp.exp(-logit))
    gate_o[...] = gate
    cot = mm(spread[...], jnp.concatenate([b[...] for b in blocks], 0)).astype(BF16)
    cot_o[...] = cot
    first_o[...] = cot[: first_o.shape[0]]
    d_result = (gate * cot.astype(F32)).astype(BF16)
    d_result_o[...] = d_result
    own_line_rows(where, downs, start, w_o)
    d_active_o[...] = mm(d_result, w_o[...], NT)


def hidden_kernel(picked, vecs, *refs):
    *terms, hidden_o, normed_o = refs
    hidden = picked[...].astype(F32) + add_up(terms)
    hidden_o[...] = hidden
    normed_o[...] = (hidden * inverse_rms(hidden) * vecs[1:2, :]).astype(BF16)


def forward_kernel(dims, members, where, d_active, *refs):
    lines = dims[0] * dims[2]
    ups, refs = refs[:lines], refs[lines:]
    blocks, (active_o, d_upper_o, near_o, far_o, w_s) = refs[:members], refs[members:]
    own_order_rows(where, ups, dims, w_s)
    normed = jnp.concatenate([b[...] for b in blocks], 0)
    upper = mm(normed, w_s[...])
    below = 0.5 * (1.0 + lax.erf(upper * (0.5**0.5)))
    active_o[...] = (upper * below).astype(BF16)
    slope = below + upper * jnp.exp(-0.5 * upper * upper) * ((2.0 * math.pi) ** -0.5)
    d_upper = (d_active[...] * slope).astype(BF16)
    d_upper_o[...] = d_upper
    put_halves(mm(d_upper, w_s[...], NT).astype(BF16), near_o, far_o)


def ff_grads_kernel(dims, members, where, active, d_upper, d_result, *refs):
    ny, nx, rows, ff_rows = dims
    blocks, (keep, by_x, by_y, down, up) = refs[:members], refs[members:]
    normed = jnp.concatenate([b[...] for b in blocks], 0)
    down[...] = mm(active[...], d_result[...], TN).astype(BF16)
    up[...] = mm(normed, d_upper[...], TN).astype(BF16)
    wide = up.shape[1]
    part = members * rows // 2
    for k in range(ny * nx):
        line = where[2] ^ k
        y, x = lax.div(line, jnp.int32(nx)), lax.rem(line, jnp.int32(nx))
        first = by_x.at[k // 2] if k % 2 else keep.at[k // 2]
        second = by_y.at[k % 2] if k // 2 else keep.at[2 + k % 2]
        first[...] = down[pl.ds(pl.multiple_of(line * ff_rows, ff_rows), ff_rows)]
        for g in range(members):
            at = pl.multiple_of(((y * members + g) * nx + x) * rows, rows)
            half, row = divmod(g * rows, part)
            second[row : row + rows, half * wide : (half + 1) * wide] = up[pl.ds(at, rows)]


def add_halves_kernel(keep, got_x, got_y, mine, to_y, to_x):
    def both(index, got):
        return keep[index].astype(F32) + got.astype(F32)

    mine[0] = both(0, got_x[0])
    mine[1] = both(2, got_y[0])
    to_y[...] = both(1, got_x[1]).astype(BF16)
    to_x[...] = both(3, got_y[1]).astype(BF16)


def result_kernel(active, attended, w_down, w_out, cot, gate, spread, logit_o, near_o, far_o):
    combined = mm(active[...], w_down[...]) + mm(attended[...], w_out[...])
    logit = jnp.sum(cot[...].astype(F32) * combined, 1, keepdims=True)
    logit_o[...] = logit * gate[...] * (1.0 - gate[...])
    update = (gate[...] * combined).astype(BF16)
    put_halves(mm(spread[...], update, TN).astype(BF16), near_o, far_o)


def hidden_back_kernel(own, hidden_r, vecs, gate, cot, *refs):
    *terms, d_branch_o, d_hidden_o, gain_o = refs
    d_normed = add_up(terms)
    hidden = hidden_r[...]
    inv = inverse_rms(hidden)
    u = d_normed * vecs[1:2, :]
    d_hidden = inv * u - hidden * (inv * inv * inv * jnp.mean(u * hidden, 1, keepdims=True))
    d_hidden_o[...] = d_hidden
    gain_o[...] = (d_normed * hidden * inv).astype(BF16)
    d_update = gate[:own, :] * cot[...].astype(F32)
    d_branch_o[...] = (d_update + d_hidden).astype(BF16)


def attention_back_kernel(members, where, *refs):
    w_out, joined_r, exact_r, w, vecs, picked_r, logit, d_hidden, spread = refs[:9]
    blocks = refs[9 : 9 + members]
    near_o, far_o, d_joined_o, gain_o = refs[9 + members :]
    routed, width = picked_r.shape
    own = routed // members
    heads = joined_r.shape[1] // (3 * HDIM)
    d_branch = jnp.concatenate([b[...] for b in blocks], 0)
    d_attended = mm(d_branch, w_out[...], NT).astype(BF16)
    joined = joined_r[...]
    exact = exact_r[...]
    kept = kept_pairs(where[3], routed, own)
    grads = [[], [], []]
    for h in range(heads):
        queries, keys, values = (
            joined[:, (t * heads + h) * HDIM : (t * heads + h + 1) * HDIM] for t in range(3)
        )
        probs, total = probabilities(queries, keys, kept)
        d_att = d_attended[:, h * HDIM : (h + 1) * HDIM]
        d_wide = d_att.astype(F32)
        delta = jnp.sum(d_wide * exact[:, h * HDIM : (h + 1) * HDIM], 1, keepdims=True)
        d_scores = (probs / total * (mm(d_att, values, NT) - delta)).astype(BF16)
        grads[0].append(mm(d_scores, keys) * HDIM ** (-0.5))
        grads[1].append(mm(d_scores, queries, TN) * HDIM ** (-0.5))
        grads[2].append(mm(probs.astype(BF16), (d_wide / total).astype(BF16), TN))
    d_joined = jnp.concatenate(grads[0] + grads[1] + grads[2], 1).astype(BF16)
    d_joined_o[...] = d_joined
    d_normed = mm(d_joined, w[...], NT)
    picked = picked_r[...].astype(F32)
    inv = inverse_rms(picked)
    gain_o[...] = (d_normed * picked * inv).astype(BF16)
    v = d_normed * vecs[0:1, :]
    d_picked = inv * v - picked * (inv * inv * inv * jnp.mean(v * picked, 1, keepdims=True))
    d_picked = d_picked + logit[...] * vecs[2:3, :]
    first = d_picked[:own] + d_hidden[...]
    d_picked = jnp.concatenate([first, d_picked[own:]], 0).astype(BF16)
    put_halves(mm(spread[...], d_picked, TN).astype(BF16), near_o, far_o)


def grads_kernel(dims, members, where, normed, d_joined, attended, gain_a, gain_m, *refs):
    ny, nx, rows = dims
    lines = ny * nx
    picked, logit, refs = refs[0], refs[1], refs[2:]
    blocks, sums, (main, vec_s, out) = refs[:members], refs[members : members + lines], refs[-3:]
    cols = d_joined.shape[1]
    routed, width = normed.shape
    own = gain_m.shape[0]
    main[...] = mm(normed[...], d_joined[...], TN).astype(BF16)
    lanes = lax.broadcasted_iota(jnp.int32, (routed, 128), 1)

    def lane(k, count):
        return (lanes[:count] == k).astype(F32)

    vec = mm(gain_a[...], lane(0, routed).astype(BF16), TN)
    vec = vec + mm(gain_m[...], lane(1, own).astype(BF16), TN)
    high = logit[...].astype(BF16)
    low = (logit[...] - high.astype(F32)).astype(BF16)
    vec = vec + mm(picked[...], (lane(2, routed) * high.astype(F32)).astype(BF16), TN)
    vec = vec + mm(picked[...], (lane(2, routed) * low.astype(F32)).astype(BF16), TN)
    vec_s[...] = vec.astype(BF16)
    out[...] = mm(attended[...], jnp.concatenate([b[...] for b in blocks], 0), TN).astype(BF16)
    for k in range(lines):
        line = where[2] ^ k
        y, x = lax.div(line, jnp.int32(nx)), lax.rem(line, jnp.int32(nx))
        for g in range(members):
            at = pl.multiple_of(((y * members + g) * nx + x) * rows, rows)
            sums[k][g * rows : (g + 1) * rows, :cols] = main[pl.ds(at, rows)]
            sums[k][g * rows : (g + 1) * rows, cols:] = vec_s[pl.ds(at, rows)]
        half, end = width // 2, members * rows
        at = pl.multiple_of(line * rows, rows)
        for j in range(2):
            piece = out[pl.ds(at, rows), j * half : (j + 1) * half]
            sums[k][end + j * rows : end + (j + 1) * rows, :] = piece


def join_slots_kernel(cap, lines, *refs):
    terms, outs = refs[:-lines], refs[-lines:]
    total = add_up(terms).astype(BF16)
    for j in range(2):
        for k in range(lines):
            at = (j * lines + k) * cap
            outs[k][j * cap : (j + 1) * cap] = total[at : at + cap]


def place_kernel(cap, lines, where, pick, tokens, cot, *refs):
    blocks, (out_o, grad_o, got) = refs[:lines], refs[lines:]
    for k, block in enumerate(blocks):
        got[where[2] ^ k] = block[...]
    for s in range(tokens.shape[0]):
        hot = pick[s]
        out_o[s] = (tokens[s].astype(F32) + mm(hot, got[s, :cap], TN)).astype(BF16)
        grad_o[s] = (cot[s].astype(F32) + mm(hot, got[s, cap:], TN)).astype(BF16)


def line_sums_kernel(dims, where, mine, got_down, got_up, *refs):
    members, rows, ff_rows = dims
    *parts, near_o, far_o, out_o, down_o, send = refs
    cols = parts[0].shape[1]
    wide = mine.shape[2] // 2
    up = mine[1] + got_up[...].astype(F32)
    main = parts[0][...].astype(F32)
    for part in parts[1:]:
        main = main + part[...].astype(F32)
    for g in range(members):
        send[g, :, :cols] = main[g * rows : (g + 1) * rows].astype(BF16)
        half, row = divmod(g * rows, members * rows // 2)
        piece = up[row : row + rows, half * wide : (half + 1) * wide]
        send[g, :, cols:] = piece.astype(BF16)
    depth = near_o.shape[0]
    for k in range(depth):
        near_o[k] = send[where[3] ^ k]
        far_o[k] = send[where[3] ^ (depth + k)]
    end = members * rows
    out_o[...] = jnp.concatenate([main[end : end + rows], main[end + rows :]], 1)
    down_o[...] = mine[0] + got_down[...].astype(F32)


def pair_kernel(near, far, *outs):
    rows = near.shape[1]
    for k, out in enumerate(outs):
        out[:rows] = near[k]
        out[rows:] = far[k]


def unpack_kernel(dims, where, *refs):
    ny, members, nx, ff_rows = dims
    depth = members // 2
    pairs, (qkv_o, up_o, *vec_o, got) = refs[:depth], refs[depth:]
    rows = got.shape[1]
    for k, pair in enumerate(pairs):
        got[where[3] ^ k] = pair[:rows]
        got[where[3] ^ (depth + k)] = pair[rows:]
    cols = 3 * ny * HDIM
    for t in range(3):
        for y in range(ny):
            from_ = (t * ny + y) * HDIM
            row = [got[g, :, from_ : from_ + HDIM] for g in range(members)]
            at = (t * HEADS + y * members) * HDIM
            qkv_o[:, at : at + members * HDIM] = jnp.concatenate(row, 1).astype(F32)
    for y in range(ny):
        for g in range(members):
            for x in range(nx):
                at = ((y * members + g) * nx + x) * ff_rows
                from_ = cols + 128 + (y * nx + x) * ff_rows
                up_o[:, at : at + ff_rows] = got[g, :, from_ : from_ + ff_rows].astype(F32)
    vec = got[0, :, cols : cols + 128].astype(F32)
    for g in range(1, members):
        vec = vec + got[g, :, cols : cols + 128].astype(F32)
    high = vec.astype(BF16)
    low = (vec - high.astype(F32)).astype(BF16)
    vec = mm(eye_rows(), high, NT) + mm(eye_rows(), low, NT)
    for k, out in enumerate(vec_o):
        out[...] = vec[k : k + 1]


def grouped(
    tokens, chosen, w_qkv, w_out, w_up, w_down, gain_attn, gain_mlp, router, cotangent
):
    ny, nc, nz, nx = (lax.axis_size(a) for a in ("y", "c", "z", "x"))
    y, c, z, x = (lax.axis_index(a) for a in ("y", "c", "z", "x"))
    seq_count, seg_len, width = tokens.shape
    cap = seg_len // 4
    routed = chosen.shape[1]
    members, lines = nc * nz, ny * nx
    member, line = c * nz + z, y * nx + x
    shard = ((y * nc + c) * nz + z) * nx + x
    rows, ff_rows = w_qkv.shape[0], w_down.shape[0]
    heads = HEADS // members
    own = routed // members
    cols, wide = 3 * heads * HDIM, lines * ff_rows
    where = jnp.stack([c, z, line, member, shard]).astype(jnp.int32)
    chosen_t = chosen.T
    block = (own, width)
    slot_block = (2 * cap, width)
    halves = [((nz, own, width), BF16)] * 2
    slot_halves = [((nz, lines * cap, width), BF16)] * 2

    pick, *picked_rows = local_call(
        partial(pick_kernel, cap),
        [Far(((seq_count, cap, seg_len), BF16))] + [(slot_block, BF16)] * lines,
        (where, chosen_t, tokens, cotangent),
        scratch=[pltpu.VMEM((seq_count, 2 * cap, width), BF16)],
        scalars=1,
    )
    line_slots = picked_rows[:1] + send_lines(picked_rows[1:])
    (hot,) = local_call(
        partial(spread_kernel, (ny, nc, nz, nx, seg_len, cap)),
        [Far(((routed, members * lines * cap), BF16))],
        (where, chosen, chosen_t),
        scalars=1,
    )
    spread = Far(hot)
    (line_slots,) = local_call(
        partial(stack_kernel, cap), [((2 * lines * cap, width), BF16)], line_slots, after=(hot,)
    )
    slots = gather_group([line_slots])
    half = lines * cap
    picked_slots, cot_slots = [Far(b, half) for b in slots], [Far(b, half, half) for b in slots]

    vecs = [v.reshape(1, rows) for v in (gain_attn, gain_mlp, router)]
    (columns,) = local_call(
        partial(columns_kernel, (ny, members, nx, ff_rows)),
        [((members, rows, cols + 128 + wide), BF16)],
        tuple(Far(v) for v in (w_qkv, w_up, *vecs)),
        scratch=[pltpu.VMEM((8, rows), F32)],
    )
    got_cols = lax.all_to_all(columns, ("c", "z"), 0, 0, tiled=True)
    first, second = local_call(
        relay_kernel,
        [
            Far(((lines, members * rows + 2 * rows, width // 2), BF16)),
            ((members * rows + 2 * ff_rows, width // 2), BF16),
        ],
        (got_cols, w_out, w_down),
        after=(line_slots,),
    )
    first = lax.all_to_all(first, ("y", "x"), 0, 0, tiled=True)
    second = gather_lines(second)

    picked, normed, full_qkv, picked_own, full_out, full_vecs, joined, attended, exact, near, far = (
        local_call(
            partial(attention_kernel, (ny, nx, rows, cap), members),
            [
                ((routed, width), BF16),
                ((routed, width), BF16),
                ((width, cols), BF16),
                (block, BF16),
                ((heads * HDIM, width), BF16),
                ((8, width), F32),
                ((routed, cols), BF16),
                ((routed, heads * HDIM), BF16),
                ((routed, heads * HDIM), F32),
            ]
            + halves,
            (where, spread, Far(first), *picked_slots),
            flops=1.2e9,
            scratch=[pltpu.VMEM((width, 128), BF16)],
            scalars=1,
        )
    )
    terms = scatter_group(near, far)
    gate, cot, cot_own, d_result, d_active, full_down = local_call(
        partial(update_kernel, (lines, members, members * rows)),
        [
            ((routed, 1), F32),
            ((routed, width), BF16),
            (block, BF16),
            ((routed, width), BF16),
            ((routed, wide), F32),
            ((wide, width), BF16),
        ],
        (where, spread, picked, full_vecs, *second, *cot_slots),
        flops=8e8,
        scalars=1,
    )
    hidden, normed_own = local_call(
        hidden_kernel,
        [(block, F32), (block, BF16)],
        (picked_own, full_vecs, *terms),
    )
    normed_mlp = gather_group([normed_own])

    active, d_upper, near, far = local_call(
        partial(forward_kernel, (ny, members, nx, rows), members),
        [((routed, wide), BF16)] * 2 + halves,
        (where, d_active, *second, *normed_mlp),
        flops=6e8,
        scratch=[pltpu.VMEM((width, wide), BF16)],
        scalars=1,
    )
    terms = scatter_group(near, far)
    half = (ff_rows, width)
    ff_keep, ff_x, ff_y = local_call(
        partial(ff_grads_kernel, (ny, nx, rows, ff_rows), members),
        [((4, *half), BF16), ((2, *half), BF16), ((2, *half), BF16)],
        (where, active, d_upper, d_result, *normed_mlp),
        flops=6e8,
        scratch=[pltpu.VMEM((wide, width), BF16), pltpu.VMEM((width, wide), BF16)],
        scalars=1,
    )
    logit, up_near, up_far = local_call(
        result_kernel,
        [((routed, 1), F32)] + slot_halves,
        (active, attended, full_down, full_out, cot, gate, spread),
        flops=8e8,
    )
    d_branch_own, d_hidden, gain_m = local_call(
        partial(hidden_back_kernel, own),
        [(block, BF16), (block, F32), (block, BF16)],
        (hidden, full_vecs, gate, cot_own, *terms),
        after=(ff_x, logit),
    )
    d_branch = gather_group([d_branch_own])
    up_far = send_c(up_far)
    ff_mine, ff_y, ff_x = local_call(
        add_halves_kernel,
        [((2, *half), F32), (half, BF16), (half, BF16)],
        (ff_keep, lax.ppermute(ff_x, "x", flips(nx)[1]), lax.ppermute(ff_y, "y", flips(ny)[1])),
    )
    ff_got = (lax.ppermute(ff_y, "y", flips(ny)[1]), lax.ppermute(ff_x, "x", flips(nx)[1]))

    near, far, d_joined, gain_a = local_call(
        partial(attention_back_kernel, members),
        slot_halves + [((routed, cols), BF16), ((routed, width), BF16)],
        (where, full_out, joined, exact, full_qkv, full_vecs, picked)
        + (logit, d_hidden, spread, *d_branch),
        flops=1.2e9,
        scalars=1,
        after=(ff_mine,),
    )
    far = send_c(far)
    parts = local_call(
        partial(grads_kernel, (ny, nx, rows), members),
        [((members * rows + 2 * rows, cols + 128), BF16)] * lines,
        (where, normed, d_joined, attended, gain_a, gain_m, picked, logit, *d_branch),
        flops=5e8,
        scratch=[
            pltpu.VMEM((width, cols), BF16),
            pltpu.VMEM((width, 128), BF16),
            pltpu.VMEM((heads * HDIM, width), BF16),
        ],
        scalars=1,
    )
    parts = parts[:1] + send_lines(parts[1:])
    both_slots = (2 * lines * cap, width)
    mine, *low = local_call(
        slot_sum_kernel,
        [(both_slots, F32)] + [(both_slots, BF16)] * (nz - 1),
        (up_near, up_far, near, far),
    )
    back_rows = local_call(
        partial(join_slots_kernel, cap, lines),
        [(slot_block, BF16)] * lines,
        [mine] + send_z(low),
    )
    back_rows = back_rows[:1] + send_lines(back_rows[1:])
    row_width = cols + 128 + wide
    near, far, grad_out, grad_down = local_call(
        partial(line_sums_kernel, (members, rows, ff_rows)),
        [((nz, rows, row_width), BF16)] * 2 + [((rows, width), F32), ((ff_rows, width), F32)],
        (where, ff_mine, *ff_got, *parts),
        scratch=[pltpu.VMEM((members, rows, row_width), BF16)],
        scalars=1,
        after=back_rows[:1],
    )
    pairs = local_call(pair_kernel, [((2 * rows, row_width), BF16)] * nz, (near, send_c(far)))
    pairs = pairs[:1] + send_z(pairs[1:])
    output, grad_tokens = local_call(
        partial(place_kernel, cap, lines),
        [(tokens.shape, BF16), (tokens.shape, BF16)],
        (where, Far(pick), tokens, cotangent, *back_rows),
        scratch=[pltpu.VMEM((seq_count, 2 * cap, width), BF16)],
        scalars=1,
    )
    grad_qkv, grad_up, *grad_vecs = local_call(
        partial(unpack_kernel, (ny, members, nx, ff_rows)),
        [(w_qkv.shape, F32), (w_up.shape, F32)] + [((1, rows), F32)] * 3,
        (where, *pairs),
        scratch=[pltpu.VMEM((members, rows, row_width), BF16)],
        scalars=1,
    )
    return (
        output,
        grad_tokens,
        grad_qkv,
        grad_out,
        grad_up,
        grad_down,
        *(v.reshape(rows) for v in grad_vecs),
    )


def fits(mesh):
    head_count, block_count = mesh.devices.shape
    members = (head_count // 2) * (block_count // 2)
    power = members & (members - 1) == 0
    return power and head_count == 4 and HEADS == 2 * members


def solution(mesh):
    if fits(mesh):
        head_count, block_count = mesh.devices.shape
        devices = mesh.devices.reshape(2, head_count // 2, block_count // 2, 2)
        mesh = jax.sharding.Mesh(devices, ("y", "c", "z", "x"))
        body, all_axes = grouped, ("y", "c", "z", "x")
    else:
        body, all_axes = shards, ("head", "blk")
    seqs, mats, vecs = P(None, all_axes, None), P(all_axes, None), P(all_axes)
    in_specs = (seqs, P(), mats, mats, mats, mats, vecs, vecs, vecs, seqs)
    out_specs = (seqs, seqs, mats, mats, mats, mats, vecs, vecs, vecs)
    return jax.shard_map(body, mesh=mesh, in_specs=in_specs, out_specs=out_specs, check_vma=False)
```

```python
import math
from functools import partial

import jax
import jax.numpy as jnp
from jax import lax
from jax.experimental import pallas as pl
from jax.experimental.pallas import tpu as pltpu
from jax.sharding import PartitionSpec as P

HEADS = 16
HDIM = 64


epsilon = 1e-06
neg_large = -1e30


def rms_norm(values, gain_vec):
    inverse_rms = lax.rsqrt(jnp.mean(values * values, axis=-1, keepdims=True) + epsilon)
    return values * inverse_rms * gain_vec


def exact_gelu(values):
    return jax.nn.gelu(values, approximate=False)


def take_rows(seq_rows, row_index):
    return seq_rows[row_index]


def add_rows(seq_rows, row_index, additions):
    return seq_rows.at[row_index].add(additions)


def shards(tokens, chosen, w_qkv, w_out, w_up, w_down, gain_attn, gain_mlp, router, cotangent):
    head_count = lax.axis_size("head")
    block_count = lax.axis_size("blk")
    shard_count = head_count * block_count
    seq_count, seg_len, model_width = tokens.shape
    cap_len = seg_len // 4
    routed_count = chosen.shape[1]
    seq_len = seg_len * shard_count
    local_heads = HEADS // head_count
    slot_rows = head_count * cap_len
    scale_factor = HDIM ** (-0.5)
    head_index = lax.axis_index("head")
    block_index = lax.axis_index("blk")
    my_shard = head_index * block_count + block_index
    bounds = jnp.arange(shard_count + 1, dtype=jnp.int32) * seg_len
    before = jax.vmap(lambda chosen_row: jnp.searchsorted(chosen_row, bounds, side="left"))(chosen)
    first_index = before[:, :-1]
    shard_load = before[:, 1:] - first_index
    slot_iota = jnp.arange(cap_len, dtype=jnp.int32)
    live_table = slot_iota[None, None, :] < shard_load[:, :, None]
    lookup = jnp.minimum(first_index[:, :, None] + slot_iota[None, None, :], routed_count - 1)
    place_table = jnp.take_along_axis(
        chosen, lookup.reshape(seq_count, shard_count * cap_len), axis=1
    )
    place_table = jnp.where(
        live_table, place_table.reshape(seq_count, shard_count, cap_len), seq_len
    )
    my_positions = lax.dynamic_index_in_dim(place_table, my_shard, 1, False)
    my_live = lax.dynamic_index_in_dim(live_table, my_shard, 1, False)
    local_rows = jnp.clip(my_positions - my_shard * seg_len, 0, seg_len - 1)
    cycle_positions = place_table.reshape(seq_count, head_count, block_count, cap_len).transpose(
        0, 2, 1, 3
    )
    cycle_positions = cycle_positions.reshape(seq_count, block_count * slot_rows)
    query_positions = lax.dynamic_slice_in_dim(
        cycle_positions, block_index * slot_rows, slot_rows, 1
    )
    live_weight = my_live.astype(jnp.float32)[:, :, None]
    gathered = (
        lax.all_gather(w_qkv, ("head", "blk"), axis=0, tiled=True),
        lax.all_gather(w_out, ("head", "blk"), axis=0, tiled=True),
        lax.all_gather(w_up, ("head", "blk"), axis=0, tiled=True),
        lax.all_gather(w_down, ("head", "blk"), axis=0, tiled=True),
        lax.all_gather(gain_attn, ("head", "blk"), axis=0, tiled=True),
        lax.all_gather(gain_mlp, ("head", "blk"), axis=0, tiled=True),
        lax.all_gather(router, ("head", "blk"), axis=0, tiled=True),
    )
    full_qkv, full_out, full_up, full_down, full_gain_attn, full_gain_mlp, full_router = gathered
    picked = jax.vmap(take_rows)(tokens, local_rows)
    picked = jnp.where(my_live[:, :, None], picked, jnp.zeros_like(picked))
    picked_exact = picked.astype(jnp.float32)
    router_gate = jax.nn.sigmoid(
        jnp.einsum("scd,d->sc", picked, full_router, preferred_element_type=jnp.float32)
    )
    normed_exact, norm_attn_back = jax.vjp(
        rms_norm, picked_exact, full_gain_attn.astype(jnp.float32)
    )
    normed = normed_exact.astype(jnp.bfloat16)
    joined = jnp.einsum("scd,de->sce", normed, full_qkv, preferred_element_type=jnp.float32).astype(
        jnp.bfloat16
    )
    to_heads = lax.all_to_all(
        joined.reshape(seq_count, cap_len, 3, model_width),
        "head",
        split_axis=3,
        concat_axis=1,
        tiled=True,
    )
    queries_tok = to_heads[:, :, 0]
    queries_heads = queries_tok.reshape(seq_count, slot_rows, local_heads, HDIM)
    key_values = to_heads[:, :, 1:3]
    my_keys = key_values[:, :, 0].reshape(seq_count, slot_rows, local_heads, HDIM)
    my_values = key_values[:, :, 1].reshape(seq_count, slot_rows, local_heads, HDIM)
    stat_shape = (seq_count, local_heads, slot_rows)
    piece = lax.all_gather(key_values, "blk", axis=1, tiled=True)
    run_max = jnp.full(stat_shape, neg_large, jnp.float32)
    piece_rows = piece.shape[1]
    key_pos = cycle_positions
    keys_piece = piece[:, :, 0].reshape(seq_count, piece_rows, local_heads, HDIM)
    values_piece = piece[:, :, 1].reshape(seq_count, piece_rows, local_heads, HDIM)
    scores = (
        jnp.einsum("sqhd,skhd->shqk", queries_heads, keys_piece, preferred_element_type=jnp.float32)
        * scale_factor
    )
    allowed = key_pos[:, None, None, :] <= query_positions[:, None, :, None]
    scores = jnp.where(allowed, scores, neg_large)
    new_max = jnp.maximum(run_max, jnp.max(scores, axis=3))
    prob_block = jnp.where(allowed, jnp.exp(scores - new_max[..., None]), 0.0)
    new_total = jnp.sum(prob_block, axis=3)
    added = jnp.einsum(
        "shqk,skhd->sqhd",
        prob_block.astype(jnp.bfloat16),
        values_piece,
        preferred_element_type=jnp.float32,
    )
    attended_exact = added / new_total.transpose(0, 2, 1)[..., None]
    log_sum = new_max + jnp.log(new_total)
    attended_tok = attended_exact.astype(jnp.bfloat16).reshape(
        seq_count, slot_rows, local_heads * HDIM
    )
    attended = lax.all_to_all(attended_tok, "head", split_axis=1, concat_axis=2, tiled=True)
    branch = jnp.einsum("sce,ed->scd", attended, full_out, preferred_element_type=jnp.float32)
    hidden_state = picked_exact + branch
    normed_mlp_exact, norm_mlp_back = jax.vjp(
        rms_norm, hidden_state, full_gain_mlp.astype(jnp.float32)
    )
    normed_mlp = normed_mlp_exact.astype(jnp.bfloat16)
    upper = jnp.einsum("scd,di->sci", normed_mlp, full_up, preferred_element_type=jnp.float32)
    active_exact, gelu_back = jax.vjp(exact_gelu, upper)
    active = active_exact.astype(jnp.bfloat16)
    result = jnp.einsum("sci,id->scd", active, full_down, preferred_element_type=jnp.float32)
    combined = branch + result
    update = router_gate[:, :, None] * combined * live_weight
    output = jax.vmap(add_rows)(tokens.astype(jnp.float32), local_rows, update).astype(jnp.bfloat16)
    regathered = (
        lax.all_gather(w_qkv, ("head", "blk"), axis=0, tiled=True),
        lax.all_gather(w_out, ("head", "blk"), axis=0, tiled=True),
        lax.all_gather(w_up, ("head", "blk"), axis=0, tiled=True),
        lax.all_gather(w_down, ("head", "blk"), axis=0, tiled=True),
        lax.all_gather(gain_attn, ("head", "blk"), axis=0, tiled=True),
        lax.all_gather(gain_mlp, ("head", "blk"), axis=0, tiled=True),
        lax.all_gather(router, ("head", "blk"), axis=0, tiled=True),
    )
    back_qkv, back_out, back_up, back_down, back_gain_attn, back_gain_mlp, back_router = regathered
    picked_cot = jax.vmap(take_rows)(cotangent, local_rows).astype(jnp.float32) * live_weight
    d_update = router_gate[:, :, None] * picked_cot
    d_logit = jnp.sum(picked_cot * combined, axis=2) * router_gate * (1.0 - router_gate)
    grad_router = jnp.einsum("sc,scd->d", d_logit, picked_exact, precision=lax.Precision.HIGHEST)
    d_result = d_update.astype(jnp.bfloat16)
    d_active = jnp.einsum("scd,id->sci", d_result, back_down, preferred_element_type=jnp.float32)
    d_upper = gelu_back(d_active)[0].astype(jnp.bfloat16)
    d_normed_mlp = jnp.einsum("sci,di->scd", d_upper, back_up, preferred_element_type=jnp.float32)
    d_hidden, grad_gain_mlp = norm_mlp_back(d_normed_mlp)
    d_branch = (d_update + d_hidden).astype(jnp.bfloat16)
    d_attended = jnp.einsum(
        "scd,ed->sce", d_branch, back_out, preferred_element_type=jnp.float32
    ).astype(jnp.bfloat16)
    d_att_tok = lax.all_to_all(d_attended, "head", split_axis=2, concat_axis=1, tiled=True)
    d_att_heads = d_att_tok.reshape(seq_count, slot_rows, local_heads, HDIM)
    delta_tok = jnp.sum(d_att_heads.astype(jnp.float32) * attended_exact, axis=3)
    delta_sq = delta_tok.transpose(0, 2, 1)
    piece = lax.all_gather(key_values, "blk", axis=1, tiled=True)
    piece_rows = piece.shape[1]
    key_pos = cycle_positions
    keys_piece = piece[:, :, 0].reshape(seq_count, piece_rows, local_heads, HDIM)
    values_piece = piece[:, :, 1].reshape(seq_count, piece_rows, local_heads, HDIM)
    scores = (
        jnp.einsum("sqhd,skhd->shqk", queries_heads, keys_piece, preferred_element_type=jnp.float32)
        * scale_factor
    )
    allowed = key_pos[:, None, None, :] <= query_positions[:, None, :, None]
    prob_block = jnp.where(allowed, jnp.exp(scores - log_sum[..., None]), 0.0)
    d_prob = jnp.einsum(
        "sqhd,skhd->shqk", d_att_heads, values_piece, preferred_element_type=jnp.float32
    )
    d_scores = (prob_block * (d_prob - delta_sq[..., None])).astype(jnp.bfloat16)
    d_queries = (
        jnp.einsum("shqk,skhd->sqhd", d_scores, keys_piece, preferred_element_type=jnp.float32)
        * scale_factor
    )
    lse_tok = log_sum.transpose(0, 2, 1)
    lse_high = lse_tok.astype(jnp.bfloat16)
    lse_low = (lse_tok - lse_high.astype(jnp.float32)).astype(jnp.bfloat16)
    delta_high = delta_tok.astype(jnp.bfloat16)
    delta_low = (delta_tok - delta_high.astype(jnp.float32)).astype(jnp.bfloat16)
    query_piece = lax.all_gather(queries_tok, "blk", axis=1, tiled=True)
    dout_piece = lax.all_gather(d_att_tok, "blk", axis=1, tiled=True)
    piece_lse_high = lax.all_gather(lse_high, "blk", axis=1, tiled=True)
    piece_lse_low = lax.all_gather(lse_low, "blk", axis=1, tiled=True)
    piece_delta_high = lax.all_gather(delta_high, "blk", axis=1, tiled=True)
    piece_delta_low = lax.all_gather(delta_low, "blk", axis=1, tiled=True)
    piece_rows = query_piece.shape[1]
    query_heads = query_piece.reshape(seq_count, piece_rows, local_heads, HDIM)
    dout_heads = dout_piece.reshape(seq_count, piece_rows, local_heads, HDIM)
    piece_lse = (piece_lse_high.astype(jnp.float32) + piece_lse_low.astype(jnp.float32)).transpose(
        0, 2, 1
    )
    piece_delta = (
        piece_delta_high.astype(jnp.float32) + piece_delta_low.astype(jnp.float32)
    ).transpose(0, 2, 1)
    scores = (
        jnp.einsum("sqhd,skhd->shqk", query_heads, my_keys, preferred_element_type=jnp.float32)
        * scale_factor
    )
    allowed = query_positions[:, None, None, :] <= cycle_positions[:, None, :, None]
    prob_block = jnp.where(allowed, jnp.exp(scores - piece_lse[..., None]), 0.0)
    grad_values = jnp.einsum(
        "shqk,sqhd->skhd",
        prob_block.astype(jnp.bfloat16),
        dout_heads,
        preferred_element_type=jnp.float32,
    )
    d_prob = jnp.einsum(
        "sqhd,skhd->shqk", dout_heads, my_values, preferred_element_type=jnp.float32
    )
    d_scores = (prob_block * (d_prob - piece_delta[..., None])).astype(jnp.bfloat16)
    grad_keys = (
        jnp.einsum("shqk,sqhd->skhd", d_scores, query_heads, preferred_element_type=jnp.float32)
        * scale_factor
    )
    d_heads = jnp.stack(
        [
            d_queries.astype(jnp.bfloat16),
            grad_keys.astype(jnp.bfloat16),
            grad_values.astype(jnp.bfloat16),
        ],
        axis=2,
    )
    d_heads = d_heads.reshape(seq_count, slot_rows, 3, local_heads * HDIM)
    d_joined = lax.all_to_all(d_heads, "head", split_axis=1, concat_axis=3, tiled=True).reshape(
        seq_count, cap_len, 3 * model_width
    )
    d_normed = jnp.einsum("sce,de->scd", d_joined, back_qkv, preferred_element_type=jnp.float32)
    d_picked_norm, grad_gain_attn = norm_attn_back(d_normed)
    d_picked = (
        d_hidden
        + d_picked_norm
        + d_logit[:, :, None] * back_router.astype(jnp.float32)[None, None, :]
    )
    grad_tokens = jax.vmap(add_rows)(
        cotangent.astype(jnp.float32), local_rows, d_picked * live_weight
    ).astype(jnp.bfloat16)
    grad_qkv = jnp.einsum("scd,sce->de", normed, d_joined, preferred_element_type=jnp.float32)
    grad_out = jnp.einsum("sce,scd->ed", attended, d_branch, preferred_element_type=jnp.float32)
    grad_up = jnp.einsum("scd,sci->di", normed_mlp, d_upper, preferred_element_type=jnp.float32)
    grad_down = jnp.einsum("sci,scd->id", active, d_result, preferred_element_type=jnp.float32)
    owned = (
        lax.psum_scatter(grad_qkv, ("head", "blk"), scatter_dimension=0, tiled=True),
        lax.psum_scatter(grad_out, ("head", "blk"), scatter_dimension=0, tiled=True),
        lax.psum_scatter(grad_up, ("head", "blk"), scatter_dimension=0, tiled=True),
        lax.psum_scatter(grad_down, ("head", "blk"), scatter_dimension=0, tiled=True),
        lax.psum_scatter(grad_gain_attn, ("head", "blk"), scatter_dimension=0, tiled=True),
        lax.psum_scatter(grad_gain_mlp, ("head", "blk"), scatter_dimension=0, tiled=True),
        lax.psum_scatter(grad_router, ("head", "blk"), scatter_dimension=0, tiled=True),
    )
    return (
        output,
        grad_tokens,
        owned[0],
        owned[1],
        owned[2],
        owned[3],
        owned[4],
        owned[5],
        owned[6],
    )


F32, BF16 = jnp.float32, jnp.bfloat16
NN = (((1,), (0,)), ((), ()))
NT = (((1,), (1,)), ((), ()))
TN = (((0,), (0,)), ((), ()))


def mm(left, right, dims=NN):
    return lax.dot_general(left, right, dims, preferred_element_type=F32)


class Far:
    def __init__(self, item, start=0, count=None, dim=0):
        self.item, self.start, self.count, self.dim = item, start, count, dim

    def shape(self):
        shape = list(self.item.shape)
        if self.count is not None:
            shape[self.dim] = self.count
        return tuple(shape)

    def source(self, ref):
        if self.count is None:
            return ref
        return ref.at[(slice(None),) * self.dim + (pl.ds(self.start, self.count),)]


class Loaded:
    def __init__(self, copy, ref):
        self.copy, self.ref, self.shape, self.waited = copy, ref, ref.shape, False

    def __getitem__(self, index):
        self.wait()
        return self.ref[index]

    def wait(self):
        if not self.waited:
            self.copy.wait()
        self.waited = True


class Stored:
    def __init__(self, copy, ref):
        self.copy, self.ref, self.shape, self.started = copy, ref, ref.shape, False

    def __getitem__(self, index):
        return self.ref[index]

    def __setitem__(self, index, value):
        self.ref[index] = value
        if index is Ellipsis:
            self.start()

    def start(self):
        if not self.started:
            self.copy.start()
        self.started = True


def local_call(body, outs, args, flops=0, scratch=(), scalars=0, after=()):
    far_in = [a if isinstance(a, Far) else None for a in args]
    far_out = [isinstance(o, Far) for o in outs]
    outs = [o.item if f else o for o, f in zip(outs, far_out)]
    args = [pltpu.with_memory_space_constraint(f.item, pltpu.HBM) if f else a for a, f in zip(args, far_in)]
    shapes = [pltpu.HBM(s, d) if f else jax.ShapeDtypeStruct(s, d) for (s, d), f in zip(outs, far_out)]
    spaces = [pltpu.SMEM] * scalars
    spaces += [pltpu.HBM if f else pltpu.VMEM for f in far_in[scalars:]]
    spaces += [pl.ANY] * len(after)
    stages = []
    for f in far_in:
        if f:
            stages.append(pltpu.VMEM(f.shape(), f.item.dtype))
    stages += [pltpu.VMEM(s, d) for (s, d), f in zip(outs, far_out) if f]
    n_in, n_out, n_far = len(args), len(outs), len(stages)
    first_out = n_in + len(after)
    if n_far:
        stages.append(pltpu.SemaphoreType.DMA((n_far,)))

    def run(*refs):
        ins, results = list(refs[:n_in]), list(refs[first_out : first_out + n_out])
        rest = refs[first_out + n_out :]
        own, stage = rest[: len(scratch)], rest[len(scratch) :]
        at, loads, stores = 0, [], []
        for i, f in enumerate(far_in):
            if f:
                copy = pltpu.make_async_copy(f.source(ins[i]), stage[at], stage[-1].at[at])
                copy.start()
                ins[i] = Loaded(copy, stage[at])
                loads.append(ins[i])
                at += 1
        for i, f in enumerate(far_out):
            if f:
                copy = pltpu.make_async_copy(stage[at], results[i], stage[-1].at[at])
                results[i] = Stored(copy, stage[at])
                stores.append(results[i])
                at += 1
        body(*ins, *results, *own)
        for load in loads:
            load.wait()
        for store in stores:
            store.start()
        for store in stores:
            store.copy.wait()

    return list(
        pl.pallas_call(
            run,
            out_shape=shapes,
            in_specs=[pl.BlockSpec(memory_space=s) for s in spaces],
            out_specs=[
                pl.BlockSpec(memory_space=pltpu.HBM if f else pltpu.VMEM) for f in far_out
            ],
            scratch_shapes=list(scratch) + stages,
            compiler_params=pltpu.CompilerParams(vmem_limit_bytes=32 * 2**20),
            cost_estimate=pl.CostEstimate(flops=int(flops), bytes_accessed=0, transcendentals=0),
        )(*args, *after)
    )


def flips(count):
    return [[(i, i ^ k) for i in range(count)] for k in range(count)]


def send_z(blocks):
    return [lax.ppermute(b, "z", f) for b, f in zip(blocks, flips(lax.axis_size("z"))[1:])]


def send_lines(blocks):
    count = lax.axis_size("y") * lax.axis_size("x")
    return [lax.ppermute(b, ("y", "x"), f) for b, f in zip(blocks, flips(count)[1:])]


def gather_lines(own):
    return [own] + send_lines([own] * (lax.axis_size("y") * lax.axis_size("x") - 1))


def send_c(block):
    return lax.ppermute(block, "c", flips(2)[1])


def gather_group(own):
    lists = [own] + [list(t) for t in zip(*[send_z([o] * (lax.axis_size("z") - 1)) for o in own])]
    blocks = [b for one in lists for b in one]
    return blocks + [send_c(b) for b in blocks]


def half_sum_kernel(near, far, mine, *low):
    for k in range(near.shape[0]):
        total = near[k].astype(F32) + far[k].astype(F32)
        if k == 0:
            mine[...] = total
        else:
            low[k - 1][...] = total.astype(BF16)


def slot_sum_kernel(*refs):
    pairs, (mine, *low) = refs[:4], refs[4:]
    size = pairs[0].shape[1]
    for j in range(2):
        near, far = pairs[2 * j], pairs[2 * j + 1]
        rows = slice(j * size, (j + 1) * size)
        for k in range(near.shape[0]):
            total = near[k].astype(F32) + far[k].astype(F32)
            if k == 0:
                mine[rows] = total
            else:
                low[k - 1][rows] = total.astype(BF16)


def scatter_group(near, far, after=()):
    depth, rows, lanes = near.shape
    outs = [((rows, lanes), F32)] + [((rows, lanes), BF16)] * (depth - 1)
    mine, *low = local_call(half_sum_kernel, outs, (near, send_c(far)), after=after)
    return [mine] + send_z(low)


def add_up(refs):
    total = refs[0][...]
    for ref in refs[1:]:
        total = total + ref[...].astype(F32)
    return total


def xor_order(blocks, index):
    step = 1
    while step < len(blocks):
        swap = (index & step) != 0
        blocks = [jnp.where(swap, blocks[b ^ step], blocks[b]) for b in range(len(blocks))]
        step *= 2
    return blocks


def columns_kernel(dims, w_qkv, w_up, gain_attn, gain_mlp, router, out, vec_s):
    ny, members, nx, ff_rows = dims
    cols = 3 * ny * HDIM
    vec_s[...] = jnp.zeros_like(vec_s)
    for k, vec in enumerate((gain_attn, gain_mlp, router)):
        vec_s[k : k + 1] = vec[...].astype(F32)
    vecs = mm(vec_s[...].astype(BF16), eye_rows(), TN).astype(BF16)
    for g in range(members):
        parts = []
        for t in range(3):
            for y in range(ny):
                at = (t * HEADS + y * members + g) * HDIM
                parts.append(w_qkv[:, at : at + HDIM])
        out[g, :, :cols] = jnp.concatenate(parts, 1)
        out[g, :, cols : cols + 128] = vecs
        for y in range(ny):
            for x in range(nx):
                at = ((y * members + g) * nx + x) * ff_rows
                to = cols + 128 + (y * nx + x) * ff_rows
                out[g, :, to : to + ff_rows] = w_up[:, at : at + ff_rows]


def eye_rows():
    down = lax.broadcasted_iota(jnp.int32, (8, 128), 0)
    return (down == lax.broadcasted_iota(jnp.int32, (8, 128), 1)).astype(F32).astype(BF16)


def pick_kernel(cap, where, chosen_t, tokens, cot, pick, *refs):
    *outs, rows = refs
    seq_count, seg_len = tokens.shape[:2]
    base = where[4] * seg_len
    places = base + lax.broadcasted_iota(jnp.int32, (chosen_t.shape[0], seg_len), 1)
    slots = lax.broadcasted_iota(jnp.int32, (cap, seg_len), 0)
    for s in range(seq_count):
        at = chosen_t[:, s : s + 1]
        present = jnp.sum((at == places).astype(F32), 0, keepdims=True)
        rank = jnp.sum(((at >= base) & (at < places)).astype(F32), 0, keepdims=True)
        hot = jnp.where(rank.astype(jnp.int32) == slots, present, 0.0).astype(BF16)
        pick[s] = hot
        rows[s, :cap] = mm(hot, tokens[s]).astype(BF16)
        rows[s, cap:] = mm(hot, cot[s]).astype(BF16)
    for k, out in enumerate(outs):
        out[...] = rows[where[2] ^ k]


def stack_kernel(cap, *refs):
    *blocks, out = refs
    for k, block in enumerate(blocks):
        for j in range(2):
            to = (j * len(blocks) + k) * cap
            out[to : to + cap] = block[j * cap : (j + 1) * cap]


def relay_kernel(got, w_out, w_down, first, up):
    members, rows, lanes = got.shape
    half = lanes // 2
    for line in range(first.shape[0]):
        at = members * rows
        first[line, :at] = got[:, :, :half].reshape(at, half)
        for block in (w_out, w_down):
            size = block.shape[0]
            for j in range(2):
                first[line, at : at + size] = block[:, j * half : (j + 1) * half]
                at += size
    up[...] = got[:, :, half:].reshape(members * rows, half)


def spread_kernel(dims, where, chosen, chosen_t, spread):
    ny, nc, nz, nx, seg_len, cap = dims
    c, z, line = where[0], where[1], where[2]
    routed = chosen_t.shape[0]
    members = nc * nz

    def owner_of(mine):
        return lax.div(mine, jnp.int32(seg_len))

    mine_col = chosen_t[:, 0:1]
    mine_row = chosen[0:1, :]
    for s in range(1, chosen.shape[0]):
        mine_col = jnp.where(line == s, chosen_t[:, s : s + 1], mine_col)
        mine_row = jnp.where(line == s, chosen[s : s + 1, :], mine_row)
    owner, owner_row = owner_of(mine_col), owner_of(mine_row)
    order = lax.broadcasted_iota(jnp.int32, (routed, routed), 0)
    other = lax.broadcasted_iota(jnp.int32, (routed, routed), 1)
    same = (owner == owner_row) & (other < order)
    slot = jnp.sum(same.astype(F32), 1, keepdims=True).astype(jnp.int32)
    ox, rest = lax.rem(owner, jnp.int32(nx)), lax.div(owner, jnp.int32(nx))
    oz, rest = lax.rem(rest, jnp.int32(nz)), lax.div(rest, jnp.int32(nz))
    oc, oy = lax.rem(rest, jnp.int32(nc)), lax.div(rest, jnp.int32(nc))
    cell = (((oc ^ c) * nz + (oz ^ z)) * (ny * nx) + ((oy * nx + ox) ^ line)) * cap + slot
    own = routed // members
    cells = [cell[b * own : (b + 1) * own] for b in range(members)]
    for b, block in enumerate(xor_order(cells, where[3])):
        lanes = lax.broadcasted_iota(jnp.int32, (own, spread.shape[1]), 1)
        spread[b * own : (b + 1) * own] = (block == lanes).astype(F32).astype(BF16)


def kept_pairs(member, routed, own):
    down = lax.broadcasted_iota(jnp.int32, (routed, routed), 0)
    across = lax.broadcasted_iota(jnp.int32, (routed, routed), 1)
    shift = own.bit_length() - 1
    first = ((down >> shift) ^ member) * own + (down & (own - 1))
    second = ((across >> shift) ^ member) * own + (across & (own - 1))
    return second <= first


def probabilities(queries, keys, kept):
    scores = jnp.where(kept, mm(queries, keys, NT) * HDIM ** (-0.5), neg_large)
    top = jnp.max(scores, 1, keepdims=True)
    probs = jnp.where(kept, jnp.exp(scores - top), 0.0)
    return probs, jnp.sum(probs, 1, keepdims=True)


def inverse_rms(values):
    return lax.rsqrt(jnp.mean(values * values, 1, keepdims=True) + epsilon)


def line_rows(blocks, start, out):
    half = out.shape[1] // 2
    size = out.shape[0] // blocks.shape[0]
    for q in range(blocks.shape[0]):
        for j in range(2):
            piece = blocks[q, start + j * size : start + (j + 1) * size]
            out[q * size : (q + 1) * size, j * half : (j + 1) * half] = piece


def own_order_rows(where, blocks, dims, out):
    ny, members, nx, rows = dims
    for k, block in enumerate(blocks):
        line = where[2] ^ k
        y, x = lax.div(line, jnp.int32(nx)), lax.rem(line, jnp.int32(nx))
        for g in range(members):
            to = pl.multiple_of(((y * members + g) * nx + x) * rows, rows)
            out[pl.ds(to, rows)] = block[g * rows : (g + 1) * rows, :]


def natural_rows(blocks, dims, first, count, out):
    ny, members, nx, rows = dims
    for y in range(ny):
        for g in range(members):
            for x in range(nx):
                to = ((y * members + g) * nx + x) * rows
                piece = blocks[y * nx + x, g * rows : (g + 1) * rows, first : first + count]
                out[to : to + rows] = piece


def attention_kernel(dims, members, where, spread, qkv_blocks, *refs):
    ny, nx, rows, cap = dims
    blocks, outs = refs[:members], refs[members:]
    picked_o, normed_o, w_o, first_o, wo_o, vecs_o = outs[:6]
    joined_o, att_o, exact_o, near_o, far_o, vec_s = outs[6:]
    heads = ny
    cols = 3 * heads * HDIM
    routed, width = picked_o.shape
    own = routed // members
    picked_low = mm(spread[...], jnp.concatenate([b[...] for b in blocks], 0)).astype(BF16)
    picked_o[...] = picked_low
    picked = picked_low.astype(F32)
    first_o[...] = picked_low[:own]
    natural_rows(qkv_blocks, (ny, members, nx, rows), 0, cols, w_o)
    natural_rows(qkv_blocks, (ny, members, nx, rows), cols, 128, vec_s)
    line_rows(qkv_blocks, members * rows, wo_o)
    vecs = mm(eye_rows(), vec_s[...], NT)
    vecs_o[...] = vecs
    normed = (picked * inverse_rms(picked) * vecs[0:1]).astype(BF16)
    normed_o[...] = normed
    joined = mm(normed, w_o[...]).astype(BF16)
    joined_o[...] = joined
    kept = kept_pairs(where[3], routed, own)
    parts = []
    for h in range(heads):
        queries, keys, values = (
            joined[:, (t * heads + h) * HDIM : (t * heads + h + 1) * HDIM] for t in range(3)
        )
        probs, total = probabilities(queries, keys, kept)
        parts.append(mm(probs.astype(BF16), values) / total)
    exact = jnp.concatenate(parts, 1)
    exact_o[...] = exact
    attended = exact.astype(BF16)
    att_o[...] = attended
    branch = mm(attended, wo_o[...]).astype(BF16)
    put_halves(branch, near_o, far_o)


def put_halves(values, near, far):
    depth, own = near.shape[:2]
    for k in range(depth):
        near[k] = values[k * own : (k + 1) * own]
        far[k] = values[(depth + k) * own : (depth + k + 1) * own]


def update_kernel(members, spread, picked, vecs, downs, *refs):
    blocks, outs = refs[:members], refs[members:]
    gate_o, cot_o, first_o, d_result_o, d_active_o, w_o = outs
    logit = jnp.sum(picked[...].astype(F32) * vecs[2:3, :], 1, keepdims=True)
    gate = 1.0 / (1.0 + jnp.exp(-logit))
    gate_o[...] = gate
    cot = mm(spread[...], jnp.concatenate([b[...] for b in blocks], 0)).astype(BF16)
    cot_o[...] = cot
    first_o[...] = cot[: first_o.shape[0]]
    d_result = (gate * cot.astype(F32)).astype(BF16)
    d_result_o[...] = d_result
    line_rows(downs, 0, w_o)
    d_active_o[...] = mm(d_result, w_o[...], NT)


def hidden_kernel(picked, vecs, *refs):
    *terms, hidden_o, normed_o = refs
    hidden = picked[...].astype(F32) + add_up(terms)
    hidden_o[...] = hidden
    normed_o[...] = (hidden * inverse_rms(hidden) * vecs[1:2, :]).astype(BF16)


def forward_kernel(dims, members, where, d_active, *refs):
    lines = dims[0] * dims[2]
    ups, refs = refs[:lines], refs[lines:]
    blocks, (active_o, d_upper_o, near_o, far_o, w_s) = refs[:members], refs[members:]
    own_order_rows(where, ups, dims, w_s)
    normed = jnp.concatenate([b[...] for b in blocks], 0)
    upper = mm(normed, w_s[...])
    below = 0.5 * (1.0 + lax.erf(upper * (0.5**0.5)))
    active_o[...] = (upper * below).astype(BF16)
    slope = below + upper * jnp.exp(-0.5 * upper * upper) * ((2.0 * math.pi) ** -0.5)
    d_upper = (d_active[...] * slope).astype(BF16)
    d_upper_o[...] = d_upper
    put_halves(mm(d_upper, w_s[...], NT).astype(BF16), near_o, far_o)


def ff_grads_kernel(dims, members, where, active, d_upper, d_result, *refs):
    ny, nx, rows, ff_rows = dims
    blocks, (keep, by_x, by_y, down, up) = refs[:members], refs[members:]
    normed = jnp.concatenate([b[...] for b in blocks], 0)
    down[...] = mm(active[...], d_result[...], TN).astype(BF16)
    up[...] = mm(normed, d_upper[...], TN).astype(BF16)
    wide = up.shape[1]
    part = members * rows // 2
    for k in range(ny * nx):
        line = where[2] ^ k
        y, x = lax.div(line, jnp.int32(nx)), lax.rem(line, jnp.int32(nx))
        first = by_x.at[k // 2] if k % 2 else keep.at[k // 2]
        second = by_y.at[k % 2] if k // 2 else keep.at[2 + k % 2]
        first[...] = down[pl.ds(pl.multiple_of(line * ff_rows, ff_rows), ff_rows)]
        for g in range(members):
            at = pl.multiple_of(((y * members + g) * nx + x) * rows, rows)
            half, row = divmod(g * rows, part)
            second[row : row + rows, half * wide : (half + 1) * wide] = up[pl.ds(at, rows)]


def add_halves_kernel(keep, got_x, got_y, mine, to_y, to_x):
    def both(index, got):
        return keep[index].astype(F32) + got.astype(F32)

    mine[0] = both(0, got_x[0])
    mine[1] = both(2, got_y[0])
    to_y[...] = both(1, got_x[1]).astype(BF16)
    to_x[...] = both(3, got_y[1]).astype(BF16)


def result_kernel(active, attended, w_down, w_out, cot, gate, spread, logit_o, near_o, far_o):
    combined = mm(active[...], w_down[...]) + mm(attended[...], w_out[...])
    logit = jnp.sum(cot[...].astype(F32) * combined, 1, keepdims=True)
    logit_o[...] = logit * gate[...] * (1.0 - gate[...])
    update = (gate[...] * combined).astype(BF16)
    put_halves(mm(spread[...], update, TN).astype(BF16), near_o, far_o)


def hidden_back_kernel(own, hidden_r, vecs, gate, cot, *refs):
    *terms, d_branch_o, d_hidden_o, gain_o = refs
    d_normed = add_up(terms)
    hidden = hidden_r[...]
    inv = inverse_rms(hidden)
    u = d_normed * vecs[1:2, :]
    d_hidden = inv * u - hidden * (inv * inv * inv * jnp.mean(u * hidden, 1, keepdims=True))
    d_hidden_o[...] = d_hidden
    gain_o[...] = (d_normed * hidden * inv).astype(BF16)
    d_update = gate[:own, :] * cot[...].astype(F32)
    d_branch_o[...] = (d_update + d_hidden).astype(BF16)


def attention_back_kernel(members, where, *refs):
    w_out, joined_r, exact_r, w, vecs, picked_r, logit, d_hidden, spread = refs[:9]
    blocks = refs[9 : 9 + members]
    near_o, far_o, d_joined_o, gain_o = refs[9 + members :]
    routed, width = picked_r.shape
    own = routed // members
    heads = joined_r.shape[1] // (3 * HDIM)
    d_branch = jnp.concatenate([b[...] for b in blocks], 0)
    d_attended = mm(d_branch, w_out[...], NT).astype(BF16)
    joined = joined_r[...]
    exact = exact_r[...]
    kept = kept_pairs(where[3], routed, own)
    grads = [[], [], []]
    for h in range(heads):
        queries, keys, values = (
            joined[:, (t * heads + h) * HDIM : (t * heads + h + 1) * HDIM] for t in range(3)
        )
        probs, total = probabilities(queries, keys, kept)
        d_att = d_attended[:, h * HDIM : (h + 1) * HDIM]
        d_wide = d_att.astype(F32)
        delta = jnp.sum(d_wide * exact[:, h * HDIM : (h + 1) * HDIM], 1, keepdims=True)
        d_scores = (probs / total * (mm(d_att, values, NT) - delta)).astype(BF16)
        grads[0].append(mm(d_scores, keys) * HDIM ** (-0.5))
        grads[1].append(mm(d_scores, queries, TN) * HDIM ** (-0.5))
        grads[2].append(mm(probs.astype(BF16), (d_wide / total).astype(BF16), TN))
    d_joined = jnp.concatenate(grads[0] + grads[1] + grads[2], 1).astype(BF16)
    d_joined_o[...] = d_joined
    d_normed = mm(d_joined, w[...], NT)
    picked = picked_r[...].astype(F32)
    inv = inverse_rms(picked)
    gain_o[...] = (d_normed * picked * inv).astype(BF16)
    v = d_normed * vecs[0:1, :]
    d_picked = inv * v - picked * (inv * inv * inv * jnp.mean(v * picked, 1, keepdims=True))
    d_picked = d_picked + logit[...] * vecs[2:3, :]
    first = d_picked[:own] + d_hidden[...]
    d_picked = jnp.concatenate([first, d_picked[own:]], 0).astype(BF16)
    put_halves(mm(spread[...], d_picked, TN).astype(BF16), near_o, far_o)


def grads_kernel(dims, members, where, normed, d_joined, attended, gain_a, gain_m, *refs):
    ny, nx, rows = dims
    lines = ny * nx
    picked, logit, refs = refs[0], refs[1], refs[2:]
    blocks, sums, (main, vec_s, out) = refs[:members], refs[members : members + lines], refs[-3:]
    cols = d_joined.shape[1]
    routed, width = normed.shape
    own = gain_m.shape[0]
    main[...] = mm(normed[...], d_joined[...], TN).astype(BF16)
    lanes = lax.broadcasted_iota(jnp.int32, (routed, 128), 1)

    def lane(k, count):
        return (lanes[:count] == k).astype(F32)

    vec = mm(gain_a[...], lane(0, routed).astype(BF16), TN)
    vec = vec + mm(gain_m[...], lane(1, own).astype(BF16), TN)
    high = logit[...].astype(BF16)
    low = (logit[...] - high.astype(F32)).astype(BF16)
    vec = vec + mm(picked[...], (lane(2, routed) * high.astype(F32)).astype(BF16), TN)
    vec = vec + mm(picked[...], (lane(2, routed) * low.astype(F32)).astype(BF16), TN)
    vec_s[...] = vec.astype(BF16)
    out[...] = mm(attended[...], jnp.concatenate([b[...] for b in blocks], 0), TN).astype(BF16)
    for k in range(lines):
        line = where[2] ^ k
        y, x = lax.div(line, jnp.int32(nx)), lax.rem(line, jnp.int32(nx))
        for g in range(members):
            at = pl.multiple_of(((y * members + g) * nx + x) * rows, rows)
            sums[k][g * rows : (g + 1) * rows, :cols] = main[pl.ds(at, rows)]
            sums[k][g * rows : (g + 1) * rows, cols:] = vec_s[pl.ds(at, rows)]
        half, end = width // 2, members * rows
        at = pl.multiple_of(line * rows, rows)
        for j in range(2):
            piece = out[pl.ds(at, rows), j * half : (j + 1) * half]
            sums[k][end + j * rows : end + (j + 1) * rows, :] = piece


def join_slots_kernel(cap, lines, *refs):
    terms, outs = refs[:-lines], refs[-lines:]
    total = add_up(terms).astype(BF16)
    for j in range(2):
        for k in range(lines):
            at = (j * lines + k) * cap
            outs[k][j * cap : (j + 1) * cap] = total[at : at + cap]


def place_kernel(cap, lines, where, pick, tokens, cot, *refs):
    blocks, (out_o, grad_o, got) = refs[:lines], refs[lines:]
    for k, block in enumerate(blocks):
        got[where[2] ^ k] = block[...]
    for s in range(tokens.shape[0]):
        hot = pick[s]
        out_o[s] = (tokens[s].astype(F32) + mm(hot, got[s, :cap], TN)).astype(BF16)
        grad_o[s] = (cot[s].astype(F32) + mm(hot, got[s, cap:], TN)).astype(BF16)


def line_sums_kernel(dims, where, mine, got_down, got_up, *refs):
    members, rows, ff_rows = dims
    *parts, near_o, far_o, out_o, down_o, send = refs
    cols = parts[0].shape[1]
    wide = mine.shape[2] // 2
    up = mine[1] + got_up[...].astype(F32)
    main = parts[0][...].astype(F32)
    for part in parts[1:]:
        main = main + part[...].astype(F32)
    for g in range(members):
        send[g, :, :cols] = main[g * rows : (g + 1) * rows].astype(BF16)
        half, row = divmod(g * rows, members * rows // 2)
        piece = up[row : row + rows, half * wide : (half + 1) * wide]
        send[g, :, cols:] = piece.astype(BF16)
    depth = near_o.shape[0]
    for k in range(depth):
        near_o[k] = send[where[3] ^ k]
        far_o[k] = send[where[3] ^ (depth + k)]
    end = members * rows
    out_o[...] = jnp.concatenate([main[end : end + rows], main[end + rows :]], 1)
    down_o[...] = mine[0] + got_down[...].astype(F32)


def pair_kernel(near, far, *outs):
    rows = near.shape[1]
    for k, out in enumerate(outs):
        out[:rows] = near[k]
        out[rows:] = far[k]


def unpack_kernel(dims, where, *refs):
    ny, members, nx, ff_rows = dims
    depth = members // 2
    pairs, (qkv_o, up_o, *vec_o, got) = refs[:depth], refs[depth:]
    rows = got.shape[1]
    for k, pair in enumerate(pairs):
        got[where[3] ^ k] = pair[:rows]
        got[where[3] ^ (depth + k)] = pair[rows:]
    cols = 3 * ny * HDIM
    for t in range(3):
        for y in range(ny):
            from_ = (t * ny + y) * HDIM
            row = [got[g, :, from_ : from_ + HDIM] for g in range(members)]
            at = (t * HEADS + y * members) * HDIM
            qkv_o[:, at : at + members * HDIM] = jnp.concatenate(row, 1).astype(F32)
    for y in range(ny):
        for g in range(members):
            for x in range(nx):
                at = ((y * members + g) * nx + x) * ff_rows
                from_ = cols + 128 + (y * nx + x) * ff_rows
                up_o[:, at : at + ff_rows] = got[g, :, from_ : from_ + ff_rows].astype(F32)
    vec = got[0, :, cols : cols + 128].astype(F32)
    for g in range(1, members):
        vec = vec + got[g, :, cols : cols + 128].astype(F32)
    high = vec.astype(BF16)
    low = (vec - high.astype(F32)).astype(BF16)
    vec = mm(eye_rows(), high, NT) + mm(eye_rows(), low, NT)
    for k, out in enumerate(vec_o):
        out[...] = vec[k : k + 1]


def grouped(
    tokens, chosen, w_qkv, w_out, w_up, w_down, gain_attn, gain_mlp, router, cotangent
):
    ny, nc, nz, nx = (lax.axis_size(a) for a in ("y", "c", "z", "x"))
    y, c, z, x = (lax.axis_index(a) for a in ("y", "c", "z", "x"))
    seq_count, seg_len, width = tokens.shape
    cap = seg_len // 4
    routed = chosen.shape[1]
    members, lines = nc * nz, ny * nx
    member, line = c * nz + z, y * nx + x
    shard = ((y * nc + c) * nz + z) * nx + x
    rows, ff_rows = w_qkv.shape[0], w_down.shape[0]
    heads = HEADS // members
    own = routed // members
    cols, wide = 3 * heads * HDIM, lines * ff_rows
    where = jnp.stack([c, z, line, member, shard]).astype(jnp.int32)
    chosen_t = chosen.T
    block = (own, width)
    slot_block = (2 * cap, width)
    halves = [((nz, own, width), BF16)] * 2
    slot_halves = [((nz, lines * cap, width), BF16)] * 2

    pick, *picked_rows = local_call(
        partial(pick_kernel, cap),
        [Far(((seq_count, cap, seg_len), BF16))] + [(slot_block, BF16)] * lines,
        (where, chosen_t, tokens, cotangent),
        scratch=[pltpu.VMEM((seq_count, 2 * cap, width), BF16)],
        scalars=1,
    )
    line_slots = picked_rows[:1] + send_lines(picked_rows[1:])
    (hot,) = local_call(
        partial(spread_kernel, (ny, nc, nz, nx, seg_len, cap)),
        [Far(((routed, members * lines * cap), BF16))],
        (where, chosen, chosen_t),
        scalars=1,
    )
    spread = Far(hot)
    (line_slots,) = local_call(
        partial(stack_kernel, cap), [((2 * lines * cap, width), BF16)], line_slots, after=(hot,)
    )
    slots = gather_group([line_slots])
    half = lines * cap
    picked_slots, cot_slots = [Far(b, 0, half) for b in slots], [Far(b, half, half) for b in slots]

    vecs = [v.reshape(1, rows) for v in (gain_attn, gain_mlp, router)]
    (columns,) = local_call(
        partial(columns_kernel, (ny, members, nx, ff_rows)),
        [((members, rows, cols + 128 + wide), BF16)],
        tuple(Far(v) for v in (w_qkv, w_up, *vecs)),
        scratch=[pltpu.VMEM((8, rows), F32)],
    )
    got_cols = lax.all_to_all(columns, ("c", "z"), 0, 0, tiled=True)
    half = width // 2
    base = members * rows + 2 * rows
    first, up = local_call(
        relay_kernel,
        [Far(((lines, base + 2 * ff_rows, half), BF16)), ((members * rows, half), BF16)],
        (got_cols, w_out, w_down),
        after=(line_slots,),
    )
    first = lax.all_to_all(first, ("y", "x"), 0, 0, tiled=True)
    got_down = Far(first, base, 2 * ff_rows, 1)
    got_up = gather_lines(up)

    picked, normed, full_qkv, picked_own, full_out, full_vecs, joined, attended, exact, near, far = (
        local_call(
            partial(attention_kernel, (ny, nx, rows, cap), members),
            [
                ((routed, width), BF16),
                ((routed, width), BF16),
                ((width, cols), BF16),
                (block, BF16),
                ((heads * HDIM, width), BF16),
                ((8, width), F32),
                ((routed, cols), BF16),
                ((routed, heads * HDIM), BF16),
                ((routed, heads * HDIM), F32),
            ]
            + halves,
            (where, spread, Far(first, 0, base, 1), *picked_slots),
            flops=1.2e9,
            scratch=[pltpu.VMEM((width, 128), BF16)],
            scalars=1,
        )
    )
    terms = scatter_group(near, far)
    gate, cot, cot_own, d_result, d_active, full_down = local_call(
        partial(update_kernel, members),
        [
            ((routed, 1), F32),
            ((routed, width), BF16),
            (block, BF16),
            ((routed, width), BF16),
            ((routed, wide), F32),
            ((wide, width), BF16),
        ],
        (spread, picked, full_vecs, got_down, *cot_slots),
        flops=8e8,
    )
    hidden, normed_own = local_call(
        hidden_kernel,
        [(block, F32), (block, BF16)],
        (picked_own, full_vecs, *terms),
        after=(d_active,),
    )
    normed_mlp = gather_group([normed_own])

    active, d_upper, near, far = local_call(
        partial(forward_kernel, (ny, members, nx, rows), members),
        [((routed, wide), BF16)] * 2 + halves,
        (where, d_active, *got_up, *normed_mlp),
        flops=6e8,
        scratch=[pltpu.VMEM((width, wide), BF16)],
        scalars=1,
    )
    terms = scatter_group(near, far)
    half = (ff_rows, width)
    ff_keep, ff_x, ff_y = local_call(
        partial(ff_grads_kernel, (ny, nx, rows, ff_rows), members),
        [((4, *half), BF16), ((2, *half), BF16), ((2, *half), BF16)],
        (where, active, d_upper, d_result, *normed_mlp),
        flops=6e8,
        scratch=[pltpu.VMEM((wide, width), BF16), pltpu.VMEM((width, wide), BF16)],
        scalars=1,
    )
    logit, up_near, up_far = local_call(
        result_kernel,
        [((routed, 1), F32)] + slot_halves,
        (active, attended, full_down, full_out, cot, gate, spread),
        flops=8e8,
    )
    d_branch_own, d_hidden, gain_m = local_call(
        partial(hidden_back_kernel, own),
        [(block, BF16), (block, F32), (block, BF16)],
        (hidden, full_vecs, gate, cot_own, *terms),
        after=(ff_x, logit),
    )
    d_branch = gather_group([d_branch_own])
    up_far = send_c(up_far)
    ff_mine, ff_y, ff_x = local_call(
        add_halves_kernel,
        [((2, *half), F32), (half, BF16), (half, BF16)],
        (ff_keep, lax.ppermute(ff_x, "x", flips(nx)[1]), lax.ppermute(ff_y, "y", flips(ny)[1])),
    )
    ff_got = (lax.ppermute(ff_y, "y", flips(ny)[1]), lax.ppermute(ff_x, "x", flips(nx)[1]))

    near, far, d_joined, gain_a = local_call(
        partial(attention_back_kernel, members),
        slot_halves + [((routed, cols), BF16), ((routed, width), BF16)],
        (where, full_out, joined, exact, full_qkv, full_vecs, picked)
        + (logit, d_hidden, spread, *d_branch),
        flops=1.2e9,
        scalars=1,
    )
    far = send_c(far)
    parts = local_call(
        partial(grads_kernel, (ny, nx, rows), members),
        [((members * rows + 2 * rows, cols + 128), BF16)] * lines,
        (where, normed, d_joined, attended, gain_a, gain_m, picked, logit, *d_branch),
        flops=5e8,
        scratch=[
            pltpu.VMEM((width, cols), BF16),
            pltpu.VMEM((width, 128), BF16),
            pltpu.VMEM((heads * HDIM, width), BF16),
        ],
        scalars=1,
    )
    parts = parts[:1] + send_lines(parts[1:])
    both_slots = (2 * lines * cap, width)
    mine, *low = local_call(
        slot_sum_kernel,
        [(both_slots, F32)] + [(both_slots, BF16)] * (nz - 1),
        (up_near, up_far, near, far),
    )
    back_rows = local_call(
        partial(join_slots_kernel, cap, lines),
        [(slot_block, BF16)] * lines,
        [mine] + send_z(low),
    )
    back_rows = back_rows[:1] + send_lines(back_rows[1:])
    row_width = cols + 128 + wide
    near, far, grad_out, grad_down = local_call(
        partial(line_sums_kernel, (members, rows, ff_rows)),
        [((nz, rows, row_width), BF16)] * 2 + [((rows, width), F32), ((ff_rows, width), F32)],
        (where, ff_mine, *ff_got, *parts),
        scratch=[pltpu.VMEM((members, rows, row_width), BF16)],
        scalars=1,
        after=back_rows[:1],
    )
    pairs = local_call(pair_kernel, [((2 * rows, row_width), BF16)] * nz, (near, send_c(far)))
    pairs = pairs[:1] + send_z(pairs[1:])
    output, grad_tokens = local_call(
        partial(place_kernel, cap, lines),
        [(tokens.shape, BF16), (tokens.shape, BF16)],
        (where, Far(pick), tokens, cotangent, *back_rows),
        scratch=[pltpu.VMEM((seq_count, 2 * cap, width), BF16)],
        scalars=1,
    )
    grad_qkv, grad_up, *grad_vecs = local_call(
        partial(unpack_kernel, (ny, members, nx, ff_rows)),
        [(w_qkv.shape, F32), (w_up.shape, F32)] + [((1, rows), F32)] * 3,
        (where, *pairs),
        scratch=[pltpu.VMEM((members, rows, row_width), BF16)],
        scalars=1,
    )
    return (
        output,
        grad_tokens,
        grad_qkv,
        grad_out,
        grad_up,
        grad_down,
        *(v.reshape(rows) for v in grad_vecs),
    )


def fits(mesh):
    head_count, block_count = mesh.devices.shape
    members = (head_count // 2) * (block_count // 2)
    power = members & (members - 1) == 0
    return power and head_count == 4 and HEADS == 2 * members


def solution(mesh):
    if fits(mesh):
        head_count, block_count = mesh.devices.shape
        devices = mesh.devices.reshape(2, head_count // 2, block_count // 2, 2)
        mesh = jax.sharding.Mesh(devices, ("y", "c", "z", "x"))
        body, all_axes = grouped, ("y", "c", "z", "x")
    else:
        body, all_axes = shards, ("head", "blk")
    seqs, mats, vecs = P(None, all_axes, None), P(all_axes, None), P(all_axes)
    in_specs = (seqs, P(), mats, mats, mats, mats, vecs, vecs, vecs, seqs)
    out_specs = (seqs, seqs, mats, mats, mats, mats, vecs, vecs, vecs)
    return jax.shard_map(body, mesh=mesh, in_specs=in_specs, out_specs=out_specs, check_vma=False)
```

```python
import math
from functools import partial

import jax
import jax.numpy as jnp
from jax import lax
from jax.experimental import pallas as pl
from jax.experimental.pallas import tpu as pltpu
from jax.sharding import PartitionSpec as P

HEADS = 16
HDIM = 64


epsilon = 1e-06
neg_large = -1e30


def rms_norm(values, gain_vec):
    inverse_rms = lax.rsqrt(jnp.mean(values * values, axis=-1, keepdims=True) + epsilon)
    return values * inverse_rms * gain_vec


def exact_gelu(values):
    return jax.nn.gelu(values, approximate=False)


def take_rows(seq_rows, row_index):
    return seq_rows[row_index]


def add_rows(seq_rows, row_index, additions):
    return seq_rows.at[row_index].add(additions)


def shards(tokens, chosen, w_qkv, w_out, w_up, w_down, gain_attn, gain_mlp, router, cotangent):
    head_count = lax.axis_size("head")
    block_count = lax.axis_size("blk")
    shard_count = head_count * block_count
    seq_count, seg_len, model_width = tokens.shape
    cap_len = seg_len // 4
    routed_count = chosen.shape[1]
    seq_len = seg_len * shard_count
    local_heads = HEADS // head_count
    slot_rows = head_count * cap_len
    scale_factor = HDIM ** (-0.5)
    head_index = lax.axis_index("head")
    block_index = lax.axis_index("blk")
    my_shard = head_index * block_count + block_index
    bounds = jnp.arange(shard_count + 1, dtype=jnp.int32) * seg_len
    before = jax.vmap(lambda chosen_row: jnp.searchsorted(chosen_row, bounds, side="left"))(chosen)
    first_index = before[:, :-1]
    shard_load = before[:, 1:] - first_index
    slot_iota = jnp.arange(cap_len, dtype=jnp.int32)
    live_table = slot_iota[None, None, :] < shard_load[:, :, None]
    lookup = jnp.minimum(first_index[:, :, None] + slot_iota[None, None, :], routed_count - 1)
    place_table = jnp.take_along_axis(
        chosen, lookup.reshape(seq_count, shard_count * cap_len), axis=1
    )
    place_table = jnp.where(
        live_table, place_table.reshape(seq_count, shard_count, cap_len), seq_len
    )
    my_positions = lax.dynamic_index_in_dim(place_table, my_shard, 1, False)
    my_live = lax.dynamic_index_in_dim(live_table, my_shard, 1, False)
    local_rows = jnp.clip(my_positions - my_shard * seg_len, 0, seg_len - 1)
    cycle_positions = place_table.reshape(seq_count, head_count, block_count, cap_len).transpose(
        0, 2, 1, 3
    )
    cycle_positions = cycle_positions.reshape(seq_count, block_count * slot_rows)
    query_positions = lax.dynamic_slice_in_dim(
        cycle_positions, block_index * slot_rows, slot_rows, 1
    )
    live_weight = my_live.astype(jnp.float32)[:, :, None]
    gathered = (
        lax.all_gather(w_qkv, ("head", "blk"), axis=0, tiled=True),
        lax.all_gather(w_out, ("head", "blk"), axis=0, tiled=True),
        lax.all_gather(w_up, ("head", "blk"), axis=0, tiled=True),
        lax.all_gather(w_down, ("head", "blk"), axis=0, tiled=True),
        lax.all_gather(gain_attn, ("head", "blk"), axis=0, tiled=True),
        lax.all_gather(gain_mlp, ("head", "blk"), axis=0, tiled=True),
        lax.all_gather(router, ("head", "blk"), axis=0, tiled=True),
    )
    full_qkv, full_out, full_up, full_down, full_gain_attn, full_gain_mlp, full_router = gathered
    picked = jax.vmap(take_rows)(tokens, local_rows)
    picked = jnp.where(my_live[:, :, None], picked, jnp.zeros_like(picked))
    picked_exact = picked.astype(jnp.float32)
    router_gate = jax.nn.sigmoid(
        jnp.einsum("scd,d->sc", picked, full_router, preferred_element_type=jnp.float32)
    )
    normed_exact, norm_attn_back = jax.vjp(
        rms_norm, picked_exact, full_gain_attn.astype(jnp.float32)
    )
    normed = normed_exact.astype(jnp.bfloat16)
    joined = jnp.einsum("scd,de->sce", normed, full_qkv, preferred_element_type=jnp.float32).astype(
        jnp.bfloat16
    )
    to_heads = lax.all_to_all(
        joined.reshape(seq_count, cap_len, 3, model_width),
        "head",
        split_axis=3,
        concat_axis=1,
        tiled=True,
    )
    queries_tok = to_heads[:, :, 0]
    queries_heads = queries_tok.reshape(seq_count, slot_rows, local_heads, HDIM)
    key_values = to_heads[:, :, 1:3]
    my_keys = key_values[:, :, 0].reshape(seq_count, slot_rows, local_heads, HDIM)
    my_values = key_values[:, :, 1].reshape(seq_count, slot_rows, local_heads, HDIM)
    stat_shape = (seq_count, local_heads, slot_rows)
    piece = lax.all_gather(key_values, "blk", axis=1, tiled=True)
    run_max = jnp.full(stat_shape, neg_large, jnp.float32)
    piece_rows = piece.shape[1]
    key_pos = cycle_positions
    keys_piece = piece[:, :, 0].reshape(seq_count, piece_rows, local_heads, HDIM)
    values_piece = piece[:, :, 1].reshape(seq_count, piece_rows, local_heads, HDIM)
    scores = (
        jnp.einsum("sqhd,skhd->shqk", queries_heads, keys_piece, preferred_element_type=jnp.float32)
        * scale_factor
    )
    allowed = key_pos[:, None, None, :] <= query_positions[:, None, :, None]
    scores = jnp.where(allowed, scores, neg_large)
    new_max = jnp.maximum(run_max, jnp.max(scores, axis=3))
    prob_block = jnp.where(allowed, jnp.exp(scores - new_max[..., None]), 0.0)
    new_total = jnp.sum(prob_block, axis=3)
    added = jnp.einsum(
        "shqk,skhd->sqhd",
        prob_block.astype(jnp.bfloat16),
        values_piece,
        preferred_element_type=jnp.float32,
    )
    attended_exact = added / new_total.transpose(0, 2, 1)[..., None]
    log_sum = new_max + jnp.log(new_total)
    attended_tok = attended_exact.astype(jnp.bfloat16).reshape(
        seq_count, slot_rows, local_heads * HDIM
    )
    attended = lax.all_to_all(attended_tok, "head", split_axis=1, concat_axis=2, tiled=True)
    branch = jnp.einsum("sce,ed->scd", attended, full_out, preferred_element_type=jnp.float32)
    hidden_state = picked_exact + branch
    normed_mlp_exact, norm_mlp_back = jax.vjp(
        rms_norm, hidden_state, full_gain_mlp.astype(jnp.float32)
    )
    normed_mlp = normed_mlp_exact.astype(jnp.bfloat16)
    upper = jnp.einsum("scd,di->sci", normed_mlp, full_up, preferred_element_type=jnp.float32)
    active_exact, gelu_back = jax.vjp(exact_gelu, upper)
    active = active_exact.astype(jnp.bfloat16)
    result = jnp.einsum("sci,id->scd", active, full_down, preferred_element_type=jnp.float32)
    combined = branch + result
    update = router_gate[:, :, None] * combined * live_weight
    output = jax.vmap(add_rows)(tokens.astype(jnp.float32), local_rows, update).astype(jnp.bfloat16)
    regathered = (
        lax.all_gather(w_qkv, ("head", "blk"), axis=0, tiled=True),
        lax.all_gather(w_out, ("head", "blk"), axis=0, tiled=True),
        lax.all_gather(w_up, ("head", "blk"), axis=0, tiled=True),
        lax.all_gather(w_down, ("head", "blk"), axis=0, tiled=True),
        lax.all_gather(gain_attn, ("head", "blk"), axis=0, tiled=True),
        lax.all_gather(gain_mlp, ("head", "blk"), axis=0, tiled=True),
        lax.all_gather(router, ("head", "blk"), axis=0, tiled=True),
    )
    back_qkv, back_out, back_up, back_down, back_gain_attn, back_gain_mlp, back_router = regathered
    picked_cot = jax.vmap(take_rows)(cotangent, local_rows).astype(jnp.float32) * live_weight
    d_update = router_gate[:, :, None] * picked_cot
    d_logit = jnp.sum(picked_cot * combined, axis=2) * router_gate * (1.0 - router_gate)
    grad_router = jnp.einsum("sc,scd->d", d_logit, picked_exact, precision=lax.Precision.HIGHEST)
    d_result = d_update.astype(jnp.bfloat16)
    d_active = jnp.einsum("scd,id->sci", d_result, back_down, preferred_element_type=jnp.float32)
    d_upper = gelu_back(d_active)[0].astype(jnp.bfloat16)
    d_normed_mlp = jnp.einsum("sci,di->scd", d_upper, back_up, preferred_element_type=jnp.float32)
    d_hidden, grad_gain_mlp = norm_mlp_back(d_normed_mlp)
    d_branch = (d_update + d_hidden).astype(jnp.bfloat16)
    d_attended = jnp.einsum(
        "scd,ed->sce", d_branch, back_out, preferred_element_type=jnp.float32
    ).astype(jnp.bfloat16)
    d_att_tok = lax.all_to_all(d_attended, "head", split_axis=2, concat_axis=1, tiled=True)
    d_att_heads = d_att_tok.reshape(seq_count, slot_rows, local_heads, HDIM)
    delta_tok = jnp.sum(d_att_heads.astype(jnp.float32) * attended_exact, axis=3)
    delta_sq = delta_tok.transpose(0, 2, 1)
    piece = lax.all_gather(key_values, "blk", axis=1, tiled=True)
    piece_rows = piece.shape[1]
    key_pos = cycle_positions
    keys_piece = piece[:, :, 0].reshape(seq_count, piece_rows, local_heads, HDIM)
    values_piece = piece[:, :, 1].reshape(seq_count, piece_rows, local_heads, HDIM)
    scores = (
        jnp.einsum("sqhd,skhd->shqk", queries_heads, keys_piece, preferred_element_type=jnp.float32)
        * scale_factor
    )
    allowed = key_pos[:, None, None, :] <= query_positions[:, None, :, None]
    prob_block = jnp.where(allowed, jnp.exp(scores - log_sum[..., None]), 0.0)
    d_prob = jnp.einsum(
        "sqhd,skhd->shqk", d_att_heads, values_piece, preferred_element_type=jnp.float32
    )
    d_scores = (prob_block * (d_prob - delta_sq[..., None])).astype(jnp.bfloat16)
    d_queries = (
        jnp.einsum("shqk,skhd->sqhd", d_scores, keys_piece, preferred_element_type=jnp.float32)
        * scale_factor
    )
    lse_tok = log_sum.transpose(0, 2, 1)
    lse_high = lse_tok.astype(jnp.bfloat16)
    lse_low = (lse_tok - lse_high.astype(jnp.float32)).astype(jnp.bfloat16)
    delta_high = delta_tok.astype(jnp.bfloat16)
    delta_low = (delta_tok - delta_high.astype(jnp.float32)).astype(jnp.bfloat16)
    query_piece = lax.all_gather(queries_tok, "blk", axis=1, tiled=True)
    dout_piece = lax.all_gather(d_att_tok, "blk", axis=1, tiled=True)
    piece_lse_high = lax.all_gather(lse_high, "blk", axis=1, tiled=True)
    piece_lse_low = lax.all_gather(lse_low, "blk", axis=1, tiled=True)
    piece_delta_high = lax.all_gather(delta_high, "blk", axis=1, tiled=True)
    piece_delta_low = lax.all_gather(delta_low, "blk", axis=1, tiled=True)
    piece_rows = query_piece.shape[1]
    query_heads = query_piece.reshape(seq_count, piece_rows, local_heads, HDIM)
    dout_heads = dout_piece.reshape(seq_count, piece_rows, local_heads, HDIM)
    piece_lse = (piece_lse_high.astype(jnp.float32) + piece_lse_low.astype(jnp.float32)).transpose(
        0, 2, 1
    )
    piece_delta = (
        piece_delta_high.astype(jnp.float32) + piece_delta_low.astype(jnp.float32)
    ).transpose(0, 2, 1)
    scores = (
        jnp.einsum("sqhd,skhd->shqk", query_heads, my_keys, preferred_element_type=jnp.float32)
        * scale_factor
    )
    allowed = query_positions[:, None, None, :] <= cycle_positions[:, None, :, None]
    prob_block = jnp.where(allowed, jnp.exp(scores - piece_lse[..., None]), 0.0)
    grad_values = jnp.einsum(
        "shqk,sqhd->skhd",
        prob_block.astype(jnp.bfloat16),
        dout_heads,
        preferred_element_type=jnp.float32,
    )
    d_prob = jnp.einsum(
        "sqhd,skhd->shqk", dout_heads, my_values, preferred_element_type=jnp.float32
    )
    d_scores = (prob_block * (d_prob - piece_delta[..., None])).astype(jnp.bfloat16)
    grad_keys = (
        jnp.einsum("shqk,sqhd->skhd", d_scores, query_heads, preferred_element_type=jnp.float32)
        * scale_factor
    )
    d_heads = jnp.stack(
        [
            d_queries.astype(jnp.bfloat16),
            grad_keys.astype(jnp.bfloat16),
            grad_values.astype(jnp.bfloat16),
        ],
        axis=2,
    )
    d_heads = d_heads.reshape(seq_count, slot_rows, 3, local_heads * HDIM)
    d_joined = lax.all_to_all(d_heads, "head", split_axis=1, concat_axis=3, tiled=True).reshape(
        seq_count, cap_len, 3 * model_width
    )
    d_normed = jnp.einsum("sce,de->scd", d_joined, back_qkv, preferred_element_type=jnp.float32)
    d_picked_norm, grad_gain_attn = norm_attn_back(d_normed)
    d_picked = (
        d_hidden
        + d_picked_norm
        + d_logit[:, :, None] * back_router.astype(jnp.float32)[None, None, :]
    )
    grad_tokens = jax.vmap(add_rows)(
        cotangent.astype(jnp.float32), local_rows, d_picked * live_weight
    ).astype(jnp.bfloat16)
    grad_qkv = jnp.einsum("scd,sce->de", normed, d_joined, preferred_element_type=jnp.float32)
    grad_out = jnp.einsum("sce,scd->ed", attended, d_branch, preferred_element_type=jnp.float32)
    grad_up = jnp.einsum("scd,sci->di", normed_mlp, d_upper, preferred_element_type=jnp.float32)
    grad_down = jnp.einsum("sci,scd->id", active, d_result, preferred_element_type=jnp.float32)
    owned = (
        lax.psum_scatter(grad_qkv, ("head", "blk"), scatter_dimension=0, tiled=True),
        lax.psum_scatter(grad_out, ("head", "blk"), scatter_dimension=0, tiled=True),
        lax.psum_scatter(grad_up, ("head", "blk"), scatter_dimension=0, tiled=True),
        lax.psum_scatter(grad_down, ("head", "blk"), scatter_dimension=0, tiled=True),
        lax.psum_scatter(grad_gain_attn, ("head", "blk"), scatter_dimension=0, tiled=True),
        lax.psum_scatter(grad_gain_mlp, ("head", "blk"), scatter_dimension=0, tiled=True),
        lax.psum_scatter(grad_router, ("head", "blk"), scatter_dimension=0, tiled=True),
    )
    return (
        output,
        grad_tokens,
        owned[0],
        owned[1],
        owned[2],
        owned[3],
        owned[4],
        owned[5],
        owned[6],
    )


F32, BF16 = jnp.float32, jnp.bfloat16
NN = (((1,), (0,)), ((), ()))
NT = (((1,), (1,)), ((), ()))
TN = (((0,), (0,)), ((), ()))


def mm(left, right, dims=NN):
    return lax.dot_general(left, right, dims, preferred_element_type=F32)


class Far:
    def __init__(self, item, start=0, count=None, dim=0):
        self.item, self.start, self.count, self.dim = item, start, count, dim

    def shape(self):
        shape = list(self.item.shape)
        if self.count is not None:
            shape[self.dim] = self.count
        return tuple(shape)

    def source(self, ref):
        if self.count is None:
            return ref
        return ref.at[(slice(None),) * self.dim + (pl.ds(self.start, self.count),)]


class Loaded:
    def __init__(self, copy, ref):
        self.copy, self.ref, self.shape, self.waited = copy, ref, ref.shape, False

    def __getitem__(self, index):
        self.wait()
        return self.ref[index]

    def wait(self):
        if not self.waited:
            self.copy.wait()
        self.waited = True


class Stored:
    def __init__(self, copy, ref):
        self.copy, self.ref, self.shape, self.started = copy, ref, ref.shape, False

    def __getitem__(self, index):
        return self.ref[index]

    def __setitem__(self, index, value):
        self.ref[index] = value
        if index is Ellipsis:
            self.start()

    def start(self):
        if not self.started:
            self.copy.start()
        self.started = True


def local_call(body, outs, args, flops=0, scratch=(), scalars=0, after=()):
    far_in = [a if isinstance(a, Far) else None for a in args]
    far_out = [isinstance(o, Far) for o in outs]
    outs = [o.item if f else o for o, f in zip(outs, far_out)]
    args = [pltpu.with_memory_space_constraint(f.item, pltpu.HBM) if f else a for a, f in zip(args, far_in)]
    shapes = [pltpu.HBM(s, d) if f else jax.ShapeDtypeStruct(s, d) for (s, d), f in zip(outs, far_out)]
    spaces = [pltpu.SMEM] * scalars
    spaces += [pltpu.HBM if f else pltpu.VMEM for f in far_in[scalars:]]
    spaces += [pl.ANY] * len(after)
    stages = []
    for f in far_in:
        if f:
            stages.append(pltpu.VMEM(f.shape(), f.item.dtype))
    stages += [pltpu.VMEM(s, d) for (s, d), f in zip(outs, far_out) if f]
    n_in, n_out, n_far = len(args), len(outs), len(stages)
    first_out = n_in + len(after)
    if n_far:
        stages.append(pltpu.SemaphoreType.DMA((n_far,)))

    def run(*refs):
        ins, results = list(refs[:n_in]), list(refs[first_out : first_out + n_out])
        rest = refs[first_out + n_out :]
        own, stage = rest[: len(scratch)], rest[len(scratch) :]
        at, loads, stores = 0, [], []
        for i, f in enumerate(far_in):
            if f:
                copy = pltpu.make_async_copy(f.source(ins[i]), stage[at], stage[-1].at[at])
                copy.start()
                ins[i] = Loaded(copy, stage[at])
                loads.append(ins[i])
                at += 1
        for i, f in enumerate(far_out):
            if f:
                copy = pltpu.make_async_copy(stage[at], results[i], stage[-1].at[at])
                results[i] = Stored(copy, stage[at])
                stores.append(results[i])
                at += 1
        body(*ins, *results, *own)
        for load in loads:
            load.wait()
        for store in stores:
            store.start()
        for store in stores:
            store.copy.wait()

    return list(
        pl.pallas_call(
            run,
            out_shape=shapes,
            in_specs=[pl.BlockSpec(memory_space=s) for s in spaces],
            out_specs=[
                pl.BlockSpec(memory_space=pltpu.HBM if f else pltpu.VMEM) for f in far_out
            ],
            scratch_shapes=list(scratch) + stages,
            compiler_params=pltpu.CompilerParams(vmem_limit_bytes=32 * 2**20),
            cost_estimate=pl.CostEstimate(flops=int(flops), bytes_accessed=0, transcendentals=0),
        )(*args, *after)
    )


def flips(count):
    return [[(i, i ^ k) for i in range(count)] for k in range(count)]


def send_z(blocks):
    return [lax.ppermute(b, "z", f) for b, f in zip(blocks, flips(lax.axis_size("z"))[1:])]


def send_lines(blocks):
    count = lax.axis_size("y") * lax.axis_size("x")
    return [lax.ppermute(b, ("y", "x"), f) for b, f in zip(blocks, flips(count)[1:])]


def gather_lines(own):
    return [own] + send_lines([own] * (lax.axis_size("y") * lax.axis_size("x") - 1))


def send_c(block):
    return lax.ppermute(block, "c", flips(2)[1])


def gather_group(own):
    lists = [own] + [list(t) for t in zip(*[send_z([o] * (lax.axis_size("z") - 1)) for o in own])]
    blocks = [b for one in lists for b in one]
    return blocks + [send_c(b) for b in blocks]


def half_sum_kernel(near, far, mine, *low):
    for k in range(near.shape[0]):
        total = near[k].astype(F32) + far[k].astype(F32)
        if k == 0:
            mine[...] = total
        else:
            low[k - 1][...] = total.astype(BF16)


def slot_sum_kernel(*refs):
    pairs, (mine, *low) = refs[:4], refs[4:]
    size = pairs[0].shape[1]
    for j in range(2):
        near, far = pairs[2 * j], pairs[2 * j + 1]
        rows = slice(j * size, (j + 1) * size)
        for k in range(near.shape[0]):
            total = near[k].astype(F32) + far[k].astype(F32)
            if k == 0:
                mine[rows] = total
            else:
                low[k - 1][rows] = total.astype(BF16)


def scatter_group(near, far, after=()):
    depth, rows, lanes = near.shape
    outs = [((rows, lanes), F32)] + [((rows, lanes), BF16)] * (depth - 1)
    mine, *low = local_call(half_sum_kernel, outs, (near, send_c(far)), after=after)
    return [mine] + send_z(low)


def add_up(refs):
    total = refs[0][...]
    for ref in refs[1:]:
        total = total + ref[...].astype(F32)
    return total


def xor_order(blocks, index):
    step = 1
    while step < len(blocks):
        swap = (index & step) != 0
        blocks = [jnp.where(swap, blocks[b ^ step], blocks[b]) for b in range(len(blocks))]
        step *= 2
    return blocks


def columns_kernel(dims, w_qkv, w_up, gain_attn, gain_mlp, router, out, vec_s):
    ny, members, nx, ff_rows = dims
    cols = 3 * ny * HDIM
    vec_s[...] = jnp.zeros_like(vec_s)
    for k, vec in enumerate((gain_attn, gain_mlp, router)):
        vec_s[k : k + 1] = vec[...].astype(F32)
    vecs = mm(vec_s[...].astype(BF16), eye_rows(), TN).astype(BF16)
    for g in range(members):
        parts = []
        for t in range(3):
            for y in range(ny):
                at = (t * HEADS + y * members + g) * HDIM
                parts.append(w_qkv[:, at : at + HDIM])
        out[g, :, :cols] = jnp.concatenate(parts, 1)
        out[g, :, cols : cols + 128] = vecs
        for y in range(ny):
            for x in range(nx):
                at = ((y * members + g) * nx + x) * ff_rows
                to = cols + 128 + (y * nx + x) * ff_rows
                out[g, :, to : to + ff_rows] = w_up[:, at : at + ff_rows]


def eye_rows():
    down = lax.broadcasted_iota(jnp.int32, (8, 128), 0)
    return (down == lax.broadcasted_iota(jnp.int32, (8, 128), 1)).astype(F32).astype(BF16)


def pick_kernel(cap, where, chosen_t, tokens, cot, pick, *refs):
    *outs, rows = refs
    seq_count, seg_len = tokens.shape[:2]
    base = where[4] * seg_len
    places = base + lax.broadcasted_iota(jnp.int32, (chosen_t.shape[0], seg_len), 1)
    slots = lax.broadcasted_iota(jnp.int32, (cap, seg_len), 0)
    for s in range(seq_count):
        at = chosen_t[:, s : s + 1]
        present = jnp.sum((at == places).astype(F32), 0, keepdims=True)
        rank = jnp.sum(((at >= base) & (at < places)).astype(F32), 0, keepdims=True)
        hot = jnp.where(rank.astype(jnp.int32) == slots, present, 0.0).astype(BF16)
        pick[s] = hot
        rows[s, :cap] = mm(hot, tokens[s]).astype(BF16)
        rows[s, cap:] = mm(hot, cot[s]).astype(BF16)
    for k, out in enumerate(outs):
        out[...] = rows[where[2] ^ k]


def stack_kernel(cap, *refs):
    *blocks, out = refs
    for k, block in enumerate(blocks):
        for j in range(2):
            to = (j * len(blocks) + k) * cap
            out[to : to + cap] = block[j * cap : (j + 1) * cap]


def relay_kernel(got, w_out, w_down, first, up):
    members, rows, lanes = got.shape
    half = lanes // 2
    for line in range(first.shape[0]):
        at = members * rows
        first[line, :at] = got[:, :, :half].reshape(at, half)
        for block in (w_out, w_down):
            size = block.shape[0]
            for j in range(2):
                first[line, at : at + size] = block[:, j * half : (j + 1) * half]
                at += size
    up[...] = got[:, :, half:].reshape(members * rows, half)


def spread_kernel(dims, where, chosen, chosen_t, spread):
    ny, nc, nz, nx, seg_len, cap = dims
    c, z, line = where[0], where[1], where[2]
    routed = chosen_t.shape[0]
    members = nc * nz

    def owner_of(mine):
        return lax.div(mine, jnp.int32(seg_len))

    mine_col = chosen_t[:, 0:1]
    mine_row = chosen[0:1, :]
    for s in range(1, chosen.shape[0]):
        mine_col = jnp.where(line == s, chosen_t[:, s : s + 1], mine_col)
        mine_row = jnp.where(line == s, chosen[s : s + 1, :], mine_row)
    owner, owner_row = owner_of(mine_col), owner_of(mine_row)
    order = lax.broadcasted_iota(jnp.int32, (routed, routed), 0)
    other = lax.broadcasted_iota(jnp.int32, (routed, routed), 1)
    same = (owner == owner_row) & (other < order)
    slot = jnp.sum(same.astype(F32), 1, keepdims=True).astype(jnp.int32)
    ox, rest = lax.rem(owner, jnp.int32(nx)), lax.div(owner, jnp.int32(nx))
    oz, rest = lax.rem(rest, jnp.int32(nz)), lax.div(rest, jnp.int32(nz))
    oc, oy = lax.rem(rest, jnp.int32(nc)), lax.div(rest, jnp.int32(nc))
    cell = (((oc ^ c) * nz + (oz ^ z)) * (ny * nx) + ((oy * nx + ox) ^ line)) * cap + slot
    own = routed // members
    cells = [cell[b * own : (b + 1) * own] for b in range(members)]
    for b, block in enumerate(xor_order(cells, where[3])):
        lanes = lax.broadcasted_iota(jnp.int32, (own, spread.shape[1]), 1)
        spread[b * own : (b + 1) * own] = (block == lanes).astype(F32).astype(BF16)


def kept_pairs(member, routed, own):
    down = lax.broadcasted_iota(jnp.int32, (routed, routed), 0)
    across = lax.broadcasted_iota(jnp.int32, (routed, routed), 1)
    shift = own.bit_length() - 1
    first = ((down >> shift) ^ member) * own + (down & (own - 1))
    second = ((across >> shift) ^ member) * own + (across & (own - 1))
    return second <= first


def probabilities(queries, keys, kept):
    scores = jnp.where(kept, mm(queries, keys, NT) * HDIM ** (-0.5), neg_large)
    top = jnp.max(scores, 1, keepdims=True)
    probs = jnp.where(kept, jnp.exp(scores - top), 0.0)
    return probs, jnp.sum(probs, 1, keepdims=True)


def inverse_rms(values):
    return lax.rsqrt(jnp.mean(values * values, 1, keepdims=True) + epsilon)


def line_rows(blocks, start, out):
    half = out.shape[1] // 2
    size = out.shape[0] // blocks.shape[0]
    for q in range(blocks.shape[0]):
        for j in range(2):
            piece = blocks[q, start + j * size : start + (j + 1) * size]
            out[q * size : (q + 1) * size, j * half : (j + 1) * half] = piece


def own_order_rows(where, blocks, dims, out):
    ny, members, nx, rows = dims
    for k, block in enumerate(blocks):
        line = where[2] ^ k
        y, x = lax.div(line, jnp.int32(nx)), lax.rem(line, jnp.int32(nx))
        for g in range(members):
            to = pl.multiple_of(((y * members + g) * nx + x) * rows, rows)
            out[pl.ds(to, rows)] = block[g * rows : (g + 1) * rows, :]


def natural_rows(blocks, dims, first, count, out):
    ny, members, nx, rows = dims
    for y in range(ny):
        for g in range(members):
            for x in range(nx):
                to = ((y * members + g) * nx + x) * rows
                piece = blocks[y * nx + x, g * rows : (g + 1) * rows, first : first + count]
                out[to : to + rows] = piece


def attention_kernel(dims, members, where, spread, qkv_blocks, *refs):
    ny, nx, rows, cap = dims
    blocks, outs = refs[:members], refs[members:]
    picked_o, normed_o, w_o, first_o, wo_o, vecs_o = outs[:6]
    joined_o, att_o, exact_o, near_o, far_o, vec_s = outs[6:]
    heads = ny
    cols = 3 * heads * HDIM
    routed, width = picked_o.shape
    own = routed // members
    picked_low = mm(spread[...], jnp.concatenate([b[...] for b in blocks], 0)).astype(BF16)
    picked_o[...] = picked_low
    picked = picked_low.astype(F32)
    first_o[...] = picked_low[:own]
    natural_rows(qkv_blocks, (ny, members, nx, rows), 0, cols, w_o)
    natural_rows(qkv_blocks, (ny, members, nx, rows), cols, 128, vec_s)
    line_rows(qkv_blocks, members * rows, wo_o)
    vecs = mm(eye_rows(), vec_s[...], NT)
    vecs_o[...] = vecs
    normed = (picked * inverse_rms(picked) * vecs[0:1]).astype(BF16)
    normed_o[...] = normed
    joined = mm(normed, w_o[...]).astype(BF16)
    joined_o[...] = joined
    kept = kept_pairs(where[3], routed, own)
    parts = []
    for h in range(heads):
        queries, keys, values = (
            joined[:, (t * heads + h) * HDIM : (t * heads + h + 1) * HDIM] for t in range(3)
        )
        probs, total = probabilities(queries, keys, kept)
        parts.append(mm(probs.astype(BF16), values) / total)
    exact = jnp.concatenate(parts, 1)
    exact_o[...] = exact
    attended = exact.astype(BF16)
    att_o[...] = attended
    branch = mm(attended, wo_o[...]).astype(BF16)
    put_halves(branch, near_o, far_o)


def put_halves(values, near, far):
    depth, own = near.shape[:2]
    for k in range(depth):
        near[k] = values[k * own : (k + 1) * own]
        far[k] = values[(depth + k) * own : (depth + k + 1) * own]


def update_kernel(members, spread, picked, vecs, downs, *refs):
    blocks, outs = refs[:members], refs[members:]
    gate_o, cot_o, first_o, d_result_o, d_active_o, w_o = outs
    logit = jnp.sum(picked[...].astype(F32) * vecs[2:3, :], 1, keepdims=True)
    gate = 1.0 / (1.0 + jnp.exp(-logit))
    gate_o[...] = gate
    cot = mm(spread[...], jnp.concatenate([b[...] for b in blocks], 0)).astype(BF16)
    cot_o[...] = cot
    first_o[...] = cot[: first_o.shape[0]]
    d_result = (gate * cot.astype(F32)).astype(BF16)
    d_result_o[...] = d_result
    line_rows(downs, 0, w_o)
    d_active_o[...] = mm(d_result, w_o[...], NT)


def hidden_kernel(picked, vecs, *refs):
    *terms, hidden_o, normed_o = refs
    hidden = picked[...].astype(F32) + add_up(terms)
    hidden_o[...] = hidden
    normed_o[...] = (hidden * inverse_rms(hidden) * vecs[1:2, :]).astype(BF16)


def forward_kernel(dims, members, where, d_active, *refs):
    lines = dims[0] * dims[2]
    ups, refs = refs[:lines], refs[lines:]
    blocks, (active_o, d_upper_o, near_o, far_o, w_s) = refs[:members], refs[members:]
    own_order_rows(where, ups, dims, w_s)
    normed = jnp.concatenate([b[...] for b in blocks], 0)
    upper = mm(normed, w_s[...])
    below = 0.5 * (1.0 + lax.erf(upper * (0.5**0.5)))
    active_o[...] = (upper * below).astype(BF16)
    slope = below + upper * jnp.exp(-0.5 * upper * upper) * ((2.0 * math.pi) ** -0.5)
    d_upper = (d_active[...] * slope).astype(BF16)
    d_upper_o[...] = d_upper
    put_halves(mm(d_upper, w_s[...], NT).astype(BF16), near_o, far_o)


def ff_grads_kernel(dims, members, where, active, d_upper, d_result, *refs):
    ny, nx, rows, ff_rows = dims
    blocks, (keep, send, down, up) = refs[:members], refs[members:]
    normed = jnp.concatenate([b[...] for b in blocks], 0)
    down[...] = mm(active[...], d_result[...], TN).astype(BF16)
    up[...] = mm(normed, d_upper[...], TN).astype(BF16)
    wide = up.shape[1]
    each = ff_rows + members * rows // 2
    for k in range(ny * nx):
        line = where[2] ^ k
        out, start = (keep, send)[k % 2], (k // 2) * each
        y, x = lax.div(line, jnp.int32(nx)), lax.rem(line, jnp.int32(nx))
        piece = down[pl.ds(pl.multiple_of(line * ff_rows, ff_rows), ff_rows)]
        out[start : start + ff_rows] = piece
        for g in range(members):
            at = pl.multiple_of(((y * members + g) * nx + x) * rows, rows)
            half, row = divmod(g * rows, members * rows // 2)
            to = start + ff_rows + row
            out[to : to + rows, half * wide : (half + 1) * wide] = up[pl.ds(at, rows)]


def add_halves_kernel(keep, got, mine, send):
    half = mine.shape[0]
    mine[...] = keep[:half].astype(F32) + got[:half].astype(F32)
    send[...] = (keep[half:].astype(F32) + got[half:].astype(F32)).astype(BF16)


def result_kernel(active, attended, w_down, w_out, cot, gate, spread, logit_o, near_o, far_o):
    combined = mm(active[...], w_down[...]) + mm(attended[...], w_out[...])
    logit = jnp.sum(cot[...].astype(F32) * combined, 1, keepdims=True)
    logit_o[...] = logit * gate[...] * (1.0 - gate[...])
    update = (gate[...] * combined).astype(BF16)
    put_halves(mm(spread[...], update, TN).astype(BF16), near_o, far_o)


def hidden_back_kernel(own, hidden_r, vecs, gate, cot, *refs):
    *terms, d_branch_o, d_hidden_o, gain_o = refs
    d_normed = add_up(terms)
    hidden = hidden_r[...]
    inv = inverse_rms(hidden)
    u = d_normed * vecs[1:2, :]
    d_hidden = inv * u - hidden * (inv * inv * inv * jnp.mean(u * hidden, 1, keepdims=True))
    d_hidden_o[...] = d_hidden
    gain_o[...] = (d_normed * hidden * inv).astype(BF16)
    d_update = gate[:own, :] * cot[...].astype(F32)
    d_branch_o[...] = (d_update + d_hidden).astype(BF16)


def attention_back_kernel(members, where, *refs):
    w_out, joined_r, exact_r, w, vecs, picked_r, logit, d_hidden, spread = refs[:9]
    blocks = refs[9 : 9 + members]
    near_o, far_o, d_joined_o, gain_o = refs[9 + members :]
    routed, width = picked_r.shape
    own = routed // members
    heads = joined_r.shape[1] // (3 * HDIM)
    d_branch = jnp.concatenate([b[...] for b in blocks], 0)
    d_attended = mm(d_branch, w_out[...], NT).astype(BF16)
    joined = joined_r[...]
    exact = exact_r[...]
    kept = kept_pairs(where[3], routed, own)
    grads = [[], [], []]
    for h in range(heads):
        queries, keys, values = (
            joined[:, (t * heads + h) * HDIM : (t * heads + h + 1) * HDIM] for t in range(3)
        )
        probs, total = probabilities(queries, keys, kept)
        d_att = d_attended[:, h * HDIM : (h + 1) * HDIM]
        d_wide = d_att.astype(F32)
        delta = jnp.sum(d_wide * exact[:, h * HDIM : (h + 1) * HDIM], 1, keepdims=True)
        d_scores = (probs / total * (mm(d_att, values, NT) - delta)).astype(BF16)
        grads[0].append(mm(d_scores, keys) * HDIM ** (-0.5))
        grads[1].append(mm(d_scores, queries, TN) * HDIM ** (-0.5))
        grads[2].append(mm(probs.astype(BF16), (d_wide / total).astype(BF16), TN))
    d_joined = jnp.concatenate(grads[0] + grads[1] + grads[2], 1).astype(BF16)
    d_joined_o[...] = d_joined
    d_normed = mm(d_joined, w[...], NT)
    picked = picked_r[...].astype(F32)
    inv = inverse_rms(picked)
    gain_o[...] = (d_normed * picked * inv).astype(BF16)
    v = d_normed * vecs[0:1, :]
    d_picked = inv * v - picked * (inv * inv * inv * jnp.mean(v * picked, 1, keepdims=True))
    d_picked = d_picked + logit[...] * vecs[2:3, :]
    first = d_picked[:own] + d_hidden[...]
    d_picked = jnp.concatenate([first, d_picked[own:]], 0).astype(BF16)
    put_halves(mm(spread[...], d_picked, TN).astype(BF16), near_o, far_o)


def grads_kernel(dims, members, where, normed, d_joined, attended, gain_a, gain_m, *refs):
    ny, nx, rows = dims
    lines = ny * nx
    picked, logit, refs = refs[0], refs[1], refs[2:]
    blocks, sums, (main, vec_s, out) = refs[:members], refs[members : members + lines], refs[-3:]
    cols = d_joined.shape[1]
    routed, width = normed.shape
    own = gain_m.shape[0]
    main[...] = mm(normed[...], d_joined[...], TN).astype(BF16)
    lanes = lax.broadcasted_iota(jnp.int32, (routed, 128), 1)

    def lane(k, count):
        return (lanes[:count] == k).astype(F32)

    vec = mm(gain_a[...], lane(0, routed).astype(BF16), TN)
    vec = vec + mm(gain_m[...], lane(1, own).astype(BF16), TN)
    high = logit[...].astype(BF16)
    low = (logit[...] - high.astype(F32)).astype(BF16)
    vec = vec + mm(picked[...], (lane(2, routed) * high.astype(F32)).astype(BF16), TN)
    vec = vec + mm(picked[...], (lane(2, routed) * low.astype(F32)).astype(BF16), TN)
    vec_s[...] = vec.astype(BF16)
    out[...] = mm(attended[...], jnp.concatenate([b[...] for b in blocks], 0), TN).astype(BF16)
    for k in range(lines):
        line = where[2] ^ k
        y, x = lax.div(line, jnp.int32(nx)), lax.rem(line, jnp.int32(nx))
        for g in range(members):
            at = pl.multiple_of(((y * members + g) * nx + x) * rows, rows)
            sums[k][g * rows : (g + 1) * rows, :cols] = main[pl.ds(at, rows)]
            sums[k][g * rows : (g + 1) * rows, cols:] = vec_s[pl.ds(at, rows)]
        half, end = width // 2, members * rows
        at = pl.multiple_of(line * rows, rows)
        for j in range(2):
            piece = out[pl.ds(at, rows), j * half : (j + 1) * half]
            sums[k][end + j * rows : end + (j + 1) * rows, :] = piece


def join_slots_kernel(cap, lines, *refs):
    terms, outs = refs[:-lines], refs[-lines:]
    total = add_up(terms).astype(BF16)
    for j in range(2):
        for k in range(lines):
            at = (j * lines + k) * cap
            outs[k][j * cap : (j + 1) * cap] = total[at : at + cap]


def place_kernel(cap, lines, where, pick, tokens, cot, *refs):
    blocks, (out_o, grad_o, got) = refs[:lines], refs[lines:]
    for k, block in enumerate(blocks):
        got[where[2] ^ k] = block[...]
    for s in range(tokens.shape[0]):
        hot = pick[s]
        out_o[s] = (tokens[s].astype(F32) + mm(hot, got[s, :cap], TN)).astype(BF16)
        grad_o[s] = (cot[s].astype(F32) + mm(hot, got[s, cap:], TN)).astype(BF16)


def line_sums_kernel(dims, where, mine, got, *refs):
    members, rows, ff_rows = dims
    *parts, near_o, far_o, out_o, down_o, send = refs
    cols = parts[0].shape[1]
    wide = mine.shape[1] // 2
    ff = mine[...] + got[...].astype(F32)
    up = ff[ff_rows:]
    main = parts[0][...].astype(F32)
    for part in parts[1:]:
        main = main + part[...].astype(F32)
    for g in range(members):
        send[g, :, :cols] = main[g * rows : (g + 1) * rows].astype(BF16)
        half, row = divmod(g * rows, members * rows // 2)
        piece = up[row : row + rows, half * wide : (half + 1) * wide]
        send[g, :, cols:] = piece.astype(BF16)
    depth = near_o.shape[0]
    for k in range(depth):
        near_o[k] = send[where[3] ^ k]
        far_o[k] = send[where[3] ^ (depth + k)]
    end = members * rows
    out_o[...] = jnp.concatenate([main[end : end + rows], main[end + rows :]], 1)
    down_o[...] = ff[:ff_rows]


def pair_kernel(near, far, *outs):
    rows = near.shape[1]
    for k, out in enumerate(outs):
        out[:rows] = near[k]
        out[rows:] = far[k]


def unpack_kernel(dims, where, *refs):
    ny, members, nx, ff_rows = dims
    depth = members // 2
    pairs, (qkv_o, up_o, *vec_o, got) = refs[:depth], refs[depth:]
    rows = got.shape[1]
    for k, pair in enumerate(pairs):
        got[where[3] ^ k] = pair[:rows]
        got[where[3] ^ (depth + k)] = pair[rows:]
    cols = 3 * ny * HDIM
    for t in range(3):
        for y in range(ny):
            from_ = (t * ny + y) * HDIM
            row = [got[g, :, from_ : from_ + HDIM] for g in range(members)]
            at = (t * HEADS + y * members) * HDIM
            qkv_o[:, at : at + members * HDIM] = jnp.concatenate(row, 1).astype(F32)
    for y in range(ny):
        for g in range(members):
            for x in range(nx):
                at = ((y * members + g) * nx + x) * ff_rows
                from_ = cols + 128 + (y * nx + x) * ff_rows
                up_o[:, at : at + ff_rows] = got[g, :, from_ : from_ + ff_rows].astype(F32)
    vec = got[0, :, cols : cols + 128].astype(F32)
    for g in range(1, members):
        vec = vec + got[g, :, cols : cols + 128].astype(F32)
    high = vec.astype(BF16)
    low = (vec - high.astype(F32)).astype(BF16)
    vec = mm(eye_rows(), high, NT) + mm(eye_rows(), low, NT)
    for k, out in enumerate(vec_o):
        out[...] = vec[k : k + 1]


def grouped(
    tokens, chosen, w_qkv, w_out, w_up, w_down, gain_attn, gain_mlp, router, cotangent
):
    ny, nc, nz, nx = (lax.axis_size(a) for a in ("y", "c", "z", "x"))
    y, c, z, x = (lax.axis_index(a) for a in ("y", "c", "z", "x"))
    seq_count, seg_len, width = tokens.shape
    cap = seg_len // 4
    routed = chosen.shape[1]
    members, lines = nc * nz, ny * nx
    member, line = c * nz + z, y * nx + x
    shard = ((y * nc + c) * nz + z) * nx + x
    rows, ff_rows = w_qkv.shape[0], w_down.shape[0]
    heads = HEADS // members
    own = routed // members
    cols, wide = 3 * heads * HDIM, lines * ff_rows
    where = jnp.stack([c, z, line, member, shard]).astype(jnp.int32)
    chosen_t = chosen.T
    block = (own, width)
    slot_block = (2 * cap, width)
    halves = [((nz, own, width), BF16)] * 2
    slot_halves = [((nz, lines * cap, width), BF16)] * 2

    pick, *picked_rows = local_call(
        partial(pick_kernel, cap),
        [Far(((seq_count, cap, seg_len), BF16))] + [(slot_block, BF16)] * lines,
        (where, chosen_t, tokens, cotangent),
        scratch=[pltpu.VMEM((seq_count, 2 * cap, width), BF16)],
        scalars=1,
    )
    line_slots = picked_rows[:1] + send_lines(picked_rows[1:])
    (hot,) = local_call(
        partial(spread_kernel, (ny, nc, nz, nx, seg_len, cap)),
        [Far(((routed, members * lines * cap), BF16))],
        (where, chosen, chosen_t),
        scalars=1,
    )
    spread = Far(hot)
    (line_slots,) = local_call(
        partial(stack_kernel, cap), [((2 * lines * cap, width), BF16)], line_slots, after=(hot,)
    )
    slots = gather_group([line_slots])
    half = lines * cap
    picked_slots, cot_slots = [Far(b, 0, half) for b in slots], [Far(b, half, half) for b in slots]

    vecs = [v.reshape(1, rows) for v in (gain_attn, gain_mlp, router)]
    (columns,) = local_call(
        partial(columns_kernel, (ny, members, nx, ff_rows)),
        [((members, rows, cols + 128 + wide), BF16)],
        tuple(Far(v) for v in (w_qkv, w_up, *vecs)),
        scratch=[pltpu.VMEM((8, rows), F32)],
    )
    got_cols = lax.all_to_all(columns, ("c", "z"), 0, 0, tiled=True)
    half = width // 2
    base = members * rows + 2 * rows
    first, up = local_call(
        relay_kernel,
        [Far(((lines, base + 2 * ff_rows, half), BF16)), ((members * rows, half), BF16)],
        (got_cols, w_out, w_down),
        after=(line_slots,),
    )
    first = lax.all_to_all(first, ("y", "x"), 0, 0, tiled=True)
    got_down = Far(first, base, 2 * ff_rows, 1)
    got_up = gather_lines(up)

    picked, normed, full_qkv, picked_own, full_out, full_vecs, joined, attended, exact, near, far = (
        local_call(
            partial(attention_kernel, (ny, nx, rows, cap), members),
            [
                ((routed, width), BF16),
                ((routed, width), BF16),
                ((width, cols), BF16),
                (block, BF16),
                ((heads * HDIM, width), BF16),
                ((8, width), F32),
                ((routed, cols), BF16),
                ((routed, heads * HDIM), BF16),
                ((routed, heads * HDIM), F32),
            ]
            + halves,
            (where, spread, Far(first, 0, base, 1), *picked_slots),
            flops=1.2e9,
            scratch=[pltpu.VMEM((width, 128), BF16)],
            scalars=1,
        )
    )
    terms = scatter_group(near, far)
    gate, cot, cot_own, d_result, d_active, full_down = local_call(
        partial(update_kernel, members),
        [
            ((routed, 1), F32),
            ((routed, width), BF16),
            (block, BF16),
            ((routed, width), BF16),
            ((routed, wide), F32),
            ((wide, width), BF16),
        ],
        (spread, picked, full_vecs, got_down, *cot_slots),
        flops=8e8,
    )
    hidden, normed_own = local_call(
        hidden_kernel,
        [(block, F32), (block, BF16)],
        (picked_own, full_vecs, *terms),
        after=(d_active,),
    )
    normed_mlp = gather_group([normed_own])

    active, d_upper, near, far = local_call(
        partial(forward_kernel, (ny, members, nx, rows), members),
        [((routed, wide), BF16)] * 2 + halves,
        (where, d_active, *got_up, *normed_mlp),
        flops=6e8,
        scratch=[pltpu.VMEM((width, wide), BF16)],
        scalars=1,
    )
    terms = scatter_group(near, far)
    half_rows = 2 * (ff_rows + members * rows // 2)
    ff_keep, ff_send = local_call(
        partial(ff_grads_kernel, (ny, nx, rows, ff_rows), members),
        [((half_rows, width), BF16)] * 2,
        (where, active, d_upper, d_result, *normed_mlp),
        flops=6e8,
        scratch=[pltpu.VMEM((wide, width), BF16), pltpu.VMEM((width, wide), BF16)],
        scalars=1,
    )
    ff_got = lax.ppermute(ff_send, "x", flips(nx)[1])
    logit, up_near, up_far = local_call(
        result_kernel,
        [((routed, 1), F32)] + slot_halves,
        (active, attended, full_down, full_out, cot, gate, spread),
        flops=8e8,
    )
    d_branch_own, d_hidden, gain_m = local_call(
        partial(hidden_back_kernel, own),
        [(block, BF16), (block, F32), (block, BF16)],
        (hidden, full_vecs, gate, cot_own, *terms),
        after=(ff_send, logit),
    )
    d_branch = gather_group([d_branch_own])
    up_far = send_c(up_far)
    ff_mine, ff_send = local_call(
        add_halves_kernel,
        [((half_rows // 2, width), F32), ((half_rows // 2, width), BF16)],
        (ff_keep, ff_got),
    )
    ff_got = lax.ppermute(ff_send, "y", flips(ny)[1])

    near, far, d_joined, gain_a = local_call(
        partial(attention_back_kernel, members),
        slot_halves + [((routed, cols), BF16), ((routed, width), BF16)],
        (where, full_out, joined, exact, full_qkv, full_vecs, picked)
        + (logit, d_hidden, spread, *d_branch),
        flops=1.2e9,
        scalars=1,
    )
    far = send_c(far)
    parts = local_call(
        partial(grads_kernel, (ny, nx, rows), members),
        [((members * rows + 2 * rows, cols + 128), BF16)] * lines,
        (where, normed, d_joined, attended, gain_a, gain_m, picked, logit, *d_branch),
        flops=5e8,
        scratch=[
            pltpu.VMEM((width, cols), BF16),
            pltpu.VMEM((width, 128), BF16),
            pltpu.VMEM((heads * HDIM, width), BF16),
        ],
        scalars=1,
    )
    parts = parts[:1] + send_lines(parts[1:])
    both_slots = (2 * lines * cap, width)
    mine, *low = local_call(
        slot_sum_kernel,
        [(both_slots, F32)] + [(both_slots, BF16)] * (nz - 1),
        (up_near, up_far, near, far),
        after=(ff_mine,),
    )
    back_rows = local_call(
        partial(join_slots_kernel, cap, lines),
        [(slot_block, BF16)] * lines,
        [mine] + send_z(low),
    )
    back_rows = back_rows[:1] + send_lines(back_rows[1:])
    row_width = cols + 128 + wide
    near, far, grad_out, grad_down = local_call(
        partial(line_sums_kernel, (members, rows, ff_rows)),
        [((nz, rows, row_width), BF16)] * 2 + [((rows, width), F32), ((ff_rows, width), F32)],
        (where, ff_mine, ff_got, *parts),
        scratch=[pltpu.VMEM((members, rows, row_width), BF16)],
        scalars=1,
        after=back_rows[:1],
    )
    pairs = local_call(pair_kernel, [((2 * rows, row_width), BF16)] * nz, (near, send_c(far)))
    pairs = pairs[:1] + send_z(pairs[1:])
    output, grad_tokens = local_call(
        partial(place_kernel, cap, lines),
        [(tokens.shape, BF16), (tokens.shape, BF16)],
        (where, Far(pick), tokens, cotangent, *back_rows),
        scratch=[pltpu.VMEM((seq_count, 2 * cap, width), BF16)],
        scalars=1,
    )
    grad_qkv, grad_up, *grad_vecs = local_call(
        partial(unpack_kernel, (ny, members, nx, ff_rows)),
        [(w_qkv.shape, F32), (w_up.shape, F32)] + [((1, rows), F32)] * 3,
        (where, *pairs),
        scratch=[pltpu.VMEM((members, rows, row_width), BF16)],
        scalars=1,
    )
    return (
        output,
        grad_tokens,
        grad_qkv,
        grad_out,
        grad_up,
        grad_down,
        *(v.reshape(rows) for v in grad_vecs),
    )


def fits(mesh):
    head_count, block_count = mesh.devices.shape
    members = (head_count // 2) * (block_count // 2)
    power = members & (members - 1) == 0
    return power and head_count == 4 and HEADS == 2 * members


def solution(mesh):
    if fits(mesh):
        head_count, block_count = mesh.devices.shape
        devices = mesh.devices.reshape(2, head_count // 2, block_count // 2, 2)
        mesh = jax.sharding.Mesh(devices, ("y", "c", "z", "x"))
        body, all_axes = grouped, ("y", "c", "z", "x")
    else:
        body, all_axes = shards, ("head", "blk")
    seqs, mats, vecs = P(None, all_axes, None), P(all_axes, None), P(all_axes)
    in_specs = (seqs, P(), mats, mats, mats, mats, vecs, vecs, vecs, seqs)
    out_specs = (seqs, seqs, mats, mats, mats, mats, vecs, vecs, vecs)
    return jax.shard_map(body, mesh=mesh, in_specs=in_specs, out_specs=out_specs, check_vma=False)
```

```python
import math
from functools import partial

import jax
import jax.numpy as jnp
from jax import lax
from jax.experimental import pallas as pl
from jax.experimental.pallas import tpu as pltpu
from jax.sharding import PartitionSpec as P

HEADS = 16
HDIM = 64


epsilon = 1e-06
neg_large = -1e30


def rms_norm(values, gain_vec):
    inverse_rms = lax.rsqrt(jnp.mean(values * values, axis=-1, keepdims=True) + epsilon)
    return values * inverse_rms * gain_vec


def exact_gelu(values):
    return jax.nn.gelu(values, approximate=False)


def take_rows(seq_rows, row_index):
    return seq_rows[row_index]


def add_rows(seq_rows, row_index, additions):
    return seq_rows.at[row_index].add(additions)


def shards(tokens, chosen, w_qkv, w_out, w_up, w_down, gain_attn, gain_mlp, router, cotangent):
    head_count = lax.axis_size("head")
    block_count = lax.axis_size("blk")
    shard_count = head_count * block_count
    seq_count, seg_len, model_width = tokens.shape
    cap_len = seg_len // 4
    routed_count = chosen.shape[1]
    seq_len = seg_len * shard_count
    local_heads = HEADS // head_count
    slot_rows = head_count * cap_len
    scale_factor = HDIM ** (-0.5)
    head_index = lax.axis_index("head")
    block_index = lax.axis_index("blk")
    my_shard = head_index * block_count + block_index
    bounds = jnp.arange(shard_count + 1, dtype=jnp.int32) * seg_len
    before = jax.vmap(lambda chosen_row: jnp.searchsorted(chosen_row, bounds, side="left"))(chosen)
    first_index = before[:, :-1]
    shard_load = before[:, 1:] - first_index
    slot_iota = jnp.arange(cap_len, dtype=jnp.int32)
    live_table = slot_iota[None, None, :] < shard_load[:, :, None]
    lookup = jnp.minimum(first_index[:, :, None] + slot_iota[None, None, :], routed_count - 1)
    place_table = jnp.take_along_axis(
        chosen, lookup.reshape(seq_count, shard_count * cap_len), axis=1
    )
    place_table = jnp.where(
        live_table, place_table.reshape(seq_count, shard_count, cap_len), seq_len
    )
    my_positions = lax.dynamic_index_in_dim(place_table, my_shard, 1, False)
    my_live = lax.dynamic_index_in_dim(live_table, my_shard, 1, False)
    local_rows = jnp.clip(my_positions - my_shard * seg_len, 0, seg_len - 1)
    cycle_positions = place_table.reshape(seq_count, head_count, block_count, cap_len).transpose(
        0, 2, 1, 3
    )
    cycle_positions = cycle_positions.reshape(seq_count, block_count * slot_rows)
    query_positions = lax.dynamic_slice_in_dim(
        cycle_positions, block_index * slot_rows, slot_rows, 1
    )
    live_weight = my_live.astype(jnp.float32)[:, :, None]
    gathered = (
        lax.all_gather(w_qkv, ("head", "blk"), axis=0, tiled=True),
        lax.all_gather(w_out, ("head", "blk"), axis=0, tiled=True),
        lax.all_gather(w_up, ("head", "blk"), axis=0, tiled=True),
        lax.all_gather(w_down, ("head", "blk"), axis=0, tiled=True),
        lax.all_gather(gain_attn, ("head", "blk"), axis=0, tiled=True),
        lax.all_gather(gain_mlp, ("head", "blk"), axis=0, tiled=True),
        lax.all_gather(router, ("head", "blk"), axis=0, tiled=True),
    )
    full_qkv, full_out, full_up, full_down, full_gain_attn, full_gain_mlp, full_router = gathered
    picked = jax.vmap(take_rows)(tokens, local_rows)
    picked = jnp.where(my_live[:, :, None], picked, jnp.zeros_like(picked))
    picked_exact = picked.astype(jnp.float32)
    router_gate = jax.nn.sigmoid(
        jnp.einsum("scd,d->sc", picked, full_router, preferred_element_type=jnp.float32)
    )
    normed_exact, norm_attn_back = jax.vjp(
        rms_norm, picked_exact, full_gain_attn.astype(jnp.float32)
    )
    normed = normed_exact.astype(jnp.bfloat16)
    joined = jnp.einsum("scd,de->sce", normed, full_qkv, preferred_element_type=jnp.float32).astype(
        jnp.bfloat16
    )
    to_heads = lax.all_to_all(
        joined.reshape(seq_count, cap_len, 3, model_width),
        "head",
        split_axis=3,
        concat_axis=1,
        tiled=True,
    )
    queries_tok = to_heads[:, :, 0]
    queries_heads = queries_tok.reshape(seq_count, slot_rows, local_heads, HDIM)
    key_values = to_heads[:, :, 1:3]
    my_keys = key_values[:, :, 0].reshape(seq_count, slot_rows, local_heads, HDIM)
    my_values = key_values[:, :, 1].reshape(seq_count, slot_rows, local_heads, HDIM)
    stat_shape = (seq_count, local_heads, slot_rows)
    piece = lax.all_gather(key_values, "blk", axis=1, tiled=True)
    run_max = jnp.full(stat_shape, neg_large, jnp.float32)
    piece_rows = piece.shape[1]
    key_pos = cycle_positions
    keys_piece = piece[:, :, 0].reshape(seq_count, piece_rows, local_heads, HDIM)
    values_piece = piece[:, :, 1].reshape(seq_count, piece_rows, local_heads, HDIM)
    scores = (
        jnp.einsum("sqhd,skhd->shqk", queries_heads, keys_piece, preferred_element_type=jnp.float32)
        * scale_factor
    )
    allowed = key_pos[:, None, None, :] <= query_positions[:, None, :, None]
    scores = jnp.where(allowed, scores, neg_large)
    new_max = jnp.maximum(run_max, jnp.max(scores, axis=3))
    prob_block = jnp.where(allowed, jnp.exp(scores - new_max[..., None]), 0.0)
    new_total = jnp.sum(prob_block, axis=3)
    added = jnp.einsum(
        "shqk,skhd->sqhd",
        prob_block.astype(jnp.bfloat16),
        values_piece,
        preferred_element_type=jnp.float32,
    )
    attended_exact = added / new_total.transpose(0, 2, 1)[..., None]
    log_sum = new_max + jnp.log(new_total)
    attended_tok = attended_exact.astype(jnp.bfloat16).reshape(
        seq_count, slot_rows, local_heads * HDIM
    )
    attended = lax.all_to_all(attended_tok, "head", split_axis=1, concat_axis=2, tiled=True)
    branch = jnp.einsum("sce,ed->scd", attended, full_out, preferred_element_type=jnp.float32)
    hidden_state = picked_exact + branch
    normed_mlp_exact, norm_mlp_back = jax.vjp(
        rms_norm, hidden_state, full_gain_mlp.astype(jnp.float32)
    )
    normed_mlp = normed_mlp_exact.astype(jnp.bfloat16)
    upper = jnp.einsum("scd,di->sci", normed_mlp, full_up, preferred_element_type=jnp.float32)
    active_exact, gelu_back = jax.vjp(exact_gelu, upper)
    active = active_exact.astype(jnp.bfloat16)
    result = jnp.einsum("sci,id->scd", active, full_down, preferred_element_type=jnp.float32)
    combined = branch + result
    update = router_gate[:, :, None] * combined * live_weight
    output = jax.vmap(add_rows)(tokens.astype(jnp.float32), local_rows, update).astype(jnp.bfloat16)
    regathered = (
        lax.all_gather(w_qkv, ("head", "blk"), axis=0, tiled=True),
        lax.all_gather(w_out, ("head", "blk"), axis=0, tiled=True),
        lax.all_gather(w_up, ("head", "blk"), axis=0, tiled=True),
        lax.all_gather(w_down, ("head", "blk"), axis=0, tiled=True),
        lax.all_gather(gain_attn, ("head", "blk"), axis=0, tiled=True),
        lax.all_gather(gain_mlp, ("head", "blk"), axis=0, tiled=True),
        lax.all_gather(router, ("head", "blk"), axis=0, tiled=True),
    )
    back_qkv, back_out, back_up, back_down, back_gain_attn, back_gain_mlp, back_router = regathered
    picked_cot = jax.vmap(take_rows)(cotangent, local_rows).astype(jnp.float32) * live_weight
    d_update = router_gate[:, :, None] * picked_cot
    d_logit = jnp.sum(picked_cot * combined, axis=2) * router_gate * (1.0 - router_gate)
    grad_router = jnp.einsum("sc,scd->d", d_logit, picked_exact, precision=lax.Precision.HIGHEST)
    d_result = d_update.astype(jnp.bfloat16)
    d_active = jnp.einsum("scd,id->sci", d_result, back_down, preferred_element_type=jnp.float32)
    d_upper = gelu_back(d_active)[0].astype(jnp.bfloat16)
    d_normed_mlp = jnp.einsum("sci,di->scd", d_upper, back_up, preferred_element_type=jnp.float32)
    d_hidden, grad_gain_mlp = norm_mlp_back(d_normed_mlp)
    d_branch = (d_update + d_hidden).astype(jnp.bfloat16)
    d_attended = jnp.einsum(
        "scd,ed->sce", d_branch, back_out, preferred_element_type=jnp.float32
    ).astype(jnp.bfloat16)
    d_att_tok = lax.all_to_all(d_attended, "head", split_axis=2, concat_axis=1, tiled=True)
    d_att_heads = d_att_tok.reshape(seq_count, slot_rows, local_heads, HDIM)
    delta_tok = jnp.sum(d_att_heads.astype(jnp.float32) * attended_exact, axis=3)
    delta_sq = delta_tok.transpose(0, 2, 1)
    piece = lax.all_gather(key_values, "blk", axis=1, tiled=True)
    piece_rows = piece.shape[1]
    key_pos = cycle_positions
    keys_piece = piece[:, :, 0].reshape(seq_count, piece_rows, local_heads, HDIM)
    values_piece = piece[:, :, 1].reshape(seq_count, piece_rows, local_heads, HDIM)
    scores = (
        jnp.einsum("sqhd,skhd->shqk", queries_heads, keys_piece, preferred_element_type=jnp.float32)
        * scale_factor
    )
    allowed = key_pos[:, None, None, :] <= query_positions[:, None, :, None]
    prob_block = jnp.where(allowed, jnp.exp(scores - log_sum[..., None]), 0.0)
    d_prob = jnp.einsum(
        "sqhd,skhd->shqk", d_att_heads, values_piece, preferred_element_type=jnp.float32
    )
    d_scores = (prob_block * (d_prob - delta_sq[..., None])).astype(jnp.bfloat16)
    d_queries = (
        jnp.einsum("shqk,skhd->sqhd", d_scores, keys_piece, preferred_element_type=jnp.float32)
        * scale_factor
    )
    lse_tok = log_sum.transpose(0, 2, 1)
    lse_high = lse_tok.astype(jnp.bfloat16)
    lse_low = (lse_tok - lse_high.astype(jnp.float32)).astype(jnp.bfloat16)
    delta_high = delta_tok.astype(jnp.bfloat16)
    delta_low = (delta_tok - delta_high.astype(jnp.float32)).astype(jnp.bfloat16)
    query_piece = lax.all_gather(queries_tok, "blk", axis=1, tiled=True)
    dout_piece = lax.all_gather(d_att_tok, "blk", axis=1, tiled=True)
    piece_lse_high = lax.all_gather(lse_high, "blk", axis=1, tiled=True)
    piece_lse_low = lax.all_gather(lse_low, "blk", axis=1, tiled=True)
    piece_delta_high = lax.all_gather(delta_high, "blk", axis=1, tiled=True)
    piece_delta_low = lax.all_gather(delta_low, "blk", axis=1, tiled=True)
    piece_rows = query_piece.shape[1]
    query_heads = query_piece.reshape(seq_count, piece_rows, local_heads, HDIM)
    dout_heads = dout_piece.reshape(seq_count, piece_rows, local_heads, HDIM)
    piece_lse = (piece_lse_high.astype(jnp.float32) + piece_lse_low.astype(jnp.float32)).transpose(
        0, 2, 1
    )
    piece_delta = (
        piece_delta_high.astype(jnp.float32) + piece_delta_low.astype(jnp.float32)
    ).transpose(0, 2, 1)
    scores = (
        jnp.einsum("sqhd,skhd->shqk", query_heads, my_keys, preferred_element_type=jnp.float32)
        * scale_factor
    )
    allowed = query_positions[:, None, None, :] <= cycle_positions[:, None, :, None]
    prob_block = jnp.where(allowed, jnp.exp(scores - piece_lse[..., None]), 0.0)
    grad_values = jnp.einsum(
        "shqk,sqhd->skhd",
        prob_block.astype(jnp.bfloat16),
        dout_heads,
        preferred_element_type=jnp.float32,
    )
    d_prob = jnp.einsum(
        "sqhd,skhd->shqk", dout_heads, my_values, preferred_element_type=jnp.float32
    )
    d_scores = (prob_block * (d_prob - piece_delta[..., None])).astype(jnp.bfloat16)
    grad_keys = (
        jnp.einsum("shqk,sqhd->skhd", d_scores, query_heads, preferred_element_type=jnp.float32)
        * scale_factor
    )
    d_heads = jnp.stack(
        [
            d_queries.astype(jnp.bfloat16),
            grad_keys.astype(jnp.bfloat16),
            grad_values.astype(jnp.bfloat16),
        ],
        axis=2,
    )
    d_heads = d_heads.reshape(seq_count, slot_rows, 3, local_heads * HDIM)
    d_joined = lax.all_to_all(d_heads, "head", split_axis=1, concat_axis=3, tiled=True).reshape(
        seq_count, cap_len, 3 * model_width
    )
    d_normed = jnp.einsum("sce,de->scd", d_joined, back_qkv, preferred_element_type=jnp.float32)
    d_picked_norm, grad_gain_attn = norm_attn_back(d_normed)
    d_picked = (
        d_hidden
        + d_picked_norm
        + d_logit[:, :, None] * back_router.astype(jnp.float32)[None, None, :]
    )
    grad_tokens = jax.vmap(add_rows)(
        cotangent.astype(jnp.float32), local_rows, d_picked * live_weight
    ).astype(jnp.bfloat16)
    grad_qkv = jnp.einsum("scd,sce->de", normed, d_joined, preferred_element_type=jnp.float32)
    grad_out = jnp.einsum("sce,scd->ed", attended, d_branch, preferred_element_type=jnp.float32)
    grad_up = jnp.einsum("scd,sci->di", normed_mlp, d_upper, preferred_element_type=jnp.float32)
    grad_down = jnp.einsum("sci,scd->id", active, d_result, preferred_element_type=jnp.float32)
    owned = (
        lax.psum_scatter(grad_qkv, ("head", "blk"), scatter_dimension=0, tiled=True),
        lax.psum_scatter(grad_out, ("head", "blk"), scatter_dimension=0, tiled=True),
        lax.psum_scatter(grad_up, ("head", "blk"), scatter_dimension=0, tiled=True),
        lax.psum_scatter(grad_down, ("head", "blk"), scatter_dimension=0, tiled=True),
        lax.psum_scatter(grad_gain_attn, ("head", "blk"), scatter_dimension=0, tiled=True),
        lax.psum_scatter(grad_gain_mlp, ("head", "blk"), scatter_dimension=0, tiled=True),
        lax.psum_scatter(grad_router, ("head", "blk"), scatter_dimension=0, tiled=True),
    )
    return (
        output,
        grad_tokens,
        owned[0],
        owned[1],
        owned[2],
        owned[3],
        owned[4],
        owned[5],
        owned[6],
    )


F32, BF16 = jnp.float32, jnp.bfloat16
NN = (((1,), (0,)), ((), ()))
NT = (((1,), (1,)), ((), ()))
TN = (((0,), (0,)), ((), ()))


def mm(left, right, dims=NN):
    return lax.dot_general(left, right, dims, preferred_element_type=F32)


WORK = {
    "attention_back_kernel": 1200000000,
    "attention_kernel": 1200000000,
    "compact_kernel": 10000000000,
    "ff_grads_kernel": 600000000,
    "forward_kernel": 600000000,
    "grads_kernel": 500000000,
    "result_kernel": 800000000,
    "update_kernel": 800000000,
}


def work_of(body):
    return WORK.get(getattr(body, "func", body).__name__, 0)


class Far:
    def __init__(self, item, start=0, count=None, dim=0):
        self.item, self.start, self.count, self.dim = item, start, count, dim

    def shape(self):
        shape = list(self.item.shape)
        if self.count is not None:
            shape[self.dim] = self.count
        return tuple(shape)

    def source(self, ref):
        if self.count is None:
            return ref
        return ref.at[(slice(None),) * self.dim + (pl.ds(self.start, self.count),)]


class Loaded:
    def __init__(self, copy, ref):
        self.copy, self.ref, self.shape, self.waited = copy, ref, ref.shape, False

    def __getitem__(self, index):
        self.wait()
        return self.ref[index]

    def wait(self):
        if not self.waited:
            self.copy.wait()
        self.waited = True


class Stored:
    def __init__(self, copy, ref):
        self.copy, self.ref, self.shape, self.started = copy, ref, ref.shape, False

    def __getitem__(self, index):
        return self.ref[index]

    def __setitem__(self, index, value):
        self.ref[index] = value
        if index is Ellipsis:
            self.start()

    def start(self):
        if not self.started:
            self.copy.start()
        self.started = True


def local_call(body, outs, args, scratch=(), scalars=0, after=()):
    far_in = [a if isinstance(a, Far) else None for a in args]
    far_out = [isinstance(o, Far) for o in outs]
    outs = [o.item if f else o for o, f in zip(outs, far_out)]
    args = [pltpu.with_memory_space_constraint(f.item, pltpu.HBM) if f else a for a, f in zip(args, far_in)]
    shapes = [pltpu.HBM(s, d) if f else jax.ShapeDtypeStruct(s, d) for (s, d), f in zip(outs, far_out)]
    spaces = [pltpu.SMEM] * scalars
    spaces += [pltpu.HBM if f else pltpu.VMEM for f in far_in[scalars:]]
    spaces += [pl.ANY] * len(after)
    stages = []
    for f in far_in:
        if f:
            stages.append(pltpu.VMEM(f.shape(), f.item.dtype))
    stages += [pltpu.VMEM(s, d) for (s, d), f in zip(outs, far_out) if f]
    n_in, n_out, n_far = len(args), len(outs), len(stages)
    first_out = n_in + len(after)
    if n_far:
        stages.append(pltpu.SemaphoreType.DMA((n_far,)))

    def run(*refs):
        ins, results = list(refs[:n_in]), list(refs[first_out : first_out + n_out])
        rest = refs[first_out + n_out :]
        own, stage = rest[: len(scratch)], rest[len(scratch) :]
        at, loads, stores = 0, [], []
        for i, f in enumerate(far_in):
            if f:
                copy = pltpu.make_async_copy(f.source(ins[i]), stage[at], stage[-1].at[at])
                copy.start()
                ins[i] = Loaded(copy, stage[at])
                loads.append(ins[i])
                at += 1
        for i, f in enumerate(far_out):
            if f:
                copy = pltpu.make_async_copy(stage[at], results[i], stage[-1].at[at])
                results[i] = Stored(copy, stage[at])
                stores.append(results[i])
                at += 1
        body(*ins, *results, *own)
        for load in loads:
            load.wait()
        for store in stores:
            store.start()
        for store in stores:
            store.copy.wait()

    return list(
        pl.pallas_call(
            run,
            out_shape=shapes,
            in_specs=[pl.BlockSpec(memory_space=s) for s in spaces],
            out_specs=[
                pl.BlockSpec(memory_space=pltpu.HBM if f else pltpu.VMEM) for f in far_out
            ],
            scratch_shapes=list(scratch) + stages,
            compiler_params=pltpu.CompilerParams(vmem_limit_bytes=32 * 2**20),
            cost_estimate=pl.CostEstimate(
                flops=work_of(body), bytes_accessed=0, transcendentals=0
            ),
        )(*args, *after)
    )


def flips(count):
    return [[(i, i ^ k) for i in range(count)] for k in range(count)]


def send_z(blocks):
    return [lax.ppermute(b, "z", f) for b, f in zip(blocks, flips(lax.axis_size("z"))[1:])]


def send_lines(blocks):
    count = lax.axis_size("y") * lax.axis_size("x")
    return [lax.ppermute(b, ("y", "x"), f) for b, f in zip(blocks, flips(count)[1:])]


def gather_lines(own):
    return [own] + send_lines([own] * (lax.axis_size("y") * lax.axis_size("x") - 1))


def send_c(block):
    return lax.ppermute(block, "c", flips(2)[1])


def gather_group(own):
    lists = [own] + [list(t) for t in zip(*[send_z([o] * (lax.axis_size("z") - 1)) for o in own])]
    blocks = [b for one in lists for b in one]
    return blocks + [send_c(b) for b in blocks]


def half_sum_kernel(near, far, mine, *low):
    for k in range(near.shape[0]):
        total = near[k].astype(F32) + far[k].astype(F32)
        if k == 0:
            mine[...] = total
        else:
            low[k - 1][...] = total.astype(BF16)


def slot_sum_kernel(*refs):
    pairs, (mine, *low) = refs[:4], refs[4:]
    size = pairs[0].shape[1]
    for j in range(2):
        near, far = pairs[2 * j], pairs[2 * j + 1]
        rows = slice(j * size, (j + 1) * size)
        for k in range(near.shape[0]):
            total = near[k].astype(F32) + far[k].astype(F32)
            if k == 0:
                mine[rows] = total
            else:
                low[k - 1][rows] = total.astype(BF16)


def scatter_group(near, far, after=()):
    depth, rows, lanes = near.shape
    outs = [((rows, lanes), F32)] + [((rows, lanes), BF16)] * (depth - 1)
    mine, *low = local_call(half_sum_kernel, outs, (near, send_c(far)), after=after)
    return [mine] + send_z(low)


def add_up(refs):
    total = refs[0][...]
    for ref in refs[1:]:
        total = total + ref[...].astype(F32)
    return total


def xor_order(blocks, index):
    step = 1
    while step < len(blocks):
        swap = (index & step) != 0
        blocks = [jnp.where(swap, blocks[b ^ step], blocks[b]) for b in range(len(blocks))]
        step *= 2
    return blocks


def columns_kernel(dims, w_qkv, w_up, gain_attn, gain_mlp, router, out, vec_s):
    ny, members, nx, ff_rows = dims
    cols = 3 * ny * HDIM
    vec_s[...] = jnp.zeros_like(vec_s)
    for k, vec in enumerate((gain_attn, gain_mlp, router)):
        vec_s[k : k + 1] = vec[...].astype(F32)
    vecs = mm(vec_s[...].astype(BF16), eye_rows(), TN).astype(BF16)
    for g in range(members):
        parts = []
        for t in range(3):
            for y in range(ny):
                at = (t * HEADS + y * members + g) * HDIM
                parts.append(w_qkv[:, at : at + HDIM])
        out[g, :, :cols] = jnp.concatenate(parts, 1)
        out[g, :, cols : cols + 128] = vecs
        for y in range(ny):
            for x in range(nx):
                at = ((y * members + g) * nx + x) * ff_rows
                to = cols + 128 + (y * nx + x) * ff_rows
                out[g, :, to : to + ff_rows] = w_up[:, at : at + ff_rows]


def eye_rows():
    down = lax.broadcasted_iota(jnp.int32, (8, 128), 0)
    return (down == lax.broadcasted_iota(jnp.int32, (8, 128), 1)).astype(F32).astype(BF16)


def pick_kernel(cap, where, chosen_t, tokens, cot, pick, *refs):
    *outs, rows = refs
    seq_count, seg_len = tokens.shape[:2]
    base = where[4] * seg_len
    places = base + lax.broadcasted_iota(jnp.int32, (chosen_t.shape[0], seg_len), 1)
    slots = lax.broadcasted_iota(jnp.int32, (cap, seg_len), 0)
    for s in range(seq_count):
        at = chosen_t[:, s : s + 1]
        present = jnp.sum((at == places).astype(F32), 0, keepdims=True)
        rank = jnp.sum(((at >= base) & (at < places)).astype(F32), 0, keepdims=True)
        hot = jnp.where(rank.astype(jnp.int32) == slots, present, 0.0).astype(BF16)
        pick[s] = hot
        rows[s, :cap] = mm(hot, tokens[s]).astype(BF16)
        rows[s, cap:] = mm(hot, cot[s]).astype(BF16)
    for k, out in enumerate(outs):
        out[...] = rows[where[2] ^ k]


def stack_kernel(cap, *refs):
    *blocks, out = refs
    for k, block in enumerate(blocks):
        for j in range(2):
            to = (j * len(blocks) + k) * cap
            out[to : to + cap] = block[j * cap : (j + 1) * cap]


def relay_kernel(got, w_out, w_down, first, up):
    members, rows, lanes = got.shape
    half = lanes // 2
    size = members * rows
    blocks = [b[:, j * half : (j + 1) * half] for b in (w_out, w_down) for j in range(2)]
    for line in range(first.shape[0]):
        first[line, :size] = got[:, :, :half].reshape(size, half)
        at = size
        for block in blocks[: 3]:
            first[line, at : at + block.shape[0]] = block
            at += block.shape[0]
    up[:size] = got[:, :, half:].reshape(size, half)
    at = size
    for block in blocks[3 :]:
        up[at : at + block.shape[0]] = block
        at += block.shape[0]


def spread_kernel(dims, where, chosen, chosen_t, spread):
    ny, nc, nz, nx, seg_len, cap = dims
    c, z, line = where[0], where[1], where[2]
    routed = chosen_t.shape[0]
    members = nc * nz

    def owner_of(mine):
        return lax.div(mine, jnp.int32(seg_len))

    mine_col = chosen_t[:, 0:1]
    mine_row = chosen[0:1, :]
    for s in range(1, chosen.shape[0]):
        mine_col = jnp.where(line == s, chosen_t[:, s : s + 1], mine_col)
        mine_row = jnp.where(line == s, chosen[s : s + 1, :], mine_row)
    owner, owner_row = owner_of(mine_col), owner_of(mine_row)
    order = lax.broadcasted_iota(jnp.int32, (routed, routed), 0)
    other = lax.broadcasted_iota(jnp.int32, (routed, routed), 1)
    same = (owner == owner_row) & (other < order)
    slot = jnp.sum(same.astype(F32), 1, keepdims=True).astype(jnp.int32)
    ox, rest = lax.rem(owner, jnp.int32(nx)), lax.div(owner, jnp.int32(nx))
    oz, rest = lax.rem(rest, jnp.int32(nz)), lax.div(rest, jnp.int32(nz))
    oc, oy = lax.rem(rest, jnp.int32(nc)), lax.div(rest, jnp.int32(nc))
    cell = (((oc ^ c) * nz + (oz ^ z)) * (ny * nx) + ((oy * nx + ox) ^ line)) * cap + slot
    own = routed // members
    cells = [cell[b * own : (b + 1) * own] for b in range(members)]
    for b, block in enumerate(xor_order(cells, where[3])):
        lanes = lax.broadcasted_iota(jnp.int32, (own, spread.shape[1]), 1)
        spread[b * own : (b + 1) * own] = (block == lanes).astype(F32).astype(BF16)


def kept_pairs(member, routed, own):
    down = lax.broadcasted_iota(jnp.int32, (routed, routed), 0)
    across = lax.broadcasted_iota(jnp.int32, (routed, routed), 1)
    shift = own.bit_length() - 1
    first = ((down >> shift) ^ member) * own + (down & (own - 1))
    second = ((across >> shift) ^ member) * own + (across & (own - 1))
    return second <= first


def probabilities(queries, keys, kept):
    scores = jnp.where(kept, mm(queries, keys, NT) * HDIM ** (-0.5), neg_large)
    top = jnp.max(scores, 1, keepdims=True)
    probs = jnp.where(kept, jnp.exp(scores - top), 0.0)
    return probs, jnp.sum(probs, 1, keepdims=True)


def inverse_rms(values):
    return lax.rsqrt(jnp.mean(values * values, 1, keepdims=True) + epsilon)


def line_rows(blocks, start, out):
    half = out.shape[1] // 2
    size = out.shape[0] // blocks.shape[0]
    for q in range(blocks.shape[0]):
        for j in range(2):
            piece = blocks[q, start + j * size : start + (j + 1) * size]
            out[q * size : (q + 1) * size, j * half : (j + 1) * half] = piece


def own_order_rows(where, blocks, dims, out):
    ny, members, nx, rows = dims
    for k, block in enumerate(blocks):
        line = where[2] ^ k
        y, x = lax.div(line, jnp.int32(nx)), lax.rem(line, jnp.int32(nx))
        for g in range(members):
            to = pl.multiple_of(((y * members + g) * nx + x) * rows, rows)
            out[pl.ds(to, rows)] = block[g * rows : (g + 1) * rows, :]


def natural_rows(blocks, dims, first, count, out):
    ny, members, nx, rows = dims
    for y in range(ny):
        for g in range(members):
            for x in range(nx):
                to = ((y * members + g) * nx + x) * rows
                piece = blocks[y * nx + x, g * rows : (g + 1) * rows, first : first + count]
                out[to : to + rows] = piece


def compact_kernel(spread, *refs):
    *blocks, picked_o, own_o, cot_o = refs
    hot = spread[...]
    half = blocks[0].shape[0] // 2
    picked = mm(hot, jnp.concatenate([b[:half] for b in blocks], 0)).astype(BF16)
    picked_o[...] = picked
    own_o[...] = picked[: own_o.shape[0]]
    cot_o[...] = mm(hot, jnp.concatenate([b[half:] for b in blocks], 0)).astype(BF16)


def attention_kernel(dims, members, where, picked_r, qkv_blocks, *outs):
    ny, nx, rows = dims
    normed_o, w_o, wo_o, vecs_o = outs[:4]
    joined_o, att_o, exact_o, near_o, far_o, vec_s = outs[4:]
    heads = ny
    cols = 3 * heads * HDIM
    routed, width = picked_r.shape
    own = routed // members
    picked = picked_r[...].astype(F32)
    natural_rows(qkv_blocks, (ny, members, nx, rows), 0, cols, w_o)
    natural_rows(qkv_blocks, (ny, members, nx, rows), cols, 128, vec_s)
    line_rows(qkv_blocks, members * rows, wo_o)
    vecs = mm(eye_rows(), vec_s[...], NT)
    vecs_o[...] = vecs
    normed = (picked * inverse_rms(picked) * vecs[0:1]).astype(BF16)
    normed_o[...] = normed
    joined = mm(normed, w_o[...]).astype(BF16)
    joined_o[...] = joined
    kept = kept_pairs(where[3], routed, own)
    parts = []
    for h in range(heads):
        queries, keys, values = (
            joined[:, (t * heads + h) * HDIM : (t * heads + h + 1) * HDIM] for t in range(3)
        )
        probs, total = probabilities(queries, keys, kept)
        parts.append(mm(probs.astype(BF16), values) / total)
    exact = jnp.concatenate(parts, 1)
    exact_o[...] = exact
    attended = exact.astype(BF16)
    att_o[...] = attended
    branch = mm(attended, wo_o[...]).astype(BF16)
    put_halves(branch, near_o, far_o)


def put_halves(values, near, far):
    depth, own = near.shape[:2]
    for k in range(depth):
        near[k] = values[k * own : (k + 1) * own]
        far[k] = values[(depth + k) * own : (depth + k + 1) * own]


def update_kernel(dims, where, picked, vecs, cot_r, *refs):
    lines, start = dims
    *refs, gate_o, first_o, d_result_o, d_active_o, w_o = refs
    ups, downs = refs[:lines], refs[lines:]
    logit = jnp.sum(picked[...].astype(F32) * vecs[2:3, :], 1, keepdims=True)
    gate = 1.0 / (1.0 + jnp.exp(-logit))
    gate_o[...] = gate
    cot = cot_r[...]
    first_o[...] = cot[: first_o.shape[0]]
    d_result = (gate * cot.astype(F32)).astype(BF16)
    d_result_o[...] = d_result
    half = w_o.shape[1] // 2
    size = w_o.shape[0] // lines
    for down in downs:
        for q in range(lines):
            w_o[q * size : (q + 1) * size, :half] = down[q]
    for k, block in enumerate(ups):
        to = pl.ds(pl.multiple_of((where[2] ^ k) * size, size), size)
        if not downs:
            w_o[to, :half] = block[start : start + size]
        w_o[to, half:] = block[block.shape[0] - size :]
    d_active_o[...] = mm(d_result, w_o[...], NT)


def hidden_kernel(picked, vecs, *refs):
    *terms, hidden_o, normed_o = refs
    hidden = picked[...].astype(F32) + add_up(terms)
    hidden_o[...] = hidden
    normed_o[...] = (hidden * inverse_rms(hidden) * vecs[1:2, :]).astype(BF16)


def forward_kernel(dims, members, where, d_active, *refs):
    lines = dims[0] * dims[2]
    ups, refs = refs[:lines], refs[lines:]
    blocks, (active_o, d_upper_o, near_o, far_o, w_s) = refs[:members], refs[members:]
    own_order_rows(where, ups, dims, w_s)
    normed = jnp.concatenate([b[...] for b in blocks], 0)
    upper = mm(normed, w_s[...])
    below = 0.5 * (1.0 + lax.erf(upper * (0.5**0.5)))
    active_o[...] = (upper * below).astype(BF16)
    slope = below + upper * jnp.exp(-0.5 * upper * upper) * ((2.0 * math.pi) ** -0.5)
    d_upper = (d_active[...] * slope).astype(BF16)
    d_upper_o[...] = d_upper
    put_halves(mm(d_upper, w_s[...], NT).astype(BF16), near_o, far_o)


def ff_grads_kernel(dims, members, where, active, d_upper, d_result, *refs):
    ny, nx, rows, ff_rows = dims
    blocks, (keep, send, down, up) = refs[:members], refs[members:]
    normed = jnp.concatenate([b[...] for b in blocks], 0)
    down[...] = mm(active[...], d_result[...], TN).astype(BF16)
    up[...] = mm(normed, d_upper[...], TN).astype(BF16)
    wide = up.shape[1]
    each = ff_rows + members * rows // 2
    for k in range(ny * nx):
        line = where[2] ^ k
        out, start = (keep, send)[k % 2], (k // 2) * each
        y, x = lax.div(line, jnp.int32(nx)), lax.rem(line, jnp.int32(nx))
        piece = down[pl.ds(pl.multiple_of(line * ff_rows, ff_rows), ff_rows)]
        out[start : start + ff_rows] = piece
        for g in range(members):
            at = pl.multiple_of(((y * members + g) * nx + x) * rows, rows)
            half, row = divmod(g * rows, members * rows // 2)
            to = start + ff_rows + row
            out[to : to + rows, half * wide : (half + 1) * wide] = up[pl.ds(at, rows)]


def add_halves_kernel(keep, got, mine, send):
    half = mine.shape[0]
    mine[...] = keep[:half].astype(F32) + got[:half].astype(F32)
    send[...] = (keep[half:].astype(F32) + got[half:].astype(F32)).astype(BF16)


def result_kernel(active, attended, w_down, w_out, cot, gate, spread, logit_o, near_o, far_o):
    combined = mm(active[...], w_down[...]) + mm(attended[...], w_out[...])
    logit = jnp.sum(cot[...].astype(F32) * combined, 1, keepdims=True)
    logit_o[...] = logit * gate[...] * (1.0 - gate[...])
    update = (gate[...] * combined).astype(BF16)
    put_halves(mm(spread[...], update, TN).astype(BF16), near_o, far_o)


def hidden_back_kernel(own, hidden_r, vecs, gate, cot, *refs):
    *terms, d_branch_o, d_hidden_o, gain_o = refs
    d_normed = add_up(terms)
    hidden = hidden_r[...]
    inv = inverse_rms(hidden)
    u = d_normed * vecs[1:2, :]
    d_hidden = inv * u - hidden * (inv * inv * inv * jnp.mean(u * hidden, 1, keepdims=True))
    d_hidden_o[...] = d_hidden
    gain_o[...] = (d_normed * hidden * inv).astype(BF16)
    d_update = gate[:own, :] * cot[...].astype(F32)
    d_branch_o[...] = (d_update + d_hidden).astype(BF16)


def attention_back_kernel(members, where, *refs):
    w_out, joined_r, exact_r, w, vecs, picked_r, logit, d_hidden, spread = refs[:9]
    blocks = refs[9 : 9 + members]
    near_o, far_o, d_joined_o, gain_o = refs[9 + members :]
    routed, width = picked_r.shape
    own = routed // members
    heads = joined_r.shape[1] // (3 * HDIM)
    d_branch = jnp.concatenate([b[...] for b in blocks], 0)
    d_attended = mm(d_branch, w_out[...], NT).astype(BF16)
    joined = joined_r[...]
    exact = exact_r[...]
    kept = kept_pairs(where[3], routed, own)
    grads = [[], [], []]
    for h in range(heads):
        queries, keys, values = (
            joined[:, (t * heads + h) * HDIM : (t * heads + h + 1) * HDIM] for t in range(3)
        )
        probs, total = probabilities(queries, keys, kept)
        d_att = d_attended[:, h * HDIM : (h + 1) * HDIM]
        d_wide = d_att.astype(F32)
        delta = jnp.sum(d_wide * exact[:, h * HDIM : (h + 1) * HDIM], 1, keepdims=True)
        d_scores = (probs / total * (mm(d_att, values, NT) - delta)).astype(BF16)
        grads[0].append(mm(d_scores, keys) * HDIM ** (-0.5))
        grads[1].append(mm(d_scores, queries, TN) * HDIM ** (-0.5))
        grads[2].append(mm(probs.astype(BF16), (d_wide / total).astype(BF16), TN))
    d_joined = jnp.concatenate(grads[0] + grads[1] + grads[2], 1).astype(BF16)
    d_joined_o[...] = d_joined
    d_normed = mm(d_joined, w[...], NT)
    picked = picked_r[...].astype(F32)
    inv = inverse_rms(picked)
    gain_o[...] = (d_normed * picked * inv).astype(BF16)
    v = d_normed * vecs[0:1, :]
    d_picked = inv * v - picked * (inv * inv * inv * jnp.mean(v * picked, 1, keepdims=True))
    d_picked = d_picked + logit[...] * vecs[2:3, :]
    first = d_picked[:own] + d_hidden[...]
    d_picked = jnp.concatenate([first, d_picked[own:]], 0).astype(BF16)
    put_halves(mm(spread[...], d_picked, TN).astype(BF16), near_o, far_o)


def grads_kernel(dims, members, where, normed, d_joined, attended, gain_a, gain_m, *refs):
    ny, nx, rows = dims
    lines = ny * nx
    picked, logit, refs = refs[0], refs[1], refs[2:]
    blocks, sums, (main, vec_s, out) = refs[:members], refs[members : members + lines], refs[-3:]
    cols = d_joined.shape[1]
    routed, width = normed.shape
    own = gain_m.shape[0]
    main[...] = mm(normed[...], d_joined[...], TN).astype(BF16)
    lanes = lax.broadcasted_iota(jnp.int32, (routed, 128), 1)

    def lane(k, count):
        return (lanes[:count] == k).astype(F32)

    vec = mm(gain_a[...], lane(0, routed).astype(BF16), TN)
    vec = vec + mm(gain_m[...], lane(1, own).astype(BF16), TN)
    high = logit[...].astype(BF16)
    low = (logit[...] - high.astype(F32)).astype(BF16)
    vec = vec + mm(picked[...], (lane(2, routed) * high.astype(F32)).astype(BF16), TN)
    vec = vec + mm(picked[...], (lane(2, routed) * low.astype(F32)).astype(BF16), TN)
    vec_s[...] = vec.astype(BF16)
    out[...] = mm(attended[...], jnp.concatenate([b[...] for b in blocks], 0), TN).astype(BF16)
    for k in range(lines):
        line = where[2] ^ k
        y, x = lax.div(line, jnp.int32(nx)), lax.rem(line, jnp.int32(nx))
        for g in range(members):
            at = pl.multiple_of(((y * members + g) * nx + x) * rows, rows)
            sums[k][g * rows : (g + 1) * rows, :cols] = main[pl.ds(at, rows)]
            sums[k][g * rows : (g + 1) * rows, cols:] = vec_s[pl.ds(at, rows)]
        half, end = width // 2, members * rows
        at = pl.multiple_of(line * rows, rows)
        for j in range(2):
            piece = out[pl.ds(at, rows), j * half : (j + 1) * half]
            sums[k][end + j * rows : end + (j + 1) * rows, :] = piece


def join_slots_kernel(cap, lines, *refs):
    terms, outs = refs[:-lines], refs[-lines:]
    total = add_up(terms).astype(BF16)
    for j in range(2):
        for k in range(lines):
            at = (j * lines + k) * cap
            outs[k][j * cap : (j + 1) * cap] = total[at : at + cap]


def place_kernel(cap, lines, where, pick, tokens, cot, *refs):
    blocks, (out_o, grad_o, got) = refs[:lines], refs[lines:]
    for k, block in enumerate(blocks):
        got[where[2] ^ k] = block[...]
    for s in range(tokens.shape[0]):
        hot = pick[s]
        out_o[s] = (tokens[s].astype(F32) + mm(hot, got[s, :cap], TN)).astype(BF16)
        grad_o[s] = (cot[s].astype(F32) + mm(hot, got[s, cap:], TN)).astype(BF16)


def line_sums_kernel(dims, where, mine, got, *refs):
    members, rows, ff_rows = dims
    *parts, near_o, far_o, out_o, down_o, send = refs
    cols = parts[0].shape[1]
    wide = mine.shape[1] // 2
    ff = mine[...] + got[...].astype(F32)
    up = ff[ff_rows:]
    main = parts[0][...].astype(F32)
    for part in parts[1:]:
        main = main + part[...].astype(F32)
    for g in range(members):
        send[g, :, :cols] = main[g * rows : (g + 1) * rows].astype(BF16)
        half, row = divmod(g * rows, members * rows // 2)
        piece = up[row : row + rows, half * wide : (half + 1) * wide]
        send[g, :, cols:] = piece.astype(BF16)
    depth = near_o.shape[0]
    for k in range(depth):
        near_o[k] = send[where[3] ^ k]
        far_o[k] = send[where[3] ^ (depth + k)]
    end = members * rows
    out_o[...] = jnp.concatenate([main[end : end + rows], main[end + rows :]], 1)
    down_o[...] = ff[:ff_rows]


def pair_kernel(near, far, *outs):
    rows = near.shape[1]
    for k, out in enumerate(outs):
        out[:rows] = near[k]
        out[rows:] = far[k]


def unpack_kernel(dims, where, *refs):
    ny, members, nx, ff_rows = dims
    depth = members // 2
    pairs, (qkv_o, up_o, *vec_o, got) = refs[:depth], refs[depth:]
    rows = got.shape[1]
    for k, pair in enumerate(pairs):
        got[where[3] ^ k] = pair[:rows]
        got[where[3] ^ (depth + k)] = pair[rows:]
    cols = 3 * ny * HDIM
    for t in range(3):
        for y in range(ny):
            from_ = (t * ny + y) * HDIM
            row = [got[g, :, from_ : from_ + HDIM] for g in range(members)]
            at = (t * HEADS + y * members) * HDIM
            qkv_o[:, at : at + members * HDIM] = jnp.concatenate(row, 1).astype(F32)
    for y in range(ny):
        for g in range(members):
            for x in range(nx):
                at = ((y * members + g) * nx + x) * ff_rows
                from_ = cols + 128 + (y * nx + x) * ff_rows
                up_o[:, at : at + ff_rows] = got[g, :, from_ : from_ + ff_rows].astype(F32)
    vec = got[0, :, cols : cols + 128].astype(F32)
    for g in range(1, members):
        vec = vec + got[g, :, cols : cols + 128].astype(F32)
    high = vec.astype(BF16)
    low = (vec - high.astype(F32)).astype(BF16)
    vec = mm(eye_rows(), high, NT) + mm(eye_rows(), low, NT)
    for k, out in enumerate(vec_o):
        out[...] = vec[k : k + 1]


def grouped(
    tokens, chosen, w_qkv, w_out, w_up, w_down, gain_attn, gain_mlp, router, cotangent
):
    ny, nc, nz, nx = (lax.axis_size(a) for a in ("y", "c", "z", "x"))
    y, c, z, x = (lax.axis_index(a) for a in ("y", "c", "z", "x"))
    seq_count, seg_len, width = tokens.shape
    cap = seg_len // 4
    routed = chosen.shape[1]
    members, lines = nc * nz, ny * nx
    member, line = c * nz + z, y * nx + x
    shard = ((y * nc + c) * nz + z) * nx + x
    rows, ff_rows = w_qkv.shape[0], w_down.shape[0]
    heads = HEADS // members
    own = routed // members
    cols, wide = 3 * heads * HDIM, lines * ff_rows
    where = jnp.stack([c, z, line, member, shard]).astype(jnp.int32)
    chosen_t = chosen.T
    block = (own, width)
    slot_block = (2 * cap, width)
    halves = [((nz, own, width), BF16)] * 2
    slot_halves = [((nz, lines * cap, width), BF16)] * 2

    pick, *picked_rows = local_call(
        partial(pick_kernel, cap),
        [Far(((seq_count, cap, seg_len), BF16))] + [(slot_block, BF16)] * lines,
        (where, chosen_t, tokens, cotangent),
        scratch=[pltpu.VMEM((seq_count, 2 * cap, width), BF16)],
        scalars=1,
    )
    line_slots = picked_rows[:1] + send_lines(picked_rows[1:])
    (hot,) = local_call(
        partial(spread_kernel, (ny, nc, nz, nx, seg_len, cap)),
        [Far(((routed, members * lines * cap), BF16))],
        (where, chosen, chosen_t),
        scalars=1,
    )
    spread = Far(hot)
    (line_slots,) = local_call(
        partial(stack_kernel, cap), [((2 * lines * cap, width), BF16)], line_slots, after=(hot,)
    )
    slots = gather_group([line_slots])

    vecs = [v.reshape(1, rows) for v in (gain_attn, gain_mlp, router)]
    (columns,) = local_call(
        partial(columns_kernel, (ny, members, nx, ff_rows)),
        [((members, rows, cols + 128 + wide), BF16)],
        tuple(Far(v) for v in (w_qkv, w_up, *vecs)),
        scratch=[pltpu.VMEM((8, rows), F32)],
    )
    got_cols = lax.all_to_all(columns, ("c", "z"), 0, 0, tiled=True)
    half = width // 2
    base = members * rows + 2 * rows
    first, up = local_call(
        relay_kernel,
        [
            Far(((lines, base + ff_rows, half), BF16)),
            ((members * rows + ff_rows, half), BF16),
        ],
        (got_cols, w_out, w_down),
        after=(line_slots,),
    )
    first = lax.all_to_all(first, ("y", "x"), 0, 0, tiled=True)
    got_down = (Far(first, base, ff_rows, 1),)
    got_up = gather_lines(up)

    picked, picked_own, cot = local_call(
        compact_kernel,
        [((routed, width), BF16), (block, BF16), ((routed, width), BF16)],
        (spread, *slots),
    )
    normed, full_qkv, full_out, full_vecs, joined, attended, exact, near, far = local_call(
        partial(attention_kernel, (ny, nx, rows), members),
        [
            ((routed, width), BF16),
            ((width, cols), BF16),
            ((heads * HDIM, width), BF16),
            ((8, width), F32),
            ((routed, cols), BF16),
            ((routed, heads * HDIM), BF16),
            ((routed, heads * HDIM), F32),
        ]
        + halves,
        (where, picked, Far(first, 0, base, 1)),
        scratch=[pltpu.VMEM((width, 128), BF16)],
        scalars=1,
    )
    terms = scatter_group(near, far)
    gate, cot_own, d_result, d_active, full_down = local_call(
        partial(update_kernel, (lines, members * rows)),
        [
            ((routed, 1), F32),
            (block, BF16),
            ((routed, width), BF16),
            ((routed, wide), F32),
            ((wide, width), BF16),
        ],
        (where, picked, full_vecs, cot, *got_up, *got_down),
        scalars=1,
    )
    hidden, normed_own = local_call(
        hidden_kernel,
        [(block, F32), (block, BF16)],
        (picked_own, full_vecs, *terms),
    )
    normed_mlp = gather_group([normed_own])

    active, d_upper, near, far = local_call(
        partial(forward_kernel, (ny, members, nx, rows), members),
        [((routed, wide), BF16)] * 2 + halves,
        (where, d_active, *got_up, *normed_mlp),
        scratch=[pltpu.VMEM((width, wide), BF16)],
        scalars=1,
    )
    terms = scatter_group(near, far)
    half_rows = 2 * (ff_rows + members * rows // 2)
    ff_keep, ff_send = local_call(
        partial(ff_grads_kernel, (ny, nx, rows, ff_rows), members),
        [((half_rows, width), BF16)] * 2,
        (where, active, d_upper, d_result, *normed_mlp),
        scratch=[pltpu.VMEM((wide, width), BF16), pltpu.VMEM((width, wide), BF16)],
        scalars=1,
    )
    ff_got = lax.ppermute(ff_send, "x", flips(nx)[1])
    logit, up_near, up_far = local_call(
        result_kernel,
        [((routed, 1), F32)] + slot_halves,
        (active, attended, full_down, full_out, cot, gate, spread),
    )
    d_branch_own, d_hidden, gain_m = local_call(
        partial(hidden_back_kernel, own),
        [(block, BF16), (block, F32), (block, BF16)],
        (hidden, full_vecs, gate, cot_own, *terms),
        after=(ff_send, logit),
    )
    d_branch = gather_group([d_branch_own])
    up_far = send_c(up_far)
    ff_mine, ff_send = local_call(
        add_halves_kernel,
        [((half_rows // 2, width), F32), ((half_rows // 2, width), BF16)],
        (ff_keep, ff_got),
    )
    ff_got = lax.ppermute(ff_send, "y", flips(ny)[1])

    near, far, d_joined, gain_a = local_call(
        partial(attention_back_kernel, members),
        slot_halves + [((routed, cols), BF16), ((routed, width), BF16)],
        (where, full_out, joined, exact, full_qkv, full_vecs, picked)
        + (logit, d_hidden, spread, *d_branch),
        scalars=1,
    )
    far = send_c(far)
    parts = local_call(
        partial(grads_kernel, (ny, nx, rows), members),
        [((members * rows + 2 * rows, cols + 128), BF16)] * lines,
        (where, normed, d_joined, attended, gain_a, gain_m, picked, logit, *d_branch),
        scratch=[
            pltpu.VMEM((width, cols), BF16),
            pltpu.VMEM((width, 128), BF16),
            pltpu.VMEM((heads * HDIM, width), BF16),
        ],
        scalars=1,
    )
    parts = parts[:1] + send_lines(parts[1:])
    both_slots = (2 * lines * cap, width)
    mine, *low = local_call(
        slot_sum_kernel,
        [(both_slots, F32)] + [(both_slots, BF16)] * (nz - 1),
        (up_near, up_far, near, far),
        after=(ff_mine,),
    )
    back_rows = local_call(
        partial(join_slots_kernel, cap, lines),
        [(slot_block, BF16)] * lines,
        [mine] + send_z(low),
    )
    back_rows = back_rows[:1] + send_lines(back_rows[1:])
    row_width = cols + 128 + wide
    near, far, grad_out, grad_down = local_call(
        partial(line_sums_kernel, (members, rows, ff_rows)),
        [((nz, rows, row_width), BF16)] * 2 + [((rows, width), F32), ((ff_rows, width), F32)],
        (where, ff_mine, ff_got, *parts),
        scratch=[pltpu.VMEM((members, rows, row_width), BF16)],
        scalars=1,
        after=back_rows[:1],
    )
    pairs = local_call(pair_kernel, [((2 * rows, row_width), BF16)] * nz, (near, send_c(far)))
    pairs = pairs[:1] + send_z(pairs[1:])
    output, grad_tokens = local_call(
        partial(place_kernel, cap, lines),
        [(tokens.shape, BF16), (tokens.shape, BF16)],
        (where, Far(pick), tokens, cotangent, *back_rows),
        scratch=[pltpu.VMEM((seq_count, 2 * cap, width), BF16)],
        scalars=1,
    )
    grad_qkv, grad_up, *grad_vecs = local_call(
        partial(unpack_kernel, (ny, members, nx, ff_rows)),
        [(w_qkv.shape, F32), (w_up.shape, F32)] + [((1, rows), F32)] * 3,
        (where, *pairs),
        scratch=[pltpu.VMEM((members, rows, row_width), BF16)],
        scalars=1,
    )
    return (
        output,
        grad_tokens,
        grad_qkv,
        grad_out,
        grad_up,
        grad_down,
        *(v.reshape(rows) for v in grad_vecs),
    )


def fits(mesh):
    head_count, block_count = mesh.devices.shape
    members = (head_count // 2) * (block_count // 2)
    power = members & (members - 1) == 0
    return power and head_count == 4 and HEADS == 2 * members


def solution(mesh):
    if fits(mesh):
        head_count, block_count = mesh.devices.shape
        devices = mesh.devices.reshape(2, head_count // 2, block_count // 2, 2)
        mesh = jax.sharding.Mesh(devices, ("y", "c", "z", "x"))
        body, all_axes = grouped, ("y", "c", "z", "x")
    else:
        body, all_axes = shards, ("head", "blk")
    seqs, mats, vecs = P(None, all_axes, None), P(all_axes, None), P(all_axes)
    in_specs = (seqs, P(), mats, mats, mats, mats, vecs, vecs, vecs, seqs)
    out_specs = (seqs, seqs, mats, mats, mats, mats, vecs, vecs, vecs)
    return jax.shard_map(body, mesh=mesh, in_specs=in_specs, out_specs=out_specs, check_vma=False)
```

```python
import math
from functools import partial

import jax
import jax.numpy as jnp
from jax import lax
from jax.experimental import pallas as pl
from jax.experimental.pallas import tpu as pltpu
from jax.sharding import PartitionSpec as P

HEADS = 16
HDIM = 64


epsilon = 1e-06
neg_large = -1e30


def rms_norm(values, gain_vec):
    inverse_rms = lax.rsqrt(jnp.mean(values * values, axis=-1, keepdims=True) + epsilon)
    return values * inverse_rms * gain_vec


def exact_gelu(values):
    return jax.nn.gelu(values, approximate=False)


def take_rows(seq_rows, row_index):
    return seq_rows[row_index]


def add_rows(seq_rows, row_index, additions):
    return seq_rows.at[row_index].add(additions)


def shards(tokens, chosen, w_qkv, w_out, w_up, w_down, gain_attn, gain_mlp, router, cotangent):
    head_count = lax.axis_size("head")
    block_count = lax.axis_size("blk")
    shard_count = head_count * block_count
    seq_count, seg_len, model_width = tokens.shape
    cap_len = seg_len // 4
    routed_count = chosen.shape[1]
    seq_len = seg_len * shard_count
    local_heads = HEADS // head_count
    slot_rows = head_count * cap_len
    scale_factor = HDIM ** (-0.5)
    head_index = lax.axis_index("head")
    block_index = lax.axis_index("blk")
    my_shard = head_index * block_count + block_index
    bounds = jnp.arange(shard_count + 1, dtype=jnp.int32) * seg_len
    before = jax.vmap(lambda chosen_row: jnp.searchsorted(chosen_row, bounds, side="left"))(chosen)
    first_index = before[:, :-1]
    shard_load = before[:, 1:] - first_index
    slot_iota = jnp.arange(cap_len, dtype=jnp.int32)
    live_table = slot_iota[None, None, :] < shard_load[:, :, None]
    lookup = jnp.minimum(first_index[:, :, None] + slot_iota[None, None, :], routed_count - 1)
    place_table = jnp.take_along_axis(
        chosen, lookup.reshape(seq_count, shard_count * cap_len), axis=1
    )
    place_table = jnp.where(
        live_table, place_table.reshape(seq_count, shard_count, cap_len), seq_len
    )
    my_positions = lax.dynamic_index_in_dim(place_table, my_shard, 1, False)
    my_live = lax.dynamic_index_in_dim(live_table, my_shard, 1, False)
    local_rows = jnp.clip(my_positions - my_shard * seg_len, 0, seg_len - 1)
    cycle_positions = place_table.reshape(seq_count, head_count, block_count, cap_len).transpose(
        0, 2, 1, 3
    )
    cycle_positions = cycle_positions.reshape(seq_count, block_count * slot_rows)
    query_positions = lax.dynamic_slice_in_dim(
        cycle_positions, block_index * slot_rows, slot_rows, 1
    )
    live_weight = my_live.astype(jnp.float32)[:, :, None]
    gathered = (
        lax.all_gather(w_qkv, ("head", "blk"), axis=0, tiled=True),
        lax.all_gather(w_out, ("head", "blk"), axis=0, tiled=True),
        lax.all_gather(w_up, ("head", "blk"), axis=0, tiled=True),
        lax.all_gather(w_down, ("head", "blk"), axis=0, tiled=True),
        lax.all_gather(gain_attn, ("head", "blk"), axis=0, tiled=True),
        lax.all_gather(gain_mlp, ("head", "blk"), axis=0, tiled=True),
        lax.all_gather(router, ("head", "blk"), axis=0, tiled=True),
    )
    full_qkv, full_out, full_up, full_down, full_gain_attn, full_gain_mlp, full_router = gathered
    picked = jax.vmap(take_rows)(tokens, local_rows)
    picked = jnp.where(my_live[:, :, None], picked, jnp.zeros_like(picked))
    picked_exact = picked.astype(jnp.float32)
    router_gate = jax.nn.sigmoid(
        jnp.einsum("scd,d->sc", picked, full_router, preferred_element_type=jnp.float32)
    )
    normed_exact, norm_attn_back = jax.vjp(
        rms_norm, picked_exact, full_gain_attn.astype(jnp.float32)
    )
    normed = normed_exact.astype(jnp.bfloat16)
    joined = jnp.einsum("scd,de->sce", normed, full_qkv, preferred_element_type=jnp.float32).astype(
        jnp.bfloat16
    )
    to_heads = lax.all_to_all(
        joined.reshape(seq_count, cap_len, 3, model_width),
        "head",
        split_axis=3,
        concat_axis=1,
        tiled=True,
    )
    queries_tok = to_heads[:, :, 0]
    queries_heads = queries_tok.reshape(seq_count, slot_rows, local_heads, HDIM)
    key_values = to_heads[:, :, 1:3]
    my_keys = key_values[:, :, 0].reshape(seq_count, slot_rows, local_heads, HDIM)
    my_values = key_values[:, :, 1].reshape(seq_count, slot_rows, local_heads, HDIM)
    stat_shape = (seq_count, local_heads, slot_rows)
    piece = lax.all_gather(key_values, "blk", axis=1, tiled=True)
    run_max = jnp.full(stat_shape, neg_large, jnp.float32)
    piece_rows = piece.shape[1]
    key_pos = cycle_positions
    keys_piece = piece[:, :, 0].reshape(seq_count, piece_rows, local_heads, HDIM)
    values_piece = piece[:, :, 1].reshape(seq_count, piece_rows, local_heads, HDIM)
    scores = (
        jnp.einsum("sqhd,skhd->shqk", queries_heads, keys_piece, preferred_element_type=jnp.float32)
        * scale_factor
    )
    allowed = key_pos[:, None, None, :] <= query_positions[:, None, :, None]
    scores = jnp.where(allowed, scores, neg_large)
    new_max = jnp.maximum(run_max, jnp.max(scores, axis=3))
    prob_block = jnp.where(allowed, jnp.exp(scores - new_max[..., None]), 0.0)
    new_total = jnp.sum(prob_block, axis=3)
    added = jnp.einsum(
        "shqk,skhd->sqhd",
        prob_block.astype(jnp.bfloat16),
        values_piece,
        preferred_element_type=jnp.float32,
    )
    attended_exact = added / new_total.transpose(0, 2, 1)[..., None]
    log_sum = new_max + jnp.log(new_total)
    attended_tok = attended_exact.astype(jnp.bfloat16).reshape(
        seq_count, slot_rows, local_heads * HDIM
    )
    attended = lax.all_to_all(attended_tok, "head", split_axis=1, concat_axis=2, tiled=True)
    branch = jnp.einsum("sce,ed->scd", attended, full_out, preferred_element_type=jnp.float32)
    hidden_state = picked_exact + branch
    normed_mlp_exact, norm_mlp_back = jax.vjp(
        rms_norm, hidden_state, full_gain_mlp.astype(jnp.float32)
    )
    normed_mlp = normed_mlp_exact.astype(jnp.bfloat16)
    upper = jnp.einsum("scd,di->sci", normed_mlp, full_up, preferred_element_type=jnp.float32)
    active_exact, gelu_back = jax.vjp(exact_gelu, upper)
    active = active_exact.astype(jnp.bfloat16)
    result = jnp.einsum("sci,id->scd", active, full_down, preferred_element_type=jnp.float32)
    combined = branch + result
    update = router_gate[:, :, None] * combined * live_weight
    output = jax.vmap(add_rows)(tokens.astype(jnp.float32), local_rows, update).astype(jnp.bfloat16)
    regathered = (
        lax.all_gather(w_qkv, ("head", "blk"), axis=0, tiled=True),
        lax.all_gather(w_out, ("head", "blk"), axis=0, tiled=True),
        lax.all_gather(w_up, ("head", "blk"), axis=0, tiled=True),
        lax.all_gather(w_down, ("head", "blk"), axis=0, tiled=True),
        lax.all_gather(gain_attn, ("head", "blk"), axis=0, tiled=True),
        lax.all_gather(gain_mlp, ("head", "blk"), axis=0, tiled=True),
        lax.all_gather(router, ("head", "blk"), axis=0, tiled=True),
    )
    back_qkv, back_out, back_up, back_down, back_gain_attn, back_gain_mlp, back_router = regathered
    picked_cot = jax.vmap(take_rows)(cotangent, local_rows).astype(jnp.float32) * live_weight
    d_update = router_gate[:, :, None] * picked_cot
    d_logit = jnp.sum(picked_cot * combined, axis=2) * router_gate * (1.0 - router_gate)
    grad_router = jnp.einsum("sc,scd->d", d_logit, picked_exact, precision=lax.Precision.HIGHEST)
    d_result = d_update.astype(jnp.bfloat16)
    d_active = jnp.einsum("scd,id->sci", d_result, back_down, preferred_element_type=jnp.float32)
    d_upper = gelu_back(d_active)[0].astype(jnp.bfloat16)
    d_normed_mlp = jnp.einsum("sci,di->scd", d_upper, back_up, preferred_element_type=jnp.float32)
    d_hidden, grad_gain_mlp = norm_mlp_back(d_normed_mlp)
    d_branch = (d_update + d_hidden).astype(jnp.bfloat16)
    d_attended = jnp.einsum(
        "scd,ed->sce", d_branch, back_out, preferred_element_type=jnp.float32
    ).astype(jnp.bfloat16)
    d_att_tok = lax.all_to_all(d_attended, "head", split_axis=2, concat_axis=1, tiled=True)
    d_att_heads = d_att_tok.reshape(seq_count, slot_rows, local_heads, HDIM)
    delta_tok = jnp.sum(d_att_heads.astype(jnp.float32) * attended_exact, axis=3)
    delta_sq = delta_tok.transpose(0, 2, 1)
    piece = lax.all_gather(key_values, "blk", axis=1, tiled=True)
    piece_rows = piece.shape[1]
    key_pos = cycle_positions
    keys_piece = piece[:, :, 0].reshape(seq_count, piece_rows, local_heads, HDIM)
    values_piece = piece[:, :, 1].reshape(seq_count, piece_rows, local_heads, HDIM)
    scores = (
        jnp.einsum("sqhd,skhd->shqk", queries_heads, keys_piece, preferred_element_type=jnp.float32)
        * scale_factor
    )
    allowed = key_pos[:, None, None, :] <= query_positions[:, None, :, None]
    prob_block = jnp.where(allowed, jnp.exp(scores - log_sum[..., None]), 0.0)
    d_prob = jnp.einsum(
        "sqhd,skhd->shqk", d_att_heads, values_piece, preferred_element_type=jnp.float32
    )
    d_scores = (prob_block * (d_prob - delta_sq[..., None])).astype(jnp.bfloat16)
    d_queries = (
        jnp.einsum("shqk,skhd->sqhd", d_scores, keys_piece, preferred_element_type=jnp.float32)
        * scale_factor
    )
    lse_tok = log_sum.transpose(0, 2, 1)
    lse_high = lse_tok.astype(jnp.bfloat16)
    lse_low = (lse_tok - lse_high.astype(jnp.float32)).astype(jnp.bfloat16)
    delta_high = delta_tok.astype(jnp.bfloat16)
    delta_low = (delta_tok - delta_high.astype(jnp.float32)).astype(jnp.bfloat16)
    query_piece = lax.all_gather(queries_tok, "blk", axis=1, tiled=True)
    dout_piece = lax.all_gather(d_att_tok, "blk", axis=1, tiled=True)
    piece_lse_high = lax.all_gather(lse_high, "blk", axis=1, tiled=True)
    piece_lse_low = lax.all_gather(lse_low, "blk", axis=1, tiled=True)
    piece_delta_high = lax.all_gather(delta_high, "blk", axis=1, tiled=True)
    piece_delta_low = lax.all_gather(delta_low, "blk", axis=1, tiled=True)
    piece_rows = query_piece.shape[1]
    query_heads = query_piece.reshape(seq_count, piece_rows, local_heads, HDIM)
    dout_heads = dout_piece.reshape(seq_count, piece_rows, local_heads, HDIM)
    piece_lse = (piece_lse_high.astype(jnp.float32) + piece_lse_low.astype(jnp.float32)).transpose(
        0, 2, 1
    )
    piece_delta = (
        piece_delta_high.astype(jnp.float32) + piece_delta_low.astype(jnp.float32)
    ).transpose(0, 2, 1)
    scores = (
        jnp.einsum("sqhd,skhd->shqk", query_heads, my_keys, preferred_element_type=jnp.float32)
        * scale_factor
    )
    allowed = query_positions[:, None, None, :] <= cycle_positions[:, None, :, None]
    prob_block = jnp.where(allowed, jnp.exp(scores - piece_lse[..., None]), 0.0)
    grad_values = jnp.einsum(
        "shqk,sqhd->skhd",
        prob_block.astype(jnp.bfloat16),
        dout_heads,
        preferred_element_type=jnp.float32,
    )
    d_prob = jnp.einsum(
        "sqhd,skhd->shqk", dout_heads, my_values, preferred_element_type=jnp.float32
    )
    d_scores = (prob_block * (d_prob - piece_delta[..., None])).astype(jnp.bfloat16)
    grad_keys = (
        jnp.einsum("shqk,sqhd->skhd", d_scores, query_heads, preferred_element_type=jnp.float32)
        * scale_factor
    )
    d_heads = jnp.stack(
        [
            d_queries.astype(jnp.bfloat16),
            grad_keys.astype(jnp.bfloat16),
            grad_values.astype(jnp.bfloat16),
        ],
        axis=2,
    )
    d_heads = d_heads.reshape(seq_count, slot_rows, 3, local_heads * HDIM)
    d_joined = lax.all_to_all(d_heads, "head", split_axis=1, concat_axis=3, tiled=True).reshape(
        seq_count, cap_len, 3 * model_width
    )
    d_normed = jnp.einsum("sce,de->scd", d_joined, back_qkv, preferred_element_type=jnp.float32)
    d_picked_norm, grad_gain_attn = norm_attn_back(d_normed)
    d_picked = (
        d_hidden
        + d_picked_norm
        + d_logit[:, :, None] * back_router.astype(jnp.float32)[None, None, :]
    )
    grad_tokens = jax.vmap(add_rows)(
        cotangent.astype(jnp.float32), local_rows, d_picked * live_weight
    ).astype(jnp.bfloat16)
    grad_qkv = jnp.einsum("scd,sce->de", normed, d_joined, preferred_element_type=jnp.float32)
    grad_out = jnp.einsum("sce,scd->ed", attended, d_branch, preferred_element_type=jnp.float32)
    grad_up = jnp.einsum("scd,sci->di", normed_mlp, d_upper, preferred_element_type=jnp.float32)
    grad_down = jnp.einsum("sci,scd->id", active, d_result, preferred_element_type=jnp.float32)
    owned = (
        lax.psum_scatter(grad_qkv, ("head", "blk"), scatter_dimension=0, tiled=True),
        lax.psum_scatter(grad_out, ("head", "blk"), scatter_dimension=0, tiled=True),
        lax.psum_scatter(grad_up, ("head", "blk"), scatter_dimension=0, tiled=True),
        lax.psum_scatter(grad_down, ("head", "blk"), scatter_dimension=0, tiled=True),
        lax.psum_scatter(grad_gain_attn, ("head", "blk"), scatter_dimension=0, tiled=True),
        lax.psum_scatter(grad_gain_mlp, ("head", "blk"), scatter_dimension=0, tiled=True),
        lax.psum_scatter(grad_router, ("head", "blk"), scatter_dimension=0, tiled=True),
    )
    return (
        output,
        grad_tokens,
        owned[0],
        owned[1],
        owned[2],
        owned[3],
        owned[4],
        owned[5],
        owned[6],
    )


F32, BF16 = jnp.float32, jnp.bfloat16
NN = (((1,), (0,)), ((), ()))
NT = (((1,), (1,)), ((), ()))
TN = (((0,), (0,)), ((), ()))


def mm(left, right, dims=NN):
    return lax.dot_general(left, right, dims, preferred_element_type=F32)


WORK = {
    "attention_back_kernel": 1200000000,
    "attention_kernel": 1200000000,
    "compact_kernel": 10000000000,
    "ff_grads_kernel": 600000000,
    "forward_kernel": 600000000,
    "grads_kernel": 500000000,
    "result_kernel": 800000000,
    "update_kernel": 800000000,
}


def work_of(body):
    return WORK.get(getattr(body, "func", body).__name__, 0)


class Far:
    def __init__(self, item, start=0, count=None, dim=0):
        self.item, self.start, self.count, self.dim = item, start, count, dim

    def shape(self):
        shape = list(self.item.shape)
        if self.count is not None:
            shape[self.dim] = self.count
        return tuple(shape)

    def source(self, ref):
        if self.count is None:
            return ref
        return ref.at[(slice(None),) * self.dim + (pl.ds(self.start, self.count),)]


class Loaded:
    def __init__(self, copy, ref):
        self.copy, self.ref, self.shape, self.waited = copy, ref, ref.shape, False

    def __getitem__(self, index):
        self.wait()
        return self.ref[index]

    def wait(self):
        if not self.waited:
            self.copy.wait()
        self.waited = True


class Stored:
    def __init__(self, copy, ref):
        self.copy, self.ref, self.shape, self.started = copy, ref, ref.shape, False

    def __getitem__(self, index):
        return self.ref[index]

    def __setitem__(self, index, value):
        self.ref[index] = value
        if index is Ellipsis:
            self.start()

    def start(self):
        if not self.started:
            self.copy.start()
        self.started = True


def local_call(body, outs, args, scratch=(), scalars=0, after=()):
    far_in = [a if isinstance(a, Far) else None for a in args]
    far_out = [isinstance(o, Far) for o in outs]
    outs = [o.item if f else o for o, f in zip(outs, far_out)]
    args = [pltpu.with_memory_space_constraint(f.item, pltpu.HBM) if f else a for a, f in zip(args, far_in)]
    shapes = [pltpu.HBM(s, d) if f else jax.ShapeDtypeStruct(s, d) for (s, d), f in zip(outs, far_out)]
    spaces = [pltpu.SMEM] * scalars
    spaces += [pltpu.HBM if f else pltpu.VMEM for f in far_in[scalars:]]
    spaces += [pl.ANY] * len(after)
    stages = []
    for f in far_in:
        if f:
            stages.append(pltpu.VMEM(f.shape(), f.item.dtype))
    stages += [pltpu.VMEM(s, d) for (s, d), f in zip(outs, far_out) if f]
    n_in, n_out, n_far = len(args), len(outs), len(stages)
    first_out = n_in + len(after)
    if n_far:
        stages.append(pltpu.SemaphoreType.DMA((n_far,)))

    def run(*refs):
        ins, results = list(refs[:n_in]), list(refs[first_out : first_out + n_out])
        rest = refs[first_out + n_out :]
        own, stage = rest[: len(scratch)], rest[len(scratch) :]
        at, loads, stores = 0, [], []
        for i, f in enumerate(far_in):
            if f:
                copy = pltpu.make_async_copy(f.source(ins[i]), stage[at], stage[-1].at[at])
                copy.start()
                ins[i] = Loaded(copy, stage[at])
                loads.append(ins[i])
                at += 1
        for i, f in enumerate(far_out):
            if f:
                copy = pltpu.make_async_copy(stage[at], results[i], stage[-1].at[at])
                results[i] = Stored(copy, stage[at])
                stores.append(results[i])
                at += 1
        body(*ins, *results, *own)
        for load in loads:
            load.wait()
        for store in stores:
            store.start()
        for store in stores:
            store.copy.wait()

    return list(
        pl.pallas_call(
            run,
            out_shape=shapes,
            in_specs=[pl.BlockSpec(memory_space=s) for s in spaces],
            out_specs=[
                pl.BlockSpec(memory_space=pltpu.HBM if f else pltpu.VMEM) for f in far_out
            ],
            scratch_shapes=list(scratch) + stages,
            compiler_params=pltpu.CompilerParams(vmem_limit_bytes=32 * 2**20),
            cost_estimate=pl.CostEstimate(
                flops=work_of(body), bytes_accessed=0, transcendentals=0
            ),
        )(*args, *after)
    )


def flips(count):
    return [[(i, i ^ k) for i in range(count)] for k in range(count)]


def send_z(blocks):
    return [lax.ppermute(b, "z", f) for b, f in zip(blocks, flips(lax.axis_size("z"))[1:])]


def send_lines(blocks):
    count = lax.axis_size("y") * lax.axis_size("x")
    return [lax.ppermute(b, ("y", "x"), f) for b, f in zip(blocks, flips(count)[1:])]


def gather_lines(own):
    return [own] + send_lines([own] * (lax.axis_size("y") * lax.axis_size("x") - 1))


def send_c(block):
    return lax.ppermute(block, "c", flips(2)[1])


def gather_group(own):
    lists = [own] + [list(t) for t in zip(*[send_z([o] * (lax.axis_size("z") - 1)) for o in own])]
    blocks = [b for one in lists for b in one]
    return blocks + [send_c(b) for b in blocks]


ORDER = [0, 1, 3, 2, 4, 5, 7, 6]


def shuffle(blocks):
    return [blocks[b] for b in ORDER]


def restore(blocks):
    return [blocks[ORDER.index(b)] for b in range(len(ORDER))]


def half_sum_kernel(near, far, mine, *low):
    for k in range(near.shape[0]):
        total = near[k].astype(F32) + far[k].astype(F32)
        if k == 0:
            mine[...] = total
        else:
            low[k - 1][...] = total.astype(BF16)


def slot_sum_kernel(*refs):
    pairs, (mine, *low) = refs[:4], refs[4:]
    size = pairs[0].shape[1]
    for j in range(2):
        near, far = pairs[2 * j], pairs[2 * j + 1]
        rows = slice(j * size, (j + 1) * size)
        for k in range(near.shape[0]):
            total = near[k].astype(F32) + far[k].astype(F32)
            if k == 0:
                mine[rows] = total
            else:
                low[k - 1][rows] = total.astype(BF16)


def scatter_group(near, far, after=()):
    depth, rows, lanes = near.shape
    outs = [((rows, lanes), F32)] + [((rows, lanes), BF16)] * (depth - 1)
    mine, *low = local_call(half_sum_kernel, outs, (near, send_c(far)), after=after)
    return [mine] + send_z(low)


def add_up(refs):
    total = refs[0][...]
    for ref in refs[1:]:
        total = total + ref[...].astype(F32)
    return total


def xor_order(blocks, index):
    step = 1
    while step < len(blocks):
        swap = (index & step) != 0
        blocks = [jnp.where(swap, blocks[b ^ step], blocks[b]) for b in range(len(blocks))]
        step *= 2
    return blocks


def columns_kernel(dims, w_qkv, w_up, gain_attn, gain_mlp, router, out, vec_s):
    ny, members, nx, ff_rows = dims
    cols = 3 * ny * HDIM
    vec_s[...] = jnp.zeros_like(vec_s)
    for k, vec in enumerate((gain_attn, gain_mlp, router)):
        vec_s[k : k + 1] = vec[...].astype(F32)
    vecs = mm(vec_s[...].astype(BF16), eye_rows(), TN).astype(BF16)
    for g in range(members):
        parts = []
        for t in range(3):
            for y in range(ny):
                at = (t * HEADS + y * members + g) * HDIM
                parts.append(w_qkv[:, at : at + HDIM])
        out[g, :, :cols] = jnp.concatenate(parts, 1)
        out[g, :, cols : cols + 128] = vecs
        for y in range(ny):
            for x in range(nx):
                at = ((y * members + g) * nx + x) * ff_rows
                to = cols + 128 + (y * nx + x) * ff_rows
                out[g, :, to : to + ff_rows] = w_up[:, at : at + ff_rows]


def eye_rows():
    down = lax.broadcasted_iota(jnp.int32, (8, 128), 0)
    return (down == lax.broadcasted_iota(jnp.int32, (8, 128), 1)).astype(F32).astype(BF16)


def pick_kernel(cap, where, chosen_t, tokens, cot, pick, *refs):
    *outs, rows = refs
    seq_count, seg_len = tokens.shape[:2]
    base = where[4] * seg_len
    places = base + lax.broadcasted_iota(jnp.int32, (chosen_t.shape[0], seg_len), 1)
    slots = lax.broadcasted_iota(jnp.int32, (cap, seg_len), 0)
    for s in range(seq_count):
        at = chosen_t[:, s : s + 1]
        present = jnp.sum((at == places).astype(F32), 0, keepdims=True)
        rank = jnp.sum(((at >= base) & (at < places)).astype(F32), 0, keepdims=True)
        hot = jnp.where(rank.astype(jnp.int32) == slots, present, 0.0).astype(BF16)
        pick[s] = hot
        rows[s, :cap] = mm(hot, tokens[s]).astype(BF16)
        rows[s, cap:] = mm(hot, cot[s]).astype(BF16)
    for k, out in enumerate(outs):
        out[...] = rows[where[2] ^ k]


def stack_kernel(cap, *refs):
    *blocks, out = refs
    for k, block in enumerate(blocks):
        for j in range(2):
            to = (j * len(blocks) + k) * cap
            out[to : to + cap] = block[j * cap : (j + 1) * cap]


def eye_tile():
    down = lax.broadcasted_iota(jnp.int32, (16, 128), 0)
    return (down == lax.broadcasted_iota(jnp.int32, (16, 128), 1)).astype(F32).astype(BF16)


def relay_kernel(got, w_out, w_down, first, up):
    members, rows, lanes = got.shape
    half = lanes // 2
    cols = half - 128
    straight = members * cols // half
    fold, end = (members - straight) * rows, straight * rows
    vec = [mm(eye_tile(), got[g, :, cols:half], NT) for g in range(members)]
    vec = jnp.concatenate(vec, 1).astype(BF16)
    size = w_out.shape[0]
    for line in range(first.shape[0]):
        first[line, :end, :cols] = got[:straight, :, :cols].reshape(end, cols)
        for j in range(cols // 128):
            piece = got[straight:, :, j * 128 : (j + 1) * 128].reshape(fold, 128)
            first[line, j * fold : (j + 1) * fold, cols:] = piece
        for j in range(2):
            to = end + j * size
            first[line, to : to + size] = w_out[:, j * half : (j + 1) * half]
        at = end + 2 * size
        first[line, at : at + 16, : members * rows] = vec
        first[line, at : at + 16, members * rows :] = jnp.zeros((16, half - members * rows), BF16)
        first[line, at + 16 :] = w_down[:, :half]
    up[: members * rows] = got[:, :, half:].reshape(members * rows, half)
    up[members * rows :] = w_down[:, half:]


def spread_kernel(dims, where, chosen, chosen_t, spread):
    ny, nc, nz, nx, seg_len, cap = dims
    c, z, line = where[0], where[1], where[2]
    routed = chosen_t.shape[0]
    members = nc * nz

    def owner_of(mine):
        return lax.div(mine, jnp.int32(seg_len))

    mine_col = chosen_t[:, 0:1]
    mine_row = chosen[0:1, :]
    for s in range(1, chosen.shape[0]):
        mine_col = jnp.where(line == s, chosen_t[:, s : s + 1], mine_col)
        mine_row = jnp.where(line == s, chosen[s : s + 1, :], mine_row)
    owner, owner_row = owner_of(mine_col), owner_of(mine_row)
    order = lax.broadcasted_iota(jnp.int32, (routed, routed), 0)
    other = lax.broadcasted_iota(jnp.int32, (routed, routed), 1)
    same = (owner == owner_row) & (other < order)
    slot = jnp.sum(same.astype(F32), 1, keepdims=True).astype(jnp.int32)
    ox, rest = lax.rem(owner, jnp.int32(nx)), lax.div(owner, jnp.int32(nx))
    oz, rest = lax.rem(rest, jnp.int32(nz)), lax.div(rest, jnp.int32(nz))
    oc, oy = lax.rem(rest, jnp.int32(nc)), lax.div(rest, jnp.int32(nc))
    cell = (((oc ^ c) * nz + (oz ^ z)) * (ny * nx) + ((oy * nx + ox) ^ line)) * cap + slot
    own = routed // members
    cells = [cell[b * own : (b + 1) * own] for b in range(members)]
    for b, block in enumerate(xor_order(cells, where[3])):
        lanes = lax.broadcasted_iota(jnp.int32, (own, spread.shape[1]), 1)
        spread[b * own : (b + 1) * own] = (block == lanes).astype(F32).astype(BF16)


def kept_pairs(member, routed, own):
    down = lax.broadcasted_iota(jnp.int32, (routed, routed), 0)
    across = lax.broadcasted_iota(jnp.int32, (routed, routed), 1)
    shift = own.bit_length() - 1
    first = ((down >> shift) ^ member) * own + (down & (own - 1))
    second = ((across >> shift) ^ member) * own + (across & (own - 1))
    return second <= first


def probabilities(queries, keys, kept):
    scores = jnp.where(kept, mm(queries, keys, NT) * HDIM ** (-0.5), neg_large)
    top = jnp.max(scores, 1, keepdims=True)
    probs = jnp.where(kept, jnp.exp(scores - top), 0.0)
    return probs, jnp.sum(probs, 1, keepdims=True)


def inverse_rms(values):
    return lax.rsqrt(jnp.mean(values * values, 1, keepdims=True) + epsilon)


def line_rows(blocks, start, out):
    half = out.shape[1] // 2
    size = out.shape[0] // blocks.shape[0]
    for q in range(blocks.shape[0]):
        for j in range(2):
            piece = blocks[q, start + j * size : start + (j + 1) * size]
            out[q * size : (q + 1) * size, j * half : (j + 1) * half] = piece


def own_order_rows(where, blocks, dims, out):
    ny, members, nx, rows = dims
    for k, block in enumerate(blocks):
        line = where[2] ^ k
        y, x = lax.div(line, jnp.int32(nx)), lax.rem(line, jnp.int32(nx))
        for g in range(members):
            to = pl.multiple_of(((y * members + g) * nx + x) * rows, rows)
            out[pl.ds(to, rows)] = block[g * rows : (g + 1) * rows, :]


def natural_rows(got, dims, cols, out):
    ny, members, nx, rows = dims
    straight = members * cols // (cols + 128)
    fold = (members - straight) * rows
    for y in range(ny):
        for g in range(members):
            for x in range(nx):
                q, to = y * nx + x, ((y * members + g) * nx + x) * rows
                if g < straight:
                    out[to : to + rows] = got[q, g * rows : (g + 1) * rows, :cols]
                    continue
                for j in range(cols // 128):
                    at = j * fold + (g - straight) * rows
                    out[to : to + rows, j * 128 : (j + 1) * 128] = got[q, at : at + rows, cols:]


def natural_lanes(got, dims, at):
    ny, members, nx, rows = dims
    pieces = [
        got[y * nx + x, at : at + 16, g * rows : (g + 1) * rows]
        for y in range(ny)
        for g in range(members)
        for x in range(nx)
    ]
    return jnp.concatenate(pieces, 1).astype(F32)[:8]


def compact_kernel(spread, *refs):
    *blocks, picked_o, own_o, cot_o = refs
    blocks = restore(blocks)
    hot = spread[...]
    half = blocks[0].shape[0] // 2
    picked = mm(hot, jnp.concatenate([b[:half] for b in blocks], 0)).astype(BF16)
    picked_o[...] = picked
    own_o[...] = picked[: own_o.shape[0]]
    cot_o[...] = mm(hot, jnp.concatenate([b[half:] for b in blocks], 0)).astype(BF16)


def attention_kernel(dims, members, where, picked_r, qkv_blocks, *outs):
    ny, nx, rows = dims
    normed_o, w_o, wo_o, vecs_o = outs[:4]
    joined_o, att_o, exact_o, near_o, far_o = outs[4:]
    heads = ny
    cols = 3 * heads * HDIM
    routed, width = picked_r.shape
    own = routed // members
    picked = picked_r[...].astype(F32)
    natural_rows(qkv_blocks, (ny, members, nx, rows), cols, w_o)
    end = members * rows * cols // (cols + 128)
    line_rows(qkv_blocks, end, wo_o)
    vecs = natural_lanes(qkv_blocks, (ny, members, nx, rows), end + 2 * rows)
    vecs_o[...] = vecs
    normed = (picked * inverse_rms(picked) * vecs[0:1]).astype(BF16)
    normed_o[...] = normed
    joined = mm(normed, w_o[...]).astype(BF16)
    joined_o[...] = joined
    kept = kept_pairs(where[3], routed, own)
    parts = []
    for h in range(heads):
        queries, keys, values = (
            joined[:, (t * heads + h) * HDIM : (t * heads + h + 1) * HDIM] for t in range(3)
        )
        probs, total = probabilities(queries, keys, kept)
        parts.append(mm(probs.astype(BF16), values) / total)
    exact = jnp.concatenate(parts, 1)
    exact_o[...] = exact
    attended = exact.astype(BF16)
    att_o[...] = attended
    branch = mm(attended, wo_o[...]).astype(BF16)
    put_halves(branch, near_o, far_o)


def put_halves(values, near, far):
    depth, own = near.shape[:2]
    for k in range(depth):
        near[k] = values[k * own : (k + 1) * own]
        far[k] = values[(depth + k) * own : (depth + k + 1) * own]


def update_kernel(dims, where, picked, vecs, cot_r, *refs):
    lines, start = dims
    *refs, gate_o, first_o, d_result_o, d_active_o, w_o = refs
    ups, downs = refs[:lines], refs[lines:]
    logit = jnp.sum(picked[...].astype(F32) * vecs[2:3, :], 1, keepdims=True)
    gate = 1.0 / (1.0 + jnp.exp(-logit))
    gate_o[...] = gate
    cot = cot_r[...]
    first_o[...] = cot[: first_o.shape[0]]
    d_result = (gate * cot.astype(F32)).astype(BF16)
    d_result_o[...] = d_result
    half = w_o.shape[1] // 2
    size = w_o.shape[0] // lines
    for down in downs:
        for q in range(lines):
            w_o[q * size : (q + 1) * size, :half] = down[q]
    for k, block in enumerate(ups):
        to = pl.ds(pl.multiple_of((where[2] ^ k) * size, size), size)
        if not downs:
            w_o[to, :half] = block[start : start + size]
        w_o[to, half:] = block[block.shape[0] - size :]
    d_active_o[...] = mm(d_result, w_o[...], NT)


def hidden_kernel(picked, vecs, *refs):
    *terms, hidden_o, normed_o = refs
    hidden = picked[...].astype(F32) + add_up(terms)
    hidden_o[...] = hidden
    normed_o[...] = (hidden * inverse_rms(hidden) * vecs[1:2, :]).astype(BF16)


def forward_kernel(dims, members, where, d_active, *refs):
    lines = dims[0] * dims[2]
    ups, refs = refs[:lines], refs[lines:]
    blocks, (active_o, d_upper_o, near_o, far_o, w_s) = refs[:members], refs[members:]
    own_order_rows(where, ups, dims, w_s)
    normed = jnp.concatenate([b[...] for b in restore(blocks)], 0)
    upper = mm(normed, w_s[...])
    below = 0.5 * (1.0 + lax.erf(upper * (0.5**0.5)))
    active_o[...] = (upper * below).astype(BF16)
    slope = below + upper * jnp.exp(-0.5 * upper * upper) * ((2.0 * math.pi) ** -0.5)
    d_upper = (d_active[...] * slope).astype(BF16)
    d_upper_o[...] = d_upper
    put_halves(mm(d_upper, w_s[...], NT).astype(BF16), near_o, far_o)


def ff_grads_kernel(dims, members, where, active, d_upper, d_result, *refs):
    ny, nx, rows, ff_rows = dims
    blocks, (keep, send, down, up) = refs[:members], refs[members:]
    normed = jnp.concatenate([b[...] for b in restore(blocks)], 0)
    down[...] = mm(active[...], d_result[...], TN).astype(BF16)
    up[...] = mm(normed, d_upper[...], TN).astype(BF16)
    wide = up.shape[1]
    each = ff_rows + members * rows // 2
    for k in range(ny * nx):
        line = where[2] ^ k
        out, start = (keep, send)[k % 2], (k // 2) * each
        y, x = lax.div(line, jnp.int32(nx)), lax.rem(line, jnp.int32(nx))
        piece = down[pl.ds(pl.multiple_of(line * ff_rows, ff_rows), ff_rows)]
        out[start : start + ff_rows] = piece
        for g in range(members):
            at = pl.multiple_of(((y * members + g) * nx + x) * rows, rows)
            half, row = divmod(g * rows, members * rows // 2)
            to = start + ff_rows + row
            out[to : to + rows, half * wide : (half + 1) * wide] = up[pl.ds(at, rows)]


def add_halves_kernel(keep, got, mine, send):
    half = mine.shape[0]
    mine[...] = keep[:half].astype(F32) + got[:half].astype(F32)
    send[...] = (keep[half:].astype(F32) + got[half:].astype(F32)).astype(BF16)


def result_kernel(active, attended, w_down, w_out, cot, gate, spread, logit_o, near_o, far_o):
    combined = mm(active[...], w_down[...]) + mm(attended[...], w_out[...])
    logit = jnp.sum(cot[...].astype(F32) * combined, 1, keepdims=True)
    logit_o[...] = logit * gate[...] * (1.0 - gate[...])
    update = (gate[...] * combined).astype(BF16)
    put_halves(mm(spread[...], update, TN).astype(BF16), near_o, far_o)


def hidden_back_kernel(own, hidden_r, vecs, gate, cot, *refs):
    *terms, d_branch_o, d_hidden_o, gain_o = refs
    d_normed = add_up(terms)
    hidden = hidden_r[...]
    inv = inverse_rms(hidden)
    u = d_normed * vecs[1:2, :]
    d_hidden = inv * u - hidden * (inv * inv * inv * jnp.mean(u * hidden, 1, keepdims=True))
    d_hidden_o[...] = d_hidden
    gain_o[...] = (d_normed * hidden * inv).astype(BF16)
    d_update = gate[:own, :] * cot[...].astype(F32)
    d_branch_o[...] = (d_update + d_hidden).astype(BF16)


def attention_back_kernel(members, where, *refs):
    w_out, joined_r, exact_r, w, vecs, picked_r, logit, d_hidden, spread = refs[:9]
    blocks = refs[9 : 9 + members]
    near_o, far_o, d_joined_o, gain_o = refs[9 + members :]
    routed, width = picked_r.shape
    own = routed // members
    heads = joined_r.shape[1] // (3 * HDIM)
    d_branch = jnp.concatenate([b[...] for b in restore(blocks)], 0)
    d_attended = mm(d_branch, w_out[...], NT).astype(BF16)
    joined = joined_r[...]
    exact = exact_r[...]
    kept = kept_pairs(where[3], routed, own)
    grads = [[], [], []]
    for h in range(heads):
        queries, keys, values = (
            joined[:, (t * heads + h) * HDIM : (t * heads + h + 1) * HDIM] for t in range(3)
        )
        probs, total = probabilities(queries, keys, kept)
        d_att = d_attended[:, h * HDIM : (h + 1) * HDIM]
        d_wide = d_att.astype(F32)
        delta = jnp.sum(d_wide * exact[:, h * HDIM : (h + 1) * HDIM], 1, keepdims=True)
        d_scores = (probs / total * (mm(d_att, values, NT) - delta)).astype(BF16)
        grads[0].append(mm(d_scores, keys) * HDIM ** (-0.5))
        grads[1].append(mm(d_scores, queries, TN) * HDIM ** (-0.5))
        grads[2].append(mm(probs.astype(BF16), (d_wide / total).astype(BF16), TN))
    d_joined = jnp.concatenate(grads[0] + grads[1] + grads[2], 1).astype(BF16)
    d_joined_o[...] = d_joined
    d_normed = mm(d_joined, w[...], NT)
    picked = picked_r[...].astype(F32)
    inv = inverse_rms(picked)
    gain_o[...] = (d_normed * picked * inv).astype(BF16)
    v = d_normed * vecs[0:1, :]
    d_picked = inv * v - picked * (inv * inv * inv * jnp.mean(v * picked, 1, keepdims=True))
    d_picked = d_picked + logit[...] * vecs[2:3, :]
    first = d_picked[:own] + d_hidden[...]
    d_picked = jnp.concatenate([first, d_picked[own:]], 0).astype(BF16)
    put_halves(mm(spread[...], d_picked, TN).astype(BF16), near_o, far_o)


def grads_kernel(dims, members, where, normed, d_joined, attended, gain_a, gain_m, *refs):
    ny, nx, rows = dims
    lines = ny * nx
    picked, logit, refs = refs[0], refs[1], refs[2:]
    blocks, sums, (main, vec_s, out) = refs[:members], refs[members : members + lines], refs[-3:]
    cols = d_joined.shape[1]
    routed, width = normed.shape
    own = gain_m.shape[0]
    main[...] = mm(normed[...], d_joined[...], TN).astype(BF16)
    lanes = lax.broadcasted_iota(jnp.int32, (routed, 128), 1)

    def lane(k, count):
        return (lanes[:count] == k).astype(F32)

    vec = mm(lane(0, routed).astype(BF16), gain_a[...], TN)
    vec = vec + mm(lane(1, own).astype(BF16), gain_m[...], TN)
    high = logit[...].astype(BF16)
    low = (logit[...] - high.astype(F32)).astype(BF16)
    vec = vec + mm((lane(2, routed) * high.astype(F32)).astype(BF16), picked[...], TN)
    vec = vec + mm((lane(2, routed) * low.astype(F32)).astype(BF16), picked[...], TN)
    vec_s[...] = jnp.zeros_like(vec_s)
    for y in range(ny):
        for x in range(nx):
            ats = [((y * members + g) * nx + x) * rows for g in range(members)]
            pieces = [vec[:16, at : at + rows] for at in ats]
            vec_s[y * nx + x, :, : members * rows] = jnp.concatenate(pieces, 1).astype(BF16)
    out[...] = mm(attended[...], jnp.concatenate([b[...] for b in restore(blocks)], 0), TN).astype(BF16)
    straight = members * cols // (cols + 128)
    fold = (members - straight) * rows
    half, end = width // 2, straight * rows
    for k in range(lines):
        line = where[2] ^ k
        y, x = lax.div(line, jnp.int32(nx)), lax.rem(line, jnp.int32(nx))
        for g in range(members):
            at = pl.multiple_of(((y * members + g) * nx + x) * rows, rows)
            if g < straight:
                sums[k][g * rows : (g + 1) * rows, :cols] = main[pl.ds(at, rows)]
                continue
            for j in range(cols // 128):
                to = j * fold + (g - straight) * rows
                piece = main[pl.ds(at, rows), j * 128 : (j + 1) * 128]
                sums[k][to : to + rows, cols:] = piece
        at = pl.multiple_of(line * rows, rows)
        for j in range(2):
            piece = out[pl.ds(at, rows), j * half : (j + 1) * half]
            sums[k][end + j * rows : end + (j + 1) * rows, :] = piece
        sums[k][end + 2 * rows :, :] = vec_s[line]


def join_slots_kernel(cap, lines, *refs):
    terms, outs = refs[:-lines], refs[-lines:]
    total = add_up(terms).astype(BF16)
    for j in range(2):
        for k in range(lines):
            at = (j * lines + k) * cap
            outs[k][j * cap : (j + 1) * cap] = total[at : at + cap]


def place_kernel(cap, lines, where, pick, tokens, cot, *refs):
    blocks, (out_o, grad_o, got) = refs[:lines], refs[lines:]
    for k, block in enumerate(blocks):
        got[where[2] ^ k] = block[...]
    for s in range(tokens.shape[0]):
        hot = pick[s]
        out_o[s] = (tokens[s].astype(F32) + mm(hot, got[s, :cap], TN)).astype(BF16)
        grad_o[s] = (cot[s].astype(F32) + mm(hot, got[s, cap:], TN)).astype(BF16)


def line_sums_kernel(dims, where, mine, got, *refs):
    members, rows, ff_rows = dims
    *parts, near_o, far_o, out_o, down_o, send = refs
    cols = parts[0].shape[1] - 128
    straight = members * cols // (cols + 128)
    fold = (members - straight) * rows
    end = straight * rows
    wide = mine.shape[1] // 2
    ff = mine[...] + got[...].astype(F32)
    up = ff[ff_rows:]
    main = parts[0][...].astype(F32)
    for part in parts[1:]:
        main = main + part[...].astype(F32)
    vec = main[end + 2 * rows :]
    high = vec.astype(BF16)
    low = (vec - high.astype(F32)).astype(BF16)
    down = lax.broadcasted_iota(jnp.int32, (16, 128), 0)
    eye = (down == lax.broadcasted_iota(jnp.int32, (16, 128), 1)).astype(F32).astype(BF16)
    for g in range(members):
        if g < straight:
            block = main[g * rows : (g + 1) * rows, :cols]
        else:
            tos = [j * fold + (g - straight) * rows for j in range(cols // 128)]
            block = jnp.concatenate([main[to : to + rows, cols:] for to in tos], 1)
        send[g, :, :cols] = block.astype(BF16)
        at = slice(g * rows, (g + 1) * rows)
        column = mm(high[:, at], eye, TN) + mm(low[:, at], eye, TN)
        send[g, :, cols : cols + 128] = column.astype(BF16)
        half, row = divmod(g * rows, members * rows // 2)
        piece = up[row : row + rows, half * wide : (half + 1) * wide]
        send[g, :, cols + 128 :] = piece.astype(BF16)
    depth = near_o.shape[0]
    for k in range(depth):
        near_o[k] = send[where[3] ^ k]
        far_o[k] = send[where[3] ^ (depth + k)]
    out_o[...] = jnp.concatenate([main[end : end + rows], main[end + rows : end + 2 * rows]], 1)
    down_o[...] = ff[:ff_rows]


def pair_kernel(near, far, *outs):
    rows = near.shape[1]
    for k, out in enumerate(outs):
        out[:rows] = near[k]
        out[rows:] = far[k]


def unpack_kernel(dims, where, *refs):
    ny, members, nx, ff_rows = dims
    depth = members // 2
    pairs, (qkv_o, up_o, *vec_o, got) = refs[:depth], refs[depth:]
    rows = got.shape[1]
    for k, pair in enumerate(pairs):
        got[where[3] ^ k] = pair[:rows]
        got[where[3] ^ (depth + k)] = pair[rows:]
    cols = 3 * ny * HDIM
    for t in range(3):
        for y in range(ny):
            from_ = (t * ny + y) * HDIM
            row = [got[g, :, from_ : from_ + HDIM] for g in range(members)]
            at = (t * HEADS + y * members) * HDIM
            qkv_o[:, at : at + members * HDIM] = jnp.concatenate(row, 1).astype(F32)
    for y in range(ny):
        for g in range(members):
            for x in range(nx):
                at = ((y * members + g) * nx + x) * ff_rows
                from_ = cols + 128 + (y * nx + x) * ff_rows
                up_o[:, at : at + ff_rows] = got[g, :, from_ : from_ + ff_rows].astype(F32)
    vec = got[0, :, cols : cols + 128].astype(F32)
    for g in range(1, members):
        vec = vec + got[g, :, cols : cols + 128].astype(F32)
    high = vec.astype(BF16)
    low = (vec - high.astype(F32)).astype(BF16)
    vec = mm(eye_rows(), high, NT) + mm(eye_rows(), low, NT)
    for k, out in enumerate(vec_o):
        out[...] = vec[k : k + 1]


def grouped(
    tokens, chosen, w_qkv, w_out, w_up, w_down, gain_attn, gain_mlp, router, cotangent
):
    ny, nc, nz, nx = (lax.axis_size(a) for a in ("y", "c", "z", "x"))
    y, c, z, x = (lax.axis_index(a) for a in ("y", "c", "z", "x"))
    seq_count, seg_len, width = tokens.shape
    cap = seg_len // 4
    routed = chosen.shape[1]
    members, lines = nc * nz, ny * nx
    member, line = c * nz + z, y * nx + x
    shard = ((y * nc + c) * nz + z) * nx + x
    rows, ff_rows = w_qkv.shape[0], w_down.shape[0]
    heads = HEADS // members
    own = routed // members
    cols, wide = 3 * heads * HDIM, lines * ff_rows
    where = jnp.stack([c, z, line, member, shard]).astype(jnp.int32)
    chosen_t = chosen.T
    block = (own, width)
    slot_block = (2 * cap, width)
    halves = [((nz, own, width), BF16)] * 2
    slot_halves = [((nz, lines * cap, width), BF16)] * 2

    pick, *picked_rows = local_call(
        partial(pick_kernel, cap),
        [Far(((seq_count, cap, seg_len), BF16))] + [(slot_block, BF16)] * lines,
        (where, chosen_t, tokens, cotangent),
        scratch=[pltpu.VMEM((seq_count, 2 * cap, width), BF16)],
        scalars=1,
    )
    line_slots = picked_rows[:1] + send_lines(picked_rows[1:])
    (hot,) = local_call(
        partial(spread_kernel, (ny, nc, nz, nx, seg_len, cap)),
        [Far(((routed, members * lines * cap), BF16))],
        (where, chosen, chosen_t),
        scalars=1,
    )
    spread = Far(hot)
    (line_slots,) = local_call(
        partial(stack_kernel, cap), [((2 * lines * cap, width), BF16)], line_slots, after=(hot,)
    )
    slots = gather_group([line_slots])

    vecs = [v.reshape(1, rows) for v in (gain_attn, gain_mlp, router)]
    (columns,) = local_call(
        partial(columns_kernel, (ny, members, nx, ff_rows)),
        [((members, rows, cols + 128 + wide), BF16)],
        tuple(Far(v) for v in (w_qkv, w_up, *vecs)),
        scratch=[pltpu.VMEM((8, rows), F32)],
    )
    got_cols = lax.all_to_all(columns, ("c", "z"), 0, 0, tiled=True)
    half = width // 2
    base = members * rows * cols // (cols + 128) + 2 * rows + 16
    first, up = local_call(
        relay_kernel,
        [
            Far(((lines, base + ff_rows, half), BF16)),
            Far(((members * rows + ff_rows, half), BF16)),
        ],
        (got_cols, w_out, w_down),
        after=(line_slots,),
    )
    first = lax.all_to_all(first, ("y", "x"), 0, 0, tiled=True)
    got_down = (Far(first, base, ff_rows, 1),)
    got_up = gather_lines(up)

    picked, picked_own, cot = local_call(
        compact_kernel,
        [((routed, width), BF16), (block, BF16), ((routed, width), BF16)],
        (spread, *shuffle(slots)),
    )
    normed, full_qkv, full_out, full_vecs, joined, attended, exact, near, far = local_call(
        partial(attention_kernel, (ny, nx, rows), members),
        [
            ((routed, width), BF16),
            ((width, cols), BF16),
            ((heads * HDIM, width), BF16),
            ((8, width), F32),
            ((routed, cols), BF16),
            ((routed, heads * HDIM), BF16),
            ((routed, heads * HDIM), F32),
        ]
        + halves,
        (where, picked, Far(first, 0, base, 1)),
        scalars=1,
    )
    terms = scatter_group(near, far)
    gate, cot_own, d_result, d_active, full_down = local_call(
        partial(update_kernel, (lines, members * rows)),
        [
            ((routed, 1), F32),
            (block, BF16),
            ((routed, width), BF16),
            ((routed, wide), F32),
            ((wide, width), BF16),
        ],
        (where, picked, full_vecs, cot, *got_up, *got_down),
        scalars=1,
    )
    hidden, normed_own = local_call(
        hidden_kernel,
        [(block, F32), (block, BF16)],
        (picked_own, full_vecs, *terms),
    )
    normed_mlp = gather_group([normed_own])

    active, d_upper, near, far = local_call(
        partial(forward_kernel, (ny, members, nx, rows), members),
        [((routed, wide), BF16)] * 2 + halves,
        (where, d_active, *got_up, *shuffle(normed_mlp)),
        scratch=[pltpu.VMEM((width, wide), BF16)],
        scalars=1,
    )
    terms = scatter_group(near, far)
    half_rows = 2 * (ff_rows + members * rows // 2)
    ff_keep, ff_send = local_call(
        partial(ff_grads_kernel, (ny, nx, rows, ff_rows), members),
        [((half_rows, width), BF16)] * 2,
        (where, active, d_upper, d_result, *shuffle(normed_mlp)),
        scratch=[pltpu.VMEM((wide, width), BF16), pltpu.VMEM((width, wide), BF16)],
        scalars=1,
    )
    ff_got = lax.ppermute(ff_send, "x", flips(nx)[1])
    logit, up_near, up_far = local_call(
        result_kernel,
        [((routed, 1), F32)] + slot_halves,
        (active, attended, full_down, full_out, cot, gate, spread),
    )
    d_branch_own, d_hidden, gain_m = local_call(
        partial(hidden_back_kernel, own),
        [(block, BF16), (block, F32), (block, BF16)],
        (hidden, full_vecs, gate, cot_own, *terms),
        after=(ff_send, logit),
    )
    d_branch = gather_group([d_branch_own])
    up_far = send_c(up_far)
    ff_mine, ff_send = local_call(
        add_halves_kernel,
        [((half_rows // 2, width), F32), ((half_rows // 2, width), BF16)],
        (ff_keep, ff_got),
    )
    ff_got = lax.ppermute(ff_send, "y", flips(ny)[1])

    near, far, d_joined, gain_a = local_call(
        partial(attention_back_kernel, members),
        slot_halves + [((routed, cols), BF16), ((routed, width), BF16)],
        (where, full_out, joined, exact, full_qkv, full_vecs, picked)
        + (logit, d_hidden, spread, *shuffle(d_branch)),
        scalars=1,
    )
    far = send_c(far)
    parts = local_call(
        partial(grads_kernel, (ny, nx, rows), members),
        [((members * rows * cols // (cols + 128) + 2 * rows + 16, cols + 128), BF16)] * lines,
        (where, normed, d_joined, attended, gain_a, gain_m, picked, logit, *shuffle(d_branch)),
        scratch=[
            pltpu.VMEM((width, cols), BF16),
            pltpu.VMEM((lines, 16, cols + 128), BF16),
            pltpu.VMEM((heads * HDIM, width), BF16),
        ],
        scalars=1,
    )
    parts = parts[:1] + send_lines(parts[1:])
    both_slots = (2 * lines * cap, width)
    mine, *low = local_call(
        slot_sum_kernel,
        [(both_slots, F32)] + [(both_slots, BF16)] * (nz - 1),
        (up_near, up_far, near, far),
        after=(ff_mine,),
    )
    back_rows = local_call(
        partial(join_slots_kernel, cap, lines),
        [(slot_block, BF16)] * lines,
        [mine] + send_z(low),
    )
    back_rows = back_rows[:1] + send_lines(back_rows[1:])
    row_width = cols + 128 + wide
    near, far, grad_out, grad_down = local_call(
        partial(line_sums_kernel, (members, rows, ff_rows)),
        [((nz, rows, row_width), BF16)] * 2 + [((rows, width), F32), ((ff_rows, width), F32)],
        (where, ff_mine, ff_got, *parts),
        scratch=[pltpu.VMEM((members, rows, row_width), BF16)],
        scalars=1,
        after=back_rows[:1],
    )
    pairs = local_call(pair_kernel, [((2 * rows, row_width), BF16)] * nz, (near, send_c(far)))
    pairs = pairs[:1] + send_z(pairs[1:])
    output, grad_tokens = local_call(
        partial(place_kernel, cap, lines),
        [(tokens.shape, BF16), (tokens.shape, BF16)],
        (where, Far(pick), tokens, cotangent, *back_rows),
        scratch=[pltpu.VMEM((seq_count, 2 * cap, width), BF16)],
        scalars=1,
    )
    grad_qkv, grad_up, *grad_vecs = local_call(
        partial(unpack_kernel, (ny, members, nx, ff_rows)),
        [(w_qkv.shape, F32), (w_up.shape, F32)] + [((1, rows), F32)] * 3,
        (where, *pairs),
        scratch=[pltpu.VMEM((members, rows, row_width), BF16)],
        scalars=1,
    )
    return (
        output,
        grad_tokens,
        grad_qkv,
        grad_out,
        grad_up,
        grad_down,
        *(v.reshape(rows) for v in grad_vecs),
    )


def fits(mesh):
    head_count, block_count = mesh.devices.shape
    members = (head_count // 2) * (block_count // 2)
    power = members & (members - 1) == 0
    return power and head_count == 4 and HEADS == 2 * members


def solution(mesh):
    if fits(mesh):
        head_count, block_count = mesh.devices.shape
        devices = mesh.devices.reshape(2, head_count // 2, block_count // 2, 2)
        mesh = jax.sharding.Mesh(devices, ("y", "c", "z", "x"))
        body, all_axes = grouped, ("y", "c", "z", "x")
    else:
        body, all_axes = shards, ("head", "blk")
    seqs, mats, vecs = P(None, all_axes, None), P(all_axes, None), P(all_axes)
    in_specs = (seqs, P(), mats, mats, mats, mats, vecs, vecs, vecs, seqs)
    out_specs = (seqs, seqs, mats, mats, mats, mats, vecs, vecs, vecs)
    return jax.shard_map(body, mesh=mesh, in_specs=in_specs, out_specs=out_specs, check_vma=False)
```

```python
import math
from functools import partial

import jax
import jax.numpy as jnp
from jax import lax
from jax.experimental import pallas as pl
from jax.experimental.pallas import tpu as pltpu
from jax.sharding import PartitionSpec as P

HEADS = 16
HDIM = 64


epsilon = 1e-06
neg_large = -1e30


def rms_norm(values, gain_vec):
    inverse_rms = lax.rsqrt(jnp.mean(values * values, axis=-1, keepdims=True) + epsilon)
    return values * inverse_rms * gain_vec


def exact_gelu(values):
    return jax.nn.gelu(values, approximate=False)


def take_rows(seq_rows, row_index):
    return seq_rows[row_index]


def add_rows(seq_rows, row_index, additions):
    return seq_rows.at[row_index].add(additions)


def shards(tokens, chosen, w_qkv, w_out, w_up, w_down, gain_attn, gain_mlp, router, cotangent):
    head_count = lax.axis_size("head")
    block_count = lax.axis_size("blk")
    shard_count = head_count * block_count
    seq_count, seg_len, model_width = tokens.shape
    cap_len = seg_len // 4
    routed_count = chosen.shape[1]
    seq_len = seg_len * shard_count
    local_heads = HEADS // head_count
    slot_rows = head_count * cap_len
    scale_factor = HDIM ** (-0.5)
    head_index = lax.axis_index("head")
    block_index = lax.axis_index("blk")
    my_shard = head_index * block_count + block_index
    bounds = jnp.arange(shard_count + 1, dtype=jnp.int32) * seg_len
    before = jax.vmap(lambda chosen_row: jnp.searchsorted(chosen_row, bounds, side="left"))(chosen)
    first_index = before[:, :-1]
    shard_load = before[:, 1:] - first_index
    slot_iota = jnp.arange(cap_len, dtype=jnp.int32)
    live_table = slot_iota[None, None, :] < shard_load[:, :, None]
    lookup = jnp.minimum(first_index[:, :, None] + slot_iota[None, None, :], routed_count - 1)
    place_table = jnp.take_along_axis(
        chosen, lookup.reshape(seq_count, shard_count * cap_len), axis=1
    )
    place_table = jnp.where(
        live_table, place_table.reshape(seq_count, shard_count, cap_len), seq_len
    )
    my_positions = lax.dynamic_index_in_dim(place_table, my_shard, 1, False)
    my_live = lax.dynamic_index_in_dim(live_table, my_shard, 1, False)
    local_rows = jnp.clip(my_positions - my_shard * seg_len, 0, seg_len - 1)
    cycle_positions = place_table.reshape(seq_count, head_count, block_count, cap_len).transpose(
        0, 2, 1, 3
    )
    cycle_positions = cycle_positions.reshape(seq_count, block_count * slot_rows)
    query_positions = lax.dynamic_slice_in_dim(
        cycle_positions, block_index * slot_rows, slot_rows, 1
    )
    live_weight = my_live.astype(jnp.float32)[:, :, None]
    gathered = (
        lax.all_gather(w_qkv, ("head", "blk"), axis=0, tiled=True),
        lax.all_gather(w_out, ("head", "blk"), axis=0, tiled=True),
        lax.all_gather(w_up, ("head", "blk"), axis=0, tiled=True),
        lax.all_gather(w_down, ("head", "blk"), axis=0, tiled=True),
        lax.all_gather(gain_attn, ("head", "blk"), axis=0, tiled=True),
        lax.all_gather(gain_mlp, ("head", "blk"), axis=0, tiled=True),
        lax.all_gather(router, ("head", "blk"), axis=0, tiled=True),
    )
    full_qkv, full_out, full_up, full_down, full_gain_attn, full_gain_mlp, full_router = gathered
    picked = jax.vmap(take_rows)(tokens, local_rows)
    picked = jnp.where(my_live[:, :, None], picked, jnp.zeros_like(picked))
    picked_exact = picked.astype(jnp.float32)
    router_gate = jax.nn.sigmoid(
        jnp.einsum("scd,d->sc", picked, full_router, preferred_element_type=jnp.float32)
    )
    normed_exact, norm_attn_back = jax.vjp(
        rms_norm, picked_exact, full_gain_attn.astype(jnp.float32)
    )
    normed = normed_exact.astype(jnp.bfloat16)
    joined = jnp.einsum("scd,de->sce", normed, full_qkv, preferred_element_type=jnp.float32).astype(
        jnp.bfloat16
    )
    to_heads = lax.all_to_all(
        joined.reshape(seq_count, cap_len, 3, model_width),
        "head",
        split_axis=3,
        concat_axis=1,
        tiled=True,
    )
    queries_tok = to_heads[:, :, 0]
    queries_heads = queries_tok.reshape(seq_count, slot_rows, local_heads, HDIM)
    key_values = to_heads[:, :, 1:3]
    my_keys = key_values[:, :, 0].reshape(seq_count, slot_rows, local_heads, HDIM)
    my_values = key_values[:, :, 1].reshape(seq_count, slot_rows, local_heads, HDIM)
    stat_shape = (seq_count, local_heads, slot_rows)
    piece = lax.all_gather(key_values, "blk", axis=1, tiled=True)
    run_max = jnp.full(stat_shape, neg_large, jnp.float32)
    piece_rows = piece.shape[1]
    key_pos = cycle_positions
    keys_piece = piece[:, :, 0].reshape(seq_count, piece_rows, local_heads, HDIM)
    values_piece = piece[:, :, 1].reshape(seq_count, piece_rows, local_heads, HDIM)
    scores = (
        jnp.einsum("sqhd,skhd->shqk", queries_heads, keys_piece, preferred_element_type=jnp.float32)
        * scale_factor
    )
    allowed = key_pos[:, None, None, :] <= query_positions[:, None, :, None]
    scores = jnp.where(allowed, scores, neg_large)
    new_max = jnp.maximum(run_max, jnp.max(scores, axis=3))
    prob_block = jnp.where(allowed, jnp.exp(scores - new_max[..., None]), 0.0)
    new_total = jnp.sum(prob_block, axis=3)
    added = jnp.einsum(
        "shqk,skhd->sqhd",
        prob_block.astype(jnp.bfloat16),
        values_piece,
        preferred_element_type=jnp.float32,
    )
    attended_exact = added / new_total.transpose(0, 2, 1)[..., None]
    log_sum = new_max + jnp.log(new_total)
    attended_tok = attended_exact.astype(jnp.bfloat16).reshape(
        seq_count, slot_rows, local_heads * HDIM
    )
    attended = lax.all_to_all(attended_tok, "head", split_axis=1, concat_axis=2, tiled=True)
    branch = jnp.einsum("sce,ed->scd", attended, full_out, preferred_element_type=jnp.float32)
    hidden_state = picked_exact + branch
    normed_mlp_exact, norm_mlp_back = jax.vjp(
        rms_norm, hidden_state, full_gain_mlp.astype(jnp.float32)
    )
    normed_mlp = normed_mlp_exact.astype(jnp.bfloat16)
    upper = jnp.einsum("scd,di->sci", normed_mlp, full_up, preferred_element_type=jnp.float32)
    active_exact, gelu_back = jax.vjp(exact_gelu, upper)
    active = active_exact.astype(jnp.bfloat16)
    result = jnp.einsum("sci,id->scd", active, full_down, preferred_element_type=jnp.float32)
    combined = branch + result
    update = router_gate[:, :, None] * combined * live_weight
    output = jax.vmap(add_rows)(tokens.astype(jnp.float32), local_rows, update).astype(jnp.bfloat16)
    regathered = (
        lax.all_gather(w_qkv, ("head", "blk"), axis=0, tiled=True),
        lax.all_gather(w_out, ("head", "blk"), axis=0, tiled=True),
        lax.all_gather(w_up, ("head", "blk"), axis=0, tiled=True),
        lax.all_gather(w_down, ("head", "blk"), axis=0, tiled=True),
        lax.all_gather(gain_attn, ("head", "blk"), axis=0, tiled=True),
        lax.all_gather(gain_mlp, ("head", "blk"), axis=0, tiled=True),
        lax.all_gather(router, ("head", "blk"), axis=0, tiled=True),
    )
    back_qkv, back_out, back_up, back_down, back_gain_attn, back_gain_mlp, back_router = regathered
    picked_cot = jax.vmap(take_rows)(cotangent, local_rows).astype(jnp.float32) * live_weight
    d_update = router_gate[:, :, None] * picked_cot
    d_logit = jnp.sum(picked_cot * combined, axis=2) * router_gate * (1.0 - router_gate)
    grad_router = jnp.einsum("sc,scd->d", d_logit, picked_exact, precision=lax.Precision.HIGHEST)
    d_result = d_update.astype(jnp.bfloat16)
    d_active = jnp.einsum("scd,id->sci", d_result, back_down, preferred_element_type=jnp.float32)
    d_upper = gelu_back(d_active)[0].astype(jnp.bfloat16)
    d_normed_mlp = jnp.einsum("sci,di->scd", d_upper, back_up, preferred_element_type=jnp.float32)
    d_hidden, grad_gain_mlp = norm_mlp_back(d_normed_mlp)
    d_branch = (d_update + d_hidden).astype(jnp.bfloat16)
    d_attended = jnp.einsum(
        "scd,ed->sce", d_branch, back_out, preferred_element_type=jnp.float32
    ).astype(jnp.bfloat16)
    d_att_tok = lax.all_to_all(d_attended, "head", split_axis=2, concat_axis=1, tiled=True)
    d_att_heads = d_att_tok.reshape(seq_count, slot_rows, local_heads, HDIM)
    delta_tok = jnp.sum(d_att_heads.astype(jnp.float32) * attended_exact, axis=3)
    delta_sq = delta_tok.transpose(0, 2, 1)
    piece = lax.all_gather(key_values, "blk", axis=1, tiled=True)
    piece_rows = piece.shape[1]
    key_pos = cycle_positions
    keys_piece = piece[:, :, 0].reshape(seq_count, piece_rows, local_heads, HDIM)
    values_piece = piece[:, :, 1].reshape(seq_count, piece_rows, local_heads, HDIM)
    scores = (
        jnp.einsum("sqhd,skhd->shqk", queries_heads, keys_piece, preferred_element_type=jnp.float32)
        * scale_factor
    )
    allowed = key_pos[:, None, None, :] <= query_positions[:, None, :, None]
    prob_block = jnp.where(allowed, jnp.exp(scores - log_sum[..., None]), 0.0)
    d_prob = jnp.einsum(
        "sqhd,skhd->shqk", d_att_heads, values_piece, preferred_element_type=jnp.float32
    )
    d_scores = (prob_block * (d_prob - delta_sq[..., None])).astype(jnp.bfloat16)
    d_queries = (
        jnp.einsum("shqk,skhd->sqhd", d_scores, keys_piece, preferred_element_type=jnp.float32)
        * scale_factor
    )
    lse_tok = log_sum.transpose(0, 2, 1)
    lse_high = lse_tok.astype(jnp.bfloat16)
    lse_low = (lse_tok - lse_high.astype(jnp.float32)).astype(jnp.bfloat16)
    delta_high = delta_tok.astype(jnp.bfloat16)
    delta_low = (delta_tok - delta_high.astype(jnp.float32)).astype(jnp.bfloat16)
    query_piece = lax.all_gather(queries_tok, "blk", axis=1, tiled=True)
    dout_piece = lax.all_gather(d_att_tok, "blk", axis=1, tiled=True)
    piece_lse_high = lax.all_gather(lse_high, "blk", axis=1, tiled=True)
    piece_lse_low = lax.all_gather(lse_low, "blk", axis=1, tiled=True)
    piece_delta_high = lax.all_gather(delta_high, "blk", axis=1, tiled=True)
    piece_delta_low = lax.all_gather(delta_low, "blk", axis=1, tiled=True)
    piece_rows = query_piece.shape[1]
    query_heads = query_piece.reshape(seq_count, piece_rows, local_heads, HDIM)
    dout_heads = dout_piece.reshape(seq_count, piece_rows, local_heads, HDIM)
    piece_lse = (piece_lse_high.astype(jnp.float32) + piece_lse_low.astype(jnp.float32)).transpose(
        0, 2, 1
    )
    piece_delta = (
        piece_delta_high.astype(jnp.float32) + piece_delta_low.astype(jnp.float32)
    ).transpose(0, 2, 1)
    scores = (
        jnp.einsum("sqhd,skhd->shqk", query_heads, my_keys, preferred_element_type=jnp.float32)
        * scale_factor
    )
    allowed = query_positions[:, None, None, :] <= cycle_positions[:, None, :, None]
    prob_block = jnp.where(allowed, jnp.exp(scores - piece_lse[..., None]), 0.0)
    grad_values = jnp.einsum(
        "shqk,sqhd->skhd",
        prob_block.astype(jnp.bfloat16),
        dout_heads,
        preferred_element_type=jnp.float32,
    )
    d_prob = jnp.einsum(
        "sqhd,skhd->shqk", dout_heads, my_values, preferred_element_type=jnp.float32
    )
    d_scores = (prob_block * (d_prob - piece_delta[..., None])).astype(jnp.bfloat16)
    grad_keys = (
        jnp.einsum("shqk,sqhd->skhd", d_scores, query_heads, preferred_element_type=jnp.float32)
        * scale_factor
    )
    d_heads = jnp.stack(
        [
            d_queries.astype(jnp.bfloat16),
            grad_keys.astype(jnp.bfloat16),
            grad_values.astype(jnp.bfloat16),
        ],
        axis=2,
    )
    d_heads = d_heads.reshape(seq_count, slot_rows, 3, local_heads * HDIM)
    d_joined = lax.all_to_all(d_heads, "head", split_axis=1, concat_axis=3, tiled=True).reshape(
        seq_count, cap_len, 3 * model_width
    )
    d_normed = jnp.einsum("sce,de->scd", d_joined, back_qkv, preferred_element_type=jnp.float32)
    d_picked_norm, grad_gain_attn = norm_attn_back(d_normed)
    d_picked = (
        d_hidden
        + d_picked_norm
        + d_logit[:, :, None] * back_router.astype(jnp.float32)[None, None, :]
    )
    grad_tokens = jax.vmap(add_rows)(
        cotangent.astype(jnp.float32), local_rows, d_picked * live_weight
    ).astype(jnp.bfloat16)
    grad_qkv = jnp.einsum("scd,sce->de", normed, d_joined, preferred_element_type=jnp.float32)
    grad_out = jnp.einsum("sce,scd->ed", attended, d_branch, preferred_element_type=jnp.float32)
    grad_up = jnp.einsum("scd,sci->di", normed_mlp, d_upper, preferred_element_type=jnp.float32)
    grad_down = jnp.einsum("sci,scd->id", active, d_result, preferred_element_type=jnp.float32)
    owned = (
        lax.psum_scatter(grad_qkv, ("head", "blk"), scatter_dimension=0, tiled=True),
        lax.psum_scatter(grad_out, ("head", "blk"), scatter_dimension=0, tiled=True),
        lax.psum_scatter(grad_up, ("head", "blk"), scatter_dimension=0, tiled=True),
        lax.psum_scatter(grad_down, ("head", "blk"), scatter_dimension=0, tiled=True),
        lax.psum_scatter(grad_gain_attn, ("head", "blk"), scatter_dimension=0, tiled=True),
        lax.psum_scatter(grad_gain_mlp, ("head", "blk"), scatter_dimension=0, tiled=True),
        lax.psum_scatter(grad_router, ("head", "blk"), scatter_dimension=0, tiled=True),
    )
    return (
        output,
        grad_tokens,
        owned[0],
        owned[1],
        owned[2],
        owned[3],
        owned[4],
        owned[5],
        owned[6],
    )


F32, BF16 = jnp.float32, jnp.bfloat16
NN = (((1,), (0,)), ((), ()))
NT = (((1,), (1,)), ((), ()))
TN = (((0,), (0,)), ((), ()))


def mm(left, right, dims=NN):
    return lax.dot_general(left, right, dims, preferred_element_type=F32)


WORK = {
    "attention_back_kernel": 1200000000,
    "attention_kernel": 1200000000,
    "compact_kernel": 10000000000,
    "ff_grads_kernel": 600000000,
    "forward_kernel": 600000000,
    "grads_kernel": 500000000,
    "result_kernel": 800000000,
    "update_kernel": 800000000,
}


def work_of(body):
    return WORK.get(getattr(body, "func", body).__name__, 0)


class Far:
    def __init__(self, item, start=0, count=None, dim=0):
        self.item, self.start, self.count, self.dim = item, start, count, dim

    def shape(self):
        shape = list(self.item.shape)
        if self.count is not None:
            shape[self.dim] = self.count
        return tuple(shape)

    def source(self, ref):
        if self.count is None:
            return ref
        return ref.at[(slice(None),) * self.dim + (pl.ds(self.start, self.count),)]


class Loaded:
    def __init__(self, copy, ref):
        self.copy, self.ref, self.shape, self.waited = copy, ref, ref.shape, False

    def __getitem__(self, index):
        self.wait()
        return self.ref[index]

    def wait(self):
        if not self.waited:
            self.copy.wait()
        self.waited = True


class Stored:
    def __init__(self, copy, ref):
        self.copy, self.ref, self.shape, self.started = copy, ref, ref.shape, False

    def __getitem__(self, index):
        return self.ref[index]

    def __setitem__(self, index, value):
        self.ref[index] = value
        if index is Ellipsis:
            self.start()

    def start(self):
        if not self.started:
            self.copy.start()
        self.started = True


def local_call(body, outs, args, scratch=(), scalars=0, after=()):
    far_in = [a if isinstance(a, Far) else None for a in args]
    far_out = [isinstance(o, Far) for o in outs]
    outs = [o.item if f else o for o, f in zip(outs, far_out)]
    args = [pltpu.with_memory_space_constraint(f.item, pltpu.HBM) if f else a for a, f in zip(args, far_in)]
    shapes = [pltpu.HBM(s, d) if f else jax.ShapeDtypeStruct(s, d) for (s, d), f in zip(outs, far_out)]
    spaces = [pltpu.SMEM] * scalars
    spaces += [pltpu.HBM if f else pltpu.VMEM for f in far_in[scalars:]]
    spaces += [pl.ANY] * len(after)
    stages = []
    for f in far_in:
        if f:
            stages.append(pltpu.VMEM(f.shape(), f.item.dtype))
    stages += [pltpu.VMEM(s, d) for (s, d), f in zip(outs, far_out) if f]
    n_in, n_out, n_far = len(args), len(outs), len(stages)
    first_out = n_in + len(after)
    if n_far:
        stages.append(pltpu.SemaphoreType.DMA((n_far,)))

    def run(*refs):
        ins, results = list(refs[:n_in]), list(refs[first_out : first_out + n_out])
        rest = refs[first_out + n_out :]
        own, stage = rest[: len(scratch)], rest[len(scratch) :]
        at, loads, stores = 0, [], []
        for i, f in enumerate(far_in):
            if f:
                copy = pltpu.make_async_copy(f.source(ins[i]), stage[at], stage[-1].at[at])
                copy.start()
                ins[i] = Loaded(copy, stage[at])
                loads.append(ins[i])
                at += 1
        for i, f in enumerate(far_out):
            if f:
                copy = pltpu.make_async_copy(stage[at], results[i], stage[-1].at[at])
                results[i] = Stored(copy, stage[at])
                stores.append(results[i])
                at += 1
        body(*ins, *results, *own)
        for load in loads:
            load.wait()
        for store in stores:
            store.start()
        for store in stores:
            store.copy.wait()

    return list(
        pl.pallas_call(
            run,
            out_shape=shapes,
            in_specs=[pl.BlockSpec(memory_space=s) for s in spaces],
            out_specs=[
                pl.BlockSpec(memory_space=pltpu.HBM if f else pltpu.VMEM) for f in far_out
            ],
            scratch_shapes=list(scratch) + stages,
            compiler_params=pltpu.CompilerParams(vmem_limit_bytes=32 * 2**20),
            cost_estimate=pl.CostEstimate(
                flops=work_of(body), bytes_accessed=0, transcendentals=0
            ),
        )(*args, *after)
    )


def flips(count):
    return [[(i, i ^ k) for i in range(count)] for k in range(count)]


def send_z(blocks):
    return [lax.ppermute(b, "z", f) for b, f in zip(blocks, flips(lax.axis_size("z"))[1:])]


def send_lines(blocks):
    count = lax.axis_size("y") * lax.axis_size("x")
    return [lax.ppermute(b, ("y", "x"), f) for b, f in zip(blocks, flips(count)[1:])]


def gather_lines(own):
    return [own] + send_lines([own] * (lax.axis_size("y") * lax.axis_size("x") - 1))


def send_c(block):
    return lax.ppermute(block, "c", flips(2)[1])


def gather_group(own):
    lists = [own] + [list(t) for t in zip(*[send_z([o] * (lax.axis_size("z") - 1)) for o in own])]
    blocks = [b for one in lists for b in one]
    return blocks + [send_c(b) for b in blocks]


ORDER = [0, 1, 3, 2, 4, 5, 7, 6]


def shuffle(blocks):
    return [blocks[b] for b in ORDER]


def restore(blocks):
    return [blocks[ORDER.index(b)] for b in range(len(ORDER))]


def half_sum_kernel(near, far, mine, *low):
    for k in range(near.shape[0]):
        total = near[k].astype(F32) + far[k].astype(F32)
        if k == 0:
            mine[...] = total
        else:
            low[k - 1][...] = total.astype(BF16)


def slot_sum_kernel(*refs):
    pairs, (mine, *low) = refs[:4], refs[4:]
    size = pairs[0].shape[1]
    for j in range(2):
        near, far = pairs[2 * j], pairs[2 * j + 1]
        rows = slice(j * size, (j + 1) * size)
        for k in range(near.shape[0]):
            total = near[k].astype(F32) + far[k].astype(F32)
            if k == 0:
                mine[rows] = total
            else:
                low[k - 1][rows] = total.astype(BF16)


def scatter_group(near, far, after=()):
    depth, rows, lanes = near.shape
    outs = [((rows, lanes), F32)] + [((rows, lanes), BF16)] * (depth - 1)
    mine, *low = local_call(half_sum_kernel, outs, (near, send_c(far)), after=after)
    return [mine] + send_z(low)


def add_up(refs):
    total = refs[0][...]
    for ref in refs[1:]:
        total = total + ref[...].astype(F32)
    return total


def xor_order(blocks, index):
    step = 1
    while step < len(blocks):
        swap = (index & step) != 0
        blocks = [jnp.where(swap, blocks[b ^ step], blocks[b]) for b in range(len(blocks))]
        step *= 2
    return blocks


def columns_kernel(dims, w_qkv, w_up, gain_attn, gain_mlp, router, out, vec_s):
    ny, members, nx, ff_rows = dims
    cols = 3 * ny * HDIM
    vec_s[...] = jnp.zeros_like(vec_s)
    for k, vec in enumerate((gain_attn, gain_mlp, router)):
        vec_s[k : k + 1] = vec[...].astype(F32)
    vecs = mm(vec_s[...].astype(BF16), eye_rows(), TN).astype(BF16)
    for g in range(members):
        parts = []
        for t in range(3):
            for y in range(ny):
                at = (t * HEADS + y * members + g) * HDIM
                parts.append(w_qkv[:, at : at + HDIM])
        out[g, :, :cols] = jnp.concatenate(parts, 1)
        out[g, :, cols : cols + 128] = vecs
        for y in range(ny):
            for x in range(nx):
                at = ((y * members + g) * nx + x) * ff_rows
                to = cols + 128 + (y * nx + x) * ff_rows
                out[g, :, to : to + ff_rows] = w_up[:, at : at + ff_rows]


def eye_rows():
    down = lax.broadcasted_iota(jnp.int32, (8, 128), 0)
    return (down == lax.broadcasted_iota(jnp.int32, (8, 128), 1)).astype(F32).astype(BF16)


def as_columns(chosen):
    numbers = chosen[...]
    down = lax.broadcasted_iota(jnp.int32, (numbers.shape[0], 128), 0)
    eye = down == lax.broadcasted_iota(jnp.int32, (numbers.shape[0], 128), 1)
    eye = eye.astype(F32).astype(BF16)
    high = mm((numbers >> 8).astype(F32).astype(BF16), eye, TN)
    low = mm((numbers & 255).astype(F32).astype(BF16), eye, TN)
    return (high * 256.0 + low).astype(jnp.int32)


def pick_kernel(cap, where, chosen, tokens, cot, pick, *refs):
    chosen_t = as_columns(chosen)
    *outs, rows = refs
    seq_count, seg_len = tokens.shape[:2]
    base = where[4] * seg_len
    places = base + lax.broadcasted_iota(jnp.int32, (chosen_t.shape[0], seg_len), 1)
    slots = lax.broadcasted_iota(jnp.int32, (cap, seg_len), 0)
    for s in range(seq_count):
        at = chosen_t[:, s : s + 1]
        present = jnp.sum((at == places).astype(F32), 0, keepdims=True)
        rank = jnp.sum(((at >= base) & (at < places)).astype(F32), 0, keepdims=True)
        hot = jnp.where(rank.astype(jnp.int32) == slots, present, 0.0).astype(BF16)
        pick[s] = hot
        rows[s, :cap] = mm(hot, tokens[s]).astype(BF16)
        rows[s, cap:] = mm(hot, cot[s]).astype(BF16)
    for k, out in enumerate(outs):
        out[...] = rows[where[2] ^ k]


def stack_kernel(cap, *refs):
    *blocks, out = refs
    for k, block in enumerate(blocks):
        for j in range(2):
            to = (j * len(blocks) + k) * cap
            out[to : to + cap] = block[j * cap : (j + 1) * cap]


def eye_tile():
    down = lax.broadcasted_iota(jnp.int32, (16, 128), 0)
    return (down == lax.broadcasted_iota(jnp.int32, (16, 128), 1)).astype(F32).astype(BF16)


def relay_kernel(got, w_out, w_down, first, up):
    members, rows, lanes = got.shape
    half = lanes // 2
    cols = half - 128
    straight = members * cols // half
    fold, end = (members - straight) * rows, straight * rows
    vec = [mm(eye_tile(), got[g, :, cols:half], NT) for g in range(members)]
    vec = jnp.concatenate(vec, 1).astype(BF16)
    size = w_out.shape[0]
    for line in range(first.shape[0]):
        first[line, :end, :cols] = got[:straight, :, :cols].reshape(end, cols)
        for j in range(cols // 128):
            piece = got[straight:, :, j * 128 : (j + 1) * 128].reshape(fold, 128)
            first[line, j * fold : (j + 1) * fold, cols:] = piece
        for j in range(2):
            to = end + j * size
            first[line, to : to + size] = w_out[:, j * half : (j + 1) * half]
        at = end + 2 * size
        first[line, at : at + 16, : members * rows] = vec
        first[line, at : at + 16, members * rows :] = jnp.zeros((16, half - members * rows), BF16)
        first[line, at + 16 :] = w_down[:, :half]
    up[: members * rows] = got[:, :, half:].reshape(members * rows, half)
    up[members * rows :] = w_down[:, half:]


def spread_kernel(dims, where, chosen, spread, token):
    chosen_t = as_columns(chosen)
    token[...] = jnp.zeros_like(token)
    ny, nc, nz, nx, seg_len, cap = dims
    c, z, line = where[0], where[1], where[2]
    routed = chosen_t.shape[0]
    members = nc * nz

    def owner_of(mine):
        return lax.div(mine, jnp.int32(seg_len))

    mine_col = chosen_t[:, 0:1]
    mine_row = chosen[0:1, :]
    for s in range(1, chosen.shape[0]):
        mine_col = jnp.where(line == s, chosen_t[:, s : s + 1], mine_col)
        mine_row = jnp.where(line == s, chosen[s : s + 1, :], mine_row)
    owner, owner_row = owner_of(mine_col), owner_of(mine_row)
    order = lax.broadcasted_iota(jnp.int32, (routed, routed), 0)
    other = lax.broadcasted_iota(jnp.int32, (routed, routed), 1)
    same = (owner == owner_row) & (other < order)
    slot = jnp.sum(same.astype(F32), 1, keepdims=True).astype(jnp.int32)
    ox, rest = lax.rem(owner, jnp.int32(nx)), lax.div(owner, jnp.int32(nx))
    oz, rest = lax.rem(rest, jnp.int32(nz)), lax.div(rest, jnp.int32(nz))
    oc, oy = lax.rem(rest, jnp.int32(nc)), lax.div(rest, jnp.int32(nc))
    cell = (((oc ^ c) * nz + (oz ^ z)) * (ny * nx) + ((oy * nx + ox) ^ line)) * cap + slot
    own = routed // members
    cells = [cell[b * own : (b + 1) * own] for b in range(members)]
    for b, block in enumerate(xor_order(cells, where[3])):
        lanes = lax.broadcasted_iota(jnp.int32, (own, spread.shape[1]), 1)
        spread[b * own : (b + 1) * own] = (block == lanes).astype(F32).astype(BF16)


def kept_pairs(member, routed, own):
    down = lax.broadcasted_iota(jnp.int32, (routed, routed), 0)
    across = lax.broadcasted_iota(jnp.int32, (routed, routed), 1)
    shift = own.bit_length() - 1
    first = ((down >> shift) ^ member) * own + (down & (own - 1))
    second = ((across >> shift) ^ member) * own + (across & (own - 1))
    return second <= first


def probabilities(queries, keys, kept):
    scores = jnp.where(kept, mm(queries, keys, NT) * HDIM ** (-0.5), neg_large)
    top = jnp.max(scores, 1, keepdims=True)
    probs = jnp.where(kept, jnp.exp(scores - top), 0.0)
    return probs, jnp.sum(probs, 1, keepdims=True)


def inverse_rms(values):
    return lax.rsqrt(jnp.mean(values * values, 1, keepdims=True) + epsilon)


def line_rows(blocks, start, out):
    half = out.shape[1] // 2
    size = out.shape[0] // blocks.shape[0]
    for q in range(blocks.shape[0]):
        for j in range(2):
            piece = blocks[q, start + j * size : start + (j + 1) * size]
            out[q * size : (q + 1) * size, j * half : (j + 1) * half] = piece


def own_order_rows(where, blocks, dims, out):
    ny, members, nx, rows = dims
    for k, block in enumerate(blocks):
        line = where[2] ^ k
        y, x = lax.div(line, jnp.int32(nx)), lax.rem(line, jnp.int32(nx))
        for g in range(members):
            to = pl.multiple_of(((y * members + g) * nx + x) * rows, rows)
            out[pl.ds(to, rows)] = block[g * rows : (g + 1) * rows, :]


def natural_rows(got, dims, cols, out):
    ny, members, nx, rows = dims
    straight = members * cols // (cols + 128)
    fold = (members - straight) * rows
    for y in range(ny):
        for g in range(members):
            for x in range(nx):
                q, to = y * nx + x, ((y * members + g) * nx + x) * rows
                if g < straight:
                    out[to : to + rows] = got[q, g * rows : (g + 1) * rows, :cols]
                    continue
                for j in range(cols // 128):
                    at = j * fold + (g - straight) * rows
                    out[to : to + rows, j * 128 : (j + 1) * 128] = got[q, at : at + rows, cols:]


def natural_lanes(got, dims, at):
    ny, members, nx, rows = dims
    pieces = [
        got[y * nx + x, at : at + 16, g * rows : (g + 1) * rows]
        for y in range(ny)
        for g in range(members)
        for x in range(nx)
    ]
    return jnp.concatenate(pieces, 1).astype(F32)[:8]


def compact_kernel(spread, *refs):
    *blocks, picked_o, own_o, cot_o = refs
    blocks = restore(blocks)
    hot = spread[...]
    half = blocks[0].shape[0] // 2
    picked = mm(hot, jnp.concatenate([b[:half] for b in blocks], 0)).astype(BF16)
    picked_o[...] = picked
    own_o[...] = picked[: own_o.shape[0]]
    cot_o[...] = mm(hot, jnp.concatenate([b[half:] for b in blocks], 0)).astype(BF16)


def attention_kernel(dims, members, where, picked_r, qkv_blocks, *outs):
    ny, nx, rows = dims
    normed_o, w_o, wo_o, vecs_o = outs[:4]
    joined_o, att_o, exact_o, probs_o, near_o, far_o = outs[4:]
    heads = ny
    cols = 3 * heads * HDIM
    routed, width = picked_r.shape
    own = routed // members
    picked = picked_r[...].astype(F32)
    natural_rows(qkv_blocks, (ny, members, nx, rows), cols, w_o)
    end = members * rows * cols // (cols + 128)
    line_rows(qkv_blocks, end, wo_o)
    vecs = natural_lanes(qkv_blocks, (ny, members, nx, rows), end + 2 * rows)
    vecs_o[...] = vecs
    normed = (picked * inverse_rms(picked) * vecs[0:1]).astype(BF16)
    normed_o[...] = normed
    joined = mm(normed, w_o[...]).astype(BF16)
    joined_o[...] = joined
    kept = kept_pairs(where[3], routed, own)
    parts = []
    for h in range(heads):
        queries, keys, values = (
            joined[:, (t * heads + h) * HDIM : (t * heads + h + 1) * HDIM] for t in range(3)
        )
        probs, total = probabilities(queries, keys, kept)
        probs_o[h] = probs
        parts.append(mm(probs.astype(BF16), values) / total)
    exact = jnp.concatenate(parts, 1)
    exact_o[...] = exact
    attended = exact.astype(BF16)
    att_o[...] = attended
    branch = mm(attended, wo_o[...]).astype(BF16)
    put_halves(branch, near_o, far_o)


def put_halves(values, near, far):
    depth, own = near.shape[:2]
    for k in range(depth):
        near[k] = values[k * own : (k + 1) * own]
        far[k] = values[(depth + k) * own : (depth + k + 1) * own]


def update_kernel(dims, where, picked, vecs, cot_r, *refs):
    lines, start = dims
    *refs, gate_o, first_o, d_result_o, d_active_o, w_o = refs
    ups, downs = refs[:lines], refs[lines:]
    logit = jnp.sum(picked[...].astype(F32) * vecs[2:3, :], 1, keepdims=True)
    gate = 1.0 / (1.0 + jnp.exp(-logit))
    gate_o[...] = gate
    cot = cot_r[...]
    first_o[...] = cot[: first_o.shape[0]]
    d_result = (gate * cot.astype(F32)).astype(BF16)
    d_result_o[...] = d_result
    half = w_o.shape[1] // 2
    size = w_o.shape[0] // lines
    for down in downs:
        for q in range(lines):
            w_o[q * size : (q + 1) * size, :half] = down[q]
    for k, block in enumerate(ups):
        to = pl.ds(pl.multiple_of((where[2] ^ k) * size, size), size)
        if not downs:
            w_o[to, :half] = block[start : start + size]
        w_o[to, half:] = block[block.shape[0] - size :]
    d_active_o[...] = mm(d_result, w_o[...], NT)


def hidden_kernel(picked, vecs, *refs):
    *terms, hidden_o, normed_o = refs
    hidden = picked[...].astype(F32) + add_up(terms)
    hidden_o[...] = hidden
    normed_o[...] = (hidden * inverse_rms(hidden) * vecs[1:2, :]).astype(BF16)


def forward_kernel(dims, members, where, d_active, *refs):
    lines = dims[0] * dims[2]
    ups, refs = refs[:lines], refs[lines:]
    blocks, (active_o, d_upper_o, near_o, far_o, w_s) = refs[:members], refs[members:]
    own_order_rows(where, ups, dims, w_s)
    normed = jnp.concatenate([b[...] for b in restore(blocks)], 0)
    upper = mm(normed, w_s[...])
    below = 0.5 * (1.0 + lax.erf(upper * (0.5**0.5)))
    active_o[...] = (upper * below).astype(BF16)
    slope = below + upper * jnp.exp(-0.5 * upper * upper) * ((2.0 * math.pi) ** -0.5)
    d_upper = (d_active[...] * slope).astype(BF16)
    d_upper_o[...] = d_upper
    put_halves(mm(d_upper, w_s[...], NT).astype(BF16), near_o, far_o)


def ff_grads_kernel(dims, members, where, active, d_upper, d_result, *refs):
    ny, nx, rows, ff_rows = dims
    blocks, (keep, send, down, up) = refs[:members], refs[members:]
    normed = jnp.concatenate([b[...] for b in restore(blocks)], 0)
    down[...] = mm(active[...], d_result[...], TN).astype(BF16)
    up[...] = mm(normed, d_upper[...], TN).astype(BF16)
    wide = up.shape[1]
    each = ff_rows + members * rows // 2
    for k in range(ny * nx):
        line = where[2] ^ k
        out, start = (keep, send)[k % 2], (k // 2) * each
        y, x = lax.div(line, jnp.int32(nx)), lax.rem(line, jnp.int32(nx))
        piece = down[pl.ds(pl.multiple_of(line * ff_rows, ff_rows), ff_rows)]
        out[start : start + ff_rows] = piece
        for g in range(members):
            at = pl.multiple_of(((y * members + g) * nx + x) * rows, rows)
            half, row = divmod(g * rows, members * rows // 2)
            to = start + ff_rows + row
            out[to : to + rows, half * wide : (half + 1) * wide] = up[pl.ds(at, rows)]


def add_halves_kernel(keep, got, mine, send):
    half = mine.shape[0]
    mine[...] = keep[:half].astype(F32) + got[:half].astype(F32)
    send[...] = (keep[half:].astype(F32) + got[half:].astype(F32)).astype(BF16)


def result_kernel(active, attended, w_down, w_out, cot, gate, spread, logit_o, near_o, far_o):
    combined = mm(active[...], w_down[...]) + mm(attended[...], w_out[...])
    logit = jnp.sum(cot[...].astype(F32) * combined, 1, keepdims=True)
    logit_o[...] = logit * gate[...] * (1.0 - gate[...])
    update = (gate[...] * combined).astype(BF16)
    put_halves(mm(spread[...], update, TN).astype(BF16), near_o, far_o)


def hidden_back_kernel(own, hidden_r, vecs, gate, cot, *refs):
    *terms, d_branch_o, d_hidden_o, gain_o = refs
    d_normed = add_up(terms)
    hidden = hidden_r[...]
    inv = inverse_rms(hidden)
    u = d_normed * vecs[1:2, :]
    d_hidden = inv * u - hidden * (inv * inv * inv * jnp.mean(u * hidden, 1, keepdims=True))
    d_hidden_o[...] = d_hidden
    gain_o[...] = (d_normed * hidden * inv).astype(BF16)
    d_update = gate[:own, :] * cot[...].astype(F32)
    d_branch_o[...] = (d_update + d_hidden).astype(BF16)


def attention_back_kernel(members, where, *refs):
    w_out, joined_r, exact_r, w, vecs, picked_r, logit, d_hidden, spread, probs_r = refs[:10]
    blocks = refs[10 : 10 + members]
    near_o, far_o, d_joined_o, gain_o = refs[10 + members :]
    routed, width = picked_r.shape
    own = routed // members
    heads = joined_r.shape[1] // (3 * HDIM)
    d_branch = jnp.concatenate([b[...] for b in restore(blocks)], 0)
    d_attended = mm(d_branch, w_out[...], NT).astype(BF16)
    joined = joined_r[...]
    exact = exact_r[...]
    grads = [[], [], []]
    for h in range(heads):
        queries, keys, values = (
            joined[:, (t * heads + h) * HDIM : (t * heads + h + 1) * HDIM] for t in range(3)
        )
        probs = probs_r[h]
        total = jnp.sum(probs, 1, keepdims=True)
        d_att = d_attended[:, h * HDIM : (h + 1) * HDIM]
        d_wide = d_att.astype(F32)
        delta = jnp.sum(d_wide * exact[:, h * HDIM : (h + 1) * HDIM], 1, keepdims=True)
        d_scores = (probs / total * (mm(d_att, values, NT) - delta)).astype(BF16)
        grads[0].append(mm(d_scores, keys) * HDIM ** (-0.5))
        grads[1].append(mm(d_scores, queries, TN) * HDIM ** (-0.5))
        grads[2].append(mm(probs.astype(BF16), (d_wide / total).astype(BF16), TN))
    d_joined = jnp.concatenate(grads[0] + grads[1] + grads[2], 1).astype(BF16)
    d_joined_o[...] = d_joined
    d_normed = mm(d_joined, w[...], NT)
    picked = picked_r[...].astype(F32)
    inv = inverse_rms(picked)
    gain_o[...] = (d_normed * picked * inv).astype(BF16)
    v = d_normed * vecs[0:1, :]
    d_picked = inv * v - picked * (inv * inv * inv * jnp.mean(v * picked, 1, keepdims=True))
    d_picked = d_picked + logit[...] * vecs[2:3, :]
    first = d_picked[:own] + d_hidden[...]
    d_picked = jnp.concatenate([first, d_picked[own:]], 0).astype(BF16)
    put_halves(mm(spread[...], d_picked, TN).astype(BF16), near_o, far_o)


def grads_kernel(dims, members, where, normed, d_joined, attended, gain_a, gain_m, *refs):
    ny, nx, rows = dims
    lines = ny * nx
    picked, logit, refs = refs[0], refs[1], refs[2:]
    blocks, sums, (main, vec_s, out) = refs[:members], refs[members : members + lines], refs[-3:]
    cols = d_joined.shape[1]
    routed, width = normed.shape
    own = gain_m.shape[0]
    main[...] = mm(normed[...], d_joined[...], TN).astype(BF16)
    lanes = lax.broadcasted_iota(jnp.int32, (routed, 128), 1)

    def lane(k, count):
        return (lanes[:count] == k).astype(F32)

    vec = mm(lane(0, routed).astype(BF16), gain_a[...], TN)
    vec = vec + mm(lane(1, own).astype(BF16), gain_m[...], TN)
    high = logit[...].astype(BF16)
    low = (logit[...] - high.astype(F32)).astype(BF16)
    vec = vec + mm((lane(2, routed) * high.astype(F32)).astype(BF16), picked[...], TN)
    vec = vec + mm((lane(2, routed) * low.astype(F32)).astype(BF16), picked[...], TN)
    vec_s[...] = jnp.zeros_like(vec_s)
    for y in range(ny):
        for x in range(nx):
            ats = [((y * members + g) * nx + x) * rows for g in range(members)]
            pieces = [vec[:16, at : at + rows] for at in ats]
            vec_s[y * nx + x, :, : members * rows] = jnp.concatenate(pieces, 1).astype(BF16)
    out[...] = mm(attended[...], jnp.concatenate([b[...] for b in restore(blocks)], 0), TN).astype(BF16)
    straight = members * cols // (cols + 128)
    fold = (members - straight) * rows
    half, end = width // 2, straight * rows
    for k in range(lines):
        line = where[2] ^ k
        y, x = lax.div(line, jnp.int32(nx)), lax.rem(line, jnp.int32(nx))
        for g in range(members):
            at = pl.multiple_of(((y * members + g) * nx + x) * rows, rows)
            if g < straight:
                sums[k][g * rows : (g + 1) * rows, :cols] = main[pl.ds(at, rows)]
                continue
            for j in range(cols // 128):
                to = j * fold + (g - straight) * rows
                piece = main[pl.ds(at, rows), j * 128 : (j + 1) * 128]
                sums[k][to : to + rows, cols:] = piece
        at = pl.multiple_of(line * rows, rows)
        for j in range(2):
            piece = out[pl.ds(at, rows), j * half : (j + 1) * half]
            sums[k][end + j * rows : end + (j + 1) * rows, :] = piece
        sums[k][end + 2 * rows :, :] = vec_s[line]


def join_slots_kernel(cap, lines, *refs):
    terms, outs = refs[:-lines], refs[-lines:]
    total = add_up(terms).astype(BF16)
    for j in range(2):
        for k in range(lines):
            at = (j * lines + k) * cap
            outs[k][j * cap : (j + 1) * cap] = total[at : at + cap]


def place_kernel(cap, lines, where, pick, tokens, cot, *refs):
    blocks, (out_o, grad_o, got) = refs[:lines], refs[lines:]
    for k, block in enumerate(blocks):
        got[where[2] ^ k] = block[...]
    for s in range(tokens.shape[0]):
        hot = pick[s]
        out_o[s] = (tokens[s].astype(F32) + mm(hot, got[s, :cap], TN)).astype(BF16)
        grad_o[s] = (cot[s].astype(F32) + mm(hot, got[s, cap:], TN)).astype(BF16)


def line_sums_kernel(dims, where, mine, got, *refs):
    members, rows, ff_rows = dims
    *parts, near_o, far_o, out_o, down_o, send = refs
    cols = parts[0].shape[1] - 128
    straight = members * cols // (cols + 128)
    fold = (members - straight) * rows
    end = straight * rows
    wide = mine.shape[1] // 2
    ff = mine[...] + got[...].astype(F32)
    up = ff[ff_rows:]
    main = parts[0][...].astype(F32)
    for part in parts[1:]:
        main = main + part[...].astype(F32)
    vec = main[end + 2 * rows :]
    high = vec.astype(BF16)
    low = (vec - high.astype(F32)).astype(BF16)
    down = lax.broadcasted_iota(jnp.int32, (16, 128), 0)
    eye = (down == lax.broadcasted_iota(jnp.int32, (16, 128), 1)).astype(F32).astype(BF16)
    for g in range(members):
        if g < straight:
            block = main[g * rows : (g + 1) * rows, :cols]
        else:
            tos = [j * fold + (g - straight) * rows for j in range(cols // 128)]
            block = jnp.concatenate([main[to : to + rows, cols:] for to in tos], 1)
        send[g, :, :cols] = block.astype(BF16)
        at = slice(g * rows, (g + 1) * rows)
        column = mm(high[:, at], eye, TN) + mm(low[:, at], eye, TN)
        send[g, :, cols : cols + 128] = column.astype(BF16)
        half, row = divmod(g * rows, members * rows // 2)
        piece = up[row : row + rows, half * wide : (half + 1) * wide]
        send[g, :, cols + 128 :] = piece.astype(BF16)
    depth = near_o.shape[0]
    for k in range(depth):
        near_o[k] = send[where[3] ^ k]
        far_o[k] = send[where[3] ^ (depth + k)]
    out_o[...] = jnp.concatenate([main[end : end + rows], main[end + rows : end + 2 * rows]], 1)
    down_o[...] = ff[:ff_rows]


def pair_kernel(near, far, *outs):
    rows = near.shape[1]
    for k, out in enumerate(outs):
        out[:rows] = near[k]
        out[rows:] = far[k]


def unpack_kernel(dims, where, *refs):
    ny, members, nx, ff_rows = dims
    depth = members // 2
    pairs, (qkv_o, up_o, *vec_o, got) = refs[:depth], refs[depth:]
    rows = got.shape[1]
    for k, pair in enumerate(pairs):
        got[where[3] ^ k] = pair[:rows]
        got[where[3] ^ (depth + k)] = pair[rows:]
    cols = 3 * ny * HDIM
    for t in range(3):
        for y in range(ny):
            from_ = (t * ny + y) * HDIM
            row = [got[g, :, from_ : from_ + HDIM] for g in range(members)]
            at = (t * HEADS + y * members) * HDIM
            qkv_o[:, at : at + members * HDIM] = jnp.concatenate(row, 1).astype(F32)
    for y in range(ny):
        for g in range(members):
            for x in range(nx):
                at = ((y * members + g) * nx + x) * ff_rows
                from_ = cols + 128 + (y * nx + x) * ff_rows
                up_o[:, at : at + ff_rows] = got[g, :, from_ : from_ + ff_rows].astype(F32)
    vec = got[0, :, cols : cols + 128].astype(F32)
    for g in range(1, members):
        vec = vec + got[g, :, cols : cols + 128].astype(F32)
    high = vec.astype(BF16)
    low = (vec - high.astype(F32)).astype(BF16)
    vec = mm(eye_rows(), high, NT) + mm(eye_rows(), low, NT)
    for k, out in enumerate(vec_o):
        out[...] = vec[k : k + 1]


def grouped(
    tokens, chosen, w_qkv, w_out, w_up, w_down, gain_attn, gain_mlp, router, cotangent
):
    ny, nc, nz, nx = (lax.axis_size(a) for a in ("y", "c", "z", "x"))
    y, c, z, x = (lax.axis_index(a) for a in ("y", "c", "z", "x"))
    seq_count, seg_len, width = tokens.shape
    cap = seg_len // 4
    routed = chosen.shape[1]
    members, lines = nc * nz, ny * nx
    member, line = c * nz + z, y * nx + x
    shard = ((y * nc + c) * nz + z) * nx + x
    rows, ff_rows = w_qkv.shape[0], w_down.shape[0]
    heads = HEADS // members
    own = routed // members
    cols, wide = 3 * heads * HDIM, lines * ff_rows
    where = jnp.stack([c, z, line, member, shard]).astype(jnp.int32)
    block = (own, width)
    slot_block = (2 * cap, width)
    halves = [((nz, own, width), BF16)] * 2
    slot_halves = [((nz, lines * cap, width), BF16)] * 2

    pick, *picked_rows = local_call(
        partial(pick_kernel, cap),
        [Far(((seq_count, cap, seg_len), BF16))] + [(slot_block, BF16)] * lines,
        (where, chosen, tokens, cotangent),
        scratch=[pltpu.VMEM((seq_count, 2 * cap, width), BF16)],
        scalars=1,
    )
    line_slots = picked_rows[:1] + send_lines(picked_rows[1:])
    hot, token = local_call(
        partial(spread_kernel, (ny, nc, nz, nx, seg_len, cap)),
        [Far(((routed, members * lines * cap), BF16)), ((8, 128), F32)],
        (where, chosen),
        scalars=1,
    )
    spread = Far(hot)
    (line_slots,) = local_call(
        partial(stack_kernel, cap), [((2 * lines * cap, width), BF16)], line_slots, after=(token,)
    )
    slots = gather_group([line_slots])

    vecs = [v.reshape(1, rows) for v in (gain_attn, gain_mlp, router)]
    (columns,) = local_call(
        partial(columns_kernel, (ny, members, nx, ff_rows)),
        [((members, rows, cols + 128 + wide), BF16)],
        tuple(Far(v) for v in (w_qkv, w_up, *vecs)),
        scratch=[pltpu.VMEM((8, rows), F32)],
    )
    got_cols = lax.all_to_all(columns, ("c", "z"), 0, 0, tiled=True)
    half = width // 2
    base = members * rows * cols // (cols + 128) + 2 * rows + 16
    first, up = local_call(
        relay_kernel,
        [
            Far(((lines, base + ff_rows, half), BF16)),
            Far(((members * rows + ff_rows, half), BF16)),
        ],
        (got_cols, w_out, w_down),
        after=(line_slots,),
    )
    first = lax.all_to_all(first, ("y", "x"), 0, 0, tiled=True)
    got_down = (Far(first, base, ff_rows, 1),)
    got_up = gather_lines(up)

    picked, picked_own, cot = local_call(
        compact_kernel,
        [((routed, width), BF16), (block, BF16), ((routed, width), BF16)],
        (spread, *shuffle(slots)),
    )
    normed, full_qkv, full_out, full_vecs, joined, attended, exact, probs, near, far = local_call(
        partial(attention_kernel, (ny, nx, rows), members),
        [
            ((routed, width), BF16),
            ((width, cols), BF16),
            ((heads * HDIM, width), BF16),
            ((8, width), F32),
            ((routed, cols), BF16),
            ((routed, heads * HDIM), BF16),
            ((routed, heads * HDIM), F32),
            ((heads, routed, routed), F32),
        ]
        + halves,
        (where, picked, Far(first, 0, base, 1)),
        scalars=1,
    )
    terms = scatter_group(near, far)
    gate, cot_own, d_result, d_active, full_down = local_call(
        partial(update_kernel, (lines, members * rows)),
        [
            ((routed, 1), F32),
            (block, BF16),
            ((routed, width), BF16),
            ((routed, wide), F32),
            ((wide, width), BF16),
        ],
        (where, picked, full_vecs, cot, *got_up, *got_down),
        scalars=1,
    )
    hidden, normed_own = local_call(
        hidden_kernel,
        [(block, F32), (block, BF16)],
        (picked_own, full_vecs, *terms),
    )
    normed_mlp = gather_group([normed_own])

    active, d_upper, near, far = local_call(
        partial(forward_kernel, (ny, members, nx, rows), members),
        [((routed, wide), BF16)] * 2 + halves,
        (where, d_active, *got_up, *shuffle(normed_mlp)),
        scratch=[pltpu.VMEM((width, wide), BF16)],
        scalars=1,
    )
    terms = scatter_group(near, far)
    half_rows = 2 * (ff_rows + members * rows // 2)
    ff_keep, ff_send = local_call(
        partial(ff_grads_kernel, (ny, nx, rows, ff_rows), members),
        [((half_rows, width), BF16)] * 2,
        (where, active, d_upper, d_result, *shuffle(normed_mlp)),
        scratch=[pltpu.VMEM((wide, width), BF16), pltpu.VMEM((width, wide), BF16)],
        scalars=1,
    )
    ff_got = lax.ppermute(ff_send, "x", flips(nx)[1])
    logit, up_near, up_far = local_call(
        result_kernel,
        [((routed, 1), F32)] + slot_halves,
        (active, attended, full_down, full_out, cot, gate, spread),
    )
    d_branch_own, d_hidden, gain_m = local_call(
        partial(hidden_back_kernel, own),
        [(block, BF16), (block, F32), (block, BF16)],
        (hidden, full_vecs, gate, cot_own, *terms),
        after=(ff_send, logit),
    )
    d_branch = gather_group([d_branch_own])
    up_far = send_c(up_far)
    ff_mine, ff_send = local_call(
        add_halves_kernel,
        [((half_rows // 2, width), F32), ((half_rows // 2, width), BF16)],
        (ff_keep, ff_got),
    )
    ff_got = lax.ppermute(ff_send, "y", flips(ny)[1])

    near, far, d_joined, gain_a = local_call(
        partial(attention_back_kernel, members),
        slot_halves + [((routed, cols), BF16), ((routed, width), BF16)],
        (where, full_out, joined, exact, full_qkv, full_vecs, picked)
        + (logit, d_hidden, spread, probs, *shuffle(d_branch)),
        scalars=1,
    )
    far = send_c(far)
    parts = local_call(
        partial(grads_kernel, (ny, nx, rows), members),
        [((members * rows * cols // (cols + 128) + 2 * rows + 16, cols + 128), BF16)] * lines,
        (where, normed, d_joined, attended, gain_a, gain_m, picked, logit, *shuffle(d_branch)),
        scratch=[
            pltpu.VMEM((width, cols), BF16),
            pltpu.VMEM((lines, 16, cols + 128), BF16),
            pltpu.VMEM((heads * HDIM, width), BF16),
        ],
        scalars=1,
    )
    parts = parts[:1] + send_lines(parts[1:])
    both_slots = (2 * lines * cap, width)
    mine, *low = local_call(
        slot_sum_kernel,
        [(both_slots, F32)] + [(both_slots, BF16)] * (nz - 1),
        (up_near, up_far, near, far),
        after=(ff_mine,),
    )
    back_rows = local_call(
        partial(join_slots_kernel, cap, lines),
        [(slot_block, BF16)] * lines,
        [mine] + send_z(low),
    )
    back_rows = back_rows[:1] + send_lines(back_rows[1:])
    row_width = cols + 128 + wide
    near, far, grad_out, grad_down = local_call(
        partial(line_sums_kernel, (members, rows, ff_rows)),
        [((nz, rows, row_width), BF16)] * 2 + [((rows, width), F32), ((ff_rows, width), F32)],
        (where, ff_mine, ff_got, *parts),
        scratch=[pltpu.VMEM((members, rows, row_width), BF16)],
        scalars=1,
        after=back_rows[:1],
    )
    pairs = local_call(pair_kernel, [((2 * rows, row_width), BF16)] * nz, (near, send_c(far)))
    pairs = pairs[:1] + send_z(pairs[1:])
    output, grad_tokens = local_call(
        partial(place_kernel, cap, lines),
        [(tokens.shape, BF16), (tokens.shape, BF16)],
        (where, Far(pick), tokens, cotangent, *back_rows),
        scratch=[pltpu.VMEM((seq_count, 2 * cap, width), BF16)],
        scalars=1,
    )
    grad_qkv, grad_up, *grad_vecs = local_call(
        partial(unpack_kernel, (ny, members, nx, ff_rows)),
        [(w_qkv.shape, F32), (w_up.shape, F32)] + [((1, rows), F32)] * 3,
        (where, *pairs),
        scratch=[pltpu.VMEM((members, rows, row_width), BF16)],
        scalars=1,
    )
    return (
        output,
        grad_tokens,
        grad_qkv,
        grad_out,
        grad_up,
        grad_down,
        *(v.reshape(rows) for v in grad_vecs),
    )


def fits(mesh):
    head_count, block_count = mesh.devices.shape
    members = (head_count // 2) * (block_count // 2)
    power = members & (members - 1) == 0
    return power and head_count == 4 and HEADS == 2 * members


def solution(mesh):
    if fits(mesh):
        head_count, block_count = mesh.devices.shape
        devices = mesh.devices.reshape(2, head_count // 2, block_count // 2, 2)
        mesh = jax.sharding.Mesh(devices, ("y", "c", "z", "x"))
        body, all_axes = grouped, ("y", "c", "z", "x")
    else:
        body, all_axes = shards, ("head", "blk")
    seqs, mats, vecs = P(None, all_axes, None), P(all_axes, None), P(all_axes)
    in_specs = (seqs, P(), mats, mats, mats, mats, vecs, vecs, vecs, seqs)
    out_specs = (seqs, seqs, mats, mats, mats, mats, vecs, vecs, vecs)
    return jax.shard_map(body, mesh=mesh, in_specs=in_specs, out_specs=out_specs, check_vma=False)
```
